32 devices in a mesh: site: 4 (over x, core), sec: 8 (over z, y).
Axes of the slice: x: 2, y: 2, z: 4, core: 2. Of those that a mesh axis runs over, the one named last changes fastest.
Arguments:
- left_iso: bfloat16 [4, 4, 8, 128, 128], P('site', None, 'sec'), may hold values from -0.03125 to 0.03125
- right_iso: bfloat16 [4, 4, 8, 128, 128], P('site', None, 'sec'), may hold values from -0.03125 to 0.03125
- centre: bfloat16 [4, 8, 128, 128], P('site', 'sec'), may hold values from -6 to 6
- left_env: bfloat16 [4, 42, 8, 128, 128], P('site', None, 'sec'), may hold values from -6 to 6
- right_env: bfloat16 [4, 42, 8, 128, 128], P('site', None, 'sec'), may hold values from -6 to 6
- mpo: bfloat16 [4, 42, 42, 4, 4], P('site'), may hold values from -1 to 1
- pattern: int32 [4, 42, 42], P('site'), may hold values from 0 to 1, as said below
Outputs:
- new_left: bfloat16 [4, 4, 8, 128, 128], P('site', None, 'sec')
- energy: float32 [4], P('site')
The draws below stay inside these ranges and needn't reach their ends.
Inputs may be any that keep to these rules, and one draw needn't show every extreme that they name: At every site n, pattern[n][0][0] is 1 and every other entry of row 0 and of column 0 is 0.
All inputs are finite; a program needn't handle non-finite values.
Results may differ from the reference program's by a relative error of at most 0.015.
Values may be sent and summed in bfloat16 or wider, within the bound.
No kernel may reach another device: no remote copies, remote signals or barrier semaphores. Data moves between devices by JAX's collectives and lax.ppermute only.
A program may use at most 128 MiB of HBM per device.

```python
import jax
import jax.numpy as jnp
import numpy as np
from jax import lax

CHANNELS = 42
STATES = 4
BLOCK = 128
SECTOR_DEV = 1
SECTORS = 8
SITES = 4
ENV_STEPS = 2
DESCENT = 2
POLAR = 6


def environment_blocks(key):
    noise = jnp.clip(jax.random.normal(key, (SITES, CHANNELS, SECTORS, BLOCK, BLOCK), jnp.float32), -5.0, 5.0)
    level_key = jax.random.fold_in(key, 11)
    levels = jax.random.uniform(level_key, (SITES, 1, SECTORS, BLOCK, 1), jnp.float32, 0.5, 1.5)
    diagonal = (jnp.arange(BLOCK)[:, None] == jnp.arange(BLOCK)[None, :]).astype(jnp.float32)
    first = (jnp.arange(CHANNELS) == 0).astype(jnp.float32)[None, :, None, None, None]
    values = noise * (1.0 - 0.8 * first) + 0.7 * first * levels * diagonal
    return values.astype(jnp.bfloat16)


def draw_left_env(key, part):
    key = jax.random.fold_in(key, 3)
    return environment_blocks(key)


def draw_right_env(key, part):
    key = jax.random.fold_in(key, 5)
    return environment_blocks(key)


def draw_mpo(key, part):
    key = jax.random.fold_in(key, 7)
    base_key = jax.random.fold_in(key, 1)
    level_key = jax.random.fold_in(key, 2)
    base = jnp.clip(jax.random.normal(base_key, (SITES, CHANNELS, CHANNELS, STATES, STATES), jnp.float32), -5.0, 5.0)
    base = base * (CHANNELS * STATES) ** (-0.5)
    levels = jax.random.uniform(level_key, (SITES, 1, 1, STATES, 1), jnp.float32, -0.7, -0.3)
    channel_in = jnp.arange(CHANNELS)[:, None, None, None]
    channel_out = jnp.arange(CHANNELS)[None, :, None, None]
    state_out = jnp.arange(STATES)[None, None, :, None]
    state_in = jnp.arange(STATES)[None, None, None, :]
    corner = (channel_in == 0) & (channel_out == 0) & (state_out == state_in)
    return jnp.where(corner[None], levels, base).astype(jnp.bfloat16)


def draw_pattern(key, part):
    key = jax.random.fold_in(key, 9)
    random_bits = jax.random.randint(key, (SITES, CHANNELS, CHANNELS), 0, 2).astype(jnp.int32)
    channel_in = jnp.arange(CHANNELS)[:, None]
    channel_out = jnp.arange(CHANNELS)[None, :]
    border = (channel_in == 0) | (channel_out == 0)
    corner = ((channel_in == 0) & (channel_out == 0)).astype(jnp.int32)
    return jnp.where(border[None], corner[None], random_bits).astype(jnp.int32)


def shard_levels(key, shape, shards, least, high):
    level, own = 1.0, jax.random.fold_in(key, 6)
    for position, parts in shards:
        steps = jnp.exp(jax.random.uniform(jax.random.fold_in(own, position), (parts,), jnp.float32, least / len(shards), high / len(shards)))
        level = level * jnp.repeat(steps, shape[position] // parts).reshape([-1 if axis == position else 1 for axis in range(len(shape))])
    return level


def scatter_about(rng, shape, scale, limit, pieces=(), held_as=jnp.bfloat16):
    entries = jax.random.normal(rng, shape, jnp.float32) * scale
    if len(pieces) > 0:
        entries = shard_levels(rng, shape, pieces, -0.22, 0.18) * entries
    return jnp.clip(entries, min=-limit, max=limit).astype(held_as)


def setup_inputs(seed: int = 0) -> dict:
    key_of = jax.random.split(jax.random.key(seed), 8)
    left_iso = scatter_about(key_of[0], (SITES, STATES, SECTORS, BLOCK, BLOCK), (STATES * BLOCK * 64) ** -0.5, 0.03125, ((0, 4), (2, 8)))
    right_iso = scatter_about(key_of[1], (SITES, STATES, SECTORS, BLOCK, BLOCK), (STATES * BLOCK * 64) ** -0.5, 0.03125, ((0, 4), (2, 8)))
    centre = scatter_about(key_of[2], (SITES, SECTORS, BLOCK, BLOCK), 1.0, 6.0, ((0, 4), (1, 8)))
    left_env = draw_left_env(jax.random.fold_in(key_of[7], 71), 0)
    right_env = draw_right_env(jax.random.fold_in(key_of[7], 71), 0)
    mpo = draw_mpo(jax.random.fold_in(key_of[7], 71), 0)
    pattern = draw_pattern(jax.random.fold_in(key_of[7], 71), 0)
    return dict(left_iso=left_iso, right_iso=right_iso, centre=centre, left_env=left_env, right_env=right_env, mpo=mpo, pattern=pattern)


TINY = 1e-06
HIGHEST = lax.Precision.HIGHEST
CHARGE_STEPS = (0, 1, -1, 2, -2)

def to_float(array):
    return array.astype(jnp.float32)

def roll_sectors(array, amount, axis):
    return jnp.roll(array, -amount, axis=axis)

def class_rolled(tensor, axis):
    copies = jnp.stack([roll_sectors(tensor, charge_step * SECTOR_DEV, axis) for charge_step in CHARGE_STEPS])
    return copies[np.arange(CHANNELS) % len(CHARGE_STEPS)]

def charge_mask():
    charge = np.array([CHARGE_STEPS[channel % 5] for channel in range(CHANNELS)]) * SECTOR_DEV
    state_shift = np.arange(STATES) * SECTOR_DEV
    balance = charge[:, None, None, None] + state_shift[None, None, None, :] - state_shift[None, None, :, None] - charge[None, :, None, None]
    return jnp.asarray((balance % SECTORS == 0).astype(np.float32)).astype(jnp.bfloat16)

def left_transfer(environment, isometry, weights):
    rolled_iso = class_rolled(isometry, 1)
    mixed_block = jnp.einsum('wkxy,wtkyz->wtkxz', to_float(environment), to_float(rolled_iso)).astype(jnp.bfloat16)
    gathered = jnp.einsum('wvst,wtkxz->vskxz', to_float(weights), to_float(mixed_block)).astype(jnp.bfloat16)
    summed = jnp.zeros(environment.shape, jnp.float32)
    for state_index in range(STATES):
        iso_part = roll_sectors(isometry[state_index], -state_index * SECTOR_DEV, 0)
        gathered_part = roll_sectors(gathered[:, state_index], -state_index * SECTOR_DEV, 1)
        summed = summed + jnp.einsum('kxy,vkxz->vkyz', to_float(iso_part), to_float(gathered_part))
    return summed

def right_transfer(environment, isometry, weights):
    stacked_env = jnp.stack([roll_sectors(environment, state_index * SECTOR_DEV, 1) for state_index in range(STATES)], 1)
    mixed_block = jnp.einsum('vtkxy,tkzy->vtkxz', to_float(stacked_env), to_float(isometry)).astype(jnp.bfloat16)
    gathered = jnp.einsum('wvst,vtkxz->wskxz', to_float(weights), to_float(mixed_block)).astype(jnp.bfloat16)
    rolled_iso = class_rolled(isometry, 1)
    return jnp.einsum('wskyx,wskxz->wkyz', to_float(rolled_iso), to_float(gathered))

def apply_operator(left_part, right_rolled, vector, weights):
    rolled_vec = class_rolled(vector, 1)
    mixed_block = jnp.einsum('wkxy,wtkyz->wtkxz', to_float(left_part), to_float(rolled_vec)).astype(jnp.bfloat16)
    gathered = jnp.einsum('wvst,wtkxz->vskxz', to_float(weights), to_float(mixed_block)).astype(jnp.bfloat16)
    return jnp.einsum('vskxz,svkzy->skxy', to_float(gathered), to_float(right_rolled))

def normalized(raw_env):
    scale_factor = lax.rsqrt(jnp.sum(raw_env * raw_env) / raw_env.size + TINY)
    return (raw_env * scale_factor).astype(jnp.bfloat16)

def reference(left_iso, right_iso, centre, left_env, right_env, mpo, pattern):
    allowed = charge_mask()
    weights = [mpo[site_index] * pattern[site_index][:, :, None, None].astype(jnp.bfloat16) * allowed for site_index in range(SITES)]
    left_states = [left_env[site_index] for site_index in range(SITES)]
    right_states = [right_env[site_index] for site_index in range(SITES)]
    for turn_index in range(ENV_STEPS):
        left_next = [normalized(left_transfer(left_states[site_index], left_iso[site_index], weights[site_index])) for site_index in range(SITES)]
        right_next = [normalized(right_transfer(right_states[site_index], right_iso[site_index], weights[site_index])) for site_index in range(SITES)]
        left_states = [left_next[(site_index - 1) % SITES] for site_index in range(SITES)]
        right_states = [right_next[(site_index + 1) % SITES] for site_index in range(SITES)]
    new_lefts = []
    energies = []
    for site_index in range(SITES):
        centre_rolled = jnp.stack([roll_sectors(centre[site_index], state_index * SECTOR_DEV, 0) for state_index in range(STATES)])
        vector = jnp.einsum('skxy,skyz->skxz', to_float(left_iso[site_index]), to_float(centre_rolled))
        right_rolled = jnp.stack([roll_sectors(right_states[site_index], state_index * SECTOR_DEV, 1) for state_index in range(STATES)])
        energy = jnp.zeros((), jnp.float32)
        for turn_index in range(DESCENT):
            applied = apply_operator(left_states[site_index], right_rolled, vector.astype(jnp.bfloat16), weights[site_index])
            correlation = jnp.sum(vector * applied)
            weight_sq = jnp.sum(vector * vector)
            energy = correlation / (weight_sq + TINY)
            residual = applied - energy * vector
            residual_sq = jnp.sum(residual * residual)
            vector = vector - 0.5 * jnp.sqrt(weight_sq / (residual_sq + TINY)) * residual
        centre_float = to_float(centre[site_index])
        scaled_vec = vector * lax.rsqrt(jnp.sum(vector * vector) + TINY)
        polar_vec = jnp.stack([roll_sectors(scaled_vec[state_index], -state_index * SECTOR_DEV, 0) for state_index in range(STATES)])
        polar_centre = centre_float * lax.rsqrt(jnp.sum(centre_float * centre_float) + TINY)
        for turn_index in range(POLAR):
            gram_matrix = jnp.einsum('skxy,skxz->kyz', polar_vec, polar_vec, precision=HIGHEST)
            polar_vec = 1.5 * polar_vec - 0.5 * jnp.einsum('skxy,kyz->skxz', polar_vec, gram_matrix, precision=HIGHEST)
            gram_centre = jnp.einsum('kxy,kxz->kyz', polar_centre, polar_centre, precision=HIGHEST)
            polar_centre = 1.5 * polar_centre - 0.5 * jnp.einsum('kxy,kyz->kxz', polar_centre, gram_centre, precision=HIGHEST)
        column_left = jnp.einsum('skxy,kzy->skxz', polar_vec, polar_centre, precision=HIGHEST).astype(jnp.bfloat16)
        new_lefts.append(jnp.stack([roll_sectors(column_left[state_index], state_index * SECTOR_DEV, 0) for state_index in range(STATES)]))
        energies.append(energy)
    return (jnp.stack(new_lefts), jnp.stack(energies))
```

```python
import functools

import jax
import jax.numpy as jnp
import numpy as np
from jax import lax
from jax.experimental import pallas as pl
from jax.experimental.pallas import tpu as pltpu
from jax.sharding import PartitionSpec as P

ENV_STEPS = 2
DESCENT = 2
POLAR = 6

TINY = 1e-06
HIGHEST = lax.Precision.HIGHEST
CHARGE_STEPS = (0, 1, -1, 2, -2)
CLASSES = len(CHARGE_STEPS)
BOTH = ("site", "sec")
VMEM_LIMIT = 44 * 1024 * 1024


def ring_order(half):
    up = (half + 1) // 2
    return list(range(up)) + list(range(half - 1, up - 1, -1))


class Places:
    def __init__(self, sites, secs):
        self.sites, self.secs = sites, secs
        self.half = secs // 2
        self.order = ring_order(self.half)

    def home(self, site, sector):
        return (site % self.sites) * self.secs + sector % self.secs

    def slot(self, chain, sector):
        chain, sector = chain % self.sites, sector % self.secs
        place = (chain % 2) * self.half + self.order[sector // 2]
        return (chain // 2 * 2 + sector % 2) * self.secs + place

    def pairs(self, source, target):
        return [
            (source(chain, sector), target(chain, sector))
            for chain in range(self.sites)
            for sector in range(self.secs)
        ]

    def fetch(self, x, site_by=0, sec_by=0):
        return lax.ppermute(
            x, BOTH, self.pairs(lambda g, k: self.home(g + site_by, k + sec_by), self.slot)
        )

    def send_home(self, x, site_by, sec_by):
        return lax.ppermute(
            x, BOTH, self.pairs(self.slot, lambda g, k: self.home(g + site_by, k + sec_by))
        )

    def ahead(self, x, by, chain_by=0):
        return lax.ppermute(
            x, BOTH, self.pairs(lambda g, k: self.slot(g + chain_by, k + by), self.slot)
        )

    def partner(self, x, bit):
        return lax.ppermute(x, BOTH, self.pairs(lambda g, k: self.slot(g, k ^ bit), self.slot))

    def my_chain(self):
        return lax.axis_index("site") // 2 * 2 + lax.axis_index("sec") // self.half

    def my_sector(self):
        positions = np.argsort(np.array(self.order))
        position = jnp.asarray(positions, jnp.int32)[lax.axis_index("sec") % self.half]
        return 2 * position + lax.axis_index("site") % 2

    def collect(self, values):
        sector = self.my_sector()
        table = values[None]
        bit = 1
        while bit < self.secs:
            other = self.partner(table, bit)
            first = (sector & bit) == 0
            table = jnp.where(
                first, jnp.concatenate([table, other]), jnp.concatenate([other, table])
            )
            bit *= 2
        return table


def padded(rows):
    return -(-rows // 16) * 16


def mix_channels(weight_ref, mixed_ref, gathered_ref, block):
    rows = weight_ref.shape[0]
    depth = weight_ref.shape[1]

    def pair(index, carry):
        first = 2 * index
        parts = [
            mixed_ref[pl.ds(first + part, depth, stride=block), :] for part in range(2)
        ]
        operand = jnp.concatenate(parts, axis=1).astype(jnp.bfloat16)
        product = jnp.dot(weight_ref[...], operand, preferred_element_type=jnp.float32)
        for part in range(2):
            gathered_ref[pl.ds(first + part, rows, stride=block), :] = product[
                :, part * block : (part + 1) * block
            ]
        return carry

    lax.fori_loop(0, block // 2, pair, 0, unroll=4)


def clear_padding(mixed_ref, used):
    if mixed_ref.shape[0] > used:
        mixed_ref[pl.ds(used, mixed_ref.shape[0] - used), :] = jnp.zeros(
            (mixed_ref.shape[0] - used, mixed_ref.shape[1]), jnp.float32
        )


def mix_left(env_ref, tensor_ref, mixed_ref):
    channels, block, _ = env_ref.shape
    states = tensor_ref.shape[1]
    for cls in range(CLASSES):
        right = jnp.concatenate([tensor_ref[cls, t] for t in range(states)], axis=1)
        count = len(range(cls, channels, CLASSES))

        def one(index, carry):
            channel = cls + CLASSES * index
            product = jnp.dot(env_ref[channel], right, preferred_element_type=jnp.float32)
            for t in range(states):
                start = pl.multiple_of((t * channels + channel) * block, block)
                mixed_ref[pl.ds(start, block), :] = product[:, t * block : (t + 1) * block]
            return carry

        lax.fori_loop(0, count, one, 0, unroll=True)


def left_kernel(env_ref, tensor_ref, weight_ref, out_ref, mixed_ref, gathered_ref):
    channels, block, _ = env_ref.shape
    states = tensor_ref.shape[1]
    clear_padding(mixed_ref, states * channels * block)
    mix_left(env_ref, tensor_ref, mixed_ref)
    mix_channels(weight_ref, mixed_ref, gathered_ref, block)

    def write(index, carry):
        start = pl.multiple_of(index * block, block)
        out_ref[index] = gathered_ref[pl.ds(start, block), :].astype(jnp.bfloat16)
        return carry

    lax.fori_loop(0, states * channels, write, 0, unroll=4)


def right_kernel(
    env0_ref, env1_ref, env2_ref, env3_ref, own_ref, tensor_ref, weight_ref, out_ref, square_ref, mixed_ref, gathered_ref
):
    envs = (env0_ref, env1_ref, env2_ref, env3_ref)
    channels, block, _ = env0_ref.shape
    states = len(envs)
    clear_padding(mixed_ref, states * channels * block)
    group = 6 if channels % 6 == 0 else 1
    for t in range(states):

        def some(index, carry):
            channel = index * group
            rows = envs[t][pl.ds(channel, group)].reshape(group * block, block)
            product = lax.dot_general(
                rows, own_ref[t], (((1,), (1,)), ((), ())), preferred_element_type=jnp.float32
            )
            start = pl.multiple_of((t * channels + channel) * block, block)
            mixed_ref[pl.ds(start, group * block), :] = product
            return carry

        lax.fori_loop(0, channels // group, some, 0, unroll=True)
    mix_channels(weight_ref, mixed_ref, gathered_ref, block)
    square_ref[...] = jnp.zeros_like(square_ref)
    for cls in range(CLASSES):
        left = jnp.concatenate([tensor_ref[cls, s] for s in range(states)], axis=1)
        count = len(range(cls, channels, CLASSES))

        def one(index, carry):
            channel = cls + CLASSES * index
            parts = [
                gathered_ref[
                    pl.ds(pl.multiple_of((s * channels + channel) * block, block), block), :
                ].astype(jnp.bfloat16)
                for s in range(states)
            ]
            product = jnp.dot(
                left, jnp.concatenate(parts, axis=0), preferred_element_type=jnp.float32
            )
            out_ref[channel] = product.astype(jnp.bfloat16)
            return carry + jnp.sum((product * product).reshape(-1, 8, block), axis=0)

        square_ref[...] += lax.fori_loop(
            0, count, one, jnp.zeros((8, block), jnp.float32), unroll=True
        )


def operator_kernel(
    env_ref, tensor_ref, weight_ref, right0_ref, right1_ref, right2_ref, right3_ref, out_ref, mixed_ref, gathered_ref
):
    rights = (right0_ref, right1_ref, right2_ref, right3_ref)
    channels, block, _ = env_ref.shape
    states = len(rights)
    clear_padding(mixed_ref, states * channels * block)
    mix_left(env_ref, tensor_ref, mixed_ref)
    mix_channels(weight_ref, mixed_ref, gathered_ref, block)
    group = 6 if channels % 6 == 0 else 1
    for s in range(states):

        def some(index, carry):
            channel = index * group
            parts = [
                gathered_ref[
                    pl.ds(pl.multiple_of((s * channels + channel + part) * block, block), block), :
                ].astype(jnp.bfloat16)
                for part in range(group)
            ]
            right = rights[s][pl.ds(channel, group)].reshape(group * block, block)
            return carry + jnp.dot(
                jnp.concatenate(parts, axis=1), right, preferred_element_type=jnp.float32
            )

        out_ref[s] = lax.fori_loop(
            0, channels // group, some, jnp.zeros((block, block), jnp.float32), unroll=True
        )


def polar_kernel(vector_ref, centre_ref, scale_ref, out_ref):
    states, block, _ = vector_ref.shape
    rows = lax.broadcasted_iota(jnp.int32, (block, block), 0)
    columns = lax.broadcasted_iota(jnp.int32, (block, block), 1)
    unit = (rows == columns).astype(jnp.float32)

    def product(x, y, contract=((1,), (0,))):
        return lax.dot_general(
            x, y, (contract, ((), ())), precision=HIGHEST, preferred_element_type=jnp.float32
        )

    vector = vector_ref[...].reshape(states * block, block) * scale_ref[0, 0]
    centre = centre_ref[...] * scale_ref[0, 1]
    grams = [product(x, x, ((0,), (0,))) for x in (vector, centre)]
    totals = [unit, unit]
    for step in range(POLAR):
        factors = [1.5 * unit - 0.5 * gram for gram in grams]
        totals = [
            factor if step == 0 else product(total, factor)
            for total, factor in zip(totals, factors)
        ]
        if step < POLAR - 1:
            grams = [
                product(product(factor, gram), factor) for gram, factor in zip(grams, factors)
            ]
    closing = product(totals[0], product(centre, totals[1]), ((1,), (1,)))
    out_ref[...] = product(vector, closing).reshape(states, block, block).astype(jnp.bfloat16)


def cost(flops, *arrays):
    return pl.CostEstimate(
        flops=flops,
        bytes_accessed=sum(int(np.prod(x.shape)) * x.dtype.itemsize for x in arrays),
        transcendentals=0,
    )


def scratch(states, channels, block):
    used = states * channels
    return [
        pltpu.VMEM((padded(used) * block, block), jnp.float32),
        pltpu.VMEM((used * block, block), jnp.float32),
    ]


def work(states, channels, block):
    return 2 * (2 * states * channels * block**3 + (states * channels * block) ** 2)


def call(kernel, out_shape, scratch_shapes, flops, operands):
    return pl.pallas_call(
        kernel,
        out_shape=out_shape,
        scratch_shapes=scratch_shapes,
        compiler_params=pltpu.CompilerParams(vmem_limit_bytes=VMEM_LIMIT),
        cost_estimate=cost(flops, *operands),
    )(*operands)


def left_front(env, tensors, weight):
    channels, block, _ = env.shape
    states = tensors.shape[1]
    out = call(
        left_kernel,
        jax.ShapeDtypeStruct((states * channels, block, block), jnp.bfloat16),
        scratch(states, channels, block),
        work(states, channels, block),
        (env, tensors, weight),
    )
    return out.reshape(states, channels, block, block)


def right_whole(envs, own, tensors, weight):
    channels, block, _ = envs[0].shape
    states = own.shape[0]
    out, square = call(
        right_kernel,
        (
            jax.ShapeDtypeStruct((channels, block, block), jnp.bfloat16),
            jax.ShapeDtypeStruct((8, block), jnp.float32),
        ),
        scratch(states, channels, block),
        work(states, channels, block),
        (*envs, own, tensors, weight),
    )
    return out, jnp.sum(square)


def apply_operator(env, tensors, weight, rights):
    channels, block, _ = env.shape
    states = tensors.shape[1]
    return call(
        operator_kernel,
        jax.ShapeDtypeStruct((states, block, block), jnp.float32),
        scratch(states, channels, block),
        work(states, channels, block),
        (env, tensors, weight, *rights),
    )


def polar(vector, centre, scales):
    return pl.pallas_call(
        polar_kernel,
        out_shape=jax.ShapeDtypeStruct(vector.shape, jnp.bfloat16),
        in_specs=[
            pl.BlockSpec(memory_space=pltpu.VMEM),
            pl.BlockSpec(memory_space=pltpu.VMEM),
            pl.BlockSpec(memory_space=pltpu.SMEM),
        ],
        compiler_params=pltpu.CompilerParams(vmem_limit_bytes=VMEM_LIMIT),
    )(vector, centre, scales)


def charge_mask(channels, states, sectors):
    charge = np.array([CHARGE_STEPS[channel % CLASSES] for channel in range(channels)])
    state = np.arange(states)
    balance = (
        charge[:, None, None, None]
        + state[None, None, None, :]
        - state[None, None, :, None]
        - charge[None, :, None, None]
    )
    return jnp.asarray((balance % sectors == 0).astype(np.float32)).astype(jnp.bfloat16)


def weight_matrices(mpo, pattern, sectors):
    channels, _, states, _ = mpo.shape
    allowed = charge_mask(channels, states, sectors)
    weights = mpo * pattern[:, :, None, None].astype(jnp.bfloat16) * allowed
    size = states * channels
    left = jnp.transpose(weights, (2, 1, 3, 0)).reshape(size, size)
    right = jnp.transpose(weights, (2, 0, 3, 1)).reshape(size, size)
    return jnp.pad(jnp.stack([left, right]), ((0, 0), (0, 0), (0, padded(size) - size)))


def classes_of(places, x):
    one, minus = places.ahead(x, 1), places.ahead(x, -1)
    return jnp.stack([x, one, minus, places.ahead(one, 1), places.ahead(minus, -1)])


def local(left_iso, right_iso, centre, left_env, right_env, mpo, pattern):
    sites, secs = lax.axis_size("site"), lax.axis_size("sec")
    places = Places(sites, secs)
    left_iso, right_iso, centre = left_iso[0, :, 0], right_iso[0, :, 0], centre[0, 0]
    states, block, _ = left_iso.shape
    channels = mpo.shape[1]
    entry_count = left_env.size * secs

    weights = lax.all_gather(weight_matrices(mpo[0], pattern[0], secs), "site")
    chain = places.my_chain()

    def weight_of(site_by, kind):
        return lax.dynamic_index_in_dim(weights, (chain + site_by) % sites, 0, False)[kind]

    right = places.fetch(right_env[0, :, 0])
    left = places.fetch(left_env[0, :, 0])
    left_isos = [places.fetch(left_iso, step) for step in range(ENV_STEPS)]
    right_isos = [places.fetch(right_iso, -step) for step in range(ENV_STEPS)]
    rolled = classes_of(places, jnp.stack(left_isos + right_isos))

    own_iso = places.fetch(left_iso, ENV_STEPS)
    own_centre = [places.fetch(centre, ENV_STEPS, s) for s in range(states)]
    vector = jnp.einsum(
        "sxy,syz->sxz", own_iso, jnp.stack(own_centre), preferred_element_type=jnp.float32
    )
    centre_float = own_centre[0].astype(jnp.float32)

    left_squares, right_squares = [], []
    for step in range(ENV_STEPS):
        envs = [right]
        for t in range(1, states):
            envs.append(places.ahead(envs[-1], 1))
        right, square = right_whole(
            envs, right_isos[step], rolled[:, ENV_STEPS + step], weight_of(-step, 1)
        )
        right_squares.append(square)

        gathered = left_front(left, rolled[:, step], weight_of(step, 0))
        total = None
        for s in reversed(range(states)):
            part = jnp.einsum(
                "xy,vxz->vyz",
                left_isos[step][s],
                gathered[s],
                preferred_element_type=jnp.float32,
            )
            if total is not None:
                part = part + places.ahead(total.astype(jnp.bfloat16), -1).astype(jnp.float32)
            total = part
        left_squares.append(jnp.sum(total * total))
        left = total.astype(jnp.bfloat16)

    sums = places.collect(
        jnp.stack(left_squares + right_squares + [jnp.sum(centre_float * centre_float)])
    )
    sums = jnp.sum(sums, axis=0)
    scales = []
    for side in range(2):
        scale = jnp.float32(1.0)
        for step in range(ENV_STEPS):
            square = sums[side * ENV_STEPS + step]
            scale = scale * lax.rsqrt(scale * scale * square / entry_count + TINY)
        scales.append(scale)
    centre_sq = sums[2 * ENV_STEPS]
    if (2 * ENV_STEPS) % sites:
        right = places.ahead(right, 0, 2 * ENV_STEPS)
        scales[1] = places.ahead(scales[1], 0, 2 * ENV_STEPS)
    scale = scales[0] * scales[1]

    rights = [right]
    for s in range(1, states):
        rights.append(places.ahead(rights[-1], 1))
    weight = weight_of(ENV_STEPS, 0)
    energy = jnp.zeros((), jnp.float32)
    for step in range(DESCENT):
        tensors = classes_of(places, vector.astype(jnp.bfloat16))
        applied = scale * apply_operator(left, tensors, weight, rights)
        own_a, own_b = jnp.sum(vector * applied), jnp.sum(vector * vector)
        own_e = jnp.where(own_b > 0, own_a / jnp.where(own_b > 0, own_b, 1.0), 0.0)
        own_rest = applied - own_e * vector
        table = places.collect(
            jnp.stack([own_a, own_b, own_e, jnp.sum(own_rest * own_rest)])
        )
        a, b, e, c = (table[:, column] for column in range(4))
        weight_sq = jnp.sum(b)
        energy = jnp.sum(a) / (weight_sq + TINY)
        off = e - energy
        residual_sq = jnp.sum(c + 2.0 * off * (a - e * b) + off * off * b)
        residual = applied - energy * vector
        factor = 0.5 * jnp.sqrt(weight_sq / (residual_sq + TINY))
        vector = vector - factor * residual
        vector_sq = (
            weight_sq
            - 2.0 * factor * (jnp.sum(a) - energy * weight_sq)
            + factor * factor * residual_sq
        )

    columns = [vector[0]] + [
        places.ahead(vector[s].astype(jnp.bfloat16), -s).astype(jnp.float32)
        for s in range(1, states)
    ]
    polar_scales = jnp.stack([lax.rsqrt(vector_sq + TINY), lax.rsqrt(centre_sq + TINY)])[None]
    column_left = polar(jnp.stack(columns), centre_float, polar_scales)
    new_left = jnp.stack(
        [places.send_home(column_left[s], ENV_STEPS, -s) for s in range(states)]
    )
    energy = places.send_home(jnp.reshape(energy, (1,)), ENV_STEPS, 0)
    return new_left[None, :, None], energy


def solution(mesh):
    placed = (
        P("site", None, "sec", None, None),
        P("site", None, "sec", None, None),
        P("site", "sec", None, None),
        P("site", None, "sec", None, None),
        P("site", None, "sec", None, None),
        P("site", None, None, None, None),
        P("site", None, None),
    )
    return jax.shard_map(
        local,
        mesh=mesh,
        in_specs=placed,
        out_specs=(P("site", None, "sec", None, None), P("site")),
        check_vma=False,
    )
```

```python
import functools

import jax
import jax.numpy as jnp
import numpy as np
from jax import lax
from jax.experimental import pallas as pl
from jax.experimental.pallas import tpu as pltpu
from jax.sharding import PartitionSpec as P

ENV_STEPS = 2
DESCENT = 2
POLAR = 6

TINY = 1e-06
HIGHEST = lax.Precision.HIGHEST
CHARGE_STEPS = (0, 1, -1, 2, -2)
CLASSES = len(CHARGE_STEPS)
BOTH = ("site", "sec")
VMEM_LIMIT = 44 * 1024 * 1024


def ring_order(half):
    up = (half + 1) // 2
    return list(range(up)) + list(range(half - 1, up - 1, -1))


class Places:
    def __init__(self, sites, secs):
        self.sites, self.secs = sites, secs
        self.half = secs // 2
        self.order = ring_order(self.half)

    def home(self, site, sector):
        return (site % self.sites) * self.secs + sector % self.secs

    def slot(self, chain, sector):
        chain, sector = chain % self.sites, sector % self.secs
        place = (chain % 2) * self.half + self.order[sector // 2]
        return (chain // 2 * 2 + sector % 2) * self.secs + place

    def pairs(self, source, target):
        return [
            (source(chain, sector), target(chain, sector))
            for chain in range(self.sites)
            for sector in range(self.secs)
        ]

    def fetch(self, x, site_by=0, sec_by=0):
        return lax.ppermute(
            x, BOTH, self.pairs(lambda g, k: self.home(g + site_by, k + sec_by), self.slot)
        )

    def send_home(self, x, site_by, sec_by):
        return lax.ppermute(
            x, BOTH, self.pairs(self.slot, lambda g, k: self.home(g + site_by, k + sec_by))
        )

    def ahead(self, x, by, chain_by=0):
        return lax.ppermute(
            x, BOTH, self.pairs(lambda g, k: self.slot(g + chain_by, k + by), self.slot)
        )

    def partner(self, x, bit):
        return lax.ppermute(x, BOTH, self.pairs(lambda g, k: self.slot(g, k ^ bit), self.slot))

    def my_chain(self):
        return lax.axis_index("site") // 2 * 2 + lax.axis_index("sec") // self.half

    def my_sector(self):
        positions = np.argsort(np.array(self.order))
        position = jnp.asarray(positions, jnp.int32)[lax.axis_index("sec") % self.half]
        return 2 * position + lax.axis_index("site") % 2

    def collect(self, values):
        sector = self.my_sector()
        table = values[None]
        bit = 1
        while bit < self.secs:
            other = self.partner(table, bit)
            first = (sector & bit) == 0
            table = jnp.where(
                first, jnp.concatenate([table, other]), jnp.concatenate([other, table])
            )
            bit *= 2
        return table


ROWS = 8


def label_groups(channels, states, sectors, sign):
    groups = {}
    for state in range(states):
        for channel in range(channels):
            label = (state + sign * CHARGE_STEPS[channel % CLASSES]) % sectors
            groups.setdefault(label, []).append((state, channel))
    return [groups[label] for label in sorted(groups)]


def even(count):
    return count + count % 2


def spread_matrix(groups, channels, states):
    rows = []
    for group in groups:
        block = np.zeros((even(len(group)), ROWS, states * channels), np.float32)
        for index, (state, channel) in enumerate(group):
            block[index, :, state * channels + channel] = 1
        rows.append(block.reshape(-1, states * channels))
    return np.concatenate(rows)


def expand_kernel(sizes, weight_ref, spread_ref, out_ref):
    start = 0
    for size in sizes:
        spread = spread_ref[pl.ds(start, size), :]
        picked = jnp.dot(spread, weight_ref[...], preferred_element_type=jnp.float32)
        full = lax.dot_general(
            picked.astype(jnp.bfloat16),
            spread,
            (((1,), (1,)), ((), ())),
            preferred_element_type=jnp.float32,
        )
        row = lax.broadcasted_iota(jnp.int32, full.shape, 0)
        column = lax.broadcasted_iota(jnp.int32, full.shape, 1)
        same = lax.rem(row, ROWS) == lax.rem(column, ROWS)
        out_ref[pl.ds(start, size), pl.ds(0, size)] = jnp.where(same, full, 0.0).astype(
            jnp.bfloat16
        )
        start += size


def mix_channels(groups, channels, weight_ref, mixed_ref, gathered_ref, block):
    def step(index, carry):
        first = index * 2 * ROWS

        def place(pair):
            state, channel = pair
            return pl.multiple_of((state * channels + channel) * block + first, 2 * ROWS)

        start = 0
        for group in groups:
            size = even(len(group)) * ROWS
            parts = []
            for pair in group:
                rows = place(pair)
                halves = [mixed_ref[pl.ds(rows + half * ROWS, ROWS), :] for half in range(2)]
                parts.append(jnp.concatenate(halves, axis=1))
            if len(group) % 2:
                parts.append(parts[0])
            operand = jnp.concatenate(parts, axis=0).astype(jnp.bfloat16)
            product = jnp.dot(
                weight_ref[pl.ds(start, size), pl.ds(0, size)],
                operand,
                preferred_element_type=jnp.float32,
            )
            for number, pair in enumerate(group):
                rows = product[number * ROWS : (number + 1) * ROWS]
                both = jnp.concatenate([rows[:, :block], rows[:, block:]], axis=0)
                gathered_ref[pl.ds(place(pair), 2 * ROWS), :] = both.astype(jnp.bfloat16)
            start += size
        return carry

    lax.fori_loop(0, block // (2 * ROWS), step, 0)


def batches(items, most):
    pieces = -(-len(items) // most)
    size = -(-len(items) // pieces)
    return [items[start : start + size] for start in range(0, len(items), size)]


def mix_left(env_ref, tensors, mixed_ref):
    channels, block, _ = env_ref.shape
    for cls in range(CLASSES):
        right = jnp.concatenate(tensors[cls], axis=1)
        for batch in batches(list(range(cls, channels, CLASSES)), 3):
            rows = jnp.concatenate([env_ref[channel] for channel in batch], axis=0)
            product = jnp.dot(rows, right, preferred_element_type=jnp.float32)
            for number, channel in enumerate(batch):
                for t in range(len(tensors[cls])):
                    mixed_ref[pl.ds((t * channels + channel) * block, block), :] = product[
                        number * block : (number + 1) * block, t * block : (t + 1) * block
                    ]


def left_kernel(groups, env_ref, tensor_ref, weight_ref, out_ref, mixed_ref):
    channels, block, _ = env_ref.shape
    states = tensor_ref.shape[1]
    tensors = [[tensor_ref[cls, t] for t in range(states)] for cls in range(CLASSES)]
    mix_left(env_ref, tensors, mixed_ref)
    mix_channels(groups, channels, weight_ref, mixed_ref, out_ref, block)


def right_kernel(groups, states, *refs):
    envs = refs[:states]
    own_ref, tensor_ref, weight_ref, out_ref, square_ref, mixed_ref, gathered_ref = refs[states:]
    channels, block, _ = envs[0].shape
    zero = jnp.zeros((block, block), jnp.bfloat16)
    for pair in batches(list(range(states)), 2):
        own = jnp.concatenate(
            [
                jnp.concatenate([own_ref[t] if t == other else zero for other in pair], axis=1)
                for t in pair
            ],
            axis=0,
        )
        for batch in batches(list(range(channels)), 3):
            rows = jnp.concatenate(
                [
                    envs[t][batch[0] : batch[-1] + 1].reshape(len(batch) * block, block)
                    for t in pair
                ],
                axis=1,
            )
            product = lax.dot_general(
                rows, own, (((1,), (1,)), ((), ())), preferred_element_type=jnp.float32
            )
            for number, t in enumerate(pair):
                mixed_ref[pl.ds((t * channels + batch[0]) * block, len(batch) * block), :] = (
                    product[:, number * block : (number + 1) * block]
                )
    mix_channels(groups, channels, weight_ref, mixed_ref, gathered_ref, block)
    square = jnp.zeros((ROWS, 2 * block), jnp.float32)
    for cls in range(CLASSES):
        left = jnp.concatenate([tensor_ref[cls, s] for s in range(states)], axis=1)
        for batch in batches(list(range(cls, channels, CLASSES)), 2):
            right = jnp.concatenate(
                [
                    jnp.concatenate(
                        [
                            gathered_ref[pl.ds((s * channels + channel) * block, block), :]
                            for s in range(states)
                        ],
                        axis=0,
                    )
                    for channel in batch
                ],
                axis=1,
            )
            product = jnp.dot(left, right, preferred_element_type=jnp.float32)
            for number, channel in enumerate(batch):
                part = product[:, number * block : (number + 1) * block]
                out_ref[channel] = part.astype(jnp.bfloat16)
                square_part = jnp.sum((part * part).reshape(-1, ROWS, block), axis=0)
                square = square + jnp.concatenate([square_part, jnp.zeros_like(square_part)], axis=1)
    square_ref[...] = square[:, :block]


def quotient(table):
    a, b, e, c = (table[:, column : column + 1] for column in range(4))

    def total(x):
        return jnp.sum(x, axis=0, keepdims=True)

    whole_a, whole_b = total(a), total(b)
    energy = whole_a / (whole_b + TINY)
    off = e - energy
    residual_sq = total(c + 2.0 * off * (a - e * b) + off * off * b)
    factor = 0.5 * jnp.sqrt(whole_b / (residual_sq + TINY))
    square = whole_b - 2.0 * factor * (whole_a - energy * whole_b) + factor * factor * residual_sq
    return energy, factor, square


def updated(vector, applied, energy, factor):
    return vector - factor * (applied - energy * vector)


def sum_all(x):
    return jnp.sum(jnp.sum(x, axis=0, keepdims=True), axis=1, keepdims=True)


def operator_kernel(groups, states, renew, *refs):
    rights = refs[:states]
    env_ref, weight_ref, scale_ref, vector_ref = refs[states : states + 4]
    rest = refs[states + 4 :]
    if renew:
        moved_ref, table_ref = rest[:2]
        rest = rest[2:]
        energy, factor, _ = quotient(table_ref[...])
    image_ref, sums_ref, new_ref, mixed_ref, gathered_ref = rest
    channels, block, _ = env_ref.shape
    tensors = []
    for cls in range(CLASSES):
        row = []
        for t in range(states):
            vector = vector_ref[cls, t]
            if renew:
                vector = updated(vector, moved_ref[cls, t], energy, factor)
            new_ref[cls, t] = vector
            row.append(vector.astype(jnp.bfloat16))
        tensors.append(row)
    mix_left(env_ref, tensors, mixed_ref)
    mix_channels(groups, channels, weight_ref, mixed_ref, gathered_ref, block)
    scale = scale_ref[0, 0]
    a = jnp.zeros((1, 1), jnp.float32)
    b = jnp.zeros((1, 1), jnp.float32)
    for s in range(states):
        total = jnp.zeros((block, block), jnp.float32)
        for batch in batches(list(range(channels)), 6):
            left = jnp.concatenate(
                [
                    gathered_ref[pl.ds((s * channels + channel) * block, block), :]
                    for channel in batch
                ],
                axis=1,
            )
            right = rights[s][batch[0] : batch[-1] + 1].reshape(len(batch) * block, block)
            total = total + jnp.dot(left, right, preferred_element_type=jnp.float32)
        total = total * scale
        image_ref[s] = total
        vector = new_ref[0, s]
        a = a + sum_all(vector * total)
        b = b + sum_all(vector * vector)
    e = jnp.where(b > 0, a / jnp.where(b > 0, b, 1.0), 0.0)
    c = jnp.zeros((1, 1), jnp.float32)
    for s in range(states):
        residual = image_ref[s] - e * new_ref[0, s]
        c = c + sum_all(residual * residual)
    lane = lax.broadcasted_iota(jnp.int32, sums_ref.shape, 1)
    sums = jnp.zeros(sums_ref.shape, jnp.float32)
    for place, value in enumerate((a, b, e, c)):
        sums = jnp.where(lane == place, value, sums)
    sums_ref[...] = sums


def polar_kernel(vector_ref, image_ref, table_ref, centre_ref, centre_sq_ref, out_ref):
    states, block, _ = vector_ref.shape
    rows = lax.broadcasted_iota(jnp.int32, (block, block), 0)
    columns = lax.broadcasted_iota(jnp.int32, (block, block), 1)
    unit = (rows == columns).astype(jnp.float32)

    def product(x, y, contract=((1,), (0,))):
        return lax.dot_general(
            x, y, (contract, ((), ())), precision=HIGHEST, preferred_element_type=jnp.float32
        )

    energy, factor, square = quotient(table_ref[...])
    vector = updated(
        vector_ref[...].reshape(states * block, block),
        image_ref[...].reshape(states * block, block),
        energy,
        factor,
    ) * lax.rsqrt(square + TINY)
    centre = centre_ref[...].astype(jnp.float32) * lax.rsqrt(centre_sq_ref[0, 0] + TINY)
    grams = [product(x, x, ((0,), (0,))) for x in (vector, centre)]
    totals = [unit, unit]
    for step in range(POLAR):
        factors = [1.5 * unit - 0.5 * gram for gram in grams]
        totals = [
            factor if step == 0 else product(total, factor)
            for total, factor in zip(totals, factors)
        ]
        if step < POLAR - 1:
            grams = [
                product(product(factor, gram), factor) for gram, factor in zip(grams, factors)
            ]
    closing = product(totals[0], product(centre, totals[1]), ((1,), (1,)))
    out_ref[...] = product(vector, closing).reshape(states, block, block).astype(jnp.bfloat16)


def call(kernel, out_shape, scratch_shapes, flops, operands, scalars=()):
    in_specs = [
        pl.BlockSpec(memory_space=pltpu.SMEM if place in scalars else pltpu.VMEM)
        for place in range(len(operands))
    ]
    return pl.pallas_call(
        kernel,
        out_shape=out_shape,
        in_specs=in_specs,
        scratch_shapes=scratch_shapes,
        compiler_params=pltpu.CompilerParams(vmem_limit_bytes=VMEM_LIMIT),
        cost_estimate=pl.CostEstimate(
            flops=flops,
            bytes_accessed=sum(int(np.prod(x.shape)) * x.dtype.itemsize for x in operands),
            transcendentals=0,
        ),
    )(*operands)


def float_out(*shape):
    return jax.ShapeDtypeStruct(shape, jnp.float32)


def half_out(*shape):
    return jax.ShapeDtypeStruct(shape, jnp.bfloat16)


def work(states, channels, block):
    return 4 * states * channels * block**3 + 2 * (states * channels * block) ** 2


def expanded(weight, groups, channels, states):
    spread = spread_matrix(groups, channels, states)
    sizes = tuple(even(len(group)) * ROWS for group in groups)
    return call(
        functools.partial(expand_kernel, sizes),
        half_out(spread.shape[0], -(-max(sizes) // 128) * 128),
        [],
        2 * spread.size * spread.shape[0],
        (weight, jnp.asarray(spread, jnp.bfloat16)),
    )


def left_front(env, tensors, weight, groups):
    channels, block, _ = env.shape
    states = tensors.shape[1]
    out = call(
        functools.partial(left_kernel, groups),
        half_out(states * channels * block, block),
        [pltpu.VMEM((states * channels * block, block), jnp.float32)],
        work(states, channels, block),
        (env, tensors, weight),
    )
    return out.reshape(states, channels, block, block)


def right_whole(envs, own, tensors, weight, groups):
    channels, block, _ = envs[0].shape
    states = own.shape[0]
    out, square = call(
        functools.partial(right_kernel, groups, states),
        (half_out(channels, block, block), float_out(ROWS, block)),
        [
            pltpu.VMEM((states * channels * block, block), jnp.float32),
            pltpu.VMEM((states * channels * block, block), jnp.bfloat16),
        ],
        work(states, channels, block),
        (*envs, own, tensors, weight),
    )
    return out, jnp.sum(square)


def apply_operator(env, rights, weight, groups, scale, vectors, images=None, table=None):
    channels, block, _ = env.shape
    states = vectors.shape[1]
    renew = images is not None
    operands = (*rights, env, weight, scale, vectors) + ((images, table) if renew else ())
    return call(
        functools.partial(operator_kernel, groups, states, renew),
        (
            float_out(states, block, block),
            float_out(1, 128),
            float_out(CLASSES, states, block, block),
        ),
        [
            pltpu.VMEM((states * channels * block, block), jnp.float32),
            pltpu.VMEM((states * channels * block, block), jnp.bfloat16),
        ],
        work(states, channels, block),
        operands,
        (states + 2,),
    )


def polar(vector, image, table, centre, centre_sq):
    return call(
        polar_kernel,
        half_out(*vector.shape),
        [],
        100 * vector.shape[1] ** 3 * 6,
        (vector, image, table, centre, centre_sq),
        (4,),
    )


def charge_mask(channels, states, sectors):
    charge = np.array([CHARGE_STEPS[channel % CLASSES] for channel in range(channels)])
    state = np.arange(states)
    balance = (
        charge[:, None, None, None]
        + state[None, None, None, :]
        - state[None, None, :, None]
        - charge[None, :, None, None]
    )
    return jnp.asarray((balance % sectors == 0).astype(np.float32)).astype(jnp.bfloat16)


def weight_matrices(mpo, pattern, sectors):
    channels, _, states, _ = mpo.shape
    allowed = charge_mask(channels, states, sectors)
    weights = mpo * pattern[:, :, None, None].astype(jnp.bfloat16) * allowed
    size = states * channels
    left = jnp.transpose(weights, (2, 1, 3, 0)).reshape(size, size)
    right = jnp.transpose(weights, (2, 0, 3, 1)).reshape(size, size)
    return jnp.stack([left, right])


def classes_of(places, x):
    one, minus = places.ahead(x, 1), places.ahead(x, -1)
    return jnp.stack([x, one, minus, places.ahead(one, 1), places.ahead(minus, -1)])


def after(first, then):
    return lax.optimization_barrier((first, then))


def local(left_iso, right_iso, centre, left_env, right_env, mpo, pattern):
    sites, secs = lax.axis_size("site"), lax.axis_size("sec")
    places = Places(sites, secs)
    left_iso, right_iso, centre = left_iso[0, :, 0], right_iso[0, :, 0], centre[0, 0]
    states, block, _ = left_iso.shape
    channels = mpo.shape[1]
    entry_count = left_env.size * secs
    left_groups = label_groups(channels, states, secs, 1)
    right_groups = label_groups(channels, states, secs, -1)

    right = places.fetch(right_env[0, :, 0])
    left_isos = [places.fetch(left_iso, step) for step in range(ENV_STEPS)]
    right_isos = [places.fetch(right_iso, -step) for step in range(ENV_STEPS)]
    own_iso = places.fetch(left_iso, ENV_STEPS)
    own_centre = [places.fetch(centre, ENV_STEPS, s) for s in range(states)]
    right, left_env = after(right, left_env)
    left = places.fetch(left_env[0, :, 0])

    weights = lax.all_gather(weight_matrices(mpo[0], pattern[0], secs), "site")
    chain = places.my_chain()

    def weight_of(site_by, kind):
        weight = lax.dynamic_index_in_dim(weights, (chain + site_by) % sites, 0, False)[kind]
        return expanded(weight, (left_groups, right_groups)[kind], channels, states)

    rolled = classes_of(places, jnp.stack(left_isos + right_isos))
    vector = jnp.einsum(
        "sxy,syz->sxz", own_iso, jnp.stack(own_centre), preferred_element_type=jnp.float32
    )
    vectors = classes_of(places, vector)
    centre_float = own_centre[0].astype(jnp.float32)
    centre_square = jnp.sum(centre_float * centre_float)

    left_squares, right_squares = [], []
    for step in range(ENV_STEPS):
        envs = [right]
        for t in range(1, states):
            envs.append(places.ahead(envs[-1], 1))
        right, square = right_whole(
            envs,
            right_isos[step],
            rolled[:, ENV_STEPS + step],
            weight_of(-step, 1),
            right_groups,
        )
        right_squares.append(square)

        gathered = left_front(left, rolled[:, step], weight_of(step, 0), left_groups)
        total = None
        for s in reversed(range(states)):
            part = jnp.einsum(
                "xy,vxz->vyz",
                left_isos[step][s],
                gathered[s],
                preferred_element_type=jnp.float32,
            )
            if total is not None:
                part = part + places.ahead(total.astype(jnp.bfloat16), -1).astype(jnp.float32)
            total = part
        left_squares.append(jnp.sum(total * total))
        left = total.astype(jnp.bfloat16)

    sums = places.collect(jnp.stack(left_squares + right_squares + [centre_square]))
    sums = jnp.sum(sums, axis=0)
    scales = []
    for side in range(2):
        scale = jnp.float32(1.0)
        for step in range(ENV_STEPS):
            square = sums[side * ENV_STEPS + step]
            scale = scale * lax.rsqrt(scale * scale * square / entry_count + TINY)
        scales.append(scale)
    centre_sq = jnp.reshape(sums[2 * ENV_STEPS], (1, 1))
    if (2 * ENV_STEPS) % sites:
        right = places.ahead(right, 0, 2 * ENV_STEPS)
        scales[1] = places.ahead(scales[1], 0, 2 * ENV_STEPS)
    scale = jnp.reshape(scales[0] * scales[1], (1, 1))

    rights = [right]
    for s in range(1, states):
        rights.append(places.ahead(rights[-1], 1))
    weight = weight_of(ENV_STEPS, 0)
    images, table = None, None
    for step in range(DESCENT):
        image, own_sums, vectors = apply_operator(
            left, rights, weight, left_groups, scale, vectors, images, table
        )
        table = places.collect(own_sums[0])
        if step < DESCENT - 1:
            images = classes_of(places, image)

    def at_columns(x):
        return jnp.stack([x[0]] + [places.ahead(x[s], -s) for s in range(1, states)])

    column_left = polar(
        at_columns(vectors[0]), at_columns(image), table, own_centre[0], centre_sq
    )
    new_left = jnp.stack(
        [places.send_home(column_left[s], ENV_STEPS, -s) for s in range(states)]
    )
    home_table = places.send_home(table, ENV_STEPS, 0)
    energy = jnp.sum(home_table[:, 0]) / (jnp.sum(home_table[:, 1]) + TINY)
    return new_left[None, :, None], jnp.reshape(energy, (1,))


def solution(mesh):
    placed = (
        P("site", None, "sec", None, None),
        P("site", None, "sec", None, None),
        P("site", "sec", None, None),
        P("site", None, "sec", None, None),
        P("site", None, "sec", None, None),
        P("site", None, None, None, None),
        P("site", None, None),
    )
    return jax.shard_map(
        local,
        mesh=mesh,
        in_specs=placed,
        out_specs=(P("site", None, "sec", None, None), P("site")),
        check_vma=False,
    )
```

```python
import functools

import jax
import jax.numpy as jnp
import numpy as np
from jax import lax
from jax.experimental import pallas as pl
from jax.experimental.pallas import tpu as pltpu
from jax.sharding import PartitionSpec as P

ENV_STEPS = 2
DESCENT = 2
POLAR = 6

TINY = 1e-06
HIGHEST = lax.Precision.HIGHEST
CHARGE_STEPS = (0, 1, -1, 2, -2)
CLASSES = len(CHARGE_STEPS)
BOTH = ("site", "sec")
VMEM_LIMIT = 44 * 1024 * 1024
PIECES = 2


def ring_order(half):
    up = (half + 1) // 2
    return list(range(up)) + list(range(half - 1, up - 1, -1))


class Places:
    def __init__(self, sites, secs):
        self.sites, self.secs = sites, secs
        self.half = secs // 2
        self.order = ring_order(self.half)

    def home(self, site, sector):
        return (site % self.sites) * self.secs + sector % self.secs

    def slot(self, chain, sector):
        chain, sector = chain % self.sites, sector % self.secs
        place = (chain % 2) * self.half + self.order[sector // 2]
        return (chain // 2 * 2 + sector % 2) * self.secs + place

    def pairs(self, source, target):
        return [
            (source(chain, sector), target(chain, sector))
            for chain in range(self.sites)
            for sector in range(self.secs)
        ]

    def fetch(self, x, site_by=0, sec_by=0):
        return lax.ppermute(
            x, BOTH, self.pairs(lambda g, k: self.home(g + site_by, k + sec_by), self.slot)
        )

    def send_home(self, x, site_by, sec_by):
        return lax.ppermute(
            x, BOTH, self.pairs(self.slot, lambda g, k: self.home(g + site_by, k + sec_by))
        )

    def ahead(self, x, by, chain_by=0):
        return lax.ppermute(
            x, BOTH, self.pairs(lambda g, k: self.slot(g + chain_by, k + by), self.slot)
        )

    def partner(self, x, bit):
        return lax.ppermute(x, BOTH, self.pairs(lambda g, k: self.slot(g, k ^ bit), self.slot))

    def my_chain(self):
        return lax.axis_index("site") // 2 * 2 + lax.axis_index("sec") // self.half

    def my_sector(self):
        positions = np.argsort(np.array(self.order))
        position = jnp.asarray(positions, jnp.int32)[lax.axis_index("sec") % self.half]
        return 2 * position + lax.axis_index("site") % 2

    def summed(self, values):
        bit = 1
        while bit < self.secs:
            values = values + self.partner(values, bit)
            bit *= 2
        return values

    def collect(self, values):
        sector = self.my_sector()
        table = values[None]
        bit = 1
        while bit < self.secs:
            other = self.partner(table, bit)
            first = (sector & bit) == 0
            table = jnp.where(
                first, jnp.concatenate([table, other]), jnp.concatenate([other, table])
            )
            bit *= 2
        return table


ROWS = 8


def label_groups(channels, states, sectors, sign):
    groups = {}
    for state in range(states):
        for channel in range(channels):
            label = (state + sign * CHARGE_STEPS[channel % CLASSES]) % sectors
            groups.setdefault(label, []).append((state, channel))
    return [groups[label] for label in sorted(groups)]


def even(count):
    return count + count % 2


def spread_matrix(groups, channels, states):
    rows = []
    for group in groups:
        block = np.zeros((even(len(group)), ROWS, states * channels), np.float32)
        for index, (state, channel) in enumerate(group):
            block[index, :, state * channels + channel] = 1
        rows.append(block.reshape(-1, states * channels))
    return np.concatenate(rows)


def expand_kernel(sizes, weight_ref, spread_ref, out_ref):
    start = 0
    for size in sizes:
        spread = spread_ref[pl.ds(start, size), :]
        picked = jnp.dot(spread, weight_ref[...], preferred_element_type=jnp.float32)
        full = lax.dot_general(
            picked.astype(jnp.bfloat16),
            spread,
            (((1,), (1,)), ((), ())),
            preferred_element_type=jnp.float32,
        )
        row = lax.broadcasted_iota(jnp.int32, full.shape, 0)
        column = lax.broadcasted_iota(jnp.int32, full.shape, 1)
        same = lax.rem(row, ROWS) == lax.rem(column, ROWS)
        out_ref[pl.ds(start, size), pl.ds(0, size)] = jnp.where(same, full, 0.0).astype(
            jnp.bfloat16
        )
        start += size


def mix_channels(groups, channels, weight_ref, mixed_ref, write, block):
    def step(index, carry):
        first = pl.multiple_of(index * 2 * ROWS, 2 * ROWS)

        def place(pair):
            state, channel = pair
            return pl.multiple_of((state * channels + channel) * block + first, 2 * ROWS)

        start = 0
        for group in groups:
            size = even(len(group)) * ROWS
            parts = []
            for pair in group:
                rows = place(pair)
                halves = [mixed_ref[pl.ds(rows + half * ROWS, ROWS), :] for half in range(2)]
                parts.append(jnp.concatenate(halves, axis=1))
            if len(group) % 2:
                parts.append(parts[0])
            operand = jnp.concatenate(parts, axis=0).astype(jnp.bfloat16)
            product = jnp.dot(
                weight_ref[pl.ds(start, size), pl.ds(0, size)],
                operand,
                preferred_element_type=jnp.float32,
            )
            for number, pair in enumerate(group):
                rows = product[number * ROWS : (number + 1) * ROWS]
                both = jnp.concatenate([rows[:, :block], rows[:, block:]], axis=0)
                write(*pair, first, both.astype(jnp.bfloat16))
            start += size
        return carry

    lax.fori_loop(0, block // (2 * ROWS), step, 0)


def into(gathered_ref, channels, block):
    def write(state, channel, first, rows):
        start = (state * channels + channel) * block
        gathered_ref[pl.ds(pl.multiple_of(start + first, 2 * ROWS), 2 * ROWS), :] = rows

    return write


def batches(items, most):
    pieces = -(-len(items) // most)
    size = -(-len(items) // pieces)
    return [items[start : start + size] for start in range(0, len(items), size)]


def channel_of(chunks, channel):
    size = chunks[0].shape[0]
    return chunks[channel // size][channel % size]


def put_channel(chunks, channel, value):
    size = chunks[0].shape[0]
    chunks[channel // size][channel % size] = value


def count_channels(chunks):
    return sum(chunk.shape[0] for chunk in chunks)


def mix_left(env, tensors, mixed_ref):
    channels, block = count_channels(env), env[0].shape[1]
    for cls in range(CLASSES):
        right = jnp.concatenate(tensors[cls], axis=1)
        for batch in batches(list(range(cls, channels, CLASSES)), 3):
            rows = jnp.concatenate([channel_of(env, channel) for channel in batch], axis=0)
            product = jnp.dot(rows, right, preferred_element_type=jnp.float32)
            for number, channel in enumerate(batch):
                for t in range(len(tensors[cls])):
                    mixed_ref[pl.ds((t * channels + channel) * block, block), :] = product[
                        number * block : (number + 1) * block, t * block : (t + 1) * block
                    ]


def left_kernel(groups, states, pieces, *refs):
    env, (tensor_ref, weight_ref) = refs[:pieces], refs[pieces : pieces + 2]
    outs, mixed_ref = refs[pieces + 2 : -1], refs[-1]
    channels, block = count_channels(env), env[0].shape[1]
    tensors = [[tensor_ref[cls, t] for t in range(states)] for cls in range(CLASSES)]
    mix_left(env, tensors, mixed_ref)

    def write(state, channel, first, rows):
        size = channels // pieces
        out_ref = outs[state * pieces + channel // size]
        out_ref[channel % size, pl.ds(first, 2 * ROWS), :] = rows

    mix_channels(groups, channels, weight_ref, mixed_ref, write, block)


def left_close_kernel(iso_ref, gathered_ref, moved_ref, out_ref, square_ref):
    channels, block, _ = gathered_ref.shape
    square = jnp.zeros((ROWS, block), jnp.float32)
    for batch in batches(list(range(channels)), 2):
        right = jnp.concatenate([gathered_ref[channel] for channel in batch], axis=1)
        product = lax.dot_general(
            iso_ref[...], right, (((0,), (0,)), ((), ())), preferred_element_type=jnp.float32
        )
        for number, channel in enumerate(batch):
            part = product[:, number * block : (number + 1) * block]
            part = part + moved_ref[channel].astype(jnp.float32)
            out_ref[channel] = part.astype(jnp.bfloat16)
            square = square + jnp.sum((part * part).reshape(-1, ROWS, block), axis=0)
    square_ref[...] = square


def right_kernel(groups, states, pieces, *refs):
    envs = [refs[t * pieces : (t + 1) * pieces] for t in range(states)]
    refs = refs[states * pieces :]
    own_ref, tensor_ref, weight_ref = refs[:3]
    outs, (square_ref, mixed_ref, gathered_ref) = refs[3 : 3 + pieces], refs[3 + pieces :]
    channels, block = count_channels(envs[0]), envs[0][0].shape[1]
    zero = jnp.zeros((block, block), jnp.bfloat16)
    for pair in batches(list(range(states)), 2):
        own = jnp.concatenate(
            [
                jnp.concatenate([own_ref[t] if t == other else zero for other in pair], axis=1)
                for t in pair
            ],
            axis=0,
        )
        for batch in batches(list(range(channels)), 3):
            rows = jnp.concatenate(
                [
                    jnp.concatenate([channel_of(envs[t], channel) for channel in batch], axis=0)
                    for t in pair
                ],
                axis=1,
            )
            product = lax.dot_general(
                rows, own, (((1,), (1,)), ((), ())), preferred_element_type=jnp.float32
            )
            for number, t in enumerate(pair):
                mixed_ref[pl.ds((t * channels + batch[0]) * block, len(batch) * block), :] = (
                    product[:, number * block : (number + 1) * block]
                )
    write = into(gathered_ref, channels, block)
    mix_channels(groups, channels, weight_ref, mixed_ref, write, block)
    square = jnp.zeros((ROWS, block), jnp.float32)
    for cls in range(CLASSES):
        left = jnp.concatenate([tensor_ref[cls, s] for s in range(states)], axis=1)
        for batch in batches(list(range(cls, channels, CLASSES)), 2):
            right = jnp.concatenate(
                [
                    jnp.concatenate(
                        [
                            gathered_ref[pl.ds((s * channels + channel) * block, block), :]
                            for s in range(states)
                        ],
                        axis=0,
                    )
                    for channel in batch
                ],
                axis=1,
            )
            product = jnp.dot(left, right, preferred_element_type=jnp.float32)
            for number, channel in enumerate(batch):
                part = product[:, number * block : (number + 1) * block]
                put_channel(outs, channel, part.astype(jnp.bfloat16))
                square = square + jnp.sum((part * part).reshape(-1, ROWS, block), axis=0)
    square_ref[...] = square


def quotient(table):
    a, b, e, c = (table[:, column : column + 1] for column in range(4))

    def total(x):
        return jnp.sum(x, axis=0, keepdims=True)

    whole_a, whole_b = total(a), total(b)
    energy = whole_a / (whole_b + TINY)
    off = e - energy
    residual_sq = total(c + 2.0 * off * (a - e * b) + off * off * b)
    factor = 0.5 * jnp.sqrt(whole_b / (residual_sq + TINY))
    square = whole_b - 2.0 * factor * (whole_a - energy * whole_b) + factor * factor * residual_sq
    return energy, factor, square


def updated(vector, applied, energy, factor):
    return vector - factor * (applied - energy * vector)


def sum_all(x):
    return jnp.sum(jnp.sum(x, axis=0, keepdims=True), axis=1, keepdims=True)


def env_scale(sums_ref, first, entry_count):
    scale = jnp.ones((1, 1), jnp.float32)
    for step in range(first, first + ENV_STEPS):
        square = sum_all(sums_ref[step])
        scale = scale * lax.rsqrt(scale * scale * square / entry_count + TINY)
    return scale


def operator_kernel(groups, states, pieces, renew, entry_count, *refs):
    rights = [refs[t * pieces : (t + 1) * pieces] for t in range(states)]
    refs = refs[states * pieces :]
    env, refs = refs[:pieces], refs[pieces:]
    weight_ref, left_sums_ref, right_sums_ref, vector_ref = refs[:4]
    rest = refs[4:]
    if renew:
        moved_ref, table_ref = rest[:2]
        rest = rest[2:]
        energy, factor, _ = quotient(table_ref[...])
    image_ref, sums_ref, new_ref, mixed_ref, gathered_ref = rest
    channels, block = count_channels(env), env[0].shape[1]
    tensors = []
    for cls in range(CLASSES):
        row = []
        for t in range(states):
            vector = vector_ref[cls, t]
            if renew:
                vector = updated(vector, moved_ref[cls, t], energy, factor)
            new_ref[cls, t] = vector
            row.append(vector.astype(jnp.bfloat16))
        tensors.append(row)
    mix_left(env, tensors, mixed_ref)
    write = into(gathered_ref, channels, block)
    mix_channels(groups, channels, weight_ref, mixed_ref, write, block)
    scale = env_scale(left_sums_ref, 0, entry_count) * env_scale(
        right_sums_ref, ENV_STEPS, entry_count
    )
    a = jnp.zeros((1, 1), jnp.float32)
    b = jnp.zeros((1, 1), jnp.float32)
    for s in range(states):
        total = jnp.zeros((block, block), jnp.float32)
        for batch in batches(list(range(channels)), 6):
            left = jnp.concatenate(
                [
                    gathered_ref[pl.ds((s * channels + channel) * block, block), :]
                    for channel in batch
                ],
                axis=1,
            )
            right = jnp.concatenate([channel_of(rights[s], channel) for channel in batch], axis=0)
            total = total + jnp.dot(left, right, preferred_element_type=jnp.float32)
        total = total * scale
        image_ref[s] = total
        vector = new_ref[0, s]
        a = a + sum_all(vector * total)
        b = b + sum_all(vector * vector)
    e = jnp.where(b > 0, a / jnp.where(b > 0, b, 1.0), 0.0)
    c = jnp.zeros((1, 1), jnp.float32)
    for s in range(states):
        residual = image_ref[s] - e * new_ref[0, s]
        c = c + sum_all(residual * residual)
    lane = lax.broadcasted_iota(jnp.int32, sums_ref.shape, 1)
    sums = jnp.zeros(sums_ref.shape, jnp.float32)
    for place, value in enumerate((a, b, e, c)):
        sums = jnp.where(lane == place, value, sums)
    sums_ref[...] = sums


def polar_kernel(both_ref, table_ref, centre_ref, sums_ref, out_ref):
    states, _, block, _ = both_ref.shape
    rows = lax.broadcasted_iota(jnp.int32, (block, block), 0)
    columns = lax.broadcasted_iota(jnp.int32, (block, block), 1)
    unit = (rows == columns).astype(jnp.float32)

    def product(x, y, contract=((1,), (0,))):
        return lax.dot_general(
            x, y, (contract, ((), ())), precision=HIGHEST, preferred_element_type=jnp.float32
        )

    energy, factor, square = quotient(table_ref[...])
    vector = updated(
        both_ref[:, 0].reshape(states * block, block),
        both_ref[:, 1].reshape(states * block, block),
        energy,
        factor,
    ) * lax.rsqrt(square + TINY)
    centre = centre_ref[...].astype(jnp.float32) * lax.rsqrt(
        sum_all(sums_ref[2 * ENV_STEPS]) + TINY
    )
    grams = [product(x, x, ((0,), (0,))) for x in (vector, centre)]
    totals = [unit, unit]
    for step in range(POLAR):
        factors = [1.5 * unit - 0.5 * gram for gram in grams]
        totals = [
            factor if step == 0 else product(total, factor)
            for total, factor in zip(totals, factors)
        ]
        if step < POLAR - 1:
            grams = [
                product(product(factor, gram), factor) for gram, factor in zip(grams, factors)
            ]
    closing = product(totals[0], product(centre, totals[1]), ((1,), (1,)))
    out_ref[...] = product(vector, closing).reshape(states, block, block).astype(jnp.bfloat16)


def call(kernel, out_shape, scratch_shapes, flops, operands):
    return pl.pallas_call(
        kernel,
        out_shape=out_shape,
        scratch_shapes=scratch_shapes,
        compiler_params=pltpu.CompilerParams(vmem_limit_bytes=VMEM_LIMIT),
        cost_estimate=pl.CostEstimate(
            flops=flops,
            bytes_accessed=sum(int(np.prod(x.shape)) * x.dtype.itemsize for x in operands),
            transcendentals=0,
        ),
    )(*operands)


def float_out(*shape):
    return jax.ShapeDtypeStruct(shape, jnp.float32)


def half_out(*shape):
    return jax.ShapeDtypeStruct(shape, jnp.bfloat16)


def work(states, channels, block):
    return 4 * states * channels * block**3 + 2 * (states * channels * block) ** 2


def expanded(weight, groups, channels, states):
    spread = spread_matrix(groups, channels, states)
    sizes = tuple(even(len(group)) * ROWS for group in groups)
    return call(
        functools.partial(expand_kernel, sizes),
        half_out(spread.shape[0], -(-max(sizes) // 128) * 128),
        [],
        2 * spread.size * spread.shape[0],
        (weight, jnp.asarray(spread, jnp.bfloat16)),
    )


def left_front(env, tensors, weight, groups):
    channels, block = count_channels(env), env[0].shape[1]
    states, pieces = tensors.shape[1], len(env)
    outs = call(
        functools.partial(left_kernel, groups, states, pieces),
        [half_out(channels // pieces, block, block)] * (states * pieces),
        [pltpu.VMEM((states * channels * block, block), jnp.float32)],
        work(states, channels, block),
        (*env, tensors, weight),
    )
    return [outs[s * pieces : (s + 1) * pieces] for s in range(states)]


def left_close(iso, gathered, moved):
    channels, block, _ = gathered.shape
    return call(
        left_close_kernel,
        (half_out(channels, block, block), float_out(ROWS, block)),
        [],
        2 * channels * block**3,
        (iso, gathered, moved),
    )


def right_whole(envs, own, tensors, weight, groups):
    channels, block = count_channels(envs[0]), envs[0][0].shape[1]
    states, pieces = len(envs), len(envs[0])
    outs = call(
        functools.partial(right_kernel, groups, states, pieces),
        [half_out(channels // pieces, block, block)] * pieces + [float_out(ROWS, block)],
        [
            pltpu.VMEM((states * channels * block, block), jnp.float32),
            pltpu.VMEM((states * channels * block, block), jnp.bfloat16),
        ],
        work(states, channels, block),
        (*(chunk for env in envs for chunk in env), own, tensors, weight),
    )
    return outs[:pieces], outs[pieces]


def apply_operator(
    env, rights, weight, groups, left_sums, right_sums, entry_count, vectors, images=None, table=None
):
    channels, block = count_channels(env), env[0].shape[1]
    states, pieces = vectors.shape[1], len(env)
    renew = images is not None
    operands = (
        *(chunk for right in rights for chunk in right),
        *env,
        weight,
        left_sums,
        right_sums,
        vectors,
    ) + ((images, table) if renew else ())
    return call(
        functools.partial(operator_kernel, groups, states, pieces, renew, entry_count),
        (
            float_out(states, block, block),
            float_out(1, 128),
            float_out(CLASSES, states, block, block),
        ),
        [
            pltpu.VMEM((states * channels * block, block), jnp.float32),
            pltpu.VMEM((states * channels * block, block), jnp.bfloat16),
        ],
        work(states, channels, block),
        operands,
    )


def polar(both, table, centre, sums):
    states, _, block, _ = both.shape
    return call(
        polar_kernel,
        half_out(states, block, block),
        [],
        600 * block**3,
        (both, table, centre, sums),
    )


def charge_mask(channels, states, sectors):
    charge = np.array([CHARGE_STEPS[channel % CLASSES] for channel in range(channels)])
    state = np.arange(states)
    balance = (
        charge[:, None, None, None]
        + state[None, None, None, :]
        - state[None, None, :, None]
        - charge[None, :, None, None]
    )
    return jnp.asarray((balance % sectors == 0).astype(np.float32)).astype(jnp.bfloat16)


def weight_matrices(mpo, pattern, sectors):
    channels, _, states, _ = mpo.shape
    allowed = charge_mask(channels, states, sectors)
    weights = mpo * pattern[:, :, None, None].astype(jnp.bfloat16) * allowed
    size = states * channels
    left = jnp.transpose(weights, (2, 1, 3, 0)).reshape(size, size)
    right = jnp.transpose(weights, (2, 0, 3, 1)).reshape(size, size)
    return jnp.stack([left, right])


def classes_of(places, x):
    one, minus = places.ahead(x, 1), places.ahead(x, -1)
    return jnp.stack([x, one, minus, places.ahead(one, 1), places.ahead(minus, -1)])


def after(first, then):
    return lax.optimization_barrier((first, then))


def local(left_iso, right_iso, centre, left_env, right_env, mpo, pattern):
    sites, secs = lax.axis_size("site"), lax.axis_size("sec")
    places = Places(sites, secs)
    left_iso, right_iso, centre = left_iso[0, :, 0], right_iso[0, :, 0], centre[0, 0]
    states, block, _ = left_iso.shape
    channels = mpo.shape[1]
    entry_count = left_env.size * secs
    left_groups = label_groups(channels, states, secs, 1)
    right_groups = label_groups(channels, states, secs, -1)

    pieces = PIECES if channels % PIECES == 0 else 1

    def split(env):
        return jnp.split(env, pieces)

    def ahead(env, by, chain_by=0):
        return [places.ahead(chunk, by, chain_by) for chunk in env]

    def fetch_env(env):
        return [places.fetch(chunk) for chunk in split(env)]

    right = fetch_env(right_env[0, :, 0])
    both_isos = places.fetch(jnp.concatenate([left_iso, right_iso]))
    left_isos, right_isos = [both_isos[:states]], [both_isos[states:]]
    for step in range(1, ENV_STEPS):
        left_isos.append(places.fetch(left_iso, step))
        right_isos.append(places.fetch(right_iso, -step))
    own_tensors = places.fetch(jnp.concatenate([left_iso, centre[None]]), ENV_STEPS)
    own_iso, own_centre = own_tensors[:states], own_tensors[states]
    centres = [own_centre] + [places.fetch(centre, ENV_STEPS, s) for s in range(1, states)]
    right, left_env = after(right, left_env)
    left = fetch_env(left_env[0, :, 0])

    gathered_weights = lax.all_gather(weight_matrices(mpo[0], pattern[0], secs), "site")
    chain = places.my_chain()

    def weight_of(site_by, kind):
        weight = lax.dynamic_index_in_dim(
            gathered_weights, (chain + site_by) % sites, 0, False
        )[kind]
        return expanded(weight, (left_groups, right_groups)[kind], channels, states)

    weights = (
        [weight_of(step, 0) for step in range(ENV_STEPS + 1)],
        [weight_of(-step, 1) for step in range(ENV_STEPS)],
    )
    isos = jnp.stack(left_isos + right_isos)
    vector = jnp.einsum(
        "sxy,syz->sxz", own_iso, jnp.stack(centres), preferred_element_type=jnp.float32
    )
    weights, (isos, vector) = after(weights, (isos, vector))
    rolled = classes_of(places, isos)
    vectors = classes_of(places, vector)
    centre_float = own_centre.astype(jnp.float32)
    centre_square = jnp.sum((centre_float * centre_float).reshape(-1, ROWS, block), axis=0)

    left_squares, right_squares = [], []
    for step in range(ENV_STEPS):
        envs = [right]
        for t in range(1, states):
            envs.append(ahead(envs[-1], 1))
        if step == 0:
            (vectors, rolled), envs = after((vectors, rolled), envs)
        right, square = right_whole(
            envs,
            right_isos[step],
            rolled[:, ENV_STEPS + step],
            weights[1][step],
            right_groups,
        )
        right_squares.append(square)

        gathered = left_front(left, rolled[:, step], weights[0][step], left_groups)
        moved = [None] * pieces
        for s in reversed(range(1, states)):
            for piece in range(pieces):
                part = jnp.einsum(
                    "xy,vxz->vyz",
                    left_isos[step][s],
                    gathered[s][piece],
                    preferred_element_type=jnp.float32,
                )
                if moved[piece] is not None:
                    part = part + moved[piece].astype(jnp.float32)
                moved[piece] = places.ahead(part.astype(jnp.bfloat16), -1)
        closed = [
            left_close(left_isos[step][0], gathered[0][piece], moved[piece])
            for piece in range(pieces)
        ]
        left = [env for env, _ in closed]
        left_squares.append(sum(square for _, square in closed))

    sums = places.summed(jnp.stack(left_squares + right_squares + [centre_square]))
    right_sums = sums
    if (2 * ENV_STEPS) % sites:
        right = ahead(right, 0, 2 * ENV_STEPS)
        right_sums = places.ahead(sums, 0, 2 * ENV_STEPS)

    rights = [right]
    for s in range(1, states):
        rights.append(ahead(rights[-1], 1))
    images, table = None, None
    for step in range(DESCENT):
        image, own_sums, vectors = apply_operator(
            left,
            rights,
            weights[0][ENV_STEPS],
            left_groups,
            sums,
            right_sums,
            entry_count,
            vectors,
            images,
            table,
        )
        table = places.collect(own_sums[0])
        if step < DESCENT - 1:
            images = classes_of(places, image)

    both = jnp.stack([vectors[0], image], axis=1)
    columns = jnp.stack([both[0]] + [places.ahead(both[s], -s) for s in range(1, states)])
    column_left = polar(columns, table, own_centre, sums)
    new_left = jnp.stack(
        [places.send_home(column_left[s], ENV_STEPS, -s) for s in range(states)]
    )
    home_table = places.send_home(table, ENV_STEPS, 0)
    energy = jnp.sum(home_table[:, 0]) / (jnp.sum(home_table[:, 1]) + TINY)
    return new_left[None, :, None], jnp.reshape(energy, (1,))


def solution(mesh):
    placed = (
        P("site", None, "sec", None, None),
        P("site", None, "sec", None, None),
        P("site", "sec", None, None),
        P("site", None, "sec", None, None),
        P("site", None, "sec", None, None),
        P("site", None, None, None, None),
        P("site", None, None),
    )
    return jax.shard_map(
        local,
        mesh=mesh,
        in_specs=placed,
        out_specs=(P("site", None, "sec", None, None), P("site")),
        check_vma=False,
    )
```

```python
import functools

import jax
import jax.numpy as jnp
import numpy as np
from jax import lax
from jax.experimental import pallas as pl
from jax.experimental.pallas import tpu as pltpu
from jax.sharding import PartitionSpec as P

ENV_STEPS = 2
DESCENT = 2
POLAR = 6

TINY = 1e-06
HIGHEST = lax.Precision.HIGHEST
CHARGE_STEPS = (0, 1, -1, 2, -2)
CLASSES = len(CHARGE_STEPS)
BOTH = ("site", "sec")
VMEM_LIMIT = 28 * 1024 * 1024
PIECES = 2


SLOW = 4


class Places:
    def __init__(self, sites, secs):
        self.sites, self.secs = sites, secs
        self.slow = SLOW if secs % (2 * SLOW) == 0 else 1
        self.fast = secs // self.slow
        self.columns = self.fast // 2

    def home(self, site, sector):
        return (site % self.sites) * self.secs + sector % self.secs

    def place(self, position):
        column, row = position // self.slow, position % self.slow
        return column, row if column % 2 == 0 else self.slow - 1 - row

    def slot(self, chain, sector):
        chain, sector = chain % self.sites, sector % self.secs
        column, row = self.place(sector // 2)
        place = row * self.fast + chain % 2 * self.columns + column
        return (chain // 2 * 2 + sector % 2) * self.secs + place

    def pairs(self, source, target):
        return [
            (source(chain, sector), target(chain, sector))
            for chain in range(self.sites)
            for sector in range(self.secs)
        ]

    def fetch(self, x, site_by=0, sec_by=0):
        return lax.ppermute(
            x, BOTH, self.pairs(lambda g, k: self.home(g + site_by, k + sec_by), self.slot)
        )

    def send_home(self, x, site_by, sec_by):
        return lax.ppermute(
            x, BOTH, self.pairs(self.slot, lambda g, k: self.home(g + site_by, k + sec_by))
        )

    def ahead(self, x, by, chain_by=0):
        return lax.ppermute(
            x, BOTH, self.pairs(lambda g, k: self.slot(g + chain_by, k + by), self.slot)
        )

    def partner(self, x, bit):
        return lax.ppermute(x, BOTH, self.pairs(lambda g, k: self.slot(g, k ^ bit), self.slot))

    def my_chain(self):
        half = lax.axis_index("sec") % self.fast // self.columns
        return lax.axis_index("site") // 2 * 2 + half

    def my_sector(self):
        sectors = np.zeros(self.sites * self.secs, np.int32)
        for chain in range(self.sites):
            for sector in range(self.secs):
                sectors[self.slot(chain, sector)] = sector
        return jnp.asarray(sectors)[lax.axis_index("site") * self.secs + lax.axis_index("sec")]

    def summed(self, values):
        bit = 1
        while bit < self.secs:
            values = values + self.partner(values, bit)
            bit *= 2
        return values

    def collect(self, values):
        sector = self.my_sector()
        table = values[None]
        bit = 1
        while bit < self.secs:
            other = self.partner(table, bit)
            first = (sector & bit) == 0
            table = jnp.where(
                first, jnp.concatenate([table, other]), jnp.concatenate([other, table])
            )
            bit *= 2
        return table


ROWS = 8


def label_groups(channels, states, sectors, sign):
    groups = {}
    for state in range(states):
        for channel in range(channels):
            label = (state + sign * CHARGE_STEPS[channel % CLASSES]) % sectors
            groups.setdefault(label, []).append((state, channel))
    return [groups[label] for label in sorted(groups)]


def even(count):
    return count + count % 2


def spread_matrix(groups, channels, states):
    rows = []
    for group in groups:
        block = np.zeros((even(len(group)), ROWS, states * channels), np.float32)
        for index, (state, channel) in enumerate(group):
            block[index, :, state * channels + channel] = 1
        rows.append(block.reshape(-1, states * channels))
    return np.concatenate(rows)


def expand_kernel(sizes, weight_ref, spread_ref, out_ref):
    start = 0
    for size in sizes:
        spread = spread_ref[pl.ds(start, size), :]
        picked = jnp.dot(spread, weight_ref[...], preferred_element_type=jnp.float32)
        full = lax.dot_general(
            picked.astype(jnp.bfloat16),
            spread,
            (((1,), (1,)), ((), ())),
            preferred_element_type=jnp.float32,
        )
        row = lax.broadcasted_iota(jnp.int32, full.shape, 0)
        column = lax.broadcasted_iota(jnp.int32, full.shape, 1)
        same = lax.rem(row, ROWS) == lax.rem(column, ROWS)
        out_ref[pl.ds(start, size), pl.ds(0, size)] = jnp.where(same, full, 0.0).astype(
            jnp.bfloat16
        )
        start += size


def mix_channels(groups, channels, weight_ref, mixed_ref, write, block):
    def step(index, carry):
        first = pl.multiple_of(index * 2 * ROWS, 2 * ROWS)

        def place(pair):
            state, channel = pair
            return pl.multiple_of((state * channels + channel) * block + first, 2 * ROWS)

        start = 0
        for group in groups:
            size = even(len(group)) * ROWS
            parts = []
            for pair in group:
                rows = place(pair)
                halves = [mixed_ref[pl.ds(rows + half * ROWS, ROWS), :] for half in range(2)]
                parts.append(jnp.concatenate(halves, axis=1))
            if len(group) % 2:
                parts.append(parts[0])
            operand = jnp.concatenate(parts, axis=0).astype(jnp.bfloat16)
            product = jnp.dot(
                weight_ref[pl.ds(start, size), pl.ds(0, size)],
                operand,
                preferred_element_type=jnp.float32,
            )
            for number, pair in enumerate(group):
                rows = product[number * ROWS : (number + 1) * ROWS]
                both = jnp.concatenate([rows[:, :block], rows[:, block:]], axis=0)
                write(*pair, first, both.astype(jnp.bfloat16))
            start += size
        return carry

    lax.fori_loop(0, block // (2 * ROWS), step, 0)


def into(gathered_ref, channels, block):
    def write(state, channel, first, rows):
        start = (state * channels + channel) * block
        gathered_ref[pl.ds(pl.multiple_of(start + first, 2 * ROWS), 2 * ROWS), :] = rows

    return write


def batches(items, most):
    pieces = -(-len(items) // most)
    size = -(-len(items) // pieces)
    return [items[start : start + size] for start in range(0, len(items), size)]


def channel_of(chunks, channel):
    size = chunks[0].shape[0]
    return chunks[channel // size][channel % size]


def put_channel(chunks, channel, value):
    size = chunks[0].shape[0]
    chunks[channel // size][channel % size] = value


def count_channels(chunks):
    return sum(chunk.shape[0] for chunk in chunks)


def mix_left(env, tensors, mixed_ref):
    channels, block = count_channels(env), env[0].shape[1]
    for cls in range(CLASSES):
        right = jnp.concatenate(tensors[cls], axis=1)
        for batch in batches(list(range(cls, channels, CLASSES)), 3):
            rows = jnp.concatenate([channel_of(env, channel) for channel in batch], axis=0)
            product = jnp.dot(rows, right, preferred_element_type=jnp.float32)
            for number, channel in enumerate(batch):
                for t in range(len(tensors[cls])):
                    mixed_ref[pl.ds((t * channels + channel) * block, block), :] = product[
                        number * block : (number + 1) * block, t * block : (t + 1) * block
                    ]


def left_kernel(groups, states, pieces, *refs):
    env, (tensor_ref, weight_ref) = refs[:pieces], refs[pieces : pieces + 2]
    outs, mixed_ref = refs[pieces + 2 : -1], refs[-1]
    channels, block = count_channels(env), env[0].shape[1]
    tensors = [[tensor_ref[cls, t] for t in range(states)] for cls in range(CLASSES)]
    mix_left(env, tensors, mixed_ref)

    def write(state, channel, first, rows):
        size = channels // pieces
        out_ref = outs[state * pieces + channel // size]
        out_ref[channel % size, pl.ds(first, 2 * ROWS), :] = rows

    mix_channels(groups, channels, weight_ref, mixed_ref, write, block)


def left_close_kernel(iso_ref, gathered_ref, moved_ref, out_ref, square_ref):
    channels, block, _ = gathered_ref.shape
    square = jnp.zeros((ROWS, block), jnp.float32)
    for batch in batches(list(range(channels)), 2):
        right = jnp.concatenate([gathered_ref[channel] for channel in batch], axis=1)
        product = lax.dot_general(
            iso_ref[...], right, (((0,), (0,)), ((), ())), preferred_element_type=jnp.float32
        )
        for number, channel in enumerate(batch):
            part = product[:, number * block : (number + 1) * block]
            part = part + moved_ref[channel].astype(jnp.float32)
            out_ref[channel] = part.astype(jnp.bfloat16)
            square = square + jnp.sum((part * part).reshape(-1, ROWS, block), axis=0)
    square_ref[...] = square


def right_kernel(groups, states, pieces, *refs):
    envs = [refs[t * pieces : (t + 1) * pieces] for t in range(states)]
    refs = refs[states * pieces :]
    own_ref, tensor_ref, weight_ref = refs[:3]
    outs, (square_ref, mixed_ref, gathered_ref) = refs[3 : 3 + pieces], refs[3 + pieces :]
    channels, block = count_channels(envs[0]), envs[0][0].shape[1]
    zero = jnp.zeros((block, block), jnp.bfloat16)
    for pair in batches(list(range(states)), 2):
        own = jnp.concatenate(
            [
                jnp.concatenate([own_ref[t] if t == other else zero for other in pair], axis=1)
                for t in pair
            ],
            axis=0,
        )
        for batch in batches(list(range(channels)), 3):
            rows = jnp.concatenate(
                [
                    jnp.concatenate([channel_of(envs[t], channel) for channel in batch], axis=0)
                    for t in pair
                ],
                axis=1,
            )
            product = lax.dot_general(
                rows, own, (((1,), (1,)), ((), ())), preferred_element_type=jnp.float32
            )
            for number, t in enumerate(pair):
                mixed_ref[pl.ds((t * channels + batch[0]) * block, len(batch) * block), :] = (
                    product[:, number * block : (number + 1) * block]
                )
    write = into(gathered_ref, channels, block)
    mix_channels(groups, channels, weight_ref, mixed_ref, write, block)
    square = jnp.zeros((ROWS, block), jnp.float32)
    for cls in range(CLASSES):
        left = jnp.concatenate([tensor_ref[cls, s] for s in range(states)], axis=1)
        for batch in batches(list(range(cls, channels, CLASSES)), 2):
            right = jnp.concatenate(
                [
                    jnp.concatenate(
                        [
                            gathered_ref[pl.ds((s * channels + channel) * block, block), :]
                            for s in range(states)
                        ],
                        axis=0,
                    )
                    for channel in batch
                ],
                axis=1,
            )
            product = jnp.dot(left, right, preferred_element_type=jnp.float32)
            for number, channel in enumerate(batch):
                part = product[:, number * block : (number + 1) * block]
                put_channel(outs, channel, part.astype(jnp.bfloat16))
                square = square + jnp.sum((part * part).reshape(-1, ROWS, block), axis=0)
    square_ref[...] = square


def quotient(table):
    a, b, e, c = (table[:, column : column + 1] for column in range(4))

    def total(x):
        return jnp.sum(x, axis=0, keepdims=True)

    whole_a, whole_b = total(a), total(b)
    energy = whole_a / (whole_b + TINY)
    off = e - energy
    residual_sq = total(c + 2.0 * off * (a - e * b) + off * off * b)
    factor = 0.5 * jnp.sqrt(whole_b / (residual_sq + TINY))
    square = whole_b - 2.0 * factor * (whole_a - energy * whole_b) + factor * factor * residual_sq
    return energy, factor, square


def updated(vector, applied, energy, factor):
    return vector - factor * (applied - energy * vector)


def sum_all(x):
    return jnp.sum(jnp.sum(x, axis=0, keepdims=True), axis=1, keepdims=True)


def env_scale(sums_ref, first, entry_count):
    scale = jnp.ones((1, 1), jnp.float32)
    for step in range(first, first + ENV_STEPS):
        square = sum_all(sums_ref[step])
        scale = scale * lax.rsqrt(scale * scale * square / entry_count + TINY)
    return scale


def operator_kernel(groups, states, pieces, renew, entry_count, *refs):
    rights = [refs[t * pieces : (t + 1) * pieces] for t in range(states)]
    refs = refs[states * pieces :]
    env, refs = refs[:pieces], refs[pieces:]
    weight_ref, left_sums_ref, right_sums_ref, vector_ref = refs[:4]
    rest = refs[4:]
    if renew:
        own_ref, moved_ref, table_ref = rest[:3]
        rest = rest[3:]
        energy, factor, _ = quotient(table_ref[...])
    image_ref, sums_ref, new_ref, mixed_ref, gathered_ref = rest
    channels, block = count_channels(env), env[0].shape[1]
    tensors = []
    for cls in range(CLASSES):
        row = []
        for t in range(states):
            vector = vector_ref[cls, t]
            if renew:
                image = own_ref[t] if cls == 0 else moved_ref[cls - 1, t].astype(jnp.float32)
                vector = updated(vector, image, energy, factor)
            new_ref[cls, t] = vector
            row.append(vector.astype(jnp.bfloat16))
        tensors.append(row)
    mix_left(env, tensors, mixed_ref)
    write = into(gathered_ref, channels, block)
    mix_channels(groups, channels, weight_ref, mixed_ref, write, block)
    scale = env_scale(left_sums_ref, 0, entry_count) * env_scale(
        right_sums_ref, ENV_STEPS, entry_count
    )
    a = jnp.zeros((1, 1), jnp.float32)
    b = jnp.zeros((1, 1), jnp.float32)
    for s in range(states):
        total = jnp.zeros((block, block), jnp.float32)
        for batch in batches(list(range(channels)), 6):
            left = jnp.concatenate(
                [
                    gathered_ref[pl.ds((s * channels + channel) * block, block), :]
                    for channel in batch
                ],
                axis=1,
            )
            right = jnp.concatenate([channel_of(rights[s], channel) for channel in batch], axis=0)
            total = total + jnp.dot(left, right, preferred_element_type=jnp.float32)
        total = total * scale
        image_ref[s] = total
        vector = new_ref[0, s]
        a = a + sum_all(vector * total)
        b = b + sum_all(vector * vector)
    e = jnp.where(b > 0, a / jnp.where(b > 0, b, 1.0), 0.0)
    c = jnp.zeros((1, 1), jnp.float32)
    for s in range(states):
        residual = image_ref[s] - e * new_ref[0, s]
        c = c + sum_all(residual * residual)
    lane = lax.broadcasted_iota(jnp.int32, sums_ref.shape, 1)
    sums = jnp.zeros(sums_ref.shape, jnp.float32)
    for place, value in enumerate((a, b, e, c)):
        sums = jnp.where(lane == place, value, sums)
    sums_ref[...] = sums


def polar_kernel(both_ref, table_ref, centre_ref, sums_ref, out_ref):
    states, _, block, _ = both_ref.shape
    rows = lax.broadcasted_iota(jnp.int32, (block, block), 0)
    columns = lax.broadcasted_iota(jnp.int32, (block, block), 1)
    unit = (rows == columns).astype(jnp.float32)

    def product(x, y, contract=((1,), (0,))):
        return lax.dot_general(
            x, y, (contract, ((), ())), precision=HIGHEST, preferred_element_type=jnp.float32
        )

    energy, factor, square = quotient(table_ref[...])
    vector = updated(
        both_ref[:, 0].reshape(states * block, block),
        both_ref[:, 1].reshape(states * block, block),
        energy,
        factor,
    ) * lax.rsqrt(square + TINY)
    centre = centre_ref[...].astype(jnp.float32) * lax.rsqrt(
        sum_all(sums_ref[2 * ENV_STEPS]) + TINY
    )
    grams = [product(x, x, ((0,), (0,))) for x in (vector, centre)]
    totals = [unit, unit]
    for step in range(POLAR):
        factors = [1.5 * unit - 0.5 * gram for gram in grams]
        totals = [
            factor if step == 0 else product(total, factor)
            for total, factor in zip(totals, factors)
        ]
        if step < POLAR - 1:
            grams = [
                product(product(factor, gram), factor) for gram, factor in zip(grams, factors)
            ]
    closing = product(totals[0], product(centre, totals[1]), ((1,), (1,)))
    out_ref[...] = product(vector, closing).reshape(states, block, block).astype(jnp.bfloat16)


def call(kernel, out_shape, scratch_shapes, flops, operands):
    return pl.pallas_call(
        kernel,
        out_shape=out_shape,
        scratch_shapes=scratch_shapes,
        compiler_params=pltpu.CompilerParams(vmem_limit_bytes=VMEM_LIMIT),
        cost_estimate=pl.CostEstimate(
            flops=flops,
            bytes_accessed=sum(int(np.prod(x.shape)) * x.dtype.itemsize for x in operands),
            transcendentals=0,
        ),
    )(*operands)


def float_out(*shape):
    return jax.ShapeDtypeStruct(shape, jnp.float32)


def half_out(*shape):
    return jax.ShapeDtypeStruct(shape, jnp.bfloat16)


def work(states, channels, block):
    return 4 * states * channels * block**3 + 2 * (states * channels * block) ** 2


def expanded(weight, groups, channels, states):
    spread = spread_matrix(groups, channels, states)
    sizes = tuple(even(len(group)) * ROWS for group in groups)
    return call(
        functools.partial(expand_kernel, sizes),
        half_out(spread.shape[0], -(-max(sizes) // 128) * 128),
        [],
        2 * spread.size * spread.shape[0],
        (weight, jnp.asarray(spread, jnp.bfloat16)),
    )


def left_front(env, tensors, weight, groups):
    channels, block = count_channels(env), env[0].shape[1]
    states, pieces = tensors.shape[1], len(env)
    outs = call(
        functools.partial(left_kernel, groups, states, pieces),
        [half_out(channels // pieces, block, block)] * (states * pieces),
        [pltpu.VMEM((states * channels * block, block), jnp.float32)],
        work(states, channels, block),
        (*env, tensors, weight),
    )
    return [outs[s * pieces : (s + 1) * pieces] for s in range(states)]


def left_close(iso, gathered, moved):
    channels, block, _ = gathered.shape
    return call(
        left_close_kernel,
        (half_out(channels, block, block), float_out(ROWS, block)),
        [],
        2 * channels * block**3,
        (iso, gathered, moved),
    )


def right_whole(envs, own, tensors, weight, groups):
    channels, block = count_channels(envs[0]), envs[0][0].shape[1]
    states, pieces = len(envs), len(envs[0])
    outs = call(
        functools.partial(right_kernel, groups, states, pieces),
        [half_out(channels // pieces, block, block)] * pieces + [float_out(ROWS, block)],
        [
            pltpu.VMEM((states * channels * block, block), jnp.float32),
            pltpu.VMEM((states * channels * block, block), jnp.bfloat16),
        ],
        work(states, channels, block),
        (*(chunk for env in envs for chunk in env), own, tensors, weight),
    )
    return outs[:pieces], outs[pieces]


def apply_operator(
    env, rights, weight, groups, left_sums, right_sums, entry_count, vectors, image=None, table=None, rolled=None
):
    channels, block = count_channels(env), env[0].shape[1]
    states, pieces = vectors.shape[1], len(env)
    renew = image is not None
    operands = (
        *(chunk for right in rights for chunk in right),
        *env,
        weight,
        left_sums,
        right_sums,
        vectors,
    ) + ((image, rolled, table) if renew else ())
    return call(
        functools.partial(operator_kernel, groups, states, pieces, renew, entry_count),
        (
            float_out(states, block, block),
            float_out(1, 128),
            float_out(CLASSES, states, block, block),
        ),
        [
            pltpu.VMEM((states * channels * block, block), jnp.float32),
            pltpu.VMEM((states * channels * block, block), jnp.bfloat16),
        ],
        work(states, channels, block),
        operands,
    )


def polar(both, table, centre, sums):
    states, _, block, _ = both.shape
    return call(
        polar_kernel,
        half_out(states, block, block),
        [],
        600 * block**3,
        (both, table, centre, sums),
    )


def charge_mask(channels, states, sectors):
    charge = np.array([CHARGE_STEPS[channel % CLASSES] for channel in range(channels)])
    state = np.arange(states)
    balance = (
        charge[:, None, None, None]
        + state[None, None, None, :]
        - state[None, None, :, None]
        - charge[None, :, None, None]
    )
    return jnp.asarray((balance % sectors == 0).astype(np.float32)).astype(jnp.bfloat16)


def weight_matrices(mpo, pattern, sectors):
    channels, _, states, _ = mpo.shape
    allowed = charge_mask(channels, states, sectors)
    weights = mpo * pattern[:, :, None, None].astype(jnp.bfloat16) * allowed
    size = states * channels
    left = jnp.transpose(weights, (2, 1, 3, 0)).reshape(size, size)
    right = jnp.transpose(weights, (2, 0, 3, 1)).reshape(size, size)
    return jnp.stack([left, right])


def classes_of(places, x):
    one, minus = places.ahead(x, 1), places.ahead(x, -1)
    return jnp.stack([x, one, minus, places.ahead(one, 1), places.ahead(minus, -1)])


def other_classes_of(places, x):
    return jnp.stack([places.ahead(x, charge) for charge in CHARGE_STEPS[1:]])


def after(first, then):
    return lax.optimization_barrier((first, then))


def local(left_iso, right_iso, centre, left_env, right_env, mpo, pattern):
    sites, secs = lax.axis_size("site"), lax.axis_size("sec")
    places = Places(sites, secs)
    left_iso, right_iso, centre = left_iso[0, :, 0], right_iso[0, :, 0], centre[0, 0]
    states, block, _ = left_iso.shape
    channels = mpo.shape[1]
    entry_count = left_env.size * secs
    left_groups = label_groups(channels, states, secs, 1)
    right_groups = label_groups(channels, states, secs, -1)

    pieces = PIECES if channels % PIECES == 0 else 1

    def split(env):
        return jnp.split(env, pieces)

    def ahead(env, by, chain_by=0):
        return [places.ahead(chunk, by, chain_by) for chunk in env]

    def fetch_env(env):
        return [places.fetch(chunk) for chunk in split(env)]

    right = fetch_env(right_env[0, :, 0])
    right, (left_iso, right_iso, centre, left_env, mpo, pattern) = after(
        right, (left_iso, right_iso, centre, left_env, mpo, pattern)
    )
    both_isos = places.fetch(jnp.concatenate([left_iso, right_iso]))
    left_isos, right_isos = [both_isos[:states]], [both_isos[states:]]
    for step in range(1, ENV_STEPS):
        left_isos.append(places.fetch(left_iso, step))
        right_isos.append(places.fetch(right_iso, -step))
    own_tensors = places.fetch(jnp.concatenate([left_iso, centre[None]]), ENV_STEPS)
    own_iso, own_centre = own_tensors[:states], own_tensors[states]
    centres = [own_centre] + [places.fetch(centre, ENV_STEPS, s) for s in range(1, states)]
    own_weights = weight_matrices(mpo[0], pattern[0], secs)

    def weight_of(site_by, kind):
        weight = places.fetch(own_weights[kind], site_by)
        return expanded(weight, (left_groups, right_groups)[kind], channels, states)

    weights = (
        [weight_of(step, 0) for step in range(ENV_STEPS + 1)],
        [weight_of(-step, 1) for step in range(ENV_STEPS)],
    )
    both_isos, left_env = after(both_isos, left_env)
    left = fetch_env(left_env[0, :, 0])
    left_isos[0], right_isos[0] = both_isos[:states], both_isos[states:]
    isos = jnp.stack(left_isos + right_isos)
    vector = jnp.einsum(
        "sxy,syz->sxz", own_iso, jnp.stack(centres), preferred_element_type=jnp.float32
    )
    rolled = classes_of(places, isos)
    vectors = classes_of(places, vector)
    centre_float = own_centre.astype(jnp.float32)
    centre_square = jnp.sum((centre_float * centre_float).reshape(-1, ROWS, block), axis=0)

    left_squares, right_squares = [], []
    for step in range(ENV_STEPS):
        envs = [right]
        for t in range(1, states):
            envs.append(ahead(envs[-1], 1))
        if step == 0:
            (vectors, rolled, weights), envs = after((vectors, rolled, weights), envs)
        right, square = right_whole(
            envs,
            right_isos[step],
            rolled[:, ENV_STEPS + step],
            weights[1][step],
            right_groups,
        )
        right_squares.append(square)

        gathered = left_front(left, rolled[:, step], weights[0][step], left_groups)
        moved = [None] * pieces
        for s in reversed(range(1, states)):
            for piece in range(pieces):
                part = jnp.einsum(
                    "xy,vxz->vyz",
                    left_isos[step][s],
                    gathered[s][piece],
                    preferred_element_type=jnp.float32,
                )
                if moved[piece] is not None:
                    part = part + moved[piece].astype(jnp.float32)
                moved[piece] = places.ahead(part.astype(jnp.bfloat16), -1)
        closed = [
            left_close(left_isos[step][0], gathered[0][piece], moved[piece])
            for piece in range(pieces)
        ]
        left = [env for env, _ in closed]
        left_squares.append(sum(square for _, square in closed))

    sums = places.summed(jnp.stack(left_squares + right_squares + [centre_square]))
    right_sums = sums
    if (2 * ENV_STEPS) % sites:
        right = ahead(right, 0, 2 * ENV_STEPS)
        right_sums = places.ahead(sums, 0, 2 * ENV_STEPS)

    rights = [right]
    for s in range(1, states):
        rights.append(ahead(rights[-1], 1))
    image, table, images = None, None, None
    for step in range(DESCENT):
        image, own_sums, vectors = apply_operator(
            left,
            rights,
            weights[0][ENV_STEPS],
            left_groups,
            sums,
            right_sums,
            entry_count,
            vectors,
            image,
            table,
            images,
        )
        table = places.collect(own_sums[0])
        if step < DESCENT - 1:
            images = other_classes_of(places, image.astype(jnp.bfloat16))

    both = jnp.stack([vectors[0], image], axis=1)
    columns = jnp.stack([both[0]] + [places.ahead(both[s], -s) for s in range(1, states)])
    column_left = polar(columns, table, own_centre, sums)
    new_left = jnp.stack(
        [places.send_home(column_left[s], ENV_STEPS, -s) for s in range(states)]
    )
    home_table = places.send_home(table, ENV_STEPS, 0)
    energy = jnp.sum(home_table[:, 0]) / (jnp.sum(home_table[:, 1]) + TINY)
    return new_left[None, :, None], jnp.reshape(energy, (1,))


def solution(mesh):
    placed = (
        P("site", None, "sec", None, None),
        P("site", None, "sec", None, None),
        P("site", "sec", None, None),
        P("site", None, "sec", None, None),
        P("site", None, "sec", None, None),
        P("site", None, None, None, None),
        P("site", None, None),
    )
    return jax.shard_map(
        local,
        mesh=mesh,
        in_specs=placed,
        out_specs=(P("site", None, "sec", None, None), P("site")),
        check_vma=False,
    )
```

```python
import functools

import jax
import jax.numpy as jnp
import numpy as np
from jax import lax
from jax.experimental import pallas as pl
from jax.experimental.pallas import tpu as pltpu
from jax.sharding import PartitionSpec as P

ENV_STEPS = 2
DESCENT = 2
POLAR = 6

TINY = 1e-06
HIGHEST = lax.Precision.HIGHEST
CHARGE_STEPS = (0, 1, -1, 2, -2)
CLASSES = len(CHARGE_STEPS)
BOTH = ("site", "sec")
VMEM_LIMIT = 20 * 1024 * 1024
PIECES = 2


class Places:
    def __init__(self, sites, secs):
        self.sites, self.secs = sites, secs
        self.half = secs // 2
        self.up = (self.half + 1) // 2

    def home(self, site, sector):
        return (site % self.sites) * self.secs + sector % self.secs

    def position(self, place):
        back = self.half - 1 + self.up - place
        if isinstance(place, int):
            return place if place < self.up else back
        return jnp.where(place < self.up, place, back)

    def slot(self, chain, sector):
        chain, sector = chain % self.sites, sector % self.secs
        place = chain % 2 * self.half + self.position(sector // 2)
        return (chain // 2 * 2 + sector % 2) * self.secs + place

    def pairs(self, source, target):
        return [
            (source(chain, sector), target(chain, sector))
            for chain in range(self.sites)
            for sector in range(self.secs)
        ]

    def fetch(self, x, site_by=0, sec_by=0):
        return lax.ppermute(
            x, BOTH, self.pairs(lambda g, k: self.home(g + site_by, k + sec_by), self.slot)
        )

    def send_home(self, x, site_by, sec_by):
        return lax.ppermute(
            x, BOTH, self.pairs(self.slot, lambda g, k: self.home(g + site_by, k + sec_by))
        )

    def ahead(self, x, by, chain_by=0):
        return lax.ppermute(
            x, BOTH, self.pairs(lambda g, k: self.slot(g + chain_by, k + by), self.slot)
        )

    def partner(self, x, bit):
        return lax.ppermute(x, BOTH, self.pairs(lambda g, k: self.slot(g, k ^ bit), self.slot))

    def my_chain(self):
        return lax.axis_index("site") // 2 * 2 + lax.axis_index("sec") // self.half

    def my_sector(self):
        position = self.position(lax.axis_index("sec") % self.half)
        return 2 * position + lax.axis_index("site") % 2

    def summed(self, values):
        bit = 1
        while bit < self.secs:
            values = values + self.partner(values, bit)
            bit *= 2
        return values

    def collect(self, values):
        sector = self.my_sector()
        table = values
        bit = 1
        while bit < self.secs:
            other = self.partner(table, bit)
            first = (sector & bit) == 0
            table = jnp.where(
                first, jnp.concatenate([table, other]), jnp.concatenate([other, table])
            )
            bit *= 2
        return table


ROWS = 8


def label_groups(channels, states, sectors, sign):
    groups = {}
    for state in range(states):
        for channel in range(channels):
            label = (state + sign * CHARGE_STEPS[channel % CLASSES]) % sectors
            groups.setdefault(label, []).append((state, channel))
    return [groups[label] for label in sorted(groups)]


def even(count):
    return count + count % 2


def spread_matrix(groups, channels, states):
    rows = []
    for group in groups:
        block = np.zeros((even(len(group)), ROWS, states * channels), np.float32)
        for index, (state, channel) in enumerate(group):
            block[index, :, state * channels + channel] = 1
        rows.append(block.reshape(-1, states * channels))
    return np.concatenate(rows)


def expand_kernel(sizes, weight_ref, spread_ref, out_ref):
    start = 0
    for size in sizes:
        spread = spread_ref[pl.ds(start, size), :]
        picked = jnp.dot(spread, weight_ref[...], preferred_element_type=jnp.float32)
        full = lax.dot_general(
            picked.astype(jnp.bfloat16),
            spread,
            (((1,), (1,)), ((), ())),
            preferred_element_type=jnp.float32,
        )
        row = lax.broadcasted_iota(jnp.int32, full.shape, 0)
        column = lax.broadcasted_iota(jnp.int32, full.shape, 1)
        same = lax.rem(row, ROWS) == lax.rem(column, ROWS)
        out_ref[pl.ds(start, size), pl.ds(0, size)] = jnp.where(same, full, 0.0).astype(
            jnp.bfloat16
        )
        start += size


def mix_channels(groups, channels, weight_ref, mixed_ref, write, block):
    def step(index, carry):
        first = pl.multiple_of(index * 2 * ROWS, 2 * ROWS)

        def place(pair):
            state, channel = pair
            return pl.multiple_of((state * channels + channel) * block + first, 2 * ROWS)

        start = 0
        for group in groups:
            size = even(len(group)) * ROWS
            parts = []
            for pair in group:
                rows = place(pair)
                halves = [mixed_ref[pl.ds(rows + half * ROWS, ROWS), :] for half in range(2)]
                parts.append(jnp.concatenate(halves, axis=1))
            if len(group) % 2:
                parts.append(parts[0])
            operand = jnp.concatenate(parts, axis=0).astype(jnp.bfloat16)
            product = jnp.dot(
                weight_ref[pl.ds(start, size), pl.ds(0, size)],
                operand,
                preferred_element_type=jnp.float32,
            )
            for number, pair in enumerate(group):
                rows = product[number * ROWS : (number + 1) * ROWS]
                both = jnp.concatenate([rows[:, :block], rows[:, block:]], axis=0)
                write(*pair, first, both.astype(jnp.bfloat16))
            start += size
        return carry

    lax.fori_loop(0, block // (2 * ROWS), step, 0)


def into(gathered_ref, channels, block):
    def write(state, channel, first, rows):
        start = (state * channels + channel) * block
        gathered_ref[pl.ds(pl.multiple_of(start + first, 2 * ROWS), 2 * ROWS), :] = rows

    return write


def batches(items, most):
    pieces = -(-len(items) // most)
    size = -(-len(items) // pieces)
    return [items[start : start + size] for start in range(0, len(items), size)]


def channel_of(chunks, channel):
    size = chunks[0].shape[0]
    return chunks[channel // size][channel % size]


def put_channel(chunks, channel, value):
    size = chunks[0].shape[0]
    chunks[channel // size][channel % size] = value


def count_channels(chunks):
    return sum(chunk.shape[0] for chunk in chunks)


def mix_left(env, tensors, mixed_ref):
    channels, block = count_channels(env), env[0].shape[1]
    for cls in range(CLASSES):
        right = jnp.concatenate(tensors[cls], axis=1)
        for batch in batches(list(range(cls, channels, CLASSES)), 3):
            rows = jnp.concatenate([channel_of(env, channel) for channel in batch], axis=0)
            product = jnp.dot(rows, right, preferred_element_type=jnp.float32)
            for number, channel in enumerate(batch):
                for t in range(len(tensors[cls])):
                    mixed_ref[pl.ds((t * channels + channel) * block, block), :] = product[
                        number * block : (number + 1) * block, t * block : (t + 1) * block
                    ]


def left_kernel(groups, states, pieces, *refs):
    env, (tensor_ref, weight_ref) = refs[:pieces], refs[pieces : pieces + 2]
    outs, mixed_ref = refs[pieces + 2 : -1], refs[-1]
    channels, block = count_channels(env), env[0].shape[1]
    tensors = [[tensor_ref[cls, t] for t in range(states)] for cls in range(CLASSES)]
    mix_left(env, tensors, mixed_ref)

    def write(state, channel, first, rows):
        size = channels // pieces
        out_ref = outs[state * pieces + channel // size]
        out_ref[channel % size, pl.ds(first, 2 * ROWS), :] = rows

    mix_channels(groups, channels, weight_ref, mixed_ref, write, block)


def left_close_kernel(iso_ref, gathered_ref, moved_ref, out_ref, square_ref):
    channels, block, _ = gathered_ref.shape
    square = jnp.zeros((ROWS, block), jnp.float32)
    for batch in batches(list(range(channels)), 2):
        right = jnp.concatenate([gathered_ref[channel] for channel in batch], axis=1)
        product = lax.dot_general(
            iso_ref[...], right, (((0,), (0,)), ((), ())), preferred_element_type=jnp.float32
        )
        for number, channel in enumerate(batch):
            part = product[:, number * block : (number + 1) * block]
            part = part + moved_ref[channel].astype(jnp.float32)
            out_ref[channel] = part.astype(jnp.bfloat16)
            square = square + jnp.sum((part * part).reshape(-1, ROWS, block), axis=0)
    square_ref[...] = square


def right_kernel(groups, states, pieces, *refs):
    envs = [refs[t * pieces : (t + 1) * pieces] for t in range(states)]
    refs = refs[states * pieces :]
    own_ref, tensor_ref, weight_ref = refs[:3]
    outs, (square_ref, mixed_ref, gathered_ref) = refs[3 : 3 + pieces], refs[3 + pieces :]
    channels, block = count_channels(envs[0]), envs[0][0].shape[1]
    zero = jnp.zeros((block, block), jnp.bfloat16)
    for pair in batches(list(range(states)), 2):
        own = jnp.concatenate(
            [
                jnp.concatenate([own_ref[t] if t == other else zero for other in pair], axis=1)
                for t in pair
            ],
            axis=0,
        )
        for batch in batches(list(range(channels)), 3):
            rows = jnp.concatenate(
                [
                    jnp.concatenate([channel_of(envs[t], channel) for channel in batch], axis=0)
                    for t in pair
                ],
                axis=1,
            )
            product = lax.dot_general(
                rows, own, (((1,), (1,)), ((), ())), preferred_element_type=jnp.float32
            )
            for number, t in enumerate(pair):
                mixed_ref[pl.ds((t * channels + batch[0]) * block, len(batch) * block), :] = (
                    product[:, number * block : (number + 1) * block]
                )
    write = into(gathered_ref, channels, block)
    mix_channels(groups, channels, weight_ref, mixed_ref, write, block)
    square = jnp.zeros((ROWS, block), jnp.float32)
    for cls in range(CLASSES):
        left = jnp.concatenate([tensor_ref[cls, s] for s in range(states)], axis=1)
        for batch in batches(list(range(cls, channels, CLASSES)), 2):
            right = jnp.concatenate(
                [
                    jnp.concatenate(
                        [
                            gathered_ref[pl.ds((s * channels + channel) * block, block), :]
                            for s in range(states)
                        ],
                        axis=0,
                    )
                    for channel in batch
                ],
                axis=1,
            )
            product = jnp.dot(left, right, preferred_element_type=jnp.float32)
            for number, channel in enumerate(batch):
                part = product[:, number * block : (number + 1) * block]
                put_channel(outs, channel, part.astype(jnp.bfloat16))
                square = square + jnp.sum((part * part).reshape(-1, ROWS, block), axis=0)
    square_ref[...] = square


def quotient(table):
    a, b, e, c = (table[:, column : column + 1] for column in range(4))

    def total(x):
        return jnp.sum(x, axis=0, keepdims=True)

    whole_a, whole_b = total(a), total(b)
    energy = whole_a / (whole_b + TINY)
    off = e - energy
    residual_sq = total(c + 2.0 * off * (a - e * b) + off * off * b)
    factor = 0.5 * jnp.sqrt(whole_b / (residual_sq + TINY))
    square = whole_b - 2.0 * factor * (whole_a - energy * whole_b) + factor * factor * residual_sq
    return energy, factor, square


def updated(vector, applied, energy, factor):
    return vector - factor * (applied - energy * vector)


def sum_all(x):
    return jnp.sum(jnp.sum(x, axis=0, keepdims=True), axis=1, keepdims=True)


def env_scale(sums_ref, first, entry_count):
    scale = jnp.ones((1, 1), jnp.float32)
    for step in range(first, first + ENV_STEPS):
        square = sum_all(sums_ref[step])
        scale = scale * lax.rsqrt(scale * scale * square / entry_count + TINY)
    return scale


def operator_front_kernel(groups, states, pieces, renew, *refs):
    env, refs = refs[:pieces], refs[pieces:]
    weight_ref, vector_ref = refs[:2]
    rest = refs[2:]
    if renew:
        own_ref, moved_ref, table_ref = rest[:3]
        rest = rest[3:]
        energy, factor, _ = quotient(table_ref[...])
    gathered_ref, new_ref, mixed_ref = rest
    channels, block = count_channels(env), env[0].shape[1]
    tensors = []
    for cls in range(CLASSES):
        row = []
        for t in range(states):
            vector = vector_ref[cls, t]
            if renew:
                image = own_ref[t] if cls == 0 else moved_ref[cls - 1, t].astype(jnp.float32)
                vector = updated(vector, image, energy, factor)
            if cls == 0:
                new_ref[t] = vector
            row.append(vector.astype(jnp.bfloat16))
        tensors.append(row)
    mix_left(env, tensors, mixed_ref)
    write = into(gathered_ref, channels, block)
    mix_channels(groups, channels, weight_ref, mixed_ref, write, block)


def operator_back_kernel(states, pieces, entry_count, *refs):
    rights = [refs[t * pieces : (t + 1) * pieces] for t in range(states)]
    refs = refs[states * pieces :]
    gathered_ref, left_sums_ref, right_sums_ref, vector_ref, image_ref, sums_ref = refs
    channels, block = count_channels(rights[0]), rights[0][0].shape[1]
    scale = env_scale(left_sums_ref, 0, entry_count) * env_scale(
        right_sums_ref, ENV_STEPS, entry_count
    )
    a = jnp.zeros((1, 1), jnp.float32)
    b = jnp.zeros((1, 1), jnp.float32)
    for s in range(states):
        total = jnp.zeros((block, block), jnp.float32)
        for batch in batches(list(range(channels)), 6):
            left = jnp.concatenate(
                [
                    gathered_ref[pl.ds((s * channels + channel) * block, block), :]
                    for channel in batch
                ],
                axis=1,
            )
            right = jnp.concatenate([channel_of(rights[s], channel) for channel in batch], axis=0)
            total = total + jnp.dot(left, right, preferred_element_type=jnp.float32)
        total = total * scale
        image_ref[s] = total
        vector = vector_ref[s]
        a = a + sum_all(vector * total)
        b = b + sum_all(vector * vector)
    e = jnp.where(b > 0, a / jnp.where(b > 0, b, 1.0), 0.0)
    c = jnp.zeros((1, 1), jnp.float32)
    for s in range(states):
        residual = image_ref[s] - e * vector_ref[s]
        c = c + sum_all(residual * residual)
    lane = lax.broadcasted_iota(jnp.int32, sums_ref.shape, 1)
    sums = jnp.zeros(sums_ref.shape, jnp.float32)
    for place, value in enumerate((a, b, e, c)):
        sums = jnp.where(lane == place, value, sums)
    sums_ref[...] = sums


def polar_kernel(both_ref, table_ref, centre_ref, sums_ref, out_ref):
    states, _, block, _ = both_ref.shape
    rows = lax.broadcasted_iota(jnp.int32, (block, block), 0)
    columns = lax.broadcasted_iota(jnp.int32, (block, block), 1)
    unit = (rows == columns).astype(jnp.float32)

    def product(x, y, contract=((1,), (0,))):
        return lax.dot_general(
            x, y, (contract, ((), ())), precision=HIGHEST, preferred_element_type=jnp.float32
        )

    energy, factor, square = quotient(table_ref[...])
    vector = updated(
        both_ref[:, 0].reshape(states * block, block),
        both_ref[:, 1].reshape(states * block, block),
        energy,
        factor,
    ) * lax.rsqrt(square + TINY)
    centre = centre_ref[...].astype(jnp.float32) * lax.rsqrt(
        sum_all(sums_ref[2 * ENV_STEPS]) + TINY
    )
    grams = [product(x, x, ((0,), (0,))) for x in (vector, centre)]
    totals = [unit, unit]
    for step in range(POLAR):
        factors = [1.5 * unit - 0.5 * gram for gram in grams]
        totals = [
            factor if step == 0 else product(total, factor)
            for total, factor in zip(totals, factors)
        ]
        if step < POLAR - 1:
            grams = [
                product(product(factor, gram), factor) for gram, factor in zip(grams, factors)
            ]
    closing = product(totals[0], product(centre, totals[1]), ((1,), (1,)))
    out_ref[...] = product(vector, closing).reshape(states, block, block).astype(jnp.bfloat16)


def call(kernel, out_shape, scratch_shapes, flops, operands):
    return pl.pallas_call(
        kernel,
        out_shape=out_shape,
        scratch_shapes=scratch_shapes,
        compiler_params=pltpu.CompilerParams(vmem_limit_bytes=VMEM_LIMIT),
        cost_estimate=pl.CostEstimate(
            flops=flops,
            bytes_accessed=sum(int(np.prod(x.shape)) * x.dtype.itemsize for x in operands),
            transcendentals=0,
        ),
    )(*operands)


def float_out(*shape):
    return jax.ShapeDtypeStruct(shape, jnp.float32)


def half_out(*shape):
    return jax.ShapeDtypeStruct(shape, jnp.bfloat16)


def work(states, channels, block):
    return 4 * states * channels * block**3 + 2 * (states * channels * block) ** 2


def expanded(weight, groups, channels, states):
    spread = spread_matrix(groups, channels, states)
    sizes = tuple(even(len(group)) * ROWS for group in groups)
    return call(
        functools.partial(expand_kernel, sizes),
        half_out(spread.shape[0], -(-max(sizes) // 128) * 128),
        [],
        2 * spread.size * spread.shape[0],
        (weight, jnp.asarray(spread, jnp.bfloat16)),
    )


def left_front(env, tensors, weight, groups):
    channels, block = count_channels(env), env[0].shape[1]
    states, pieces = tensors.shape[1], len(env)
    outs = call(
        functools.partial(left_kernel, groups, states, pieces),
        [half_out(channels // pieces, block, block)] * (states * pieces),
        [pltpu.VMEM((states * channels * block, block), jnp.float32)],
        work(states, channels, block),
        (*env, tensors, weight),
    )
    return [outs[s * pieces : (s + 1) * pieces] for s in range(states)]


def left_close(iso, gathered, moved):
    channels, block, _ = gathered.shape
    return call(
        left_close_kernel,
        (half_out(channels, block, block), float_out(ROWS, block)),
        [],
        2 * channels * block**3,
        (iso, gathered, moved),
    )


def right_whole(envs, own, tensors, weight, groups):
    channels, block = count_channels(envs[0]), envs[0][0].shape[1]
    states, pieces = len(envs), len(envs[0])
    outs = call(
        functools.partial(right_kernel, groups, states, pieces),
        [half_out(channels // pieces, block, block)] * pieces + [float_out(ROWS, block)],
        [
            pltpu.VMEM((states * channels * block, block), jnp.float32),
            pltpu.VMEM((states * channels * block, block), jnp.bfloat16),
        ],
        work(states, channels, block),
        (*(chunk for env in envs for chunk in env), own, tensors, weight),
    )
    return outs[:pieces], outs[pieces]


def operator_front(env, weight, groups, vectors, image=None, rolled=None, table=None):
    channels, block = count_channels(env), env[0].shape[1]
    states, pieces = vectors.shape[1], len(env)
    renew = image is not None
    return call(
        functools.partial(operator_front_kernel, groups, states, pieces, renew),
        (half_out(states * channels * block, block), float_out(states, block, block)),
        [pltpu.VMEM((states * channels * block, block), jnp.float32)],
        work(states, channels, block),
        (*env, weight, vectors) + ((image, rolled, table) if renew else ()),
    )


def operator_back(rights, gathered, left_sums, right_sums, entry_count, vector):
    channels, block = count_channels(rights[0]), rights[0][0].shape[1]
    states, pieces = len(rights), len(rights[0])
    return call(
        functools.partial(operator_back_kernel, states, pieces, entry_count),
        (float_out(states, block, block), float_out(1, 128)),
        [],
        2 * states * channels * block**3,
        (
            *(chunk for right in rights for chunk in right),
            gathered,
            left_sums,
            right_sums,
            vector,
        ),
    )


def polar(both, table, centre, sums):
    states, _, block, _ = both.shape
    return call(
        polar_kernel,
        half_out(states, block, block),
        [],
        600 * block**3,
        (both, table, centre, sums),
    )


def charge_mask(channels, states, sectors):
    charge = np.array([CHARGE_STEPS[channel % CLASSES] for channel in range(channels)])
    state = np.arange(states)
    balance = (
        charge[:, None, None, None]
        + state[None, None, None, :]
        - state[None, None, :, None]
        - charge[None, :, None, None]
    )
    return jnp.asarray((balance % sectors == 0).astype(np.float32)).astype(jnp.bfloat16)


def weight_matrices(mpo, pattern, sectors):
    channels, _, states, _ = mpo.shape
    allowed = charge_mask(channels, states, sectors)
    weights = mpo * pattern[:, :, None, None].astype(jnp.bfloat16) * allowed
    size = states * channels
    left = jnp.transpose(weights, (2, 1, 3, 0)).reshape(size, size)
    right = jnp.transpose(weights, (2, 0, 3, 1)).reshape(size, size)
    return jnp.stack([left, right])


def classes_of(places, x):
    one, minus = places.ahead(x, 1), places.ahead(x, -1)
    return jnp.stack([x, one, minus, places.ahead(one, 1), places.ahead(minus, -1)])


def other_classes_of(places, x):
    return jnp.stack([places.ahead(x, charge) for charge in CHARGE_STEPS[1:]])


def after(first, then):
    return lax.optimization_barrier((first, then))


def local(left_iso, right_iso, centre, left_env, right_env, mpo, pattern):
    sites, secs = lax.axis_size("site"), lax.axis_size("sec")
    places = Places(sites, secs)
    left_iso, right_iso, centre = left_iso[0, :, 0], right_iso[0, :, 0], centre[0, 0]
    states, block, _ = left_iso.shape
    channels = mpo.shape[1]
    entry_count = left_env.size * secs
    left_groups = label_groups(channels, states, secs, 1)
    right_groups = label_groups(channels, states, secs, -1)

    pieces = PIECES if channels % PIECES == 0 else 1

    def split(env):
        return jnp.split(env, pieces)

    def ahead(env, by, chain_by=0):
        return [places.ahead(chunk, by, chain_by) for chunk in env]

    def fetch_env(env):
        return [places.fetch(chunk) for chunk in split(env)]

    both_isos = places.fetch(jnp.concatenate([left_iso, right_iso]))
    left_isos, right_isos = [both_isos[:states]], [both_isos[states:]]
    for step in range(1, ENV_STEPS):
        left_isos.append(places.fetch(left_iso, step))
        right_isos.append(places.fetch(right_iso, -step))
    own_tensors = places.fetch(jnp.concatenate([left_iso, centre[None]]), ENV_STEPS)
    centres = [places.fetch(centre, ENV_STEPS, s) for s in range(1, states)]
    (left_isos, right_isos, own_tensors, centres), right_env = after(
        (left_isos, right_isos, own_tensors, centres), right_env
    )
    right = fetch_env(right_env[0, :, 0])
    right, left_env = after(right, left_env)
    left = fetch_env(left_env[0, :, 0])
    own_iso, own_centre = own_tensors[:states], own_tensors[states]
    centres = [own_centre] + centres

    gathered_weights = lax.all_gather(weight_matrices(mpo[0], pattern[0], secs), "site")
    chain = places.my_chain()

    def weight_of(site_by, kind):
        weight = lax.dynamic_index_in_dim(
            gathered_weights, (chain + site_by) % sites, 0, False
        )[kind]
        return expanded(weight, (left_groups, right_groups)[kind], channels, states)

    weights = (
        [weight_of(step, 0) for step in range(ENV_STEPS + 1)],
        [weight_of(-step, 1) for step in range(ENV_STEPS)],
    )
    isos = jnp.stack(left_isos + right_isos)
    vector = jnp.einsum(
        "sxy,syz->sxz", own_iso, jnp.stack(centres), preferred_element_type=jnp.float32
    )
    rolled = classes_of(places, isos)
    vectors = classes_of(places, vector)
    centre_float = own_centre.astype(jnp.float32)
    centre_square = jnp.sum((centre_float * centre_float).reshape(-1, ROWS, block), axis=0)

    left_squares, right_squares = [], []
    for step in range(ENV_STEPS):
        envs = [right]
        for t in range(1, states):
            envs.append(ahead(envs[-1], 1))
        if step == 0:
            (vectors, rolled, weights), envs = after((vectors, rolled, weights), envs)
        right, square = right_whole(
            envs,
            right_isos[step],
            rolled[:, ENV_STEPS + step],
            weights[1][step],
            right_groups,
        )
        right_squares.append(square)

        gathered = left_front(left, rolled[:, step], weights[0][step], left_groups)
        moved = [None] * pieces
        for s in reversed(range(1, states)):
            for piece in range(pieces):
                part = jnp.einsum(
                    "xy,vxz->vyz",
                    left_isos[step][s],
                    gathered[s][piece],
                    preferred_element_type=jnp.float32,
                )
                if moved[piece] is not None:
                    part = part + moved[piece].astype(jnp.float32)
                moved[piece] = places.ahead(part.astype(jnp.bfloat16), -1)
        closed = [
            left_close(left_isos[step][0], gathered[0][piece], moved[piece])
            for piece in range(pieces)
        ]
        left = [env for env, _ in closed]
        left_squares.append(sum(square for _, square in closed))

    sums = places.summed(jnp.stack(left_squares + right_squares + [centre_square]))
    right_sums = sums
    if (2 * ENV_STEPS) % sites:
        right = ahead(right, 0, 2 * ENV_STEPS)
        right_sums = places.ahead(sums, 0, 2 * ENV_STEPS)

    rights = [right]
    for s in range(1, states):
        rights.append(ahead(rights[-1], 1))
    news = ()
    for step in range(DESCENT):
        gathered, vector = operator_front(
            left, weights[0][ENV_STEPS], left_groups, vectors, *news
        )
        image, own_sums = operator_back(rights, gathered, sums, right_sums, entry_count, vector)
        table = places.collect(own_sums)
        if step < DESCENT - 1:
            rolled_image = other_classes_of(places, image.astype(jnp.bfloat16))
            news = (image, rolled_image, table)

    both = jnp.stack([vector, image], axis=1)
    columns = jnp.stack([both[0]] + [places.ahead(both[s], -s) for s in range(1, states)])
    column_left = polar(columns, table, own_centre, sums)
    new_left = jnp.stack(
        [places.send_home(column_left[s], ENV_STEPS, -s) for s in range(states)]
    )
    home_table = places.send_home(table, ENV_STEPS, 0)
    energy = jnp.sum(home_table[:, 0]) / (jnp.sum(home_table[:, 1]) + TINY)
    return new_left[None, :, None], jnp.reshape(energy, (1,))


def solution(mesh):
    placed = (
        P("site", None, "sec", None, None),
        P("site", None, "sec", None, None),
        P("site", "sec", None, None),
        P("site", None, "sec", None, None),
        P("site", None, "sec", None, None),
        P("site", None, None, None, None),
        P("site", None, None),
    )
    return jax.shard_map(
        local,
        mesh=mesh,
        in_specs=placed,
        out_specs=(P("site", None, "sec", None, None), P("site")),
        check_vma=False,
    )
```

```python
import functools

import jax
import jax.numpy as jnp
import numpy as np
from jax import lax
from jax.experimental import pallas as pl
from jax.experimental.pallas import tpu as pltpu
from jax.sharding import PartitionSpec as P

ENV_STEPS = 2
DESCENT = 2
POLAR = 6

TINY = 1e-06
HIGHEST = lax.Precision.HIGHEST
CHARGE_STEPS = (0, 1, -1, 2, -2)
CLASSES = len(CHARGE_STEPS)
BOTH = ("site", "sec")
VMEM_LIMIT = 15 * 1024 * 1024
PIECES = 2


class Places:
    def __init__(self, sites, secs):
        self.sites, self.secs = sites, secs
        self.half = secs // 2
        self.up = (self.half + 1) // 2

    def home(self, site, sector):
        return (site % self.sites) * self.secs + sector % self.secs

    def position(self, place):
        back = self.half - 1 + self.up - place
        if isinstance(place, int):
            return place if place < self.up else back
        return jnp.where(place < self.up, place, back)

    def slot(self, chain, sector):
        chain, sector = chain % self.sites, sector % self.secs
        place = chain % 2 * self.half + self.position(sector // 2)
        return (chain // 2 * 2 + sector % 2) * self.secs + place

    def pairs(self, source, target):
        return [
            (source(chain, sector), target(chain, sector))
            for chain in range(self.sites)
            for sector in range(self.secs)
        ]

    def fetch(self, x, site_by=0, sec_by=0):
        return lax.ppermute(
            x, BOTH, self.pairs(lambda g, k: self.home(g + site_by, k + sec_by), self.slot)
        )

    def send_home(self, x, site_by, sec_by):
        return lax.ppermute(
            x, BOTH, self.pairs(self.slot, lambda g, k: self.home(g + site_by, k + sec_by))
        )

    def ahead(self, x, by, chain_by=0):
        return lax.ppermute(
            x, BOTH, self.pairs(lambda g, k: self.slot(g + chain_by, k + by), self.slot)
        )

    def partner(self, x, bit):
        return lax.ppermute(x, BOTH, self.pairs(lambda g, k: self.slot(g, k ^ bit), self.slot))

    def my_chain(self):
        return lax.axis_index("site") // 2 * 2 + lax.axis_index("sec") // self.half

    def my_sector(self):
        position = self.position(lax.axis_index("sec") % self.half)
        return 2 * position + lax.axis_index("site") % 2

    def collect(self, values):
        sector = self.my_sector()
        table = values
        bit = 1
        while bit < self.secs:
            other = self.partner(table, bit)
            first = (sector & bit) == 0
            table = jnp.where(
                first, jnp.concatenate([table, other]), jnp.concatenate([other, table])
            )
            bit *= 2
        return table


ROWS = 8
PARTS = 2


def label_groups(channels, states, sectors, sign):
    groups = {}
    for state in range(states):
        for channel in range(channels):
            label = (state + sign * CHARGE_STEPS[channel % CLASSES]) % sectors
            groups.setdefault(label, []).append((state, channel))
    return [groups[label] for label in sorted(groups)]


def even(count):
    return count + count % 2


def spread_matrix(groups, channels, states):
    rows = []
    for group in groups:
        block = np.zeros((even(len(group)), ROWS, states * channels), np.float32)
        for index, (state, channel) in enumerate(group):
            block[index, :, state * channels + channel] = 1
        rows.append(block.reshape(-1, states * channels))
    return np.concatenate(rows)


def expand_kernel(sizes, weight_ref, spread_ref, out_ref):
    start = 0
    for size in sizes:
        spread = spread_ref[pl.ds(start, size), :]
        picked = jnp.dot(spread, weight_ref[...], preferred_element_type=jnp.float32)
        full = lax.dot_general(
            picked.astype(jnp.bfloat16),
            spread,
            (((1,), (1,)), ((), ())),
            preferred_element_type=jnp.float32,
        )
        row = lax.broadcasted_iota(jnp.int32, full.shape, 0)
        column = lax.broadcasted_iota(jnp.int32, full.shape, 1)
        same = lax.rem(row, ROWS) == lax.rem(column, ROWS)
        out_ref[pl.ds(start, size), pl.ds(0, size)] = jnp.where(same, full, 0.0).astype(
            jnp.bfloat16
        )
        start += size


def mix_channels(groups, channels, weight_ref, mixed_ref, write, offset, height):
    def step(index, carry):
        first = pl.multiple_of(index * 2 * ROWS, 2 * ROWS)
        start = 0
        for group in groups:
            size = even(len(group)) * ROWS
            parts = []
            for state, channel in group:
                rows = (state * channels + channel) * height + first
                halves = [
                    mixed_ref[pl.ds(pl.multiple_of(rows + half * ROWS, ROWS), ROWS), :]
                    for half in range(2)
                ]
                parts.append(jnp.concatenate(halves, axis=1))
            if len(group) % 2:
                parts.append(parts[0])
            operand = jnp.concatenate(parts, axis=0).astype(jnp.bfloat16)
            product = jnp.dot(
                weight_ref[pl.ds(start, size), pl.ds(0, size)],
                operand,
                preferred_element_type=jnp.float32,
            )
            block = product.shape[1] // 2
            for number, pair in enumerate(group):
                rows = product[number * ROWS : (number + 1) * ROWS]
                both = jnp.concatenate([rows[:, :block], rows[:, block:]], axis=0)
                write(*pair, pl.multiple_of(offset + first, 2 * ROWS), both.astype(jnp.bfloat16))
            start += size
        return carry

    lax.fori_loop(0, height // (2 * ROWS), step, 0)


def by_parts(block, body):
    height = block // PARTS

    def one(part, carry):
        body(pl.multiple_of(part * height, height), height)
        return carry

    lax.fori_loop(0, PARTS, one, 0)


def into(gathered_ref, channels, block):
    def write(state, channel, first, rows):
        start = (state * channels + channel) * block
        gathered_ref[pl.ds(pl.multiple_of(start + first, 2 * ROWS), 2 * ROWS), :] = rows

    return write


def batches(items, most):
    pieces = -(-len(items) // most)
    size = -(-len(items) // pieces)
    return [items[start : start + size] for start in range(0, len(items), size)]


def rows_of(chunks, channel, offset, height):
    size = chunks[0].shape[0]
    return chunks[channel // size][channel % size, pl.ds(offset, height), :]


def channel_of(chunks, channel):
    size = chunks[0].shape[0]
    return chunks[channel // size][channel % size]


def put_channel(chunks, channel, value):
    size = chunks[0].shape[0]
    chunks[channel // size][channel % size] = value


def count_channels(chunks):
    return sum(chunk.shape[0] for chunk in chunks)


def mix_left(env, tensors, mixed_ref, offset, height):
    channels, block = count_channels(env), env[0].shape[1]
    for cls in range(CLASSES):
        right = jnp.concatenate(tensors[cls], axis=1)
        for batch in batches(list(range(cls, channels, CLASSES)), 5):
            rows = jnp.concatenate(
                [rows_of(env, channel, offset, height) for channel in batch], axis=0
            )
            product = jnp.dot(rows, right, preferred_element_type=jnp.float32)
            for number, channel in enumerate(batch):
                for t in range(len(tensors[cls])):
                    mixed_ref[pl.ds((t * channels + channel) * height, height), :] = product[
                        number * height : (number + 1) * height, t * block : (t + 1) * block
                    ]


def left_kernel(groups, states, pieces, *refs):
    env, (tensor_ref, weight_ref) = refs[:pieces], refs[pieces : pieces + 2]
    outs, mixed_ref = refs[pieces + 2 : -1], refs[-1]
    channels, block = count_channels(env), env[0].shape[1]

    def write(state, channel, first, rows):
        size = channels // pieces
        out_ref = outs[state * pieces + channel // size]
        out_ref[channel % size, pl.ds(first, 2 * ROWS), :] = rows

    def body(offset, height):
        tensors = [[tensor_ref[cls, t] for t in range(states)] for cls in range(CLASSES)]
        mix_left(env, tensors, mixed_ref, offset, height)
        mix_channels(groups, channels, weight_ref, mixed_ref, write, offset, height)

    by_parts(block, body)


def left_close_kernel(iso_ref, gathered_ref, moved_ref, out_ref, square_ref):
    channels, block, _ = gathered_ref.shape
    square = jnp.zeros((ROWS, block), jnp.float32)
    for batch in batches(list(range(channels)), 2):
        right = jnp.concatenate([gathered_ref[channel] for channel in batch], axis=1)
        product = lax.dot_general(
            iso_ref[...], right, (((0,), (0,)), ((), ())), preferred_element_type=jnp.float32
        )
        for number, channel in enumerate(batch):
            part = product[:, number * block : (number + 1) * block]
            part = part + moved_ref[channel].astype(jnp.float32)
            out_ref[channel] = part.astype(jnp.bfloat16)
            square = square + jnp.sum((part * part).reshape(-1, ROWS, block), axis=0)
    square_ref[...] = square


def right_kernel(groups, states, pieces, *refs):
    envs = [refs[t * pieces : (t + 1) * pieces] for t in range(states)]
    refs = refs[states * pieces :]
    own_ref, tensor_ref, weight_ref = refs[:3]
    outs, (square_ref, mixed_ref, gathered_ref) = refs[3 : 3 + pieces], refs[3 + pieces :]
    channels, block = count_channels(envs[0]), envs[0][0].shape[1]
    zero = jnp.zeros((block, block), jnp.bfloat16)
    write = into(gathered_ref, channels, block)

    def body(offset, height):
        for pair in batches(list(range(states)), 2):
            own = jnp.concatenate(
                [
                    jnp.concatenate([own_ref[t] if t == other else zero for other in pair], axis=1)
                    for t in pair
                ],
                axis=0,
            )
            for batch in batches(list(range(channels)), 6):
                rows = jnp.concatenate(
                    [
                        jnp.concatenate(
                            [rows_of(envs[t], channel, offset, height) for channel in batch], axis=0
                        )
                        for t in pair
                    ],
                    axis=1,
                )
                product = lax.dot_general(
                    rows, own, (((1,), (1,)), ((), ())), preferred_element_type=jnp.float32
                )
                for number, t in enumerate(pair):
                    start = (t * channels + batch[0]) * height
                    mixed_ref[pl.ds(start, len(batch) * height), :] = product[
                        :, number * block : (number + 1) * block
                    ]
        mix_channels(groups, channels, weight_ref, mixed_ref, write, offset, height)

    by_parts(block, body)
    square = jnp.zeros((ROWS, block), jnp.float32)
    for cls in range(CLASSES):
        left = jnp.concatenate([tensor_ref[cls, s] for s in range(states)], axis=1)
        for batch in batches(list(range(cls, channels, CLASSES)), 2):
            right = jnp.concatenate(
                [
                    jnp.concatenate(
                        [
                            gathered_ref[pl.ds((s * channels + channel) * block, block), :]
                            for s in range(states)
                        ],
                        axis=0,
                    )
                    for channel in batch
                ],
                axis=1,
            )
            product = jnp.dot(left, right, preferred_element_type=jnp.float32)
            for number, channel in enumerate(batch):
                part = product[:, number * block : (number + 1) * block]
                put_channel(outs, channel, part.astype(jnp.bfloat16))
                square = square + jnp.sum((part * part).reshape(-1, ROWS, block), axis=0)
    square_ref[...] = square


ENV_LANE = 5
LANES = 128


def quotient(table, entry_count):
    def total(x):
        return jnp.sum(x, axis=0, keepdims=True)

    squares = [
        total(table[:, lane : lane + 1]) for lane in range(ENV_LANE, ENV_LANE + 2 * ENV_STEPS + 1)
    ]
    scale = jnp.ones((1, 1), jnp.float32)
    for side in range(2):
        side_scale = jnp.ones((1, 1), jnp.float32)
        for square in squares[side * ENV_STEPS : (side + 1) * ENV_STEPS]:
            side_scale = side_scale * lax.rsqrt(side_scale * side_scale * square / entry_count + TINY)
        scale = scale * side_scale
    a, b, e, c, unit = (table[:, lane : lane + 1] for lane in range(ENV_LANE))
    a, e, unit = scale * a, scale * e, scale * unit
    c = unit * unit * c
    whole_a, whole_b = total(a), total(b)
    energy = whole_a / (whole_b + TINY)
    off = e - energy
    residual_sq = total(c + 2.0 * off * (a - e * b) + off * off * b)
    factor = 0.5 * jnp.sqrt(whole_b / (residual_sq + TINY))
    square = whole_b - 2.0 * factor * (whole_a - energy * whole_b) + factor * factor * residual_sq
    return scale, energy, factor, square, squares[2 * ENV_STEPS]


def updated(vector, image, scale, energy, factor):
    return vector - factor * (scale * image - energy * vector)


def sum_all(x):
    return jnp.sum(jnp.sum(x, axis=0, keepdims=True), axis=1, keepdims=True)


def operator_front_kernel(groups, states, pieces, renew, entry_count, *refs):
    env, refs = refs[:pieces], refs[pieces:]
    weight_ref, vector_ref, rolled_ref = refs[:3]
    rest = refs[3:]
    if renew:
        image_ref, moved_ref, table_ref = rest[:3]
        rest = rest[3:]
        scale, energy, factor, _, _ = quotient(table_ref[...], entry_count)
    gathered_ref, new_ref, tensor_ref, mixed_ref = rest
    channels, block = count_channels(env), env[0].shape[1]
    for t in range(states):
        vector = vector_ref[t]
        if renew:
            vector = updated(vector, image_ref[t], scale, energy, factor)
        new_ref[t] = vector
        tensor_ref[0, t] = vector.astype(jnp.bfloat16)
        for cls in range(1, CLASSES):
            vector = rolled_ref[cls - 1, t]
            if renew:
                moved = moved_ref[cls - 1, t].astype(jnp.float32)
                vector = updated(vector.astype(jnp.float32), moved, scale, energy, factor)
            tensor_ref[cls, t] = vector.astype(jnp.bfloat16)
    write = into(gathered_ref, channels, block)

    def body(offset, height):
        tensors = [[tensor_ref[cls, t] for t in range(states)] for cls in range(CLASSES)]
        mix_left(env, tensors, mixed_ref, offset, height)
        mix_channels(groups, channels, weight_ref, mixed_ref, write, offset, height)

    by_parts(block, body)


def operator_back_kernel(states, pieces, *refs):
    rights = [refs[t * pieces : (t + 1) * pieces] for t in range(states)]
    refs = refs[states * pieces :]
    squares, refs = refs[: 2 * ENV_STEPS + 1], refs[2 * ENV_STEPS + 1 :]
    gathered_ref, vector_ref, image_ref, half_ref, sums_ref = refs
    channels, block = count_channels(rights[0]), rights[0][0].shape[1]
    a = jnp.zeros((1, 1), jnp.float32)
    b = jnp.zeros((1, 1), jnp.float32)
    for s in range(states):
        total = jnp.zeros((block, block), jnp.float32)
        for batch in batches(list(range(channels)), 6):
            left = jnp.concatenate(
                [
                    gathered_ref[pl.ds((s * channels + channel) * block, block), :]
                    for channel in batch
                ],
                axis=1,
            )
            right = jnp.concatenate([channel_of(rights[s], channel) for channel in batch], axis=0)
            total = total + jnp.dot(left, right, preferred_element_type=jnp.float32)
        image_ref[s] = total
        half_ref[s] = total.astype(jnp.bfloat16)
        vector = vector_ref[s]
        a = a + sum_all(vector * total)
        b = b + sum_all(vector * vector)
    e = jnp.where(b > 0, a / jnp.where(b > 0, b, 1.0), 0.0)
    residual = image_ref[...].reshape(states * block, block) - e * vector_ref[...].reshape(
        states * block, block
    )
    unit = jnp.max(jnp.max(jnp.abs(residual), axis=0, keepdims=True), axis=1, keepdims=True)
    unit = jnp.where(unit > 0, unit, 1.0)
    residual = residual / unit
    lane = lax.broadcasted_iota(jnp.int32, sums_ref.shape, 1)
    sums = jnp.zeros(sums_ref.shape, jnp.float32)
    values = (a, b, e, sum_all(residual * residual), unit, *(sum_all(x[...]) for x in squares))
    for place, value in enumerate(values):
        sums = jnp.where(lane == place, value, sums)
    sums_ref[...] = sums


def polar_kernel(entry_count, both_ref, table_ref, centre_ref, out_ref, energy_ref):
    states, _, block, _ = both_ref.shape
    rows = lax.broadcasted_iota(jnp.int32, (block, block), 0)
    columns = lax.broadcasted_iota(jnp.int32, (block, block), 1)
    unit = (rows == columns).astype(jnp.float32)

    def product(x, y, contract=((1,), (0,))):
        return lax.dot_general(
            x, y, (contract, ((), ())), precision=HIGHEST, preferred_element_type=jnp.float32
        )

    scale, energy, factor, square, centre_sq = quotient(table_ref[...], entry_count)
    energy_ref[...] = jnp.broadcast_to(energy, energy_ref.shape)
    vector = updated(
        both_ref[:, 0].reshape(states * block, block),
        both_ref[:, 1].reshape(states * block, block),
        scale,
        energy,
        factor,
    ) * lax.rsqrt(square + TINY)
    centre = centre_ref[...].astype(jnp.float32) * lax.rsqrt(centre_sq + TINY)
    grams = [product(x, x, ((0,), (0,))) for x in (vector, centre)]
    totals = [unit, unit]
    for step in range(POLAR):
        factors = [1.5 * unit - 0.5 * gram for gram in grams]
        totals = [
            factor if step == 0 else product(total, factor)
            for total, factor in zip(totals, factors)
        ]
        if step < POLAR - 1:
            grams = [
                product(product(factor, gram), factor) for gram, factor in zip(grams, factors)
            ]
    closing = product(totals[0], product(centre, totals[1]), ((1,), (1,)))
    out_ref[...] = product(vector, closing).reshape(states, block, block).astype(jnp.bfloat16)


def call(kernel, out_shape, scratch_shapes, flops, operands):
    return pl.pallas_call(
        kernel,
        out_shape=out_shape,
        scratch_shapes=scratch_shapes,
        compiler_params=pltpu.CompilerParams(vmem_limit_bytes=VMEM_LIMIT),
        cost_estimate=pl.CostEstimate(
            flops=flops,
            bytes_accessed=sum(int(np.prod(x.shape)) * x.dtype.itemsize for x in operands),
            transcendentals=0,
        ),
    )(*operands)


def float_out(*shape):
    return jax.ShapeDtypeStruct(shape, jnp.float32)


def half_out(*shape):
    return jax.ShapeDtypeStruct(shape, jnp.bfloat16)


def work(states, channels, block):
    return 4 * states * channels * block**3 + 2 * (states * channels * block) ** 2


def expanded(weight, groups, channels, states):
    spread = spread_matrix(groups, channels, states)
    sizes = tuple(even(len(group)) * ROWS for group in groups)
    return call(
        functools.partial(expand_kernel, sizes),
        half_out(spread.shape[0], -(-max(sizes) // 128) * 128),
        [],
        2 * spread.size * spread.shape[0],
        (weight, jnp.asarray(spread, jnp.bfloat16)),
    )


def left_front(env, tensors, weight, groups):
    channels, block = count_channels(env), env[0].shape[1]
    states, pieces = tensors.shape[1], len(env)
    outs = call(
        functools.partial(left_kernel, groups, states, pieces),
        [half_out(channels // pieces, block, block)] * (states * pieces),
        [pltpu.VMEM((states * channels * block // PARTS, block), jnp.float32)],
        work(states, channels, block),
        (*env, tensors, weight),
    )
    return [outs[s * pieces : (s + 1) * pieces] for s in range(states)]


def left_close(iso, gathered, moved):
    channels, block, _ = gathered.shape
    return call(
        left_close_kernel,
        (half_out(channels, block, block), float_out(ROWS, block)),
        [],
        2 * channels * block**3,
        (iso, gathered, moved),
    )


def right_whole(envs, own, tensors, weight, groups):
    channels, block = count_channels(envs[0]), envs[0][0].shape[1]
    states, pieces = len(envs), len(envs[0])
    outs = call(
        functools.partial(right_kernel, groups, states, pieces),
        [half_out(channels // pieces, block, block)] * pieces + [float_out(ROWS, block)],
        [
            pltpu.VMEM((states * channels * block // PARTS, block), jnp.float32),
            pltpu.VMEM((states * channels * block, block), jnp.bfloat16),
        ],
        work(states, channels, block),
        (*(chunk for env in envs for chunk in env), own, tensors, weight),
    )
    return outs[:pieces], outs[pieces]


def operator_front(env, weight, groups, entry_count, vector, rolled, news):
    channels, block = count_channels(env), env[0].shape[1]
    states, pieces = vector.shape[0], len(env)
    return call(
        functools.partial(
            operator_front_kernel, groups, states, pieces, len(news) > 0, entry_count
        ),
        (half_out(states * channels * block, block), float_out(states, block, block)),
        [
            pltpu.VMEM((CLASSES, states, block, block), jnp.bfloat16),
            pltpu.VMEM((states * channels * block // PARTS, block), jnp.float32),
        ],
        work(states, channels, block),
        (*env, weight, vector, rolled, *news),
    )


def operator_back(rights, squares, gathered, vector):
    channels, block = count_channels(rights[0]), rights[0][0].shape[1]
    states, pieces = len(rights), len(rights[0])
    return call(
        functools.partial(operator_back_kernel, states, pieces),
        (
            float_out(states, block, block),
            half_out(states, block, block),
            float_out(1, LANES),
        ),
        [],
        2 * states * channels * block**3,
        (*(chunk for right in rights for chunk in right), *squares, gathered, vector),
    )


def polar(both, table, centre, entry_count):
    states, _, block, _ = both.shape
    return call(
        functools.partial(polar_kernel, entry_count),
        (half_out(states, block, block), float_out(1, LANES)),
        [],
        600 * block**3,
        (both, table, centre),
    )


def charge_mask(channels, states, sectors):
    charge = np.array([CHARGE_STEPS[channel % CLASSES] for channel in range(channels)])
    state = np.arange(states)
    balance = (
        charge[:, None, None, None]
        + state[None, None, None, :]
        - state[None, None, :, None]
        - charge[None, :, None, None]
    )
    return jnp.asarray((balance % sectors == 0).astype(np.float32)).astype(jnp.bfloat16)


def weight_matrices(mpo, pattern, sectors):
    channels, _, states, _ = mpo.shape
    allowed = charge_mask(channels, states, sectors)
    weights = mpo * pattern[:, :, None, None].astype(jnp.bfloat16) * allowed
    size = states * channels
    left = jnp.transpose(weights, (2, 1, 3, 0)).reshape(size, size)
    right = jnp.transpose(weights, (2, 0, 3, 1)).reshape(size, size)
    return jnp.stack([left, right])


def classes_of(places, x):
    one, minus = places.ahead(x, 1), places.ahead(x, -1)
    return jnp.stack([x, one, minus, places.ahead(one, 1), places.ahead(minus, -1)])


def other_classes_of(places, x):
    return jnp.stack([places.ahead(x, charge) for charge in CHARGE_STEPS[1:]])


def after(first, then):
    return lax.optimization_barrier((first, then))


def local(left_iso, right_iso, centre, left_env, right_env, mpo, pattern):
    sites, secs = lax.axis_size("site"), lax.axis_size("sec")
    places = Places(sites, secs)
    left_iso, right_iso, centre = left_iso[0, :, 0], right_iso[0, :, 0], centre[0, 0]
    states, block, _ = left_iso.shape
    channels = mpo.shape[1]
    entry_count = left_env.size * secs
    left_groups = label_groups(channels, states, secs, 1)
    right_groups = label_groups(channels, states, secs, -1)

    pieces = PIECES if channels % PIECES == 0 else 1

    def split(env):
        return jnp.split(env, pieces)

    def ahead(env, by, chain_by=0):
        return [places.ahead(chunk, by, chain_by) for chunk in env]

    def fetch_env(env):
        return [places.fetch(chunk) for chunk in split(env)]

    both_isos = places.fetch(jnp.concatenate([left_iso, right_iso]))
    left_isos, right_isos = [both_isos[:states]], [both_isos[states:]]
    for step in range(1, ENV_STEPS):
        left_isos.append(places.fetch(left_iso, step))
        right_isos.append(places.fetch(right_iso, -step))
    own_tensors = places.fetch(jnp.concatenate([left_iso, centre[None]]), ENV_STEPS)
    centres = [places.fetch(centre, ENV_STEPS, s) for s in range(1, states)]
    (left_isos, right_isos, own_tensors, centres), right_env = after(
        (left_isos, right_isos, own_tensors, centres), right_env
    )
    right = fetch_env(right_env[0, :, 0])
    left = []
    for piece, env in enumerate(split(left_env[0, :, 0])):
        right[piece], env = after(right[piece], env)
        left.append(places.fetch(env))
    own_iso, own_centre = own_tensors[:states], own_tensors[states]
    centres = [own_centre] + centres

    gathered_weights = lax.all_gather(weight_matrices(mpo[0], pattern[0], secs), "site")
    chain = places.my_chain()

    def weight_of(site_by, kind):
        weight = lax.dynamic_index_in_dim(
            gathered_weights, (chain + site_by) % sites, 0, False
        )[kind]
        return expanded(weight, (left_groups, right_groups)[kind], channels, states)

    weights = (
        [weight_of(step, 0) for step in range(ENV_STEPS + 1)],
        [weight_of(-step, 1) for step in range(ENV_STEPS)],
    )
    isos = jnp.stack(left_isos + right_isos)
    vector = jnp.einsum(
        "sxy,syz->sxz", own_iso, jnp.stack(centres), preferred_element_type=jnp.float32
    )
    rolled = classes_of(places, isos)
    rolled_vector = classes_of(places, vector.astype(jnp.bfloat16))[1:]
    (rolled, rolled_vector), right = after((rolled, rolled_vector), right)
    centre_float = own_centre.astype(jnp.float32)
    centre_square = jnp.sum((centre_float * centre_float).reshape(-1, ROWS, block), axis=0)

    left_squares, right_squares = [], []
    for step in range(ENV_STEPS):
        envs = [right]
        for t in range(1, states):
            if step == 0 and t == states - 1:
                left, envs[-1] = after(left, envs[-1])
            envs.append(ahead(envs[-1], 1))
        if step == 0:
            weights, envs = after(weights, envs)
        right, square = right_whole(
            envs,
            right_isos[step],
            rolled[:, ENV_STEPS + step],
            weights[1][step],
            right_groups,
        )
        right_squares.append(square)

        gathered = left_front(left, rolled[:, step], weights[0][step], left_groups)
        moved = [None] * pieces
        for s in reversed(range(1, states)):
            for piece in range(pieces):
                part = jnp.einsum(
                    "xy,vxz->vyz",
                    left_isos[step][s],
                    gathered[s][piece],
                    preferred_element_type=jnp.float32,
                )
                if moved[piece] is not None:
                    part = part + moved[piece].astype(jnp.float32)
                moved[piece] = places.ahead(part.astype(jnp.bfloat16), -1)
        closed = [
            left_close(left_isos[step][0], gathered[0][piece], moved[piece])
            for piece in range(pieces)
        ]
        left = [env for env, _ in closed]
        left_squares.append(sum(square for _, square in closed))

    if (2 * ENV_STEPS) % sites:
        right = ahead(right, 0, 2 * ENV_STEPS)
        right_squares = ahead(right_squares, 0, 2 * ENV_STEPS)
    squares = left_squares + right_squares + [centre_square]
    rights = [right]
    for s in range(1, states):
        rights.append(ahead(rights[-1], 1))
    news = ()
    for step in range(DESCENT):
        gathered, vector = operator_front(
            left, weights[0][ENV_STEPS], left_groups, entry_count, vector, rolled_vector, news
        )
        image, half_image, own_sums = operator_back(rights, squares, gathered, vector)
        table = places.collect(own_sums)
        if step < DESCENT - 1:
            news = (image, other_classes_of(places, half_image), table)

    both = jnp.stack([vector, image], axis=1)
    columns = jnp.stack([both[0]] + [places.ahead(both[s], -s) for s in range(1, states)])
    column_left, energy = polar(columns, table, own_centre, entry_count)
    new_left = jnp.stack(
        [places.send_home(column_left[s], ENV_STEPS, -s) for s in range(states)]
    )
    energy = places.send_home(energy, ENV_STEPS, 0)
    return new_left[None, :, None], energy[0, :1]


def solution(mesh):
    placed = (
        P("site", None, "sec", None, None),
        P("site", None, "sec", None, None),
        P("site", "sec", None, None),
        P("site", None, "sec", None, None),
        P("site", None, "sec", None, None),
        P("site", None, None, None, None),
        P("site", None, None),
    )
    return jax.shard_map(
        local,
        mesh=mesh,
        in_specs=placed,
        out_specs=(P("site", None, "sec", None, None), P("site")),
        check_vma=False,
    )
```

```python
import functools

import jax
import jax.numpy as jnp
import numpy as np
from jax import lax
from jax.experimental import pallas as pl
from jax.experimental.pallas import tpu as pltpu
from jax.sharding import PartitionSpec as P

ENV_STEPS = 2
DESCENT = 2
POLAR = 6

TINY = 1e-06
HIGHEST = lax.Precision.HIGHEST
CHARGE_STEPS = (0, 1, -1, 2, -2)
CLASSES = len(CHARGE_STEPS)
BOTH = ("site", "sec")
VMEM_LIMIT = 15 * 1024 * 1024
PIECES = 2


class Places:
    def __init__(self, sites, secs):
        self.sites, self.secs = sites, secs
        self.half = secs // 2
        self.up = (self.half + 1) // 2

    def home(self, site, sector):
        return (site % self.sites) * self.secs + sector % self.secs

    def position(self, place):
        back = self.half - 1 + self.up - place
        if isinstance(place, int):
            return place if place < self.up else back
        return jnp.where(place < self.up, place, back)

    def slot(self, chain, sector):
        chain, sector = chain % self.sites, sector % self.secs
        place = chain % 2 * self.half + self.position(sector // 2)
        return (chain // 2 * 2 + sector % 2) * self.secs + place

    def pairs(self, source, target):
        return [
            (source(chain, sector), target(chain, sector))
            for chain in range(self.sites)
            for sector in range(self.secs)
        ]

    def fetch(self, x, site_by=0, sec_by=0):
        return lax.ppermute(
            x, BOTH, self.pairs(lambda g, k: self.home(g + site_by, k + sec_by), self.slot)
        )

    def send_home(self, x, site_by, sec_by):
        return lax.ppermute(
            x, BOTH, self.pairs(self.slot, lambda g, k: self.home(g + site_by, k + sec_by))
        )

    def ahead(self, x, by, chain_by=0):
        return lax.ppermute(
            x, BOTH, self.pairs(lambda g, k: self.slot(g + chain_by, k + by), self.slot)
        )

    def partner(self, x, bit):
        return lax.ppermute(x, BOTH, self.pairs(lambda g, k: self.slot(g, k ^ bit), self.slot))

    def my_chain(self):
        return lax.axis_index("site") // 2 * 2 + lax.axis_index("sec") // self.half

    def my_sector(self):
        position = self.position(lax.axis_index("sec") % self.half)
        return 2 * position + lax.axis_index("site") % 2

    def collect(self, values):
        sector = self.my_sector()
        table = values
        bit = 1
        while bit < self.secs:
            other = self.partner(table, bit)
            first = (sector & bit) == 0
            table = jnp.where(
                first, jnp.concatenate([table, other]), jnp.concatenate([other, table])
            )
            bit *= 2
        return table


ROWS = 8
PARTS = 2


def label_groups(channels, states, sectors, sign):
    groups = {}
    for state in range(states):
        for channel in range(channels):
            label = (state + sign * CHARGE_STEPS[channel % CLASSES]) % sectors
            groups.setdefault(label, []).append((state, channel))
    return [groups[label] for label in sorted(groups)]


def even(count):
    return count + count % 2


def spread_matrix(groups, channels, states):
    rows = []
    for group in groups:
        block = np.zeros((even(len(group)), ROWS, states * channels), np.float32)
        for index, (state, channel) in enumerate(group):
            block[index, :, state * channels + channel] = 1
        rows.append(block.reshape(-1, states * channels))
    return np.concatenate(rows)


def expand_kernel(sizes, weight_ref, spread_ref, out_ref):
    start = 0
    for size in sizes:
        spread = spread_ref[pl.ds(start, size), :]
        picked = jnp.dot(spread, weight_ref[...], preferred_element_type=jnp.float32)
        full = lax.dot_general(
            picked.astype(jnp.bfloat16),
            spread,
            (((1,), (1,)), ((), ())),
            preferred_element_type=jnp.float32,
        )
        row = lax.broadcasted_iota(jnp.int32, full.shape, 0)
        column = lax.broadcasted_iota(jnp.int32, full.shape, 1)
        same = lax.rem(row, ROWS) == lax.rem(column, ROWS)
        out_ref[pl.ds(start, size), pl.ds(0, size)] = jnp.where(same, full, 0.0).astype(
            jnp.bfloat16
        )
        start += size


def mix_channels(groups, channels, weight_ref, mixed_ref, write, offset, height):
    def step(index, carry):
        first = pl.multiple_of(index * 2 * ROWS, 2 * ROWS)
        start = 0
        for group in groups:
            size = even(len(group)) * ROWS
            parts = []
            for state, channel in group:
                rows = (state * channels + channel) * height + first
                halves = [
                    mixed_ref[pl.ds(pl.multiple_of(rows + half * ROWS, ROWS), ROWS), :]
                    for half in range(2)
                ]
                parts.append(jnp.concatenate(halves, axis=1))
            if len(group) % 2:
                parts.append(parts[0])
            operand = jnp.concatenate(parts, axis=0).astype(jnp.bfloat16)
            product = jnp.dot(
                weight_ref[pl.ds(start, size), pl.ds(0, size)],
                operand,
                preferred_element_type=jnp.float32,
            )
            block = product.shape[1] // 2
            for number, pair in enumerate(group):
                rows = product[number * ROWS : (number + 1) * ROWS]
                both = jnp.concatenate([rows[:, :block], rows[:, block:]], axis=0)
                write(*pair, pl.multiple_of(offset + first, 2 * ROWS), both.astype(jnp.bfloat16))
            start += size
        return carry

    lax.fori_loop(0, height // (2 * ROWS), step, 0)


def by_parts(block, body):
    height = block // PARTS

    def one(part, carry):
        body(pl.multiple_of(part * height, height), height)
        return carry

    lax.fori_loop(0, PARTS, one, 0)


def into(gathered_ref, channels, block):
    def write(state, channel, first, rows):
        start = (state * channels + channel) * block
        gathered_ref[pl.ds(pl.multiple_of(start + first, 2 * ROWS), 2 * ROWS), :] = rows

    return write


def batches(items, most):
    pieces = -(-len(items) // most)
    size = -(-len(items) // pieces)
    return [items[start : start + size] for start in range(0, len(items), size)]


def rows_of(chunks, channel, offset, height):
    size = chunks[0].shape[0]
    return chunks[channel // size][channel % size, pl.ds(offset, height), :]


def channel_of(chunks, channel):
    size = chunks[0].shape[0]
    return chunks[channel // size][channel % size]


def put_channel(chunks, channel, value):
    size = chunks[0].shape[0]
    chunks[channel // size][channel % size] = value


def count_channels(chunks):
    return sum(chunk.shape[0] for chunk in chunks)


def mix_left(env, tensors, mixed_ref, offset, height):
    channels, block = count_channels(env), env[0].shape[1]
    for cls in range(CLASSES):
        right = jnp.concatenate(tensors[cls], axis=1)
        for batch in batches(list(range(cls, channels, CLASSES)), 5):
            rows = jnp.concatenate(
                [rows_of(env, channel, offset, height) for channel in batch], axis=0
            )
            product = jnp.dot(rows, right, preferred_element_type=jnp.float32)
            for number, channel in enumerate(batch):
                for t in range(len(tensors[cls])):
                    mixed_ref[pl.ds((t * channels + channel) * height, height), :] = product[
                        number * height : (number + 1) * height, t * block : (t + 1) * block
                    ]


def left_kernel(groups, states, pieces, *refs):
    env, (tensor_ref, weight_ref) = refs[:pieces], refs[pieces : pieces + 2]
    outs, mixed_ref = refs[pieces + 2 : -1], refs[-1]
    channels, block = count_channels(env), env[0].shape[1]

    def write(state, channel, first, rows):
        size = channels // pieces
        out_ref = outs[state * pieces + channel // size]
        out_ref[channel % size, pl.ds(first, 2 * ROWS), :] = rows

    def body(offset, height):
        tensors = [[tensor_ref[cls, t] for t in range(states)] for cls in range(CLASSES)]
        mix_left(env, tensors, mixed_ref, offset, height)
        mix_channels(groups, channels, weight_ref, mixed_ref, write, offset, height)

    by_parts(block, body)


def left_close_kernel(iso_ref, gathered_ref, moved_ref, out_ref, square_ref):
    channels, block, _ = gathered_ref.shape
    square = jnp.zeros((ROWS, block), jnp.float32)
    for batch in batches(list(range(channels)), 2):
        right = jnp.concatenate([gathered_ref[channel] for channel in batch], axis=1)
        product = lax.dot_general(
            iso_ref[...], right, (((0,), (0,)), ((), ())), preferred_element_type=jnp.float32
        )
        for number, channel in enumerate(batch):
            part = product[:, number * block : (number + 1) * block]
            part = part + moved_ref[channel].astype(jnp.float32)
            out_ref[channel] = part.astype(jnp.bfloat16)
            square = square + jnp.sum((part * part).reshape(-1, ROWS, block), axis=0)
    square_ref[...] = square


def right_kernel(groups, states, pieces, *refs):
    envs = [refs[t * pieces : (t + 1) * pieces] for t in range(states)]
    refs = refs[states * pieces :]
    own_ref, tensor_ref, weight_ref = refs[:3]
    outs, (square_ref, mixed_ref, gathered_ref) = refs[3 : 3 + pieces], refs[3 + pieces :]
    channels, block = count_channels(envs[0]), envs[0][0].shape[1]
    zero = jnp.zeros((block, block), jnp.bfloat16)
    write = into(gathered_ref, channels, block)

    def body(offset, height):
        for pair in batches(list(range(states)), 2):
            own = jnp.concatenate(
                [
                    jnp.concatenate([own_ref[t] if t == other else zero for other in pair], axis=1)
                    for t in pair
                ],
                axis=0,
            )
            for batch in batches(list(range(channels)), 6):
                rows = jnp.concatenate(
                    [
                        jnp.concatenate(
                            [rows_of(envs[t], channel, offset, height) for channel in batch], axis=0
                        )
                        for t in pair
                    ],
                    axis=1,
                )
                product = lax.dot_general(
                    rows, own, (((1,), (1,)), ((), ())), preferred_element_type=jnp.float32
                )
                for number, t in enumerate(pair):
                    start = (t * channels + batch[0]) * height
                    mixed_ref[pl.ds(start, len(batch) * height), :] = product[
                        :, number * block : (number + 1) * block
                    ]
        mix_channels(groups, channels, weight_ref, mixed_ref, write, offset, height)

    by_parts(block, body)
    square = jnp.zeros((ROWS, block), jnp.float32)
    for cls in range(CLASSES):
        left = jnp.concatenate([tensor_ref[cls, s] for s in range(states)], axis=1)
        for batch in batches(list(range(cls, channels, CLASSES)), 2):
            right = jnp.concatenate(
                [
                    jnp.concatenate(
                        [
                            gathered_ref[pl.ds((s * channels + channel) * block, block), :]
                            for s in range(states)
                        ],
                        axis=0,
                    )
                    for channel in batch
                ],
                axis=1,
            )
            product = jnp.dot(left, right, preferred_element_type=jnp.float32)
            for number, channel in enumerate(batch):
                part = product[:, number * block : (number + 1) * block]
                put_channel(outs, channel, part.astype(jnp.bfloat16))
                square = square + jnp.sum((part * part).reshape(-1, ROWS, block), axis=0)
    square_ref[...] = square


ENV_LANE = 5
LANES = 128


def quotient(table, entry_count):
    def total(x):
        return jnp.sum(x, axis=0, keepdims=True)

    squares = [
        total(table[:, lane : lane + 1]) for lane in range(ENV_LANE, ENV_LANE + 2 * ENV_STEPS + 1)
    ]
    scale = jnp.ones((1, 1), jnp.float32)
    for side in range(2):
        side_scale = jnp.ones((1, 1), jnp.float32)
        for square in squares[side * ENV_STEPS : (side + 1) * ENV_STEPS]:
            side_scale = side_scale * lax.rsqrt(side_scale * side_scale * square / entry_count + TINY)
        scale = scale * side_scale
    a, b, e, c, unit = (table[:, lane : lane + 1] for lane in range(ENV_LANE))
    a, e, unit = scale * a, scale * e, scale * unit
    c = unit * unit * c
    whole_a, whole_b = total(a), total(b)
    energy = whole_a / (whole_b + TINY)
    off = e - energy
    residual_sq = total(c + 2.0 * off * (a - e * b) + off * off * b)
    factor = 0.5 * jnp.sqrt(whole_b / (residual_sq + TINY))
    square = whole_b - 2.0 * factor * (whole_a - energy * whole_b) + factor * factor * residual_sq
    return scale, energy, factor, square, squares[2 * ENV_STEPS]


def updated(vector, image, scale, energy, factor):
    return vector - factor * (scale * image - energy * vector)


def sum_all(x):
    return jnp.sum(jnp.sum(x, axis=0, keepdims=True), axis=1, keepdims=True)


def operator_front_kernel(groups, states, pieces, renew, entry_count, *refs):
    env, refs = refs[:pieces], refs[pieces:]
    others = CLASSES - 1
    weight_ref, vector_ref, rolled = refs[0], refs[1], refs[2 : 2 + others]
    rest = refs[2 + others :]
    if renew:
        image_ref, moved, table_ref = rest[0], rest[1 : 1 + others], rest[1 + others]
        rest = rest[2 + others :]
        scale, energy, factor, _, _ = quotient(table_ref[...], entry_count)
    gathered_ref, new_ref, tensor_ref, mixed_ref = rest
    channels, block = count_channels(env), env[0].shape[1]
    for t in range(states):
        vector = vector_ref[t]
        if renew:
            vector = updated(vector, image_ref[t], scale, energy, factor)
        new_ref[t] = vector
        tensor_ref[0, t] = vector.astype(jnp.bfloat16)
        for cls in range(1, CLASSES):
            vector = rolled[cls - 1][t]
            if renew:
                image = moved[cls - 1][t].astype(jnp.float32)
                vector = updated(vector.astype(jnp.float32), image, scale, energy, factor)
            tensor_ref[cls, t] = vector.astype(jnp.bfloat16)
    write = into(gathered_ref, channels, block)

    def body(offset, height):
        tensors = [[tensor_ref[cls, t] for t in range(states)] for cls in range(CLASSES)]
        mix_left(env, tensors, mixed_ref, offset, height)
        mix_channels(groups, channels, weight_ref, mixed_ref, write, offset, height)

    by_parts(block, body)


def operator_back_kernel(states, pieces, *refs):
    rights = [refs[t * pieces : (t + 1) * pieces] for t in range(states)]
    refs = refs[states * pieces :]
    squares, refs = refs[: 2 * ENV_STEPS + 1], refs[2 * ENV_STEPS + 1 :]
    gathered_ref, vector_ref, image_ref, half_ref, sums_ref, held_ref, arrived = refs
    channels, block = count_channels(rights[0]), rights[0][0].shape[1]
    size = channels // pieces
    copies = []
    for s in range(states):
        for piece in range(pieces):
            copy = pltpu.make_async_copy(
                rights[s][piece],
                held_ref.at[s, pl.ds(piece * size, size)],
                arrived.at[s, piece],
            )
            copy.start()
            copies.append(copy)
    a = jnp.zeros((1, 1), jnp.float32)
    b = jnp.zeros((1, 1), jnp.float32)
    for s in range(states):
        for copy in copies[s * pieces : (s + 1) * pieces]:
            copy.wait()
        total = jnp.zeros((block, block), jnp.float32)
        for batch in batches(list(range(channels)), 6):
            left = jnp.concatenate(
                [
                    gathered_ref[pl.ds((s * channels + channel) * block, block), :]
                    for channel in batch
                ],
                axis=1,
            )
            right = held_ref[s, batch[0] : batch[-1] + 1].reshape(len(batch) * block, block)
            total = total + jnp.dot(left, right, preferred_element_type=jnp.float32)
        image_ref[s] = total
        half_ref[s] = total.astype(jnp.bfloat16)
        vector = vector_ref[s]
        a = a + sum_all(vector * total)
        b = b + sum_all(vector * vector)
    e = jnp.where(b > 0, a / jnp.where(b > 0, b, 1.0), 0.0)
    residual = image_ref[...].reshape(states * block, block) - e * vector_ref[...].reshape(
        states * block, block
    )
    unit = jnp.max(jnp.max(jnp.abs(residual), axis=0, keepdims=True), axis=1, keepdims=True)
    unit = jnp.where(unit > 0, unit, 1.0)
    residual = residual / unit
    lane = lax.broadcasted_iota(jnp.int32, sums_ref.shape, 1)
    sums = jnp.zeros(sums_ref.shape, jnp.float32)
    values = (a, b, e, sum_all(residual * residual), unit, *(sum_all(x[...]) for x in squares))
    for place, value in enumerate(values):
        sums = jnp.where(lane == place, value, sums)
    sums_ref[...] = sums


def polar_kernel(entry_count, both_ref, table_ref, centre_ref, out_ref, energy_ref):
    states, _, block, _ = both_ref.shape
    rows = lax.broadcasted_iota(jnp.int32, (block, block), 0)
    columns = lax.broadcasted_iota(jnp.int32, (block, block), 1)
    unit = (rows == columns).astype(jnp.float32)

    def product(x, y, contract=((1,), (0,))):
        return lax.dot_general(
            x, y, (contract, ((), ())), precision=HIGHEST, preferred_element_type=jnp.float32
        )

    scale, energy, factor, square, centre_sq = quotient(table_ref[...], entry_count)
    energy_ref[...] = jnp.broadcast_to(energy, energy_ref.shape)
    vector = updated(
        both_ref[:, 0].reshape(states * block, block),
        both_ref[:, 1].reshape(states * block, block),
        scale,
        energy,
        factor,
    ) * lax.rsqrt(square + TINY)
    centre = centre_ref[...].astype(jnp.float32) * lax.rsqrt(centre_sq + TINY)
    grams = [product(x, x, ((0,), (0,))) for x in (vector, centre)]
    totals = [unit, unit]
    for step in range(POLAR):
        factors = [1.5 * unit - 0.5 * gram for gram in grams]
        totals = [
            factor if step == 0 else product(total, factor)
            for total, factor in zip(totals, factors)
        ]
        if step < POLAR - 1:
            grams = [
                product(product(factor, gram), factor) for gram, factor in zip(grams, factors)
            ]
    closing = product(totals[0], product(centre, totals[1]), ((1,), (1,)))
    out_ref[...] = product(vector, closing).reshape(states, block, block).astype(jnp.bfloat16)


def call(kernel, out_shape, scratch_shapes, flops, operands, in_hbm=0):
    places = [pltpu.HBM] * in_hbm + [pltpu.VMEM] * (len(operands) - in_hbm)
    return pl.pallas_call(
        kernel,
        out_shape=out_shape,
        in_specs=[pl.BlockSpec(memory_space=place) for place in places],
        scratch_shapes=scratch_shapes,
        compiler_params=pltpu.CompilerParams(vmem_limit_bytes=VMEM_LIMIT),
        cost_estimate=pl.CostEstimate(
            flops=flops,
            bytes_accessed=sum(int(np.prod(x.shape)) * x.dtype.itemsize for x in operands),
            transcendentals=0,
        ),
    )(*operands)


def float_out(*shape):
    return jax.ShapeDtypeStruct(shape, jnp.float32)


def half_out(*shape):
    return jax.ShapeDtypeStruct(shape, jnp.bfloat16)


def work(states, channels, block):
    return 4 * states * channels * block**3 + 2 * (states * channels * block) ** 2


def expanded(weight, groups, channels, states):
    spread = spread_matrix(groups, channels, states)
    sizes = tuple(even(len(group)) * ROWS for group in groups)
    return call(
        functools.partial(expand_kernel, sizes),
        half_out(spread.shape[0], -(-max(sizes) // 128) * 128),
        [],
        2 * spread.size * spread.shape[0],
        (weight, jnp.asarray(spread, jnp.bfloat16)),
    )


def left_front(env, tensors, weight, groups):
    channels, block = count_channels(env), env[0].shape[1]
    states, pieces = tensors.shape[1], len(env)
    outs = call(
        functools.partial(left_kernel, groups, states, pieces),
        [half_out(channels // pieces, block, block)] * (states * pieces),
        [pltpu.VMEM((states * channels * block // PARTS, block), jnp.float32)],
        work(states, channels, block),
        (*env, tensors, weight),
    )
    return [outs[s * pieces : (s + 1) * pieces] for s in range(states)]


def left_close(iso, gathered, moved):
    channels, block, _ = gathered.shape
    return call(
        left_close_kernel,
        (half_out(channels, block, block), float_out(ROWS, block)),
        [],
        2 * channels * block**3,
        (iso, gathered, moved),
    )


def right_whole(envs, own, tensors, weight, groups):
    channels, block = count_channels(envs[0]), envs[0][0].shape[1]
    states, pieces = len(envs), len(envs[0])
    outs = call(
        functools.partial(right_kernel, groups, states, pieces),
        [half_out(channels // pieces, block, block)] * pieces + [float_out(ROWS, block)],
        [
            pltpu.VMEM((states * channels * block // PARTS, block), jnp.float32),
            pltpu.VMEM((states * channels * block, block), jnp.bfloat16),
        ],
        work(states, channels, block),
        (*(chunk for env in envs for chunk in env), own, tensors, weight),
    )
    return outs[:pieces], outs[pieces]


def operator_front(env, weight, groups, entry_count, vector, rolled, news):
    channels, block = count_channels(env), env[0].shape[1]
    states, pieces = vector.shape[0], len(env)
    return call(
        functools.partial(
            operator_front_kernel, groups, states, pieces, len(news) > 0, entry_count
        ),
        (half_out(states * channels * block, block), float_out(states, block, block)),
        [
            pltpu.VMEM((CLASSES, states, block, block), jnp.bfloat16),
            pltpu.VMEM((states * channels * block // PARTS, block), jnp.float32),
        ],
        work(states, channels, block),
        (*env, weight, vector, *rolled, *news),
    )


def operator_back(rights, squares, gathered, vector):
    channels, block = count_channels(rights[0]), rights[0][0].shape[1]
    states, pieces = len(rights), len(rights[0])
    return call(
        functools.partial(operator_back_kernel, states, pieces),
        (
            float_out(states, block, block),
            half_out(states, block, block),
            float_out(1, LANES),
        ),
        [
            pltpu.VMEM((states, channels, block, block), jnp.bfloat16),
            pltpu.SemaphoreType.DMA((states, pieces)),
        ],
        2 * states * channels * block**3,
        (*(chunk for right in rights for chunk in right), *squares, gathered, vector),
        states * pieces,
    )


def polar(both, table, centre, entry_count):
    states, _, block, _ = both.shape
    return call(
        functools.partial(polar_kernel, entry_count),
        (half_out(states, block, block), float_out(1, LANES)),
        [],
        600 * block**3,
        (both, table, centre),
    )


def charge_mask(channels, states, sectors):
    charge = np.array([CHARGE_STEPS[channel % CLASSES] for channel in range(channels)])
    state = np.arange(states)
    balance = (
        charge[:, None, None, None]
        + state[None, None, None, :]
        - state[None, None, :, None]
        - charge[None, :, None, None]
    )
    return jnp.asarray((balance % sectors == 0).astype(np.float32)).astype(jnp.bfloat16)


def weight_matrices(mpo, pattern, sectors):
    channels, _, states, _ = mpo.shape
    allowed = charge_mask(channels, states, sectors)
    weights = mpo * pattern[:, :, None, None].astype(jnp.bfloat16) * allowed
    size = states * channels
    left = jnp.transpose(weights, (2, 1, 3, 0)).reshape(size, size)
    right = jnp.transpose(weights, (2, 0, 3, 1)).reshape(size, size)
    return jnp.stack([left, right])


def other_classes_of(places, x):
    one, minus = places.ahead(x, 1), places.ahead(x, -1)
    return one, minus, places.ahead(one, 1), places.ahead(minus, -1)


def classes_of(places, x):
    return jnp.stack([x, *other_classes_of(places, x)])


def other_classes_at_once(places, x):
    return tuple(places.ahead(x, charge) for charge in CHARGE_STEPS[1:])


def after(first, then):
    return lax.optimization_barrier((first, then))


def local(left_iso, right_iso, centre, left_env, right_env, mpo, pattern):
    sites, secs = lax.axis_size("site"), lax.axis_size("sec")
    places = Places(sites, secs)
    left_iso, right_iso, centre = left_iso[0, :, 0], right_iso[0, :, 0], centre[0, 0]
    states, block, _ = left_iso.shape
    channels = mpo.shape[1]
    entry_count = left_env.size * secs
    left_groups = label_groups(channels, states, secs, 1)
    right_groups = label_groups(channels, states, secs, -1)

    pieces = PIECES if channels % PIECES == 0 else 1

    def split(env):
        return jnp.split(env, pieces)

    def ahead(env, by, chain_by=0):
        return [places.ahead(chunk, by, chain_by) for chunk in env]

    def fetch_env(env):
        return [places.fetch(chunk) for chunk in split(env)]

    both_isos = places.fetch(jnp.concatenate([left_iso, right_iso]))
    both_isos, right_env = after(both_isos, right_env)
    right = fetch_env(right_env[0, :, 0])
    left = []
    for piece, env in enumerate(split(left_env[0, :, 0])):
        right[piece], env = after(right[piece], env)
        left.append(places.fetch(env))
    right, (left_iso, right_iso, centre) = after(right, (left_iso, right_iso, centre))
    left_isos, right_isos = [both_isos[:states]], [both_isos[states:]]
    rolled = [classes_of(places, both_isos)]
    for step in range(1, ENV_STEPS):
        left_isos.append(places.fetch(left_iso, step))
        right_isos.append(places.fetch(right_iso, -step))
        rolled.append(
            classes_of(places, jnp.concatenate([left_isos[step], right_isos[step]]))
        )
    own_tensors = places.fetch(jnp.concatenate([left_iso, centre[None]]), ENV_STEPS)
    own_iso, own_centre = own_tensors[:states], own_tensors[states]
    centres = [own_centre]
    for s in range(1, states):
        centres.append(places.ahead(centres[-1], 1))

    gathered_weights = lax.all_gather(weight_matrices(mpo[0], pattern[0], secs), "site")
    chain = places.my_chain()

    def weight_of(site_by, kind):
        weight = lax.dynamic_index_in_dim(
            gathered_weights, (chain + site_by) % sites, 0, False
        )[kind]
        return expanded(weight, (left_groups, right_groups)[kind], channels, states)

    weights = (
        [weight_of(step, 0) for step in range(ENV_STEPS + 1)],
        [weight_of(-step, 1) for step in range(ENV_STEPS)],
    )
    vector = jnp.einsum(
        "sxy,syz->sxz", own_iso, jnp.stack(centres), preferred_element_type=jnp.float32
    )
    rolled_vector = other_classes_of(places, vector.astype(jnp.bfloat16))
    rolled[0], right = after(rolled[0], right)
    centre_float = own_centre.astype(jnp.float32)
    centre_square = jnp.sum((centre_float * centre_float).reshape(-1, ROWS, block), axis=0)

    left_squares, right_squares = [], []
    for step in range(ENV_STEPS):
        envs = [right]
        for t in range(1, states):
            if step == 0 and t == states - 1:
                left, envs[-1] = after(left, envs[-1])
            envs.append(ahead(envs[-1], 1))
        if step == 0:
            (weights, rolled, rolled_vector), envs = after((weights, rolled, rolled_vector), envs)
        right, square = right_whole(
            envs,
            right_isos[step],
            rolled[step][:, states:],
            weights[1][step],
            right_groups,
        )
        right_squares.append(square)

        gathered = left_front(left, rolled[step][:, :states], weights[0][step], left_groups)
        moved = [None] * pieces
        for s in reversed(range(1, states)):
            for piece in range(pieces):
                part = jnp.einsum(
                    "xy,vxz->vyz",
                    left_isos[step][s],
                    gathered[s][piece],
                    preferred_element_type=jnp.float32,
                )
                if moved[piece] is not None:
                    part = part + moved[piece].astype(jnp.float32)
                moved[piece] = places.ahead(part.astype(jnp.bfloat16), -1)
        closed = [
            left_close(left_isos[step][0], gathered[0][piece], moved[piece])
            for piece in range(pieces)
        ]
        left = [env for env, _ in closed]
        left_squares.append(sum(square for _, square in closed))

    if (2 * ENV_STEPS) % sites:
        right = ahead(right, 0, 2 * ENV_STEPS)
        right_squares = ahead(right_squares, 0, 2 * ENV_STEPS)
    squares = left_squares + right_squares + [centre_square]
    rights = [right]
    for s in range(1, states):
        rights.append(ahead(rights[-1], 1))
    news = ()
    for step in range(DESCENT):
        gathered, vector = operator_front(
            left, weights[0][ENV_STEPS], left_groups, entry_count, vector, rolled_vector, news
        )
        image, half_image, own_sums = operator_back(rights, squares, gathered, vector)
        table = places.collect(own_sums)
        if step < DESCENT - 1:
            news = (image, *other_classes_at_once(places, half_image), table)

    both = jnp.stack([vector, image], axis=1)
    columns = jnp.stack([both[0]] + [places.ahead(both[s], -s) for s in range(1, states)])
    column_left, energy = polar(columns, table, own_centre, entry_count)
    new_left = jnp.stack(
        [places.send_home(column_left[s], ENV_STEPS, -s) for s in range(states)]
    )
    energy = places.send_home(energy, ENV_STEPS, 0)
    return new_left[None, :, None], energy[0, :1]


def solution(mesh):
    placed = (
        P("site", None, "sec", None, None),
        P("site", None, "sec", None, None),
        P("site", "sec", None, None),
        P("site", None, "sec", None, None),
        P("site", None, "sec", None, None),
        P("site", None, None, None, None),
        P("site", None, None),
    )
    return jax.shard_map(
        local,
        mesh=mesh,
        in_specs=placed,
        out_specs=(P("site", None, "sec", None, None), P("site")),
        check_vma=False,
    )
```

```python
import functools

import jax
import jax.numpy as jnp
import numpy as np
from jax import lax
from jax.experimental import pallas as pl
from jax.experimental.pallas import tpu as pltpu
from jax.sharding import PartitionSpec as P

ENV_STEPS = 2
DESCENT = 2
POLAR = 6

TINY = 1e-06
HIGHEST = lax.Precision.HIGHEST
CHARGE_STEPS = (0, 1, -1, 2, -2)
CLASSES = len(CHARGE_STEPS)
BOTH = ("site", "sec")
VMEM_LIMIT = 24 * 1024 * 1024
PIECES = 2


class Places:
    def __init__(self, sites, secs):
        self.sites, self.secs = sites, secs
        self.half = secs // 2
        self.up = (self.half + 1) // 2

    def home(self, site, sector):
        return (site % self.sites) * self.secs + sector % self.secs

    def position(self, place):
        back = self.half - 1 + self.up - place
        if isinstance(place, int):
            return place if place < self.up else back
        return jnp.where(place < self.up, place, back)

    def slot(self, chain, sector):
        chain, sector = chain % self.sites, sector % self.secs
        place = chain % 2 * self.half + self.position(sector // 2)
        return (chain // 2 * 2 + sector % 2) * self.secs + place

    def pairs(self, source, target):
        return [
            (source(chain, sector), target(chain, sector))
            for chain in range(self.sites)
            for sector in range(self.secs)
        ]

    def fetch(self, x, site_by=0, sec_by=0):
        return lax.ppermute(
            x, BOTH, self.pairs(lambda g, k: self.home(g + site_by, k + sec_by), self.slot)
        )

    def send_home(self, x, site_by, sec_by):
        return lax.ppermute(
            x, BOTH, self.pairs(self.slot, lambda g, k: self.home(g + site_by, k + sec_by))
        )

    def ahead(self, x, by, chain_by=0):
        return lax.ppermute(
            x, BOTH, self.pairs(lambda g, k: self.slot(g + chain_by, k + by), self.slot)
        )

    def partner(self, x, bit):
        return lax.ppermute(x, BOTH, self.pairs(lambda g, k: self.slot(g, k ^ bit), self.slot))

    def my_chain(self):
        return lax.axis_index("site") // 2 * 2 + lax.axis_index("sec") // self.half

    def my_sector(self):
        position = self.position(lax.axis_index("sec") % self.half)
        return 2 * position + lax.axis_index("site") % 2

    def collect(self, values):
        sector = self.my_sector()
        table = values
        bit = 1
        while bit < self.secs:
            other = self.partner(table, bit)
            first = (sector & bit) == 0
            table = jnp.where(
                first, jnp.concatenate([table, other]), jnp.concatenate([other, table])
            )
            bit *= 2
        return table


ROWS = 8
PARTS = 2


def label_groups(channels, states, sectors, sign):
    groups = {}
    for state in range(states):
        for channel in range(channels):
            label = (state + sign * CHARGE_STEPS[channel % CLASSES]) % sectors
            groups.setdefault(label, []).append((state, channel))
    return [groups[label] for label in sorted(groups)]


def even(count):
    return count + count % 2


def spread_matrix(groups, channels, states):
    rows = []
    for group in groups:
        block = np.zeros((even(len(group)), ROWS, states * channels), np.float32)
        for index, (state, channel) in enumerate(group):
            block[index, :, state * channels + channel] = 1
        rows.append(block.reshape(-1, states * channels))
    return np.concatenate(rows)


def expand_kernel(sizes, weight_ref, spread_ref, out_ref):
    start = 0
    for size in sizes:
        spread = spread_ref[pl.ds(start, size), :]
        picked = jnp.dot(spread, weight_ref[...], preferred_element_type=jnp.float32)
        full = lax.dot_general(
            picked.astype(jnp.bfloat16),
            spread,
            (((1,), (1,)), ((), ())),
            preferred_element_type=jnp.float32,
        )
        row = lax.broadcasted_iota(jnp.int32, full.shape, 0)
        column = lax.broadcasted_iota(jnp.int32, full.shape, 1)
        same = lax.rem(row, ROWS) == lax.rem(column, ROWS)
        out_ref[pl.ds(start, size), pl.ds(0, size)] = jnp.where(same, full, 0.0).astype(
            jnp.bfloat16
        )
        start += size


def mix_channels(groups, channels, weight_ref, mixed_ref, write, offset, height):
    def step(index, carry):
        first = pl.multiple_of(index * 2 * ROWS, 2 * ROWS)
        start = 0
        for group in groups:
            size = even(len(group)) * ROWS
            parts = []
            for state, channel in group:
                rows = (state * channels + channel) * height + first
                halves = [
                    mixed_ref[pl.ds(pl.multiple_of(rows + half * ROWS, ROWS), ROWS), :]
                    for half in range(2)
                ]
                parts.append(jnp.concatenate(halves, axis=1))
            if len(group) % 2:
                parts.append(parts[0])
            operand = jnp.concatenate(parts, axis=0).astype(jnp.bfloat16)
            product = jnp.dot(
                weight_ref[pl.ds(start, size), pl.ds(0, size)],
                operand,
                preferred_element_type=jnp.float32,
            )
            block = product.shape[1] // 2
            for number, pair in enumerate(group):
                rows = product[number * ROWS : (number + 1) * ROWS]
                both = jnp.concatenate([rows[:, :block], rows[:, block:]], axis=0)
                write(*pair, pl.multiple_of(offset + first, 2 * ROWS), both.astype(jnp.bfloat16))
            start += size
        return carry

    lax.fori_loop(0, height // (2 * ROWS), step, 0)


def by_parts(block, body):
    height = block // PARTS

    def one(part, carry):
        body(pl.multiple_of(part * height, height), height)
        return carry

    lax.fori_loop(0, PARTS, one, 0)


def into(gathered_ref, channels, block):
    def write(state, channel, first, rows):
        start = (state * channels + channel) * block
        gathered_ref[pl.ds(pl.multiple_of(start + first, 2 * ROWS), 2 * ROWS), :] = rows

    return write


def batches(items, most):
    pieces = -(-len(items) // most)
    size = -(-len(items) // pieces)
    return [items[start : start + size] for start in range(0, len(items), size)]


def rows_of(chunks, channel, offset, height):
    size = chunks[0].shape[0]
    return chunks[channel // size][channel % size, pl.ds(offset, height), :]


def channel_of(chunks, channel):
    size = chunks[0].shape[0]
    return chunks[channel // size][channel % size]


def put_channel(chunks, channel, value):
    size = chunks[0].shape[0]
    chunks[channel // size][channel % size] = value


def count_channels(chunks):
    return sum(chunk.shape[0] for chunk in chunks)


def mix_left(env, tensors, mixed_ref, offset, height):
    channels, block = count_channels(env), env[0].shape[1]
    for cls in range(CLASSES):
        right = jnp.concatenate(tensors[cls], axis=1)
        for batch in batches(list(range(cls, channels, CLASSES)), 5):
            rows = jnp.concatenate(
                [rows_of(env, channel, offset, height) for channel in batch], axis=0
            )
            product = jnp.dot(rows, right, preferred_element_type=jnp.float32)
            for number, channel in enumerate(batch):
                for t in range(len(tensors[cls])):
                    mixed_ref[pl.ds((t * channels + channel) * height, height), :] = product[
                        number * height : (number + 1) * height, t * block : (t + 1) * block
                    ]


def left_kernel(groups, states, pieces, *refs):
    env, (tensor_ref, weight_ref) = refs[:pieces], refs[pieces : pieces + 2]
    outs, mixed_ref = refs[pieces + 2 : -1], refs[-1]
    channels, block = count_channels(env), env[0].shape[1]

    def write(state, channel, first, rows):
        size = channels // pieces
        out_ref = outs[state * pieces + channel // size]
        out_ref[channel % size, pl.ds(first, 2 * ROWS), :] = rows

    def body(offset, height):
        tensors = [[tensor_ref[cls, t] for t in range(states)] for cls in range(CLASSES)]
        mix_left(env, tensors, mixed_ref, offset, height)
        mix_channels(groups, channels, weight_ref, mixed_ref, write, offset, height)

    by_parts(block, body)


def left_close_kernel(iso_ref, gathered_ref, moved_ref, out_ref, square_ref):
    channels, block, _ = gathered_ref.shape
    square = jnp.zeros((ROWS, block), jnp.float32)
    for batch in batches(list(range(channels)), 2):
        right = jnp.concatenate([gathered_ref[channel] for channel in batch], axis=1)
        product = lax.dot_general(
            iso_ref[...], right, (((0,), (0,)), ((), ())), preferred_element_type=jnp.float32
        )
        for number, channel in enumerate(batch):
            part = product[:, number * block : (number + 1) * block]
            part = part + moved_ref[channel].astype(jnp.float32)
            out_ref[channel] = part.astype(jnp.bfloat16)
            square = square + jnp.sum((part * part).reshape(-1, ROWS, block), axis=0)
    square_ref[...] = square


def right_kernel(groups, states, pieces, *refs):
    envs = [refs[t * pieces : (t + 1) * pieces] for t in range(states)]
    refs = refs[states * pieces :]
    own_ref, tensor_ref, weight_ref = refs[:3]
    outs, (square_ref, mixed_ref, gathered_ref) = refs[3 : 3 + pieces], refs[3 + pieces :]
    channels, block = count_channels(envs[0]), envs[0][0].shape[1]
    zero = jnp.zeros((block, block), jnp.bfloat16)
    write = into(gathered_ref, channels, block)

    def body(offset, height):
        for pair in batches(list(range(states)), 2):
            own = jnp.concatenate(
                [
                    jnp.concatenate([own_ref[t] if t == other else zero for other in pair], axis=1)
                    for t in pair
                ],
                axis=0,
            )
            for batch in batches(list(range(channels)), 6):
                rows = jnp.concatenate(
                    [
                        jnp.concatenate(
                            [rows_of(envs[t], channel, offset, height) for channel in batch], axis=0
                        )
                        for t in pair
                    ],
                    axis=1,
                )
                product = lax.dot_general(
                    rows, own, (((1,), (1,)), ((), ())), preferred_element_type=jnp.float32
                )
                for number, t in enumerate(pair):
                    start = (t * channels + batch[0]) * height
                    mixed_ref[pl.ds(start, len(batch) * height), :] = product[
                        :, number * block : (number + 1) * block
                    ]
        mix_channels(groups, channels, weight_ref, mixed_ref, write, offset, height)

    by_parts(block, body)
    square = jnp.zeros((ROWS, block), jnp.float32)
    for cls in range(CLASSES):
        left = jnp.concatenate([tensor_ref[cls, s] for s in range(states)], axis=1)
        for batch in batches(list(range(cls, channels, CLASSES)), 2):
            right = jnp.concatenate(
                [
                    jnp.concatenate(
                        [
                            gathered_ref[pl.ds((s * channels + channel) * block, block), :]
                            for s in range(states)
                        ],
                        axis=0,
                    )
                    for channel in batch
                ],
                axis=1,
            )
            product = jnp.dot(left, right, preferred_element_type=jnp.float32)
            for number, channel in enumerate(batch):
                part = product[:, number * block : (number + 1) * block]
                put_channel(outs, channel, part.astype(jnp.bfloat16))
                square = square + jnp.sum((part * part).reshape(-1, ROWS, block), axis=0)
    square_ref[...] = square


ENV_LANE = 5
LANES = 128


def quotient(table, entry_count):
    def total(x):
        return jnp.sum(x, axis=0, keepdims=True)

    squares = [
        total(table[:, lane : lane + 1]) for lane in range(ENV_LANE, ENV_LANE + 2 * ENV_STEPS + 1)
    ]
    scale = jnp.ones((1, 1), jnp.float32)
    for side in range(2):
        side_scale = jnp.ones((1, 1), jnp.float32)
        for square in squares[side * ENV_STEPS : (side + 1) * ENV_STEPS]:
            side_scale = side_scale * lax.rsqrt(side_scale * side_scale * square / entry_count + TINY)
        scale = scale * side_scale
    a, b, e, c, unit = (table[:, lane : lane + 1] for lane in range(ENV_LANE))
    a, e, unit = scale * a, scale * e, scale * unit
    c = unit * unit * c
    whole_a, whole_b = total(a), total(b)
    energy = whole_a / (whole_b + TINY)
    off = e - energy
    residual_sq = total(c + 2.0 * off * (a - e * b) + off * off * b)
    factor = 0.5 * jnp.sqrt(whole_b / (residual_sq + TINY))
    square = whole_b - 2.0 * factor * (whole_a - energy * whole_b) + factor * factor * residual_sq
    return scale, energy, factor, square, squares[2 * ENV_STEPS]


def updated(vector, image, scale, energy, factor):
    return vector - factor * (scale * image - energy * vector)


def sum_all(x):
    return jnp.sum(jnp.sum(x, axis=0, keepdims=True), axis=1, keepdims=True)


def operator_front_kernel(groups, states, pieces, renew, entry_count, held, arrive, *refs):
    for place in held:
        arrive(place)
    env, refs = refs[:pieces], refs[pieces:]
    others = CLASSES - 1
    weight_ref, vector_ref, rolled = refs[0], refs[1], refs[2 : 2 + others]
    rest = refs[2 + others :]
    if renew:
        image_ref, moved, table_ref = rest[0], rest[1 : 1 + others], rest[1 + others]
        rest = rest[2 + others :]
        scale, energy, factor, _, _ = quotient(table_ref[...], entry_count)
    gathered_ref, new_ref, tensor_ref, mixed_ref = rest
    channels, block = count_channels(env), env[0].shape[1]
    for t in range(states):
        vector = vector_ref[t]
        if renew:
            vector = updated(vector, image_ref[t], scale, energy, factor)
        new_ref[t] = vector
        tensor_ref[0, t] = vector.astype(jnp.bfloat16)
        for cls in range(1, CLASSES):
            vector = rolled[cls - 1][t]
            if renew:
                image = moved[cls - 1][t].astype(jnp.float32)
                vector = updated(vector.astype(jnp.float32), image, scale, energy, factor)
            tensor_ref[cls, t] = vector.astype(jnp.bfloat16)
    write = into(gathered_ref, channels, block)

    def body(offset, height):
        tensors = [[tensor_ref[cls, t] for t in range(states)] for cls in range(CLASSES)]
        mix_left(env, tensors, mixed_ref, offset, height)
        mix_channels(groups, channels, weight_ref, mixed_ref, write, offset, height)

    by_parts(block, body)


def operator_back_kernel(states, pieces, arrive, *refs):
    rights = [refs[t * pieces : (t + 1) * pieces] for t in range(states)]
    refs = refs[states * pieces :]
    squares, refs = refs[: 2 * ENV_STEPS + 1], refs[2 * ENV_STEPS + 1 :]
    gathered_ref, vector_ref, image_ref, half_ref, sums_ref = refs
    channels, block = count_channels(rights[0]), rights[0][0].shape[1]
    a = jnp.zeros((1, 1), jnp.float32)
    b = jnp.zeros((1, 1), jnp.float32)
    for s in range(states):
        for piece in range(pieces):
            arrive(s * pieces + piece)
        total = jnp.zeros((block, block), jnp.float32)
        for batch in batches(list(range(channels)), 6):
            left = jnp.concatenate(
                [
                    gathered_ref[pl.ds((s * channels + channel) * block, block), :]
                    for channel in batch
                ],
                axis=1,
            )
            right = jnp.concatenate([channel_of(rights[s], channel) for channel in batch], axis=0)
            total = total + jnp.dot(left, right, preferred_element_type=jnp.float32)
        image_ref[s] = total
        half_ref[s] = total.astype(jnp.bfloat16)
        vector = vector_ref[s]
        a = a + sum_all(vector * total)
        b = b + sum_all(vector * vector)
    e = jnp.where(b > 0, a / jnp.where(b > 0, b, 1.0), 0.0)
    residual = image_ref[...].reshape(states * block, block) - e * vector_ref[...].reshape(
        states * block, block
    )
    unit = jnp.max(jnp.max(jnp.abs(residual), axis=0, keepdims=True), axis=1, keepdims=True)
    unit = jnp.where(unit > 0, unit, 1.0)
    residual = residual / unit
    lane = lax.broadcasted_iota(jnp.int32, sums_ref.shape, 1)
    sums = jnp.zeros(sums_ref.shape, jnp.float32)
    values = (a, b, e, sum_all(residual * residual), unit, *(sum_all(x[...]) for x in squares))
    for place, value in enumerate(values):
        sums = jnp.where(lane == place, value, sums)
    sums_ref[...] = sums


def polar_kernel(entry_count, both_ref, table_ref, centre_ref, out_ref, energy_ref):
    states, _, block, _ = both_ref.shape
    rows = lax.broadcasted_iota(jnp.int32, (block, block), 0)
    columns = lax.broadcasted_iota(jnp.int32, (block, block), 1)
    unit = (rows == columns).astype(jnp.float32)

    def product(x, y, contract=((1,), (0,))):
        return lax.dot_general(
            x, y, (contract, ((), ())), precision=HIGHEST, preferred_element_type=jnp.float32
        )

    scale, energy, factor, square, centre_sq = quotient(table_ref[...], entry_count)
    energy_ref[...] = jnp.broadcast_to(energy, energy_ref.shape)
    vector = updated(
        both_ref[:, 0].reshape(states * block, block),
        both_ref[:, 1].reshape(states * block, block),
        scale,
        energy,
        factor,
    ) * lax.rsqrt(square + TINY)
    centre = centre_ref[...].astype(jnp.float32) * lax.rsqrt(centre_sq + TINY)
    grams = [product(x, x, ((0,), (0,))) for x in (vector, centre)]
    totals = [unit, unit]
    for step in range(POLAR):
        factors = [1.5 * unit - 0.5 * gram for gram in grams]
        totals = [
            factor if step == 0 else product(total, factor)
            for total, factor in zip(totals, factors)
        ]
        if step < POLAR - 1:
            grams = [
                product(product(factor, gram), factor) for gram, factor in zip(grams, factors)
            ]
    closing = product(totals[0], product(centre, totals[1]), ((1,), (1,)))
    out_ref[...] = product(vector, closing).reshape(states, block, block).astype(jnp.bfloat16)


def holding(kernel, count, held, *refs):
    operands, rest = list(refs[:count]), refs[count:]
    rest, buffers, arrived = rest[: -len(held) - 1], rest[-len(held) - 1 : -1], rest[-1]
    copies = {}
    for number, place in enumerate(held):
        copies[place] = pltpu.make_async_copy(
            operands[place], buffers[number], arrived.at[number]
        )
        copies[place].start()
        operands[place] = buffers[number]
    kernel(lambda place: copies[place].wait(), *operands, *rest)


def call(kernel, out_shape, scratch_shapes, flops, operands, held=()):
    if held:
        kernel = functools.partial(holding, kernel, len(operands), held)
        scratch_shapes = [
            *scratch_shapes,
            *(pltpu.VMEM(operands[place].shape, operands[place].dtype) for place in held),
            pltpu.SemaphoreType.DMA((len(held),)),
        ]
    return pl.pallas_call(
        kernel,
        out_shape=out_shape,
        in_specs=[
            pl.BlockSpec(memory_space=pl.ANY if place in held else pltpu.VMEM)
            for place in range(len(operands))
        ],
        scratch_shapes=scratch_shapes,
        compiler_params=pltpu.CompilerParams(vmem_limit_bytes=VMEM_LIMIT),
        cost_estimate=pl.CostEstimate(
            flops=flops,
            bytes_accessed=sum(int(np.prod(x.shape)) * x.dtype.itemsize for x in operands),
            transcendentals=0,
        ),
    )(*operands)


def float_out(*shape):
    return jax.ShapeDtypeStruct(shape, jnp.float32)


def half_out(*shape):
    return jax.ShapeDtypeStruct(shape, jnp.bfloat16)


def work(states, channels, block):
    return 4 * states * channels * block**3 + 2 * (states * channels * block) ** 2


def expanded(weight, groups, channels, states):
    spread = spread_matrix(groups, channels, states)
    sizes = tuple(even(len(group)) * ROWS for group in groups)
    return call(
        functools.partial(expand_kernel, sizes),
        half_out(spread.shape[0], -(-max(sizes) // 128) * 128),
        [],
        2 * spread.size * spread.shape[0],
        (weight, jnp.asarray(spread, jnp.bfloat16)),
    )


def left_front(env, tensors, weight, groups):
    channels, block = count_channels(env), env[0].shape[1]
    states, pieces = tensors.shape[1], len(env)
    outs = call(
        functools.partial(left_kernel, groups, states, pieces),
        [half_out(channels // pieces, block, block)] * (states * pieces),
        [pltpu.VMEM((states * channels * block // PARTS, block), jnp.float32)],
        work(states, channels, block),
        (*env, tensors, weight),
    )
    return [outs[s * pieces : (s + 1) * pieces] for s in range(states)]


def left_close(iso, gathered, moved):
    channels, block, _ = gathered.shape
    return call(
        left_close_kernel,
        (half_out(channels, block, block), float_out(ROWS, block)),
        [],
        2 * channels * block**3,
        (iso, gathered, moved),
    )


def right_whole(envs, own, tensors, weight, groups):
    channels, block = count_channels(envs[0]), envs[0][0].shape[1]
    states, pieces = len(envs), len(envs[0])
    outs = call(
        functools.partial(right_kernel, groups, states, pieces),
        [half_out(channels // pieces, block, block)] * pieces + [float_out(ROWS, block)],
        [
            pltpu.VMEM((states * channels * block // PARTS, block), jnp.float32),
            pltpu.VMEM((states * channels * block, block), jnp.bfloat16),
        ],
        work(states, channels, block),
        (*(chunk for env in envs for chunk in env), own, tensors, weight),
    )
    return outs[:pieces], outs[pieces]


def operator_front(env, weight, groups, entry_count, vector, rolled, news):
    channels, block = count_channels(env), env[0].shape[1]
    states, pieces = vector.shape[0], len(env)
    operands = (*env, weight, vector, *rolled, *news)
    held = tuple(range(len(operands) - 1 if news else len(operands)))
    return call(
        functools.partial(
            operator_front_kernel, groups, states, pieces, len(news) > 0, entry_count, held
        ),
        (half_out(states * channels * block, block), float_out(states, block, block)),
        [
            pltpu.VMEM((CLASSES, states, block, block), jnp.bfloat16),
            pltpu.VMEM((states * channels * block // PARTS, block), jnp.float32),
        ],
        work(states, channels, block),
        operands,
        held,
    )


def operator_back(rights, squares, gathered, vector):
    channels, block = count_channels(rights[0]), rights[0][0].shape[1]
    states, pieces = len(rights), len(rights[0])
    return call(
        functools.partial(operator_back_kernel, states, pieces),
        (
            float_out(states, block, block),
            half_out(states, block, block),
            float_out(1, LANES),
        ),
        [],
        2 * states * channels * block**3,
        (*(chunk for right in rights for chunk in right), *squares, gathered, vector),
        tuple(range(states * pieces)),
    )


def polar(both, table, centre, entry_count):
    states, _, block, _ = both.shape
    return call(
        functools.partial(polar_kernel, entry_count),
        (half_out(states, block, block), float_out(1, LANES)),
        [],
        600 * block**3,
        (both, table, centre),
    )


def charge_mask(channels, states, sectors):
    charge = np.array([CHARGE_STEPS[channel % CLASSES] for channel in range(channels)])
    state = np.arange(states)
    balance = (
        charge[:, None, None, None]
        + state[None, None, None, :]
        - state[None, None, :, None]
        - charge[None, :, None, None]
    )
    return jnp.asarray((balance % sectors == 0).astype(np.float32)).astype(jnp.bfloat16)


def weight_matrices(mpo, pattern, sectors):
    channels, _, states, _ = mpo.shape
    allowed = charge_mask(channels, states, sectors)
    weights = mpo * pattern[:, :, None, None].astype(jnp.bfloat16) * allowed
    size = states * channels
    left = jnp.transpose(weights, (2, 1, 3, 0)).reshape(size, size)
    right = jnp.transpose(weights, (2, 0, 3, 1)).reshape(size, size)
    return jnp.stack([left, right])


def other_classes_of(places, x):
    one, minus = places.ahead(x, 1), places.ahead(x, -1)
    return one, minus, places.ahead(one, 1), places.ahead(minus, -1)


def classes_of(places, x):
    return jnp.stack([x, *other_classes_of(places, x)])


def other_classes_at_once(places, x):
    return tuple(places.ahead(x, charge) for charge in CHARGE_STEPS[1:])


def after(first, then):
    return lax.optimization_barrier((first, then))


def local(left_iso, right_iso, centre, left_env, right_env, mpo, pattern):
    sites, secs = lax.axis_size("site"), lax.axis_size("sec")
    places = Places(sites, secs)
    left_iso, right_iso, centre = left_iso[0, :, 0], right_iso[0, :, 0], centre[0, 0]
    states, block, _ = left_iso.shape
    channels = mpo.shape[1]
    entry_count = left_env.size * secs
    left_groups = label_groups(channels, states, secs, 1)
    right_groups = label_groups(channels, states, secs, -1)

    pieces = PIECES if channels % PIECES == 0 else 1

    def split(env):
        return jnp.split(env, pieces)

    def ahead(env, by, chain_by=0):
        return [places.ahead(chunk, by, chain_by) for chunk in env]

    def fetch_env(env):
        return [places.fetch(chunk) for chunk in split(env)]

    right = fetch_env(right_env[0, :, 0])
    left = fetch_env(left_env[0, :, 0])
    both_isos = places.fetch(jnp.concatenate([left_iso, right_iso]))
    left_isos, right_isos = [both_isos[:states]], [both_isos[states:]]
    rolled = [classes_of(places, both_isos)]
    right[0], (own_iso, centre) = after(right[0], (left_iso, centre))
    right[-1], (left_iso, right_iso) = after(right[-1], (left_iso, right_iso))
    for step in range(1, ENV_STEPS):
        left_isos.append(places.fetch(left_iso, step))
        right_isos.append(places.fetch(right_iso, -step))
        isos = jnp.concatenate([left_isos[step], right_isos[step]])
        left[0], isos = after(left[0], isos)
        rolled.append(classes_of(places, isos))
    own_tensors = places.fetch(jnp.concatenate([own_iso, centre[None]]), ENV_STEPS)
    own_iso, own_centre = own_tensors[:states], own_tensors[states]
    centres = [own_centre] + [places.ahead(own_centre, s) for s in range(1, states)]

    gathered_weights = lax.all_gather(weight_matrices(mpo[0], pattern[0], secs), "site")
    chain = places.my_chain()

    def weight_of(site_by, kind):
        weight = lax.dynamic_index_in_dim(
            gathered_weights, (chain + site_by) % sites, 0, False
        )[kind]
        return expanded(weight, (left_groups, right_groups)[kind], channels, states)

    weights = (
        [weight_of(step, 0) for step in range(ENV_STEPS + 1)],
        [weight_of(-step, 1) for step in range(ENV_STEPS)],
    )
    vector = jnp.einsum(
        "sxy,syz->sxz", own_iso, jnp.stack(centres), preferred_element_type=jnp.float32
    )
    rolled_vector = other_classes_of(places, vector.astype(jnp.bfloat16))
    (right, left), (rolled, rolled_vector, weights) = after(
        (right, left), (rolled, rolled_vector, weights)
    )
    centre_float = own_centre.astype(jnp.float32)
    centre_square = jnp.sum((centre_float * centre_float).reshape(-1, ROWS, block), axis=0)

    left_squares, right_squares = [], []
    for step in range(ENV_STEPS):
        envs = [right]
        for t in range(1, states):
            envs.append(ahead(envs[-1], 1))
        right, square = right_whole(
            envs,
            right_isos[step],
            rolled[step][:, states:],
            weights[1][step],
            right_groups,
        )
        right_squares.append(square)

        gathered = left_front(left, rolled[step][:, :states], weights[0][step], left_groups)
        moved = [None] * pieces
        for s in reversed(range(1, states)):
            for piece in range(pieces):
                part = jnp.einsum(
                    "xy,vxz->vyz",
                    left_isos[step][s],
                    gathered[s][piece],
                    preferred_element_type=jnp.float32,
                )
                if moved[piece] is not None:
                    part = part + moved[piece].astype(jnp.float32)
                moved[piece] = places.ahead(part.astype(jnp.bfloat16), -1)
        closed = [
            left_close(left_isos[step][0], gathered[0][piece], moved[piece])
            for piece in range(pieces)
        ]
        left = [env for env, _ in closed]
        left_squares.append(sum(square for _, square in closed))

    if (2 * ENV_STEPS) % sites:
        right = ahead(right, 0, 2 * ENV_STEPS)
        right_squares = ahead(right_squares, 0, 2 * ENV_STEPS)
    squares = left_squares + right_squares + [centre_square]
    rights = [right]
    for s in range(1, states):
        rights.append(ahead(rights[-1], 1))
    news = ()
    for step in range(DESCENT):
        gathered, vector = operator_front(
            left, weights[0][ENV_STEPS], left_groups, entry_count, vector, rolled_vector, news
        )
        image, half_image, own_sums = operator_back(rights, squares, gathered, vector)
        table = places.collect(own_sums)
        if step < DESCENT - 1:
            news = (image, *other_classes_at_once(places, half_image), table)

    both = jnp.stack([vector, image], axis=1)
    columns = jnp.stack([both[0]] + [places.ahead(both[s], -s) for s in range(1, states)])
    column_left, energy = polar(columns, table, own_centre, entry_count)
    new_left = jnp.stack(
        [places.send_home(column_left[s], ENV_STEPS, -s) for s in range(states)]
    )
    energy = places.send_home(energy, ENV_STEPS, 0)
    return new_left[None, :, None], energy[0, :1]


def solution(mesh):
    placed = (
        P("site", None, "sec", None, None),
        P("site", None, "sec", None, None),
        P("site", "sec", None, None),
        P("site", None, "sec", None, None),
        P("site", None, "sec", None, None),
        P("site", None, None, None, None),
        P("site", None, None),
    )
    return jax.shard_map(
        local,
        mesh=mesh,
        in_specs=placed,
        out_specs=(P("site", None, "sec", None, None), P("site")),
        check_vma=False,
    )
```

```python
import functools

import jax
import jax.numpy as jnp
import numpy as np
from jax import lax
from jax.experimental import pallas as pl
from jax.experimental.pallas import tpu as pltpu
from jax.sharding import PartitionSpec as P

ENV_STEPS = 2
POLAR = 6

TINY = 1e-06
HIGHEST = lax.Precision.HIGHEST
CHARGE_STEPS = (0, 1, -1, 2, -2)
CLASSES = len(CHARGE_STEPS)
BOTH = ("site", "sec")
VMEM_LIMIT = 24 * 1024 * 1024
PIECES = 2


class Places:
    def __init__(self, sites, secs):
        self.sites, self.secs = sites, secs
        self.half = secs // 2
        self.up = (self.half + 1) // 2

    def home(self, site, sector):
        return (site % self.sites) * self.secs + sector % self.secs

    def position(self, place):
        back = self.half - 1 + self.up - place
        if isinstance(place, int):
            return place if place < self.up else back
        return jnp.where(place < self.up, place, back)

    def slot(self, chain, sector):
        chain, sector = chain % self.sites, sector % self.secs
        place = chain % 2 * self.half + self.position(sector // 2)
        return (chain // 2 * 2 + sector % 2) * self.secs + place

    def pairs(self, source, target):
        return [
            (source(chain, sector), target(chain, sector))
            for chain in range(self.sites)
            for sector in range(self.secs)
        ]

    def fetch(self, x, site_by=0, sec_by=0):
        return lax.ppermute(
            x, BOTH, self.pairs(lambda g, k: self.home(g + site_by, k + sec_by), self.slot)
        )

    def send_home(self, x, site_by, sec_by):
        return lax.ppermute(
            x, BOTH, self.pairs(self.slot, lambda g, k: self.home(g + site_by, k + sec_by))
        )

    def ahead(self, x, by, chain_by=0):
        return lax.ppermute(
            x, BOTH, self.pairs(lambda g, k: self.slot(g + chain_by, k + by), self.slot)
        )

    def partner(self, x, bit):
        return lax.ppermute(x, BOTH, self.pairs(lambda g, k: self.slot(g, k ^ bit), self.slot))

    def my_chain(self):
        return lax.axis_index("site") // 2 * 2 + lax.axis_index("sec") // self.half

    def my_sector(self):
        position = self.position(lax.axis_index("sec") % self.half)
        return 2 * position + lax.axis_index("site") % 2

    def collect(self, values):
        sector = self.my_sector()
        table = values
        bit = 1
        while bit < self.secs:
            other = self.partner(table, bit)
            first = (sector & bit) == 0
            table = jnp.where(
                first, jnp.concatenate([table, other]), jnp.concatenate([other, table])
            )
            bit *= 2
        return table


ROWS = 8
PARTS = 2


def label_groups(channels, states, sectors, sign):
    groups = {}
    for state in range(states):
        for channel in range(channels):
            label = (state + sign * CHARGE_STEPS[channel % CLASSES]) % sectors
            groups.setdefault(label, []).append((state, channel))
    return [groups[label] for label in sorted(groups)]


def even(count):
    return count + count % 2


def spread_matrix(groups, channels, states):
    rows = []
    for group in groups:
        block = np.zeros((even(len(group)), ROWS, states * channels), np.float32)
        for index, (state, channel) in enumerate(group):
            block[index, :, state * channels + channel] = 1
        rows.append(block.reshape(-1, states * channels))
    return np.concatenate(rows)


def expand_kernel(sizes, weight_ref, spread_ref, out_ref):
    start = 0
    for size in sizes:
        spread = spread_ref[pl.ds(start, size), :]
        picked = jnp.dot(spread, weight_ref[...], preferred_element_type=jnp.float32)
        full = lax.dot_general(
            picked.astype(jnp.bfloat16),
            spread,
            (((1,), (1,)), ((), ())),
            preferred_element_type=jnp.float32,
        )
        row = lax.broadcasted_iota(jnp.int32, full.shape, 0)
        column = lax.broadcasted_iota(jnp.int32, full.shape, 1)
        same = lax.rem(row, ROWS) == lax.rem(column, ROWS)
        out_ref[pl.ds(start, size), pl.ds(0, size)] = jnp.where(same, full, 0.0).astype(
            jnp.bfloat16
        )
        start += size


def mix_channels(groups, channels, weight_ref, mixed_ref, write, offset, height):
    def step(index, carry):
        first = pl.multiple_of(index * 2 * ROWS, 2 * ROWS)
        start = 0
        for group in groups:
            size = even(len(group)) * ROWS
            parts = []
            for state, channel in group:
                rows = (state * channels + channel) * height + first
                halves = [
                    mixed_ref[pl.ds(pl.multiple_of(rows + half * ROWS, ROWS), ROWS), :]
                    for half in range(2)
                ]
                parts.append(jnp.concatenate(halves, axis=1))
            if len(group) % 2:
                parts.append(parts[0])
            operand = jnp.concatenate(parts, axis=0).astype(jnp.bfloat16)
            product = jnp.dot(
                weight_ref[pl.ds(start, size), pl.ds(0, size)],
                operand,
                preferred_element_type=jnp.float32,
            )
            block = product.shape[1] // 2
            for number, pair in enumerate(group):
                rows = product[number * ROWS : (number + 1) * ROWS]
                both = jnp.concatenate([rows[:, :block], rows[:, block:]], axis=0)
                write(*pair, pl.multiple_of(offset + first, 2 * ROWS), both.astype(jnp.bfloat16))
            start += size
        return carry

    lax.fori_loop(0, height // (2 * ROWS), step, 0)


def by_parts(block, body):
    height = block // PARTS

    def one(part, carry):
        body(pl.multiple_of(part * height, height), height)
        return carry

    lax.fori_loop(0, PARTS, one, 0)


def into(gathered_ref, channels, block):
    def write(state, channel, first, rows):
        start = (state * channels + channel) * block
        gathered_ref[pl.ds(pl.multiple_of(start + first, 2 * ROWS), 2 * ROWS), :] = rows

    return write


def batches(items, most):
    pieces = -(-len(items) // most)
    size = -(-len(items) // pieces)
    return [items[start : start + size] for start in range(0, len(items), size)]


def rows_of(chunks, channel, offset, height):
    size = chunks[0].shape[0]
    return chunks[channel // size][channel % size, pl.ds(offset, height), :]


def channel_of(chunks, channel):
    size = chunks[0].shape[0]
    return chunks[channel // size][channel % size]


def put_channel(chunks, channel, value):
    size = chunks[0].shape[0]
    chunks[channel // size][channel % size] = value


def count_channels(chunks):
    return sum(chunk.shape[0] for chunk in chunks)


def mix_left(env, tensors, mixed_ref, offset, height):
    channels, block = count_channels(env), env[0].shape[1]
    for cls in range(CLASSES):
        right = jnp.concatenate(tensors[cls], axis=1)
        for batch in batches(list(range(cls, channels, CLASSES)), 5):
            rows = jnp.concatenate(
                [rows_of(env, channel, offset, height) for channel in batch], axis=0
            )
            product = jnp.dot(rows, right, preferred_element_type=jnp.float32)
            for number, channel in enumerate(batch):
                for t in range(len(tensors[cls])):
                    mixed_ref[pl.ds((t * channels + channel) * height, height), :] = product[
                        number * height : (number + 1) * height, t * block : (t + 1) * block
                    ]


def left_kernel(groups, states, pieces, *refs):
    env, (tensor_ref, weight_ref) = refs[:pieces], refs[pieces : pieces + 2]
    outs, mixed_ref = refs[pieces + 2 : -1], refs[-1]
    channels, block = count_channels(env), env[0].shape[1]

    def write(state, channel, first, rows):
        size = channels // pieces
        out_ref = outs[state * pieces + channel // size]
        out_ref[channel % size, pl.ds(first, 2 * ROWS), :] = rows

    def body(offset, height):
        tensors = [[tensor_ref[cls, t] for t in range(states)] for cls in range(CLASSES)]
        mix_left(env, tensors, mixed_ref, offset, height)
        mix_channels(groups, channels, weight_ref, mixed_ref, write, offset, height)

    by_parts(block, body)


def left_close_kernel(iso_ref, gathered_ref, moved_ref, out_ref, square_ref):
    channels, block, _ = gathered_ref.shape
    square = jnp.zeros((ROWS, block), jnp.float32)
    for batch in batches(list(range(channels)), 2):
        right = jnp.concatenate([gathered_ref[channel] for channel in batch], axis=1)
        product = lax.dot_general(
            iso_ref[...], right, (((0,), (0,)), ((), ())), preferred_element_type=jnp.float32
        )
        for number, channel in enumerate(batch):
            part = product[:, number * block : (number + 1) * block]
            part = part + moved_ref[channel].astype(jnp.float32)
            out_ref[channel] = part.astype(jnp.bfloat16)
            square = square + jnp.sum((part * part).reshape(-1, ROWS, block), axis=0)
    square_ref[...] = square


def right_kernel(groups, states, pieces, *refs):
    envs = [refs[t * pieces : (t + 1) * pieces] for t in range(states)]
    refs = refs[states * pieces :]
    own_ref, tensor_ref, weight_ref = refs[:3]
    outs, (square_ref, mixed_ref, gathered_ref) = refs[3 : 3 + pieces], refs[3 + pieces :]
    channels, block = count_channels(envs[0]), envs[0][0].shape[1]
    zero = jnp.zeros((block, block), jnp.bfloat16)
    write = into(gathered_ref, channels, block)

    def body(offset, height):
        for pair in batches(list(range(states)), 2):
            own = jnp.concatenate(
                [
                    jnp.concatenate([own_ref[t] if t == other else zero for other in pair], axis=1)
                    for t in pair
                ],
                axis=0,
            )
            for batch in batches(list(range(channels)), 6):
                rows = jnp.concatenate(
                    [
                        jnp.concatenate(
                            [rows_of(envs[t], channel, offset, height) for channel in batch], axis=0
                        )
                        for t in pair
                    ],
                    axis=1,
                )
                product = lax.dot_general(
                    rows, own, (((1,), (1,)), ((), ())), preferred_element_type=jnp.float32
                )
                for number, t in enumerate(pair):
                    start = (t * channels + batch[0]) * height
                    mixed_ref[pl.ds(start, len(batch) * height), :] = product[
                        :, number * block : (number + 1) * block
                    ]
        mix_channels(groups, channels, weight_ref, mixed_ref, write, offset, height)

    by_parts(block, body)
    square = jnp.zeros((ROWS, block), jnp.float32)
    for cls in range(CLASSES):
        left = jnp.concatenate([tensor_ref[cls, s] for s in range(states)], axis=1)
        for batch in batches(list(range(cls, channels, CLASSES)), 2):
            right = jnp.concatenate(
                [
                    jnp.concatenate(
                        [
                            gathered_ref[pl.ds((s * channels + channel) * block, block), :]
                            for s in range(states)
                        ],
                        axis=0,
                    )
                    for channel in batch
                ],
                axis=1,
            )
            product = jnp.dot(left, right, preferred_element_type=jnp.float32)
            for number, channel in enumerate(batch):
                part = product[:, number * block : (number + 1) * block]
                put_channel(outs, channel, part.astype(jnp.bfloat16))
                square = square + jnp.sum((part * part).reshape(-1, ROWS, block), axis=0)
    square_ref[...] = square


ENV_LANE = 5
LANES = 128


def quotient(table, entry_count):
    def total(x):
        return jnp.sum(x, axis=0, keepdims=True)

    squares = [
        total(table[:, lane : lane + 1]) for lane in range(ENV_LANE, ENV_LANE + 2 * ENV_STEPS + 1)
    ]
    scale = jnp.ones((1, 1), jnp.float32)
    for side in range(2):
        side_scale = jnp.ones((1, 1), jnp.float32)
        for square in squares[side * ENV_STEPS : (side + 1) * ENV_STEPS]:
            side_scale = side_scale * lax.rsqrt(side_scale * side_scale * square / entry_count + TINY)
        scale = scale * side_scale
    a, b, e, c, unit = (table[:, lane : lane + 1] for lane in range(ENV_LANE))
    a, e, unit = scale * a, scale * e, scale * unit
    c = unit * unit * c
    whole_a, whole_b = total(a), total(b)
    energy = whole_a / (whole_b + TINY)
    off = e - energy
    residual_sq = total(c + 2.0 * off * (a - e * b) + off * off * b)
    factor = 0.5 * jnp.sqrt(whole_b / (residual_sq + TINY))
    square = whole_b - 2.0 * factor * (whole_a - energy * whole_b) + factor * factor * residual_sq
    return scale, energy, factor, square, squares[2 * ENV_STEPS]


def updated(vector, image, scale, energy, factor):
    return vector - factor * (scale * image - energy * vector)


def sum_all(x):
    return jnp.sum(jnp.sum(x, axis=0, keepdims=True), axis=1, keepdims=True)


def operator_front_kernel(groups, states, pieces, renew, entry_count, *refs):
    env, refs = refs[:pieces], refs[pieces:]
    others = CLASSES - 1
    weight_ref, vector_ref, rolled = refs[0], refs[1], refs[2 : 2 + others]
    rest = refs[2 + others :]
    if renew:
        image_ref, moved, table_ref = rest[0], rest[1 : 1 + others], rest[1 + others]
        rest = rest[2 + others :]
        scale, energy, factor, _, _ = quotient(table_ref[...], entry_count)
    gathered_ref, new_ref, tensor_ref, mixed_ref = rest
    channels, block = count_channels(env), env[0].shape[1]
    for t in range(states):
        vector = vector_ref[t]
        if renew:
            vector = updated(vector, image_ref[t], scale, energy, factor)
        new_ref[t] = vector
        tensor_ref[0, t] = vector.astype(jnp.bfloat16)
        for cls in range(1, CLASSES):
            vector = rolled[cls - 1][t]
            if renew:
                image = moved[cls - 1][t].astype(jnp.float32)
                vector = updated(vector.astype(jnp.float32), image, scale, energy, factor)
            tensor_ref[cls, t] = vector.astype(jnp.bfloat16)
    write = into(gathered_ref, channels, block)

    def body(offset, height):
        tensors = [[tensor_ref[cls, t] for t in range(states)] for cls in range(CLASSES)]
        mix_left(env, tensors, mixed_ref, offset, height)
        mix_channels(groups, channels, weight_ref, mixed_ref, write, offset, height)

    by_parts(block, body)


def operator_back_kernel(states, pieces, *refs):
    rights = [refs[t * pieces : (t + 1) * pieces] for t in range(states)]
    refs = refs[states * pieces :]
    squares, refs = refs[: 2 * ENV_STEPS + 1], refs[2 * ENV_STEPS + 1 :]
    gathered_ref, vector_ref, image_ref, half_ref, sums_ref = refs
    channels, block = count_channels(rights[0]), rights[0][0].shape[1]
    a = jnp.zeros((1, 1), jnp.float32)
    b = jnp.zeros((1, 1), jnp.float32)
    for s in range(states):
        total = jnp.zeros((block, block), jnp.float32)
        for batch in batches(list(range(channels)), 6):
            left = jnp.concatenate(
                [
                    gathered_ref[pl.ds((s * channels + channel) * block, block), :]
                    for channel in batch
                ],
                axis=1,
            )
            right = jnp.concatenate([channel_of(rights[s], channel) for channel in batch], axis=0)
            total = total + jnp.dot(left, right, preferred_element_type=jnp.float32)
        image_ref[s] = total
        half_ref[s] = total.astype(jnp.bfloat16)
        vector = vector_ref[s]
        a = a + sum_all(vector * total)
        b = b + sum_all(vector * vector)
    e = jnp.where(b > 0, a / jnp.where(b > 0, b, 1.0), 0.0)
    residual = image_ref[...].reshape(states * block, block) - e * vector_ref[...].reshape(
        states * block, block
    )
    unit = jnp.max(jnp.max(jnp.abs(residual), axis=0, keepdims=True), axis=1, keepdims=True)
    unit = jnp.where(unit > 0, unit, 1.0)
    residual = residual / unit
    lane = lax.broadcasted_iota(jnp.int32, sums_ref.shape, 1)
    sums = jnp.zeros(sums_ref.shape, jnp.float32)
    values = (a, b, e, sum_all(residual * residual), unit, *(sum_all(x[...]) for x in squares))
    for place, value in enumerate(values):
        sums = jnp.where(lane == place, value, sums)
    sums_ref[...] = sums


def operator_whole_kernel(groups, states, pieces, entry_count, counts, *refs):
    front, refs = refs[: counts[0]], refs[counts[0] :]
    back, refs = refs[: counts[1]], refs[counts[1] :]
    image_ref, half_ref, sums_ref, new_ref, gathered_ref, tensor_ref, mixed_ref = refs
    operator_front_kernel(
        groups, states, pieces, True, entry_count, *front, gathered_ref, new_ref, tensor_ref, mixed_ref
    )
    operator_back_kernel(
        states, pieces, *back, gathered_ref, new_ref, image_ref, half_ref, sums_ref
    )


def polar_kernel(entry_count, both_ref, table_ref, centre_ref, out_ref, energy_ref):
    states, _, block, _ = both_ref.shape
    rows = lax.broadcasted_iota(jnp.int32, (block, block), 0)
    columns = lax.broadcasted_iota(jnp.int32, (block, block), 1)
    unit = (rows == columns).astype(jnp.float32)

    def product(x, y, contract=((1,), (0,))):
        return lax.dot_general(
            x, y, (contract, ((), ())), precision=HIGHEST, preferred_element_type=jnp.float32
        )

    scale, energy, factor, square, centre_sq = quotient(table_ref[...], entry_count)
    energy_ref[...] = jnp.broadcast_to(energy, energy_ref.shape)
    vector = updated(
        both_ref[:, 0].reshape(states * block, block),
        both_ref[:, 1].reshape(states * block, block),
        scale,
        energy,
        factor,
    ) * lax.rsqrt(square + TINY)
    centre = centre_ref[...].astype(jnp.float32) * lax.rsqrt(centre_sq + TINY)
    grams = [product(x, x, ((0,), (0,))) for x in (vector, centre)]
    totals = [unit, unit]
    for step in range(POLAR):
        factors = [1.5 * unit - 0.5 * gram for gram in grams]
        totals = [
            factor if step == 0 else product(total, factor)
            for total, factor in zip(totals, factors)
        ]
        if step < POLAR - 1:
            grams = [
                product(product(factor, gram), factor) for gram, factor in zip(grams, factors)
            ]
    closing = product(totals[0], product(centre, totals[1]), ((1,), (1,)))
    out_ref[...] = product(vector, closing).reshape(states, block, block).astype(jnp.bfloat16)


def call(kernel, out_shape, scratch_shapes, flops, operands):
    return pl.pallas_call(
        kernel,
        out_shape=out_shape,
        scratch_shapes=scratch_shapes,
        compiler_params=pltpu.CompilerParams(vmem_limit_bytes=VMEM_LIMIT),
        cost_estimate=pl.CostEstimate(
            flops=flops,
            bytes_accessed=sum(int(np.prod(x.shape)) * x.dtype.itemsize for x in operands),
            transcendentals=0,
        ),
    )(*operands)


def float_out(*shape):
    return jax.ShapeDtypeStruct(shape, jnp.float32)


def half_out(*shape):
    return jax.ShapeDtypeStruct(shape, jnp.bfloat16)


def work(states, channels, block):
    return 4 * states * channels * block**3 + 2 * (states * channels * block) ** 2


def expanded(weight, groups, channels, states):
    spread = spread_matrix(groups, channels, states)
    sizes = tuple(even(len(group)) * ROWS for group in groups)
    return call(
        functools.partial(expand_kernel, sizes),
        half_out(spread.shape[0], -(-max(sizes) // 128) * 128),
        [],
        2 * spread.size * spread.shape[0],
        (weight, jnp.asarray(spread, jnp.bfloat16)),
    )


def left_front(env, tensors, weight, groups):
    channels, block = count_channels(env), env[0].shape[1]
    states, pieces = tensors.shape[1], len(env)
    outs = call(
        functools.partial(left_kernel, groups, states, pieces),
        [half_out(channels // pieces, block, block)] * (states * pieces),
        [pltpu.VMEM((states * channels * block // PARTS, block), jnp.float32)],
        work(states, channels, block),
        (*env, tensors, weight),
    )
    return [outs[s * pieces : (s + 1) * pieces] for s in range(states)]


def left_close(iso, gathered, moved):
    channels, block, _ = gathered.shape
    return call(
        left_close_kernel,
        (half_out(channels, block, block), float_out(ROWS, block)),
        [],
        2 * channels * block**3,
        (iso, gathered, moved),
    )


def right_whole(envs, own, tensors, weight, groups):
    channels, block = count_channels(envs[0]), envs[0][0].shape[1]
    states, pieces = len(envs), len(envs[0])
    outs = call(
        functools.partial(right_kernel, groups, states, pieces),
        [half_out(channels // pieces, block, block)] * pieces + [float_out(ROWS, block)],
        [
            pltpu.VMEM((states * channels * block // PARTS, block), jnp.float32),
            pltpu.VMEM((states * channels * block, block), jnp.bfloat16),
        ],
        work(states, channels, block),
        (*(chunk for env in envs for chunk in env), own, tensors, weight),
    )
    return outs[:pieces], outs[pieces]


def front_scratch(states, channels, block):
    return [
        pltpu.VMEM((CLASSES, states, block, block), jnp.bfloat16),
        pltpu.VMEM((states * channels * block // PARTS, block), jnp.float32),
    ]


def back_outs(states, block):
    return (
        float_out(states, block, block),
        half_out(states, block, block),
        float_out(1, LANES),
    )


def operator_front(env, weight, groups, entry_count, vector, rolled):
    channels, block = count_channels(env), env[0].shape[1]
    states, pieces = vector.shape[0], len(env)
    return call(
        functools.partial(operator_front_kernel, groups, states, pieces, False, entry_count),
        (half_out(states * channels * block, block), float_out(states, block, block)),
        front_scratch(states, channels, block),
        work(states, channels, block),
        (*env, weight, vector, *rolled),
    )


def operator_back(rights, squares, gathered, vector):
    channels, block = count_channels(rights[0]), rights[0][0].shape[1]
    states, pieces = len(rights), len(rights[0])
    return call(
        functools.partial(operator_back_kernel, states, pieces),
        back_outs(states, block),
        [],
        2 * states * channels * block**3,
        (*(chunk for right in rights for chunk in right), *squares, gathered, vector),
    )


def operator_whole(env, weight, groups, entry_count, vector, rolled, news, rights, squares):
    channels, block = count_channels(env), env[0].shape[1]
    states, pieces = vector.shape[0], len(env)
    front = (*env, weight, vector, *rolled, *news)
    back = (*(chunk for right in rights for chunk in right), *squares)
    counts = (len(front), len(back))
    return call(
        functools.partial(operator_whole_kernel, groups, states, pieces, entry_count, counts),
        (*back_outs(states, block), float_out(states, block, block)),
        [
            pltpu.VMEM((states * channels * block, block), jnp.bfloat16),
            *front_scratch(states, channels, block),
        ],
        work(states, channels, block) + 2 * states * channels * block**3,
        (*front, *back),
    )


def polar(both, table, centre, entry_count):
    states, _, block, _ = both.shape
    return call(
        functools.partial(polar_kernel, entry_count),
        (half_out(states, block, block), float_out(1, LANES)),
        [],
        600 * block**3,
        (both, table, centre),
    )


def charge_mask(channels, states, sectors):
    charge = np.array([CHARGE_STEPS[channel % CLASSES] for channel in range(channels)])
    state = np.arange(states)
    balance = (
        charge[:, None, None, None]
        + state[None, None, None, :]
        - state[None, None, :, None]
        - charge[None, :, None, None]
    )
    return jnp.asarray((balance % sectors == 0).astype(np.float32)).astype(jnp.bfloat16)


def weight_matrices(mpo, pattern, sectors):
    channels, _, states, _ = mpo.shape
    allowed = charge_mask(channels, states, sectors)
    weights = mpo * pattern[:, :, None, None].astype(jnp.bfloat16) * allowed
    size = states * channels
    left = jnp.transpose(weights, (2, 1, 3, 0)).reshape(size, size)
    right = jnp.transpose(weights, (2, 0, 3, 1)).reshape(size, size)
    return jnp.stack([left, right])


def other_classes_of(places, x):
    one, minus = places.ahead(x, 1), places.ahead(x, -1)
    return one, minus, places.ahead(one, 1), places.ahead(minus, -1)


def classes_of(places, x):
    return jnp.stack([x, *other_classes_of(places, x)])


def other_classes_at_once(places, x):
    return tuple(places.ahead(x, charge) for charge in CHARGE_STEPS[1:])


def after(first, then):
    return lax.optimization_barrier((first, then))


def local(left_iso, right_iso, centre, left_env, right_env, mpo, pattern):
    sites, secs = lax.axis_size("site"), lax.axis_size("sec")
    places = Places(sites, secs)
    left_iso, right_iso, centre = left_iso[0, :, 0], right_iso[0, :, 0], centre[0, 0]
    states, block, _ = left_iso.shape
    channels = mpo.shape[1]
    entry_count = left_env.size * secs
    left_groups = label_groups(channels, states, secs, 1)
    right_groups = label_groups(channels, states, secs, -1)

    pieces = PIECES if channels % PIECES == 0 else 1

    def ahead(env, by, chain_by=0):
        return [places.ahead(chunk, by, chain_by) for chunk in env]

    both_isos = places.fetch(jnp.concatenate([left_iso, right_iso]))
    left_isos, right_isos = [both_isos[:states]], [both_isos[states:]]
    for step in range(1, ENV_STEPS):
        left_isos.append(places.fetch(left_iso, step))
        right_isos.append(places.fetch(right_iso, -step))
    own_tensors = places.fetch(jnp.concatenate([left_iso, centre[None]]), ENV_STEPS)
    (left_isos, right_isos, own_tensors), envs = after(
        (left_isos, right_isos, own_tensors),
        jnp.concatenate([right_env[0, :, 0], left_env[0, :, 0]]),
    )
    envs = jnp.split(places.fetch(envs), 2 * pieces)
    right, left = envs[:pieces], envs[pieces:]
    rolled = [
        classes_of(places, jnp.concatenate([left_isos[step], right_isos[step]]))
        for step in range(ENV_STEPS)
    ]
    own_iso, own_centre = own_tensors[:states], own_tensors[states]
    centres = [own_centre] + [places.ahead(own_centre, s) for s in range(1, states)]

    gathered_weights = lax.all_gather(weight_matrices(mpo[0], pattern[0], secs), "site")
    chain = places.my_chain()

    def weight_of(site_by, kind):
        weight = lax.dynamic_index_in_dim(
            gathered_weights, (chain + site_by) % sites, 0, False
        )[kind]
        return expanded(weight, (left_groups, right_groups)[kind], channels, states)

    weights = (
        [weight_of(step, 0) for step in range(ENV_STEPS + 1)],
        [weight_of(-step, 1) for step in range(ENV_STEPS)],
    )
    vector = jnp.einsum(
        "sxy,syz->sxz", own_iso, jnp.stack(centres), preferred_element_type=jnp.float32
    )
    rolled_vector = other_classes_of(places, vector.astype(jnp.bfloat16))
    (right, left), (rolled, rolled_vector, weights) = after(
        (right, left), (rolled, rolled_vector, weights)
    )
    centre_float = own_centre.astype(jnp.float32)
    centre_square = jnp.sum((centre_float * centre_float).reshape(-1, ROWS, block), axis=0)

    left_squares, right_squares = [], []
    for step in range(ENV_STEPS):
        envs = [right]
        for t in range(1, states):
            envs.append(ahead(envs[-1], 1))
        right, square = right_whole(
            envs,
            right_isos[step],
            rolled[step][:, states:],
            weights[1][step],
            right_groups,
        )
        right_squares.append(square)

        gathered = left_front(left, rolled[step][:, :states], weights[0][step], left_groups)
        moved = [None] * pieces
        for s in reversed(range(1, states)):
            for piece in range(pieces):
                part = jnp.einsum(
                    "xy,vxz->vyz",
                    left_isos[step][s],
                    gathered[s][piece],
                    preferred_element_type=jnp.float32,
                )
                if moved[piece] is not None:
                    part = part + moved[piece].astype(jnp.float32)
                moved[piece] = places.ahead(part.astype(jnp.bfloat16), -1)
        closed = [
            left_close(left_isos[step][0], gathered[0][piece], moved[piece])
            for piece in range(pieces)
        ]
        left = [env for env, _ in closed]
        left_squares.append(sum(square for _, square in closed))

    if (2 * ENV_STEPS) % sites:
        right = ahead(right, 0, 2 * ENV_STEPS)
        right_squares = ahead(right_squares, 0, 2 * ENV_STEPS)
    squares = left_squares + right_squares + [centre_square]
    rights = [right]
    for s in range(1, states):
        rights.append(ahead(rights[-1], 1))
    weight = weights[0][ENV_STEPS]
    gathered, vector = operator_front(
        left, weight, left_groups, entry_count, vector, rolled_vector
    )
    image, half_image, own_sums = operator_back(rights, squares, gathered, vector)
    table = places.collect(own_sums)
    news = (image, *other_classes_at_once(places, half_image), table)
    image, _, own_sums, vector = operator_whole(
        left, weight, left_groups, entry_count, vector, rolled_vector, news, rights, squares
    )
    table = places.collect(own_sums)

    both = jnp.stack([vector, image], axis=1)
    columns = jnp.stack([both[0]] + [places.ahead(both[s], -s) for s in range(1, states)])
    column_left, energy = polar(columns, table, own_centre, entry_count)
    new_left = jnp.stack(
        [places.send_home(column_left[s], ENV_STEPS, -s) for s in range(states)]
    )
    energy = places.send_home(energy, ENV_STEPS, 0)
    return new_left[None, :, None], energy[0, :1]


def solution(mesh):
    placed = (
        P("site", None, "sec", None, None),
        P("site", None, "sec", None, None),
        P("site", "sec", None, None),
        P("site", None, "sec", None, None),
        P("site", None, "sec", None, None),
        P("site", None, None, None, None),
        P("site", None, None),
    )
    return jax.shard_map(
        local,
        mesh=mesh,
        in_specs=placed,
        out_specs=(P("site", None, "sec", None, None), P("site")),
        check_vma=False,
    )
```

```python
import functools

import jax
import jax.numpy as jnp
import numpy as np
from jax import lax
from jax.experimental import pallas as pl
from jax.experimental.pallas import tpu as pltpu
from jax.sharding import PartitionSpec as P

ENV_STEPS = 2
POLAR = 6

TINY = 1e-06
HIGHEST = lax.Precision.HIGHEST
CHARGE_STEPS = (0, 1, -1, 2, -2)
CLASSES = len(CHARGE_STEPS)
BOTH = ("site", "sec")
VMEM_LIMIT = 20 * 1024 * 1024
PIECES = 2


class Places:
    def __init__(self, sites, secs):
        self.sites, self.secs = sites, secs
        self.half = secs // 2
        self.up = (self.half + 1) // 2

    def home(self, site, sector):
        return (site % self.sites) * self.secs + sector % self.secs

    def position(self, place):
        back = self.half - 1 + self.up - place
        if isinstance(place, int):
            return place if place < self.up else back
        return jnp.where(place < self.up, place, back)

    def slot(self, chain, sector):
        chain, sector = chain % self.sites, sector % self.secs
        place = chain % 2 * self.half + self.position(sector // 2)
        return (chain // 2 * 2 + sector % 2) * self.secs + place

    def pairs(self, source, target):
        return [
            (source(chain, sector), target(chain, sector))
            for chain in range(self.sites)
            for sector in range(self.secs)
        ]

    def fetch(self, x, site_by=0, sec_by=0):
        return lax.ppermute(
            x, BOTH, self.pairs(lambda g, k: self.home(g + site_by, k + sec_by), self.slot)
        )

    def send_home(self, x, site_by, sec_by):
        return lax.ppermute(
            x, BOTH, self.pairs(self.slot, lambda g, k: self.home(g + site_by, k + sec_by))
        )

    def ahead(self, x, by, chain_by=0):
        return lax.ppermute(
            x, BOTH, self.pairs(lambda g, k: self.slot(g + chain_by, k + by), self.slot)
        )

    def partner(self, x, bit):
        return lax.ppermute(x, BOTH, self.pairs(lambda g, k: self.slot(g, k ^ bit), self.slot))

    def my_chain(self):
        return lax.axis_index("site") // 2 * 2 + lax.axis_index("sec") // self.half

    def my_sector(self):
        position = self.position(lax.axis_index("sec") % self.half)
        return 2 * position + lax.axis_index("site") % 2

    def collect(self, values):
        sector = self.my_sector()
        table = values
        bit = 1
        while bit < self.secs:
            other = self.partner(table, bit)
            first = (sector & bit) == 0
            table = jnp.where(
                first, jnp.concatenate([table, other]), jnp.concatenate([other, table])
            )
            bit *= 2
        return table


ROWS = 8
PARTS = 2


def label_groups(channels, states, sectors, sign):
    groups = {}
    for state in range(states):
        for channel in range(channels):
            label = (state + sign * CHARGE_STEPS[channel % CLASSES]) % sectors
            groups.setdefault(label, []).append((state, channel))
    return [groups[label] for label in sorted(groups)]


def even(count):
    return count + count % 2


def spread_matrix(groups, channels, states):
    rows = []
    for group in groups:
        block = np.zeros((even(len(group)), ROWS, states * channels), np.float32)
        for index, (state, channel) in enumerate(group):
            block[index, :, state * channels + channel] = 1
        rows.append(block.reshape(-1, states * channels))
    return np.concatenate(rows)


def expand_kernel(sizes, weight_ref, spread_ref, out_ref):
    start = 0
    for size in sizes:
        spread = spread_ref[pl.ds(start, size), :]
        picked = jnp.dot(spread, weight_ref[...], preferred_element_type=jnp.float32)
        full = lax.dot_general(
            picked.astype(jnp.bfloat16),
            spread,
            (((1,), (1,)), ((), ())),
            preferred_element_type=jnp.float32,
        )
        row = lax.broadcasted_iota(jnp.int32, full.shape, 0)
        column = lax.broadcasted_iota(jnp.int32, full.shape, 1)
        same = lax.rem(row, ROWS) == lax.rem(column, ROWS)
        out_ref[pl.ds(start, size), pl.ds(0, size)] = jnp.where(same, full, 0.0).astype(
            jnp.bfloat16
        )
        start += size


def mix_channels(groups, channels, weight_ref, mixed_ref, write, offset, height):
    def step(index, carry):
        first = pl.multiple_of(index * 2 * ROWS, 2 * ROWS)
        start = 0
        for group in groups:
            size = even(len(group)) * ROWS
            parts = []
            for state, channel in group:
                rows = (state * channels + channel) * height + first
                halves = [
                    mixed_ref[pl.ds(pl.multiple_of(rows + half * ROWS, ROWS), ROWS), :]
                    for half in range(2)
                ]
                parts.append(jnp.concatenate(halves, axis=1))
            if len(group) % 2:
                parts.append(parts[0])
            operand = jnp.concatenate(parts, axis=0).astype(jnp.bfloat16)
            product = jnp.dot(
                weight_ref[pl.ds(start, size), pl.ds(0, size)],
                operand,
                preferred_element_type=jnp.float32,
            )
            block = product.shape[1] // 2
            for number, pair in enumerate(group):
                rows = product[number * ROWS : (number + 1) * ROWS]
                both = jnp.concatenate([rows[:, :block], rows[:, block:]], axis=0)
                write(*pair, pl.multiple_of(offset + first, 2 * ROWS), both.astype(jnp.bfloat16))
            start += size
        return carry

    lax.fori_loop(0, height // (2 * ROWS), step, 0)


def by_parts(block, body):
    height = block // PARTS

    def one(part, carry):
        body(pl.multiple_of(part * height, height), height)
        return carry

    lax.fori_loop(0, PARTS, one, 0)


def into(gathered_ref, channels, block):
    def write(state, channel, first, rows):
        start = (state * channels + channel) * block
        gathered_ref[pl.ds(pl.multiple_of(start + first, 2 * ROWS), 2 * ROWS), :] = rows

    return write


def batches(items, most):
    pieces = -(-len(items) // most)
    size = -(-len(items) // pieces)
    return [items[start : start + size] for start in range(0, len(items), size)]


def rows_of(chunks, channel, offset, height):
    size = chunks[0].shape[0]
    return chunks[channel // size][channel % size, pl.ds(offset, height), :]


def channel_of(chunks, channel):
    size = chunks[0].shape[0]
    return chunks[channel // size][channel % size]


def put_channel(chunks, channel, value):
    size = chunks[0].shape[0]
    chunks[channel // size][channel % size] = value


def count_channels(chunks):
    return sum(chunk.shape[0] for chunk in chunks)


def mix_left(env, tensors, mixed_ref, offset, height):
    channels, block = count_channels(env), env[0].shape[1]
    for cls in range(CLASSES):
        right = jnp.concatenate(tensors[cls], axis=1)
        for batch in batches(list(range(cls, channels, CLASSES)), 5):
            rows = jnp.concatenate(
                [rows_of(env, channel, offset, height) for channel in batch], axis=0
            )
            product = jnp.dot(rows, right, preferred_element_type=jnp.float32)
            for number, channel in enumerate(batch):
                for t in range(len(tensors[cls])):
                    mixed_ref[pl.ds((t * channels + channel) * height, height), :] = product[
                        number * height : (number + 1) * height, t * block : (t + 1) * block
                    ]


def left_kernel(groups, states, pieces, *refs):
    env, (tensor_ref, weight_ref) = refs[:pieces], refs[pieces : pieces + 2]
    outs, mixed_ref = refs[pieces + 2 : -1], refs[-1]
    channels, block = count_channels(env), env[0].shape[1]

    def write(state, channel, first, rows):
        size = channels // pieces
        out_ref = outs[state * pieces + channel // size]
        out_ref[channel % size, pl.ds(first, 2 * ROWS), :] = rows

    def body(offset, height):
        tensors = [[tensor_ref[cls, t] for t in range(states)] for cls in range(CLASSES)]
        mix_left(env, tensors, mixed_ref, offset, height)
        mix_channels(groups, channels, weight_ref, mixed_ref, write, offset, height)

    by_parts(block, body)


def left_close_kernel(iso_ref, gathered_ref, moved_ref, out_ref, square_ref):
    channels, block, _ = gathered_ref.shape
    square = jnp.zeros((ROWS, block), jnp.float32)
    for batch in batches(list(range(channels)), 2):
        right = jnp.concatenate([gathered_ref[channel] for channel in batch], axis=1)
        product = lax.dot_general(
            iso_ref[...], right, (((0,), (0,)), ((), ())), preferred_element_type=jnp.float32
        )
        for number, channel in enumerate(batch):
            part = product[:, number * block : (number + 1) * block]
            part = part + moved_ref[channel].astype(jnp.float32)
            out_ref[channel] = part.astype(jnp.bfloat16)
            square = square + jnp.sum((part * part).reshape(-1, ROWS, block), axis=0)
    square_ref[...] = square


def right_kernel(groups, states, pieces, *refs):
    envs = [refs[t * pieces : (t + 1) * pieces] for t in range(states)]
    refs = refs[states * pieces :]
    own_ref, tensor_ref, weight_ref = refs[:3]
    outs, (square_ref, mixed_ref, gathered_ref) = refs[3 : 3 + pieces], refs[3 + pieces :]
    channels, block = count_channels(envs[0]), envs[0][0].shape[1]
    zero = jnp.zeros((block, block), jnp.bfloat16)
    write = into(gathered_ref, channels, block)

    def body(offset, height):
        for pair in batches(list(range(states)), 2):
            own = jnp.concatenate(
                [
                    jnp.concatenate([own_ref[t] if t == other else zero for other in pair], axis=1)
                    for t in pair
                ],
                axis=0,
            )
            for batch in batches(list(range(channels)), 6):
                rows = jnp.concatenate(
                    [
                        jnp.concatenate(
                            [rows_of(envs[t], channel, offset, height) for channel in batch], axis=0
                        )
                        for t in pair
                    ],
                    axis=1,
                )
                product = lax.dot_general(
                    rows, own, (((1,), (1,)), ((), ())), preferred_element_type=jnp.float32
                )
                for number, t in enumerate(pair):
                    start = (t * channels + batch[0]) * height
                    mixed_ref[pl.ds(start, len(batch) * height), :] = product[
                        :, number * block : (number + 1) * block
                    ]
        mix_channels(groups, channels, weight_ref, mixed_ref, write, offset, height)

    by_parts(block, body)
    square = jnp.zeros((ROWS, block), jnp.float32)
    for cls in range(CLASSES):
        left = jnp.concatenate([tensor_ref[cls, s] for s in range(states)], axis=1)
        for batch in batches(list(range(cls, channels, CLASSES)), 2):
            right = jnp.concatenate(
                [
                    jnp.concatenate(
                        [
                            gathered_ref[pl.ds((s * channels + channel) * block, block), :]
                            for s in range(states)
                        ],
                        axis=0,
                    )
                    for channel in batch
                ],
                axis=1,
            )
            product = jnp.dot(left, right, preferred_element_type=jnp.float32)
            for number, channel in enumerate(batch):
                part = product[:, number * block : (number + 1) * block]
                put_channel(outs, channel, part.astype(jnp.bfloat16))
                square = square + jnp.sum((part * part).reshape(-1, ROWS, block), axis=0)
    square_ref[...] = square


ENV_LANE = 5
LANES = 128


def quotient(table, entry_count):
    def total(x):
        return jnp.sum(x, axis=0, keepdims=True)

    squares = [
        total(table[:, lane : lane + 1]) for lane in range(ENV_LANE, ENV_LANE + 2 * ENV_STEPS + 1)
    ]
    scale = jnp.ones((1, 1), jnp.float32)
    for side in range(2):
        side_scale = jnp.ones((1, 1), jnp.float32)
        for square in squares[side * ENV_STEPS : (side + 1) * ENV_STEPS]:
            side_scale = side_scale * lax.rsqrt(side_scale * side_scale * square / entry_count + TINY)
        scale = scale * side_scale
    a, b, e, c, unit = (table[:, lane : lane + 1] for lane in range(ENV_LANE))
    a, e, unit = scale * a, scale * e, scale * unit
    c = unit * unit * c
    whole_a, whole_b = total(a), total(b)
    energy = whole_a / (whole_b + TINY)
    off = e - energy
    residual_sq = total(c + 2.0 * off * (a - e * b) + off * off * b)
    factor = 0.5 * jnp.sqrt(whole_b / (residual_sq + TINY))
    square = whole_b - 2.0 * factor * (whole_a - energy * whole_b) + factor * factor * residual_sq
    return scale, energy, factor, square, squares[2 * ENV_STEPS]


def updated(vector, image, scale, energy, factor):
    return vector - factor * (scale * image - energy * vector)


def sum_all(x):
    return jnp.sum(jnp.sum(x, axis=0, keepdims=True), axis=1, keepdims=True)


def operator_front_kernel(groups, states, pieces, renew, entry_count, *refs):
    env, refs = refs[:pieces], refs[pieces:]
    others = CLASSES - 1
    weight_ref, vector_ref, rolled = refs[0], refs[1], refs[2 : 2 + others]
    rest = refs[2 + others :]
    if renew:
        image_ref, moved, table_ref = rest[0], rest[1 : 1 + others], rest[1 + others]
        rest = rest[2 + others :]
        scale, energy, factor, _, _ = quotient(table_ref[...], entry_count)
    gathered_ref, new_ref, tensor_ref, mixed_ref = rest
    channels, block = count_channels(env), env[0].shape[1]
    for t in range(states):
        vector = vector_ref[t]
        if renew:
            vector = updated(vector, image_ref[t], scale, energy, factor)
        new_ref[t] = vector
        tensor_ref[0, t] = vector.astype(jnp.bfloat16)
        for cls in range(1, CLASSES):
            vector = rolled[cls - 1][t]
            if renew:
                image = moved[cls - 1][t].astype(jnp.float32)
                vector = updated(vector.astype(jnp.float32), image, scale, energy, factor)
            tensor_ref[cls, t] = vector.astype(jnp.bfloat16)
    write = into(gathered_ref, channels, block)

    def body(offset, height):
        tensors = [[tensor_ref[cls, t] for t in range(states)] for cls in range(CLASSES)]
        mix_left(env, tensors, mixed_ref, offset, height)
        mix_channels(groups, channels, weight_ref, mixed_ref, write, offset, height)

    by_parts(block, body)


def operator_back_kernel(states, pieces, *refs):
    rights = [refs[t * pieces : (t + 1) * pieces] for t in range(states)]
    refs = refs[states * pieces :]
    squares, refs = refs[: 2 * ENV_STEPS + 1], refs[2 * ENV_STEPS + 1 :]
    gathered_ref, vector_ref, image_ref, half_ref, sums_ref = refs
    channels, block = count_channels(rights[0]), rights[0][0].shape[1]
    a = jnp.zeros((1, 1), jnp.float32)
    b = jnp.zeros((1, 1), jnp.float32)
    for s in range(states):
        total = jnp.zeros((block, block), jnp.float32)
        for batch in batches(list(range(channels)), 6):
            left = jnp.concatenate(
                [
                    gathered_ref[pl.ds((s * channels + channel) * block, block), :]
                    for channel in batch
                ],
                axis=1,
            )
            right = jnp.concatenate([channel_of(rights[s], channel) for channel in batch], axis=0)
            total = total + jnp.dot(left, right, preferred_element_type=jnp.float32)
        image_ref[s] = total
        half_ref[s] = total.astype(jnp.bfloat16)
        vector = vector_ref[s]
        a = a + sum_all(vector * total)
        b = b + sum_all(vector * vector)
    e = jnp.where(b > 0, a / jnp.where(b > 0, b, 1.0), 0.0)
    residual = image_ref[...].reshape(states * block, block) - e * vector_ref[...].reshape(
        states * block, block
    )
    unit = jnp.max(jnp.max(jnp.abs(residual), axis=0, keepdims=True), axis=1, keepdims=True)
    unit = jnp.where(unit > 0, unit, 1.0)
    residual = residual / unit
    lane = lax.broadcasted_iota(jnp.int32, sums_ref.shape, 1)
    sums = jnp.zeros(sums_ref.shape, jnp.float32)
    values = (a, b, e, sum_all(residual * residual), unit, *(sum_all(x[...]) for x in squares))
    for place, value in enumerate(values):
        sums = jnp.where(lane == place, value, sums)
    sums_ref[...] = sums


def operator_whole_kernel(groups, states, pieces, entry_count, counts, *refs):
    front, refs = refs[: counts[0]], refs[counts[0] :]
    back, refs = refs[: counts[1]], refs[counts[1] :]
    image_ref, half_ref, sums_ref, new_ref, gathered_ref, tensor_ref, mixed_ref = refs
    operator_front_kernel(
        groups, states, pieces, True, entry_count, *front, gathered_ref, new_ref, tensor_ref, mixed_ref
    )
    operator_back_kernel(
        states, pieces, *back, gathered_ref, new_ref, image_ref, half_ref, sums_ref
    )


def energy_kernel(entry_count, table_ref, out_ref):
    energy = quotient(table_ref[...], entry_count)[1]
    out_ref[...] = jnp.broadcast_to(energy, out_ref.shape)


def polar_kernel(entry_count, both_ref, table_ref, centre_ref, out_ref):
    states, _, block, _ = both_ref.shape
    rows = lax.broadcasted_iota(jnp.int32, (block, block), 0)
    columns = lax.broadcasted_iota(jnp.int32, (block, block), 1)
    unit = (rows == columns).astype(jnp.float32)

    def product(x, y, contract=((1,), (0,))):
        return lax.dot_general(
            x, y, (contract, ((), ())), precision=HIGHEST, preferred_element_type=jnp.float32
        )

    scale, energy, factor, square, centre_sq = quotient(table_ref[...], entry_count)
    vector = updated(
        both_ref[:, 0].reshape(states * block, block),
        both_ref[:, 1].reshape(states * block, block),
        scale,
        energy,
        factor,
    ) * lax.rsqrt(square + TINY)
    centre = centre_ref[...].astype(jnp.float32) * lax.rsqrt(centre_sq + TINY)
    grams = [product(x, x, ((0,), (0,))) for x in (vector, centre)]
    totals = [unit, unit]
    for step in range(POLAR):
        factors = [1.5 * unit - 0.5 * gram for gram in grams]
        totals = [
            factor if step == 0 else product(total, factor)
            for total, factor in zip(totals, factors)
        ]
        if step < POLAR - 1:
            grams = [
                product(product(factor, gram), factor) for gram, factor in zip(grams, factors)
            ]
    closing = product(totals[0], product(centre, totals[1]), ((1,), (1,)))
    out_ref[...] = product(vector, closing).reshape(states, block, block).astype(jnp.bfloat16)


def call(kernel, out_shape, scratch_shapes, flops, operands):
    return pl.pallas_call(
        kernel,
        out_shape=out_shape,
        scratch_shapes=scratch_shapes,
        compiler_params=pltpu.CompilerParams(vmem_limit_bytes=VMEM_LIMIT),
        cost_estimate=pl.CostEstimate(
            flops=flops,
            bytes_accessed=sum(int(np.prod(x.shape)) * x.dtype.itemsize for x in operands),
            transcendentals=0,
        ),
    )(*operands)


def float_out(*shape):
    return jax.ShapeDtypeStruct(shape, jnp.float32)


def half_out(*shape):
    return jax.ShapeDtypeStruct(shape, jnp.bfloat16)


def work(states, channels, block):
    return 4 * states * channels * block**3 + 2 * (states * channels * block) ** 2


def expanded(weight, groups, channels, states):
    spread = spread_matrix(groups, channels, states)
    sizes = tuple(even(len(group)) * ROWS for group in groups)
    return call(
        functools.partial(expand_kernel, sizes),
        half_out(spread.shape[0], -(-max(sizes) // 128) * 128),
        [],
        2 * spread.size * spread.shape[0],
        (weight, jnp.asarray(spread, jnp.bfloat16)),
    )


def left_front(env, tensors, weight, groups):
    channels, block = count_channels(env), env[0].shape[1]
    states, pieces = tensors.shape[1], len(env)
    outs = call(
        functools.partial(left_kernel, groups, states, pieces),
        [half_out(channels // pieces, block, block)] * (states * pieces),
        [pltpu.VMEM((states * channels * block // PARTS, block), jnp.float32)],
        work(states, channels, block),
        (*env, tensors, weight),
    )
    return [outs[s * pieces : (s + 1) * pieces] for s in range(states)]


def left_close(iso, gathered, moved):
    channels, block, _ = gathered.shape
    return call(
        left_close_kernel,
        (half_out(channels, block, block), float_out(ROWS, block)),
        [],
        2 * channels * block**3,
        (iso, gathered, moved),
    )


def right_whole(envs, own, tensors, weight, groups):
    channels, block = count_channels(envs[0]), envs[0][0].shape[1]
    states, pieces = len(envs), len(envs[0])
    outs = call(
        functools.partial(right_kernel, groups, states, pieces),
        [half_out(channels // pieces, block, block)] * pieces + [float_out(ROWS, block)],
        [
            pltpu.VMEM((states * channels * block // PARTS, block), jnp.float32),
            pltpu.VMEM((states * channels * block, block), jnp.bfloat16),
        ],
        work(states, channels, block),
        (*(chunk for env in envs for chunk in env), own, tensors, weight),
    )
    return outs[:pieces], outs[pieces]


def front_scratch(states, channels, block):
    return [
        pltpu.VMEM((CLASSES, states, block, block), jnp.bfloat16),
        pltpu.VMEM((states * channels * block // PARTS, block), jnp.float32),
    ]


def back_outs(states, block):
    return (
        float_out(states, block, block),
        half_out(states, block, block),
        float_out(1, LANES),
    )


def operator_front(env, weight, groups, entry_count, vector, rolled):
    channels, block = count_channels(env), env[0].shape[1]
    states, pieces = vector.shape[0], len(env)
    return call(
        functools.partial(operator_front_kernel, groups, states, pieces, False, entry_count),
        (half_out(states * channels * block, block), float_out(states, block, block)),
        front_scratch(states, channels, block),
        work(states, channels, block),
        (*env, weight, vector, *rolled),
    )


def operator_back(rights, squares, gathered, vector):
    channels, block = count_channels(rights[0]), rights[0][0].shape[1]
    states, pieces = len(rights), len(rights[0])
    return call(
        functools.partial(operator_back_kernel, states, pieces),
        back_outs(states, block),
        [],
        2 * states * channels * block**3,
        (*(chunk for right in rights for chunk in right), *squares, gathered, vector),
    )


def operator_whole(env, weight, groups, entry_count, vector, rolled, news, rights, squares):
    channels, block = count_channels(env), env[0].shape[1]
    states, pieces = vector.shape[0], len(env)
    front = (*env, weight, vector, *rolled, *news)
    back = (*(chunk for right in rights for chunk in right), *squares)
    counts = (len(front), len(back))
    return call(
        functools.partial(operator_whole_kernel, groups, states, pieces, entry_count, counts),
        (*back_outs(states, block), float_out(states, block, block)),
        [
            pltpu.VMEM((states * channels * block, block), jnp.bfloat16),
            *front_scratch(states, channels, block),
        ],
        work(states, channels, block) + 2 * states * channels * block**3,
        (*front, *back),
    )


def polar(both, table, centre, entry_count):
    states, _, block, _ = both.shape
    return call(
        functools.partial(polar_kernel, entry_count),
        half_out(states, block, block),
        [],
        600 * block**3,
        (both, table, centre),
    )


def energy_of(table, entry_count):
    return call(
        functools.partial(energy_kernel, entry_count), float_out(1, LANES), [], 0, (table,)
    )


def charge_mask(channels, states, sectors):
    charge = np.array([CHARGE_STEPS[channel % CLASSES] for channel in range(channels)])
    state = np.arange(states)
    balance = (
        charge[:, None, None, None]
        + state[None, None, None, :]
        - state[None, None, :, None]
        - charge[None, :, None, None]
    )
    return jnp.asarray((balance % sectors == 0).astype(np.float32)).astype(jnp.bfloat16)


def weight_matrices(mpo, pattern, sectors):
    channels, _, states, _ = mpo.shape
    allowed = charge_mask(channels, states, sectors)
    weights = mpo * pattern[:, :, None, None].astype(jnp.bfloat16) * allowed
    size = states * channels
    left = jnp.transpose(weights, (2, 1, 3, 0)).reshape(size, size)
    right = jnp.transpose(weights, (2, 0, 3, 1)).reshape(size, size)
    return jnp.stack([left, right])


def other_classes_of(places, x):
    one, minus = places.ahead(x, 1), places.ahead(x, -1)
    return one, minus, places.ahead(one, 1), places.ahead(minus, -1)


def classes_of(places, x):
    return jnp.stack([x, *other_classes_of(places, x)])


def other_classes_at_once(places, x):
    return tuple(places.ahead(x, charge) for charge in CHARGE_STEPS[1:])


def after(first, then):
    return lax.optimization_barrier((first, then))


def local(left_iso, right_iso, centre, left_env, right_env, mpo, pattern):
    sites, secs = lax.axis_size("site"), lax.axis_size("sec")
    places = Places(sites, secs)
    left_iso, right_iso, centre = left_iso[0, :, 0], right_iso[0, :, 0], centre[0, 0]
    states, block, _ = left_iso.shape
    channels = mpo.shape[1]
    entry_count = left_env.size * secs
    left_groups = label_groups(channels, states, secs, 1)
    right_groups = label_groups(channels, states, secs, -1)

    pieces = PIECES if channels % PIECES == 0 else 1

    def ahead(env, by, chain_by=0):
        return [places.ahead(chunk, by, chain_by) for chunk in env]

    first = places.fetch(jnp.concatenate([right_env[0, :, 0], left_iso, right_iso]))
    left_isos = [first[channels : channels + states]]
    right_isos = [first[channels + states :]]
    for step in range(1, ENV_STEPS):
        left_isos.append(places.fetch(left_iso, step))
        right_isos.append(places.fetch(right_iso, -step))
    own_tensors = places.fetch(jnp.concatenate([left_iso, centre[None]]), ENV_STEPS)
    right = jnp.split(first[:channels], pieces)
    right, left_env = after(right, left_env)
    left = jnp.split(places.fetch(left_env[0, :, 0]), pieces)
    rolled = [
        classes_of(places, jnp.concatenate([left_isos[step], right_isos[step]]))
        for step in range(ENV_STEPS)
    ]
    own_iso, own_centre = own_tensors[:states], own_tensors[states]
    centres = [own_centre] + [places.ahead(own_centre, s) for s in range(1, states)]

    gathered_weights = lax.all_gather(weight_matrices(mpo[0], pattern[0], secs), "site")
    chain = places.my_chain()

    def weight_of(site_by, kind):
        weight = lax.dynamic_index_in_dim(
            gathered_weights, (chain + site_by) % sites, 0, False
        )[kind]
        return expanded(weight, (left_groups, right_groups)[kind], channels, states)

    weights = (
        [weight_of(step, 0) for step in range(ENV_STEPS + 1)],
        [weight_of(-step, 1) for step in range(ENV_STEPS)],
    )
    vector = jnp.einsum(
        "sxy,syz->sxz", own_iso, jnp.stack(centres), preferred_element_type=jnp.float32
    )
    rolled_vector = other_classes_of(places, vector.astype(jnp.bfloat16))
    right, (rolled[1:], rolled_vector, weights) = after(
        right, (rolled[1:], rolled_vector, weights)
    )
    centre_float = own_centre.astype(jnp.float32)
    centre_square = jnp.sum((centre_float * centre_float).reshape(-1, ROWS, block), axis=0)

    left_squares, right_squares = [], []
    for step in range(ENV_STEPS):
        envs = [right]
        for t in range(1, states):
            if step == 0 and t == states - 1:
                left, envs[-1] = after(left, envs[-1])
            envs.append(ahead(envs[-1], 1))
        right, square = right_whole(
            envs,
            right_isos[step],
            rolled[step][:, states:],
            weights[1][step],
            right_groups,
        )
        right_squares.append(square)

        gathered = left_front(left, rolled[step][:, :states], weights[0][step], left_groups)
        moved = [None] * pieces
        for s in reversed(range(1, states)):
            for piece in range(pieces):
                part = jnp.einsum(
                    "xy,vxz->vyz",
                    left_isos[step][s],
                    gathered[s][piece],
                    preferred_element_type=jnp.float32,
                )
                if moved[piece] is not None:
                    part = part + moved[piece].astype(jnp.float32)
                moved[piece] = places.ahead(part.astype(jnp.bfloat16), -1)
        closed = [
            left_close(left_isos[step][0], gathered[0][piece], moved[piece])
            for piece in range(pieces)
        ]
        left = [env for env, _ in closed]
        left_squares.append(sum(square for _, square in closed))

    if (2 * ENV_STEPS) % sites:
        right = ahead(right, 0, 2 * ENV_STEPS)
        right_squares = ahead(right_squares, 0, 2 * ENV_STEPS)
    squares = left_squares + right_squares + [centre_square]
    rights = [right]
    for s in range(1, states):
        rights.append(ahead(rights[-1], 1))
    weight = weights[0][ENV_STEPS]
    gathered, vector = operator_front(
        left, weight, left_groups, entry_count, vector, rolled_vector
    )
    image, half_image, own_sums = operator_back(rights, squares, gathered, vector)
    table = places.collect(own_sums)
    news = (image, *other_classes_at_once(places, half_image), table)
    image, _, own_sums, vector = operator_whole(
        left, weight, left_groups, entry_count, vector, rolled_vector, news, rights, squares
    )
    table = places.collect(own_sums)

    both = jnp.stack([vector, image], axis=1)
    columns = jnp.stack([both[0]] + [places.ahead(both[s], -s) for s in range(1, states)])
    home_table = places.send_home(table, ENV_STEPS, 0)
    home_table, columns = after(home_table, columns)
    column_left = polar(columns, table, own_centre, entry_count)
    new_left = jnp.stack(
        [places.send_home(column_left[s], ENV_STEPS, -s) for s in range(states)]
    )
    energy = energy_of(home_table, entry_count)
    return new_left[None, :, None], energy[0, :1]


def solution(mesh):
    placed = (
        P("site", None, "sec", None, None),
        P("site", None, "sec", None, None),
        P("site", "sec", None, None),
        P("site", None, "sec", None, None),
        P("site", None, "sec", None, None),
        P("site", None, None, None, None),
        P("site", None, None),
    )
    return jax.shard_map(
        local,
        mesh=mesh,
        in_specs=placed,
        out_specs=(P("site", None, "sec", None, None), P("site")),
        check_vma=False,
    )
```

```python
import functools

import jax
import jax.numpy as jnp
import numpy as np
from jax import lax
from jax.experimental import pallas as pl
from jax.experimental.pallas import tpu as pltpu
from jax.sharding import PartitionSpec as P

ENV_STEPS = 2
POLAR = 6

TINY = 1e-06
HIGHEST = lax.Precision.HIGHEST
CHARGE_STEPS = (0, 1, -1, 2, -2)
CLASSES = len(CHARGE_STEPS)
BOTH = ("site", "sec")
VMEM_LIMIT = 20 * 1024 * 1024
PIECES = 2


class Places:
    def __init__(self, sites, secs):
        self.sites, self.secs = sites, secs
        self.half = secs // 2
        self.up = (self.half + 1) // 2

    def home(self, site, sector):
        return (site % self.sites) * self.secs + sector % self.secs

    def position(self, place):
        back = self.half - 1 + self.up - place
        if isinstance(place, int):
            return place if place < self.up else back
        return jnp.where(place < self.up, place, back)

    def slot(self, chain, sector):
        chain, sector = chain % self.sites, sector % self.secs
        place = chain % 2 * self.half + self.position(sector // 2)
        return (chain // 2 * 2 + sector % 2) * self.secs + place

    def pairs(self, source, target):
        return [
            (source(chain, sector), target(chain, sector))
            for chain in range(self.sites)
            for sector in range(self.secs)
        ]

    def fetch(self, x, site_by=0, sec_by=0):
        return lax.ppermute(
            x, BOTH, self.pairs(lambda g, k: self.home(g + site_by, k + sec_by), self.slot)
        )

    def send_home(self, x, site_by, sec_by):
        return lax.ppermute(
            x, BOTH, self.pairs(self.slot, lambda g, k: self.home(g + site_by, k + sec_by))
        )

    def ahead(self, x, by, chain_by=0):
        return lax.ppermute(
            x, BOTH, self.pairs(lambda g, k: self.slot(g + chain_by, k + by), self.slot)
        )

    def from_sector(self, x, source):
        return lax.ppermute(x, BOTH, self.pairs(lambda g, k: self.slot(g, source(k)), self.slot))

    def gather_ahead(self, x, count):
        if count != 3 or self.secs != 8:
            found = [x]
            for _ in range(count):
                found.append(self.ahead(found[-1], 1))
            return found
        one = self.ahead(x, 1)
        onward = self.from_sector(x, lambda k: k - 2 if k % 2 == 0 else k)
        three = self.from_sector(onward, lambda k: k + 3 if k % 2 == 0 else k - 3)
        even = lax.axis_index("site") % 2 == 0
        two = self.partner(jnp.where(even, three, one), 1)
        return [x, one, two, three]

    def partner(self, x, bit):
        return lax.ppermute(x, BOTH, self.pairs(lambda g, k: self.slot(g, k ^ bit), self.slot))

    def my_chain(self):
        return lax.axis_index("site") // 2 * 2 + lax.axis_index("sec") // self.half

    def my_sector(self):
        position = self.position(lax.axis_index("sec") % self.half)
        return 2 * position + lax.axis_index("site") % 2

    def collect(self, values):
        sector = self.my_sector()
        table = values
        bit = 1
        while bit < self.secs:
            other = self.partner(table, bit)
            first = (sector & bit) == 0
            table = jnp.where(
                first, jnp.concatenate([table, other]), jnp.concatenate([other, table])
            )
            bit *= 2
        return table


ROWS = 8
PARTS = 2


def label_groups(channels, states, sectors, sign):
    groups = {}
    for state in range(states):
        for channel in range(channels):
            label = (state + sign * CHARGE_STEPS[channel % CLASSES]) % sectors
            groups.setdefault(label, []).append((state, channel))
    return [groups[label] for label in sorted(groups)]


def even(count):
    return count + count % 2


def spread_matrix(groups, channels, states):
    rows = []
    for group in groups:
        block = np.zeros((even(len(group)), ROWS, states * channels), np.float32)
        for index, (state, channel) in enumerate(group):
            block[index, :, state * channels + channel] = 1
        rows.append(block.reshape(-1, states * channels))
    return np.concatenate(rows)


def expand_kernel(sizes, weight_ref, spread_ref, out_ref):
    start = 0
    for size in sizes:
        spread = spread_ref[pl.ds(start, size), :]
        picked = jnp.dot(spread, weight_ref[...], preferred_element_type=jnp.float32)
        full = lax.dot_general(
            picked.astype(jnp.bfloat16),
            spread,
            (((1,), (1,)), ((), ())),
            preferred_element_type=jnp.float32,
        )
        row = lax.broadcasted_iota(jnp.int32, full.shape, 0)
        column = lax.broadcasted_iota(jnp.int32, full.shape, 1)
        same = lax.rem(row, ROWS) == lax.rem(column, ROWS)
        out_ref[pl.ds(start, size), pl.ds(0, size)] = jnp.where(same, full, 0.0).astype(
            jnp.bfloat16
        )
        start += size


def mix_channels(groups, channels, weight_ref, mixed_ref, write, offset, height):
    def step(index, carry):
        first = pl.multiple_of(index * 2 * ROWS, 2 * ROWS)
        start = 0
        for group in groups:
            size = even(len(group)) * ROWS
            parts = []
            for state, channel in group:
                rows = (state * channels + channel) * height + first
                halves = [
                    mixed_ref[pl.ds(pl.multiple_of(rows + half * ROWS, ROWS), ROWS), :]
                    for half in range(2)
                ]
                parts.append(jnp.concatenate(halves, axis=1))
            if len(group) % 2:
                parts.append(parts[0])
            operand = jnp.concatenate(parts, axis=0).astype(jnp.bfloat16)
            product = jnp.dot(
                weight_ref[pl.ds(start, size), pl.ds(0, size)],
                operand,
                preferred_element_type=jnp.float32,
            )
            block = product.shape[1] // 2
            for number, pair in enumerate(group):
                rows = product[number * ROWS : (number + 1) * ROWS]
                both = jnp.concatenate([rows[:, :block], rows[:, block:]], axis=0)
                write(*pair, pl.multiple_of(offset + first, 2 * ROWS), both.astype(jnp.bfloat16))
            start += size
        return carry

    lax.fori_loop(0, height // (2 * ROWS), step, 0)


def by_parts(block, body):
    height = block // PARTS

    def one(part, carry):
        body(pl.multiple_of(part * height, height), height)
        return carry

    lax.fori_loop(0, PARTS, one, 0)


def into(gathered_ref, channels, block):
    def write(state, channel, first, rows):
        start = (state * channels + channel) * block
        gathered_ref[pl.ds(pl.multiple_of(start + first, 2 * ROWS), 2 * ROWS), :] = rows

    return write


def batches(items, most):
    pieces = -(-len(items) // most)
    size = -(-len(items) // pieces)
    return [items[start : start + size] for start in range(0, len(items), size)]


def rows_of(chunks, channel, offset, height):
    size = chunks[0].shape[0]
    return chunks[channel // size][channel % size, pl.ds(offset, height), :]


def channel_of(chunks, channel):
    size = chunks[0].shape[0]
    return chunks[channel // size][channel % size]


def put_channel(chunks, channel, value):
    size = chunks[0].shape[0]
    chunks[channel // size][channel % size] = value


def count_channels(chunks):
    return sum(chunk.shape[0] for chunk in chunks)


def mix_left(env, tensors, mixed_ref, offset, height):
    channels, block = count_channels(env), env[0].shape[1]
    for cls in range(CLASSES):
        right = jnp.concatenate(tensors[cls], axis=1)
        for batch in batches(list(range(cls, channels, CLASSES)), 5):
            rows = jnp.concatenate(
                [rows_of(env, channel, offset, height) for channel in batch], axis=0
            )
            product = jnp.dot(rows, right, preferred_element_type=jnp.float32)
            for number, channel in enumerate(batch):
                for t in range(len(tensors[cls])):
                    mixed_ref[pl.ds((t * channels + channel) * height, height), :] = product[
                        number * height : (number + 1) * height, t * block : (t + 1) * block
                    ]


def left_kernel(groups, states, pieces, *refs):
    env, (tensor_ref, weight_ref) = refs[:pieces], refs[pieces : pieces + 2]
    outs, mixed_ref = refs[pieces + 2 : -1], refs[-1]
    channels, block = count_channels(env), env[0].shape[1]

    def write(state, channel, first, rows):
        size = channels // pieces
        out_ref = outs[state * pieces + channel // size]
        out_ref[channel % size, pl.ds(first, 2 * ROWS), :] = rows

    def body(offset, height):
        tensors = [[tensor_ref[cls, t] for t in range(states)] for cls in range(CLASSES)]
        mix_left(env, tensors, mixed_ref, offset, height)
        mix_channels(groups, channels, weight_ref, mixed_ref, write, offset, height)

    by_parts(block, body)


def left_close_kernel(iso_ref, gathered_ref, moved_ref, out_ref, square_ref):
    channels, block, _ = gathered_ref.shape
    square = jnp.zeros((ROWS, block), jnp.float32)
    for batch in batches(list(range(channels)), 2):
        right = jnp.concatenate([gathered_ref[channel] for channel in batch], axis=1)
        product = lax.dot_general(
            iso_ref[...], right, (((0,), (0,)), ((), ())), preferred_element_type=jnp.float32
        )
        for number, channel in enumerate(batch):
            part = product[:, number * block : (number + 1) * block]
            part = part + moved_ref[channel].astype(jnp.float32)
            out_ref[channel] = part.astype(jnp.bfloat16)
            square = square + jnp.sum((part * part).reshape(-1, ROWS, block), axis=0)
    square_ref[...] = square


def right_kernel(groups, states, pieces, *refs):
    envs = [refs[t * pieces : (t + 1) * pieces] for t in range(states)]
    refs = refs[states * pieces :]
    own_ref, tensor_ref, weight_ref = refs[:3]
    outs, (square_ref, mixed_ref, gathered_ref) = refs[3 : 3 + pieces], refs[3 + pieces :]
    channels, block = count_channels(envs[0]), envs[0][0].shape[1]
    zero = jnp.zeros((block, block), jnp.bfloat16)
    write = into(gathered_ref, channels, block)

    def body(offset, height):
        for pair in batches(list(range(states)), 2):
            own = jnp.concatenate(
                [
                    jnp.concatenate([own_ref[t] if t == other else zero for other in pair], axis=1)
                    for t in pair
                ],
                axis=0,
            )
            for batch in batches(list(range(channels)), 6):
                rows = jnp.concatenate(
                    [
                        jnp.concatenate(
                            [rows_of(envs[t], channel, offset, height) for channel in batch], axis=0
                        )
                        for t in pair
                    ],
                    axis=1,
                )
                product = lax.dot_general(
                    rows, own, (((1,), (1,)), ((), ())), preferred_element_type=jnp.float32
                )
                for number, t in enumerate(pair):
                    start = (t * channels + batch[0]) * height
                    mixed_ref[pl.ds(start, len(batch) * height), :] = product[
                        :, number * block : (number + 1) * block
                    ]
        mix_channels(groups, channels, weight_ref, mixed_ref, write, offset, height)

    by_parts(block, body)
    square = jnp.zeros((ROWS, block), jnp.float32)
    for cls in range(CLASSES):
        left = jnp.concatenate([tensor_ref[cls, s] for s in range(states)], axis=1)
        for batch in batches(list(range(cls, channels, CLASSES)), 2):
            right = jnp.concatenate(
                [
                    jnp.concatenate(
                        [
                            gathered_ref[pl.ds((s * channels + channel) * block, block), :]
                            for s in range(states)
                        ],
                        axis=0,
                    )
                    for channel in batch
                ],
                axis=1,
            )
            product = jnp.dot(left, right, preferred_element_type=jnp.float32)
            for number, channel in enumerate(batch):
                part = product[:, number * block : (number + 1) * block]
                put_channel(outs, channel, part.astype(jnp.bfloat16))
                square = square + jnp.sum((part * part).reshape(-1, ROWS, block), axis=0)
    square_ref[...] = square


ENV_LANE = 5
LANES = 128


def quotient(table, entry_count):
    def total(x):
        return jnp.sum(x, axis=0, keepdims=True)

    squares = [
        total(table[:, lane : lane + 1]) for lane in range(ENV_LANE, ENV_LANE + 2 * ENV_STEPS + 1)
    ]
    scale = jnp.ones((1, 1), jnp.float32)
    for side in range(2):
        side_scale = jnp.ones((1, 1), jnp.float32)
        for square in squares[side * ENV_STEPS : (side + 1) * ENV_STEPS]:
            side_scale = side_scale * lax.rsqrt(side_scale * side_scale * square / entry_count + TINY)
        scale = scale * side_scale
    a, b, e, c, unit = (table[:, lane : lane + 1] for lane in range(ENV_LANE))
    a, e, unit = scale * a, scale * e, scale * unit
    c = unit * unit * c
    whole_a, whole_b = total(a), total(b)
    energy = whole_a / (whole_b + TINY)
    off = e - energy
    residual_sq = total(c + 2.0 * off * (a - e * b) + off * off * b)
    factor = 0.5 * jnp.sqrt(whole_b / (residual_sq + TINY))
    square = whole_b - 2.0 * factor * (whole_a - energy * whole_b) + factor * factor * residual_sq
    return scale, energy, factor, square, squares[2 * ENV_STEPS]


def updated(vector, image, scale, energy, factor):
    return vector - factor * (scale * image - energy * vector)


def sum_all(x):
    return jnp.sum(jnp.sum(x, axis=0, keepdims=True), axis=1, keepdims=True)


def operator_front_kernel(groups, states, pieces, renew, entry_count, *refs):
    env, refs = refs[:pieces], refs[pieces:]
    others = CLASSES - 1
    weight_ref, vector_ref, rolled = refs[0], refs[1], refs[2 : 2 + others]
    rest = refs[2 + others :]
    if renew:
        image_ref, moved, table_ref = rest[0], rest[1 : 1 + others], rest[1 + others]
        rest = rest[2 + others :]
        scale, energy, factor, _, _ = quotient(table_ref[...], entry_count)
    gathered_ref, new_ref, tensor_ref, mixed_ref = rest
    channels, block = count_channels(env), env[0].shape[1]
    for t in range(states):
        vector = vector_ref[t]
        if renew:
            vector = updated(vector, image_ref[t], scale, energy, factor)
        new_ref[t] = vector
        tensor_ref[0, t] = vector.astype(jnp.bfloat16)
        for cls in range(1, CLASSES):
            vector = rolled[cls - 1][t]
            if renew:
                image = moved[cls - 1][t].astype(jnp.float32)
                vector = updated(vector.astype(jnp.float32), image, scale, energy, factor)
            tensor_ref[cls, t] = vector.astype(jnp.bfloat16)
    write = into(gathered_ref, channels, block)

    def body(offset, height):
        tensors = [[tensor_ref[cls, t] for t in range(states)] for cls in range(CLASSES)]
        mix_left(env, tensors, mixed_ref, offset, height)
        mix_channels(groups, channels, weight_ref, mixed_ref, write, offset, height)

    by_parts(block, body)


def operator_back_kernel(states, pieces, *refs):
    rights = [refs[t * pieces : (t + 1) * pieces] for t in range(states)]
    refs = refs[states * pieces :]
    squares, refs = refs[: 2 * ENV_STEPS + 1], refs[2 * ENV_STEPS + 1 :]
    gathered_ref, vector_ref, image_ref, half_ref, sums_ref = refs
    channels, block = count_channels(rights[0]), rights[0][0].shape[1]
    a = jnp.zeros((1, 1), jnp.float32)
    b = jnp.zeros((1, 1), jnp.float32)
    for s in range(states):
        total = jnp.zeros((block, block), jnp.float32)
        for batch in batches(list(range(channels)), 6):
            left = jnp.concatenate(
                [
                    gathered_ref[pl.ds((s * channels + channel) * block, block), :]
                    for channel in batch
                ],
                axis=1,
            )
            right = jnp.concatenate([channel_of(rights[s], channel) for channel in batch], axis=0)
            total = total + jnp.dot(left, right, preferred_element_type=jnp.float32)
        image_ref[s] = total
        half_ref[s] = total.astype(jnp.bfloat16)
        vector = vector_ref[s]
        a = a + sum_all(vector * total)
        b = b + sum_all(vector * vector)
    e = jnp.where(b > 0, a / jnp.where(b > 0, b, 1.0), 0.0)
    residual = image_ref[...].reshape(states * block, block) - e * vector_ref[...].reshape(
        states * block, block
    )
    unit = jnp.max(jnp.max(jnp.abs(residual), axis=0, keepdims=True), axis=1, keepdims=True)
    unit = jnp.where(unit > 0, unit, 1.0)
    residual = residual / unit
    lane = lax.broadcasted_iota(jnp.int32, sums_ref.shape, 1)
    sums = jnp.zeros(sums_ref.shape, jnp.float32)
    values = (a, b, e, sum_all(residual * residual), unit, *(sum_all(x[...]) for x in squares))
    for place, value in enumerate(values):
        sums = jnp.where(lane == place, value, sums)
    sums_ref[...] = sums


def operator_whole_kernel(groups, states, pieces, entry_count, counts, *refs):
    front, refs = refs[: counts[0]], refs[counts[0] :]
    back, refs = refs[: counts[1]], refs[counts[1] :]
    image_ref, half_ref, sums_ref, new_ref, gathered_ref, tensor_ref, mixed_ref = refs
    operator_front_kernel(
        groups, states, pieces, True, entry_count, *front, gathered_ref, new_ref, tensor_ref, mixed_ref
    )
    operator_back_kernel(
        states, pieces, *back, gathered_ref, new_ref, image_ref, half_ref, sums_ref
    )


def energy_kernel(entry_count, table_ref, out_ref):
    energy = quotient(table_ref[...], entry_count)[1]
    out_ref[...] = jnp.broadcast_to(energy, out_ref.shape)


def polar_kernel(entry_count, both_ref, table_ref, centre_ref, out_ref):
    states, _, block, _ = both_ref.shape
    rows = lax.broadcasted_iota(jnp.int32, (block, block), 0)
    columns = lax.broadcasted_iota(jnp.int32, (block, block), 1)
    unit = (rows == columns).astype(jnp.float32)

    def product(x, y, contract=((1,), (0,))):
        return lax.dot_general(
            x, y, (contract, ((), ())), precision=HIGHEST, preferred_element_type=jnp.float32
        )

    scale, energy, factor, square, centre_sq = quotient(table_ref[...], entry_count)
    vector = updated(
        both_ref[:, 0].reshape(states * block, block),
        both_ref[:, 1].reshape(states * block, block),
        scale,
        energy,
        factor,
    ) * lax.rsqrt(square + TINY)
    centre = centre_ref[...].astype(jnp.float32) * lax.rsqrt(centre_sq + TINY)
    grams = [product(x, x, ((0,), (0,))) for x in (vector, centre)]
    totals = [unit, unit]
    for step in range(POLAR):
        factors = [1.5 * unit - 0.5 * gram for gram in grams]
        totals = [
            factor if step == 0 else product(total, factor)
            for total, factor in zip(totals, factors)
        ]
        if step < POLAR - 1:
            grams = [
                product(product(factor, gram), factor) for gram, factor in zip(grams, factors)
            ]
    closing = product(totals[0], product(centre, totals[1]), ((1,), (1,)))
    out_ref[...] = product(vector, closing).reshape(states, block, block).astype(jnp.bfloat16)


def call(kernel, out_shape, scratch_shapes, flops, operands):
    return pl.pallas_call(
        kernel,
        out_shape=out_shape,
        scratch_shapes=scratch_shapes,
        compiler_params=pltpu.CompilerParams(vmem_limit_bytes=VMEM_LIMIT),
        cost_estimate=pl.CostEstimate(
            flops=flops,
            bytes_accessed=sum(int(np.prod(x.shape)) * x.dtype.itemsize for x in operands),
            transcendentals=0,
        ),
    )(*operands)


def float_out(*shape):
    return jax.ShapeDtypeStruct(shape, jnp.float32)


def half_out(*shape):
    return jax.ShapeDtypeStruct(shape, jnp.bfloat16)


def work(states, channels, block):
    return 4 * states * channels * block**3 + 2 * (states * channels * block) ** 2


def expanded(weight, groups, channels, states):
    spread = spread_matrix(groups, channels, states)
    sizes = tuple(even(len(group)) * ROWS for group in groups)
    return call(
        functools.partial(expand_kernel, sizes),
        half_out(spread.shape[0], -(-max(sizes) // 128) * 128),
        [],
        2 * spread.size * spread.shape[0],
        (weight, jnp.asarray(spread, jnp.bfloat16)),
    )


def left_front(env, tensors, weight, groups):
    channels, block = count_channels(env), env[0].shape[1]
    states, pieces = tensors.shape[1], len(env)
    outs = call(
        functools.partial(left_kernel, groups, states, pieces),
        [half_out(channels // pieces, block, block)] * (states * pieces),
        [pltpu.VMEM((states * channels * block // PARTS, block), jnp.float32)],
        work(states, channels, block),
        (*env, tensors, weight),
    )
    return [outs[s * pieces : (s + 1) * pieces] for s in range(states)]


def left_close(iso, gathered, moved):
    channels, block, _ = gathered.shape
    return call(
        left_close_kernel,
        (half_out(channels, block, block), float_out(ROWS, block)),
        [],
        2 * channels * block**3,
        (iso, gathered, moved),
    )


def right_whole(envs, own, tensors, weight, groups):
    channels, block = count_channels(envs[0]), envs[0][0].shape[1]
    states, pieces = len(envs), len(envs[0])
    outs = call(
        functools.partial(right_kernel, groups, states, pieces),
        [half_out(channels // pieces, block, block)] * pieces + [float_out(ROWS, block)],
        [
            pltpu.VMEM((states * channels * block // PARTS, block), jnp.float32),
            pltpu.VMEM((states * channels * block, block), jnp.bfloat16),
        ],
        work(states, channels, block),
        (*(chunk for env in envs for chunk in env), own, tensors, weight),
    )
    return outs[:pieces], outs[pieces]


def front_scratch(states, channels, block):
    return [
        pltpu.VMEM((CLASSES, states, block, block), jnp.bfloat16),
        pltpu.VMEM((states * channels * block // PARTS, block), jnp.float32),
    ]


def back_outs(states, block):
    return (
        float_out(states, block, block),
        half_out(states, block, block),
        float_out(1, LANES),
    )


def operator_front(env, weight, groups, entry_count, vector, rolled):
    channels, block = count_channels(env), env[0].shape[1]
    states, pieces = vector.shape[0], len(env)
    return call(
        functools.partial(operator_front_kernel, groups, states, pieces, False, entry_count),
        (half_out(states * channels * block, block), float_out(states, block, block)),
        front_scratch(states, channels, block),
        work(states, channels, block),
        (*env, weight, vector, *rolled),
    )


def operator_back(rights, squares, gathered, vector):
    channels, block = count_channels(rights[0]), rights[0][0].shape[1]
    states, pieces = len(rights), len(rights[0])
    return call(
        functools.partial(operator_back_kernel, states, pieces),
        back_outs(states, block),
        [],
        2 * states * channels * block**3,
        (*(chunk for right in rights for chunk in right), *squares, gathered, vector),
    )


def operator_whole(env, weight, groups, entry_count, vector, rolled, news, rights, squares):
    channels, block = count_channels(env), env[0].shape[1]
    states, pieces = vector.shape[0], len(env)
    front = (*env, weight, vector, *rolled, *news)
    back = (*(chunk for right in rights for chunk in right), *squares)
    counts = (len(front), len(back))
    return call(
        functools.partial(operator_whole_kernel, groups, states, pieces, entry_count, counts),
        (*back_outs(states, block), float_out(states, block, block)),
        [
            pltpu.VMEM((states * channels * block, block), jnp.bfloat16),
            *front_scratch(states, channels, block),
        ],
        work(states, channels, block) + 2 * states * channels * block**3,
        (*front, *back),
    )


def polar(both, table, centre, entry_count):
    states, _, block, _ = both.shape
    return call(
        functools.partial(polar_kernel, entry_count),
        half_out(states, block, block),
        [],
        600 * block**3,
        (both, table, centre),
    )


def energy_of(table, entry_count):
    return call(
        functools.partial(energy_kernel, entry_count), float_out(1, LANES), [], 0, (table,)
    )


def charge_mask(channels, states, sectors):
    charge = np.array([CHARGE_STEPS[channel % CLASSES] for channel in range(channels)])
    state = np.arange(states)
    balance = (
        charge[:, None, None, None]
        + state[None, None, None, :]
        - state[None, None, :, None]
        - charge[None, :, None, None]
    )
    return jnp.asarray((balance % sectors == 0).astype(np.float32)).astype(jnp.bfloat16)


def weight_matrices(mpo, pattern, sectors):
    channels, _, states, _ = mpo.shape
    allowed = charge_mask(channels, states, sectors)
    weights = mpo * pattern[:, :, None, None].astype(jnp.bfloat16) * allowed
    size = states * channels
    left = jnp.transpose(weights, (2, 1, 3, 0)).reshape(size, size)
    right = jnp.transpose(weights, (2, 0, 3, 1)).reshape(size, size)
    return jnp.stack([left, right])


def other_classes_of(places, x):
    one, minus = places.ahead(x, 1), places.ahead(x, -1)
    return one, minus, places.ahead(one, 1), places.ahead(minus, -1)


def classes_of(places, x):
    return jnp.stack([x, *other_classes_of(places, x)])


def other_classes_at_once(places, x):
    return tuple(places.ahead(x, charge) for charge in CHARGE_STEPS[1:])


def after(first, then):
    return lax.optimization_barrier((first, then))


def local(left_iso, right_iso, centre, left_env, right_env, mpo, pattern):
    sites, secs = lax.axis_size("site"), lax.axis_size("sec")
    places = Places(sites, secs)
    left_iso, right_iso, centre = left_iso[0, :, 0], right_iso[0, :, 0], centre[0, 0]
    states, block, _ = left_iso.shape
    channels = mpo.shape[1]
    entry_count = left_env.size * secs
    left_groups = label_groups(channels, states, secs, 1)
    right_groups = label_groups(channels, states, secs, -1)

    pieces = PIECES if channels % PIECES == 0 else 1

    def ahead(env, by, chain_by=0):
        return [places.ahead(chunk, by, chain_by) for chunk in env]

    right = places.fetch(right_env[0, :, 0])
    left = places.fetch(left_env[0, :, 0])
    both_isos = places.fetch(jnp.concatenate([left_iso, right_iso]))
    left_isos, right_isos = [both_isos[:states]], [both_isos[states:]]
    for step in range(1, ENV_STEPS):
        left_isos.append(places.fetch(left_iso, step))
        right_isos.append(places.fetch(right_iso, -step))
    own_tensors = places.fetch(jnp.concatenate([left_iso, centre[None]]), ENV_STEPS)
    rolled = [
        classes_of(places, jnp.concatenate([left_isos[step], right_isos[step]]))
        for step in range(ENV_STEPS)
    ]
    own_iso, own_centre = own_tensors[:states], own_tensors[states]
    centres = [own_centre] + [places.ahead(own_centre, s) for s in range(1, states)]

    gathered_weights = lax.all_gather(weight_matrices(mpo[0], pattern[0], secs), "site")
    chain = places.my_chain()

    def weight_of(site_by, kind):
        weight = lax.dynamic_index_in_dim(
            gathered_weights, (chain + site_by) % sites, 0, False
        )[kind]
        return expanded(weight, (left_groups, right_groups)[kind], channels, states)

    weights = (
        [weight_of(step, 0) for step in range(ENV_STEPS + 1)],
        [weight_of(-step, 1) for step in range(ENV_STEPS)],
    )
    vector = jnp.einsum(
        "sxy,syz->sxz", own_iso, jnp.stack(centres), preferred_element_type=jnp.float32
    )
    rolled_vector = other_classes_of(places, vector.astype(jnp.bfloat16))
    (right, left), (rolled, rolled_vector, weights) = after(
        (right, left), (rolled, rolled_vector, weights)
    )
    right, left = jnp.split(right, pieces), jnp.split(left, pieces)
    centre_float = own_centre.astype(jnp.float32)
    centre_square = jnp.sum((centre_float * centre_float).reshape(-1, ROWS, block), axis=0)

    left_squares, right_squares = [], []
    for step in range(ENV_STEPS):
        envs = [right]
        for t in range(1, states):
            envs.append(ahead(envs[-1], 1))
        right, square = right_whole(
            envs,
            right_isos[step],
            rolled[step][:, states:],
            weights[1][step],
            right_groups,
        )
        right_squares.append(square)

        gathered = left_front(left, rolled[step][:, :states], weights[0][step], left_groups)
        moved = [None] * pieces
        for s in reversed(range(1, states)):
            for piece in range(pieces):
                part = jnp.einsum(
                    "xy,vxz->vyz",
                    left_isos[step][s],
                    gathered[s][piece],
                    preferred_element_type=jnp.float32,
                )
                if moved[piece] is not None:
                    part = part + moved[piece].astype(jnp.float32)
                moved[piece] = places.ahead(part.astype(jnp.bfloat16), -1)
        closed = [
            left_close(left_isos[step][0], gathered[0][piece], moved[piece])
            for piece in range(pieces)
        ]
        left = [env for env, _ in closed]
        left_squares.append(sum(square for _, square in closed))

    if (2 * ENV_STEPS) % sites:
        right = ahead(right, 0, 2 * ENV_STEPS)
        right_squares = ahead(right_squares, 0, 2 * ENV_STEPS)
    squares = left_squares + right_squares + [centre_square]
    rights = [places.gather_ahead(chunk, states - 1) for chunk in right]
    rights = [[chunks[s] for chunks in rights] for s in range(states)]
    weight = weights[0][ENV_STEPS]
    gathered, vector = operator_front(
        left, weight, left_groups, entry_count, vector, rolled_vector
    )
    image, half_image, own_sums = operator_back(rights, squares, gathered, vector)
    table = places.collect(own_sums)
    news = (image, *other_classes_at_once(places, half_image), table)
    image, _, own_sums, vector = operator_whole(
        left, weight, left_groups, entry_count, vector, rolled_vector, news, rights, squares
    )
    table = places.collect(own_sums)

    both = jnp.stack([vector, image], axis=1)
    columns = jnp.stack([both[0]] + [places.ahead(both[s], -s) for s in range(1, states)])
    home_table = places.send_home(table, ENV_STEPS, 0)
    home_table, columns = after(home_table, columns)
    column_left = polar(columns, table, own_centre, entry_count)
    new_left = jnp.stack(
        [places.send_home(column_left[s], ENV_STEPS, -s) for s in range(states)]
    )
    energy = energy_of(home_table, entry_count)
    return new_left[None, :, None], energy[0, :1]


def solution(mesh):
    placed = (
        P("site", None, "sec", None, None),
        P("site", None, "sec", None, None),
        P("site", "sec", None, None),
        P("site", None, "sec", None, None),
        P("site", None, "sec", None, None),
        P("site", None, None, None, None),
        P("site", None, None),
    )
    return jax.shard_map(
        local,
        mesh=mesh,
        in_specs=placed,
        out_specs=(P("site", None, "sec", None, None), P("site")),
        check_vma=False,
    )
```

```python
import functools

import jax
import jax.numpy as jnp
import numpy as np
from jax import lax
from jax.experimental import pallas as pl
from jax.experimental.pallas import tpu as pltpu
from jax.sharding import PartitionSpec as P

ENV_STEPS = 2
POLAR = 6

TINY = 1e-06
HIGHEST = lax.Precision.HIGHEST
CHARGE_STEPS = (0, 1, -1, 2, -2)
CLASSES = len(CHARGE_STEPS)
BOTH = ("site", "sec")
VMEM_LIMIT = 20 * 1024 * 1024
PIECES = 2


class Places:
    def __init__(self, sites, secs):
        self.sites, self.secs = sites, secs
        self.half = secs // 2
        self.up = (self.half + 1) // 2

    def home(self, site, sector):
        return (site % self.sites) * self.secs + sector % self.secs

    def position(self, place):
        back = self.half - 1 + self.up - place
        if isinstance(place, int):
            return place if place < self.up else back
        return jnp.where(place < self.up, place, back)

    def slot(self, chain, sector):
        chain, sector = chain % self.sites, sector % self.secs
        place = chain % 2 * self.half + self.position(sector // 2)
        return (chain // 2 * 2 + sector % 2) * self.secs + place

    def pairs(self, source, target):
        return [
            (source(chain, sector), target(chain, sector))
            for chain in range(self.sites)
            for sector in range(self.secs)
        ]

    def fetch(self, x, site_by=0, sec_by=0):
        return lax.ppermute(
            x, BOTH, self.pairs(lambda g, k: self.home(g + site_by, k + sec_by), self.slot)
        )

    def send_home(self, x, site_by, sec_by):
        return lax.ppermute(
            x, BOTH, self.pairs(self.slot, lambda g, k: self.home(g + site_by, k + sec_by))
        )

    def ahead(self, x, by, chain_by=0):
        return lax.ppermute(
            x, BOTH, self.pairs(lambda g, k: self.slot(g + chain_by, k + by), self.slot)
        )

    def partner(self, x, bit):
        return lax.ppermute(x, BOTH, self.pairs(lambda g, k: self.slot(g, k ^ bit), self.slot))

    def my_chain(self):
        return lax.axis_index("site") // 2 * 2 + lax.axis_index("sec") // self.half

    def my_sector(self):
        position = self.position(lax.axis_index("sec") % self.half)
        return 2 * position + lax.axis_index("site") % 2

    def collect(self, values):
        sector = self.my_sector()
        table = values
        bit = 1
        while bit < self.secs:
            other = self.partner(table, bit)
            first = (sector & bit) == 0
            table = jnp.where(
                first, jnp.concatenate([table, other]), jnp.concatenate([other, table])
            )
            bit *= 2
        return table


ROWS = 8
PARTS = 2


def label_groups(channels, states, sectors, sign):
    groups = {}
    for state in range(states):
        for channel in range(channels):
            label = (state + sign * CHARGE_STEPS[channel % CLASSES]) % sectors
            groups.setdefault(label, []).append((state, channel))
    return [groups[label] for label in sorted(groups)]


def even(count):
    return count + count % 2


def spread_matrix(groups, channels, states):
    rows = []
    for group in groups:
        block = np.zeros((even(len(group)), ROWS, states * channels), np.float32)
        for index, (state, channel) in enumerate(group):
            block[index, :, state * channels + channel] = 1
        rows.append(block.reshape(-1, states * channels))
    return np.concatenate(rows)


def expand_kernel(sizes, weight_ref, spread_ref, out_ref):
    start = 0
    for size in sizes:
        spread = spread_ref[pl.ds(start, size), :]
        picked = jnp.dot(spread, weight_ref[...], preferred_element_type=jnp.float32)
        full = lax.dot_general(
            picked.astype(jnp.bfloat16),
            spread,
            (((1,), (1,)), ((), ())),
            preferred_element_type=jnp.float32,
        )
        row = lax.broadcasted_iota(jnp.int32, full.shape, 0)
        column = lax.broadcasted_iota(jnp.int32, full.shape, 1)
        same = lax.rem(row, ROWS) == lax.rem(column, ROWS)
        out_ref[pl.ds(start, size), pl.ds(0, size)] = jnp.where(same, full, 0.0).astype(
            jnp.bfloat16
        )
        start += size


def mix_channels(groups, channels, weight_ref, mixed_ref, write, offset, height):
    def step(index, carry):
        first = pl.multiple_of(index * 2 * ROWS, 2 * ROWS)
        start = 0
        for group in groups:
            size = even(len(group)) * ROWS
            parts = []
            for state, channel in group:
                rows = (state * channels + channel) * height + first
                halves = [
                    mixed_ref[pl.ds(pl.multiple_of(rows + half * ROWS, ROWS), ROWS), :]
                    for half in range(2)
                ]
                parts.append(jnp.concatenate(halves, axis=1))
            if len(group) % 2:
                parts.append(parts[0])
            operand = jnp.concatenate(parts, axis=0).astype(jnp.bfloat16)
            product = jnp.dot(
                weight_ref[pl.ds(start, size), pl.ds(0, size)],
                operand,
                preferred_element_type=jnp.float32,
            )
            block = product.shape[1] // 2
            for number, pair in enumerate(group):
                rows = product[number * ROWS : (number + 1) * ROWS]
                both = jnp.concatenate([rows[:, :block], rows[:, block:]], axis=0)
                write(*pair, pl.multiple_of(offset + first, 2 * ROWS), both.astype(jnp.bfloat16))
            start += size
        return carry

    lax.fori_loop(0, height // (2 * ROWS), step, 0)


def by_parts(block, body):
    height = block // PARTS

    def one(part, carry):
        body(pl.multiple_of(part * height, height), height)
        return carry

    lax.fori_loop(0, PARTS, one, 0)


def into(gathered_ref, channels, block):
    def write(state, channel, first, rows):
        start = (state * channels + channel) * block
        gathered_ref[pl.ds(pl.multiple_of(start + first, 2 * ROWS), 2 * ROWS), :] = rows

    return write


def batches(items, most):
    pieces = -(-len(items) // most)
    size = -(-len(items) // pieces)
    return [items[start : start + size] for start in range(0, len(items), size)]


def rows_of(chunks, channel, offset, height):
    size = chunks[0].shape[0]
    return chunks[channel // size][channel % size, pl.ds(offset, height), :]


def channel_of(chunks, channel):
    size = chunks[0].shape[0]
    return chunks[channel // size][channel % size]


def put_channel(chunks, channel, value):
    size = chunks[0].shape[0]
    chunks[channel // size][channel % size] = value


def count_channels(chunks):
    return sum(chunk.shape[0] for chunk in chunks)


def mix_left(env, tensors, mixed_ref, offset, height):
    channels, block = count_channels(env), env[0].shape[1]
    for cls in range(CLASSES):
        right = jnp.concatenate(tensors[cls], axis=1)
        for batch in batches(list(range(cls, channels, CLASSES)), 5):
            rows = jnp.concatenate(
                [rows_of(env, channel, offset, height) for channel in batch], axis=0
            )
            product = jnp.dot(rows, right, preferred_element_type=jnp.float32)
            for number, channel in enumerate(batch):
                for t in range(len(tensors[cls])):
                    mixed_ref[pl.ds((t * channels + channel) * height, height), :] = product[
                        number * height : (number + 1) * height, t * block : (t + 1) * block
                    ]


def left_kernel(groups, states, pieces, *refs):
    env, (tensor_ref, weight_ref) = refs[:pieces], refs[pieces : pieces + 2]
    outs, mixed_ref = refs[pieces + 2 : -1], refs[-1]
    channels, block = count_channels(env), env[0].shape[1]

    def write(state, channel, first, rows):
        size = channels // pieces
        out_ref = outs[state * pieces + channel // size]
        out_ref[channel % size, pl.ds(first, 2 * ROWS), :] = rows

    def body(offset, height):
        tensors = [[tensor_ref[cls, t] for t in range(states)] for cls in range(CLASSES)]
        mix_left(env, tensors, mixed_ref, offset, height)
        mix_channels(groups, channels, weight_ref, mixed_ref, write, offset, height)

    by_parts(block, body)


def left_close_kernel(iso_ref, gathered_ref, moved_ref, out_ref, square_ref):
    channels, block, _ = gathered_ref.shape
    square = jnp.zeros((ROWS, block), jnp.float32)
    for batch in batches(list(range(channels)), 2):
        right = jnp.concatenate([gathered_ref[channel] for channel in batch], axis=1)
        product = lax.dot_general(
            iso_ref[...], right, (((0,), (0,)), ((), ())), preferred_element_type=jnp.float32
        )
        for number, channel in enumerate(batch):
            part = product[:, number * block : (number + 1) * block]
            part = part + moved_ref[channel].astype(jnp.float32)
            out_ref[channel] = part.astype(jnp.bfloat16)
            square = square + jnp.sum((part * part).reshape(-1, ROWS, block), axis=0)
    square_ref[...] = square


def right_kernel(groups, states, pieces, *refs):
    envs = [refs[t * pieces : (t + 1) * pieces] for t in range(states)]
    refs = refs[states * pieces :]
    own_ref, tensor_ref, weight_ref = refs[:3]
    outs, (square_ref, mixed_ref, gathered_ref) = refs[3 : 3 + pieces], refs[3 + pieces :]
    channels, block = count_channels(envs[0]), envs[0][0].shape[1]
    zero = jnp.zeros((block, block), jnp.bfloat16)
    write = into(gathered_ref, channels, block)

    def body(offset, height):
        for pair in batches(list(range(states)), 2):
            own = jnp.concatenate(
                [
                    jnp.concatenate([own_ref[t] if t == other else zero for other in pair], axis=1)
                    for t in pair
                ],
                axis=0,
            )
            for batch in batches(list(range(channels)), 6):
                rows = jnp.concatenate(
                    [
                        jnp.concatenate(
                            [rows_of(envs[t], channel, offset, height) for channel in batch], axis=0
                        )
                        for t in pair
                    ],
                    axis=1,
                )
                product = lax.dot_general(
                    rows, own, (((1,), (1,)), ((), ())), preferred_element_type=jnp.float32
                )
                for number, t in enumerate(pair):
                    start = (t * channels + batch[0]) * height
                    mixed_ref[pl.ds(start, len(batch) * height), :] = product[
                        :, number * block : (number + 1) * block
                    ]
        mix_channels(groups, channels, weight_ref, mixed_ref, write, offset, height)

    by_parts(block, body)
    square = jnp.zeros((ROWS, block), jnp.float32)
    for cls in range(CLASSES):
        left = jnp.concatenate([tensor_ref[cls, s] for s in range(states)], axis=1)
        for batch in batches(list(range(cls, channels, CLASSES)), 2):
            right = jnp.concatenate(
                [
                    jnp.concatenate(
                        [
                            gathered_ref[pl.ds((s * channels + channel) * block, block), :]
                            for s in range(states)
                        ],
                        axis=0,
                    )
                    for channel in batch
                ],
                axis=1,
            )
            product = jnp.dot(left, right, preferred_element_type=jnp.float32)
            for number, channel in enumerate(batch):
                part = product[:, number * block : (number + 1) * block]
                put_channel(outs, channel, part.astype(jnp.bfloat16))
                square = square + jnp.sum((part * part).reshape(-1, ROWS, block), axis=0)
    square_ref[...] = square


ENV_LANE = 5
LANES = 128


def quotient(table, entry_count):
    def total(x):
        return jnp.sum(x, axis=0, keepdims=True)

    squares = [
        total(table[:, lane : lane + 1]) for lane in range(ENV_LANE, ENV_LANE + 2 * ENV_STEPS + 1)
    ]
    scale = jnp.ones((1, 1), jnp.float32)
    for side in range(2):
        side_scale = jnp.ones((1, 1), jnp.float32)
        for square in squares[side * ENV_STEPS : (side + 1) * ENV_STEPS]:
            side_scale = side_scale * lax.rsqrt(side_scale * side_scale * square / entry_count + TINY)
        scale = scale * side_scale
    a, b, e, c, unit = (table[:, lane : lane + 1] for lane in range(ENV_LANE))
    a, e, unit = scale * a, scale * e, scale * unit
    c = unit * unit * c
    whole_a, whole_b = total(a), total(b)
    energy = whole_a / (whole_b + TINY)
    off = e - energy
    residual_sq = total(c + 2.0 * off * (a - e * b) + off * off * b)
    factor = 0.5 * jnp.sqrt(whole_b / (residual_sq + TINY))
    square = whole_b - 2.0 * factor * (whole_a - energy * whole_b) + factor * factor * residual_sq
    return scale, energy, factor, square, squares[2 * ENV_STEPS]


def updated(vector, image, scale, energy, factor):
    return vector - factor * (scale * image - energy * vector)


def sum_all(x):
    return jnp.sum(jnp.sum(x, axis=0, keepdims=True), axis=1, keepdims=True)


def operator_front_kernel(groups, states, pieces, *refs):
    env, refs = refs[:pieces], refs[pieces:]
    weight_ref, classes, refs = refs[0], refs[1 : 1 + CLASSES], refs[1 + CLASSES :]
    gathered_ref, mixed_ref = refs
    channels, block = count_channels(env), env[0].shape[1]
    write = into(gathered_ref, channels, block)

    def body(offset, height):
        tensors = [[classes[cls][t] for t in range(states)] for cls in range(CLASSES)]
        mix_left(env, tensors, mixed_ref, offset, height)
        mix_channels(groups, channels, weight_ref, mixed_ref, write, offset, height)

    by_parts(block, body)


def products(rights, gathered_ref, s):
    channels, block = count_channels(rights[0]), rights[0][0].shape[1]
    total = jnp.zeros((block, block), jnp.float32)
    for batch in batches(list(range(channels)), 6):
        left = jnp.concatenate(
            [gathered_ref[pl.ds((s * channels + channel) * block, block), :] for channel in batch],
            axis=1,
        )
        right = jnp.concatenate([channel_of(rights[s], channel) for channel in batch], axis=0)
        total = total + jnp.dot(left, right, preferred_element_type=jnp.float32)
    return total


def write_sums(vector, image, squares, sums_ref):
    a, b = sum_all(vector * image), sum_all(vector * vector)
    e = jnp.where(b > 0, a / jnp.where(b > 0, b, 1.0), 0.0)
    residual = image - e * vector
    unit = jnp.max(jnp.max(jnp.abs(residual), axis=0, keepdims=True), axis=1, keepdims=True)
    unit = jnp.where(unit > 0, unit, 1.0)
    residual = residual / unit
    lane = lax.broadcasted_iota(jnp.int32, sums_ref.shape, 1)
    sums = jnp.zeros(sums_ref.shape, jnp.float32)
    values = (a, b, e, sum_all(residual * residual), unit, *(sum_all(x[...]) for x in squares))
    for place, value in enumerate(values):
        sums = jnp.where(lane == place, value, sums)
    sums_ref[...] = sums


def flat(ref):
    states, block, _ = ref.shape
    return ref[...].reshape(states * block, block)


UNIT_ROWS = 16


def power_above(x):
    top = jnp.max(jnp.max(jnp.abs(x), axis=0, keepdims=True), axis=1, keepdims=True)
    steps = jnp.ceil(jnp.log(jnp.where(top > 0, top, 1.0)) * (1 / np.log(2)))
    return jnp.exp(steps * np.log(2)).astype(jnp.bfloat16).astype(jnp.float32)


def operator_back_kernel(states, pieces, *refs):
    rights = [refs[t * pieces : (t + 1) * pieces] for t in range(states)]
    refs = refs[states * pieces :]
    squares, refs = refs[: 2 * ENV_STEPS + 1], refs[2 * ENV_STEPS + 1 :]
    gathered_ref, vector_ref, image_ref, half_ref, sums_ref = refs
    for s in range(states):
        image_ref[s] = products(rights, gathered_ref, s)
    image = flat(image_ref)
    unit = power_above(image)
    half_ref[: image.shape[0]] = (image / unit).astype(jnp.bfloat16)
    half_ref[image.shape[0] :] = jnp.broadcast_to(unit, (UNIT_ROWS, LANES)).astype(jnp.bfloat16)
    write_sums(flat(vector_ref), image, squares, sums_ref)


def operator_whole_kernel(groups, states, pieces, front_count, *refs):
    front, refs = refs[:front_count], refs[front_count:]
    env_and_weight, sent = front[:-CLASSES], front[-CLASSES:]
    rights = [refs[t * pieces : (t + 1) * pieces] for t in range(states)]
    image_ref, unit_ref, gathered_ref, tensor_ref, mixed_ref = refs[states * pieces :]
    block = image_ref.shape[1]
    units = [
        x[pl.ds(states * block, UNIT_ROWS), :].astype(jnp.float32)[:1, :1] for x in sent
    ]
    unit = functools.reduce(jnp.maximum, units)
    unit_ref[...] = jnp.broadcast_to(unit, unit_ref.shape)
    for cls in range(CLASSES):
        for t in range(states):
            tensor = sent[cls][pl.ds(t * block, block), :].astype(jnp.float32)
            tensor_ref[cls, t] = (tensor * (units[cls] / unit)).astype(jnp.bfloat16)
    classes = [tensor_ref.at[cls] for cls in range(CLASSES)]
    operator_front_kernel(groups, states, pieces, *env_and_weight, *classes, gathered_ref, mixed_ref)
    for s in range(states):
        image_ref[s] = products(rights, gathered_ref, s)


def renew_kernel(entry_count, *refs):
    table_ref, vector_ref, image_ref, second_ref, unit_ref = refs[:5]
    squares, (both_ref, sums_ref) = refs[5:-2], refs[-2:]
    states, block, _ = vector_ref.shape
    scale, energy, factor, _, _ = quotient(table_ref[...], entry_count)
    vector, image = flat(vector_ref), flat(image_ref)
    part = factor * (scale * unit_ref[:, :1])
    new_image = (1.0 + factor * energy) * image - part * flat(second_ref)
    new = updated(vector, image, scale, energy, factor)
    both_ref[:, 0] = new.reshape(states, block, block)
    both_ref[:, 1] = new_image.reshape(states, block, block)
    write_sums(new, new_image, squares, sums_ref)


def energy_kernel(entry_count, table_ref, out_ref):
    energy = quotient(table_ref[...], entry_count)[1]
    out_ref[...] = jnp.broadcast_to(energy, out_ref.shape)


def polar_kernel(entry_count, both_ref, table_ref, centre_ref, out_ref):
    states, _, block, _ = both_ref.shape
    rows = lax.broadcasted_iota(jnp.int32, (block, block), 0)
    columns = lax.broadcasted_iota(jnp.int32, (block, block), 1)
    unit = (rows == columns).astype(jnp.float32)

    def product(x, y, contract=((1,), (0,))):
        return lax.dot_general(
            x, y, (contract, ((), ())), precision=HIGHEST, preferred_element_type=jnp.float32
        )

    scale, energy, factor, square, centre_sq = quotient(table_ref[...], entry_count)
    vector = updated(
        both_ref[:, 0].reshape(states * block, block),
        both_ref[:, 1].reshape(states * block, block),
        scale,
        energy,
        factor,
    ) * lax.rsqrt(square + TINY)
    centre = centre_ref[...].astype(jnp.float32) * lax.rsqrt(centre_sq + TINY)
    grams = [product(x, x, ((0,), (0,))) for x in (vector, centre)]
    totals = [unit, unit]
    for step in range(POLAR):
        factors = [1.5 * unit - 0.5 * gram for gram in grams]
        totals = [
            factor if step == 0 else product(total, factor)
            for total, factor in zip(totals, factors)
        ]
        if step < POLAR - 1:
            grams = [
                product(product(factor, gram), factor) for gram, factor in zip(grams, factors)
            ]
    closing = product(totals[0], product(centre, totals[1]), ((1,), (1,)))
    out_ref[...] = product(vector, closing).reshape(states, block, block).astype(jnp.bfloat16)


def call(kernel, out_shape, scratch_shapes, flops, operands):
    return pl.pallas_call(
        kernel,
        out_shape=out_shape,
        scratch_shapes=scratch_shapes,
        compiler_params=pltpu.CompilerParams(vmem_limit_bytes=VMEM_LIMIT),
        cost_estimate=pl.CostEstimate(
            flops=flops,
            bytes_accessed=sum(int(np.prod(x.shape)) * x.dtype.itemsize for x in operands),
            transcendentals=0,
        ),
    )(*operands)


def float_out(*shape):
    return jax.ShapeDtypeStruct(shape, jnp.float32)


def half_out(*shape):
    return jax.ShapeDtypeStruct(shape, jnp.bfloat16)


def work(states, channels, block):
    return 4 * states * channels * block**3 + 2 * (states * channels * block) ** 2


def expanded(weight, groups, channels, states):
    spread = spread_matrix(groups, channels, states)
    sizes = tuple(even(len(group)) * ROWS for group in groups)
    return call(
        functools.partial(expand_kernel, sizes),
        half_out(spread.shape[0], -(-max(sizes) // 128) * 128),
        [],
        2 * spread.size * spread.shape[0],
        (weight, jnp.asarray(spread, jnp.bfloat16)),
    )


def left_front(env, tensors, weight, groups):
    channels, block = count_channels(env), env[0].shape[1]
    states, pieces = tensors.shape[1], len(env)
    outs = call(
        functools.partial(left_kernel, groups, states, pieces),
        [half_out(channels // pieces, block, block)] * (states * pieces),
        [pltpu.VMEM((states * channels * block // PARTS, block), jnp.float32)],
        work(states, channels, block),
        (*env, tensors, weight),
    )
    return [outs[s * pieces : (s + 1) * pieces] for s in range(states)]


def left_close(iso, gathered, moved):
    channels, block, _ = gathered.shape
    return call(
        left_close_kernel,
        (half_out(channels, block, block), float_out(ROWS, block)),
        [],
        2 * channels * block**3,
        (iso, gathered, moved),
    )


def right_whole(envs, own, tensors, weight, groups):
    channels, block = count_channels(envs[0]), envs[0][0].shape[1]
    states, pieces = len(envs), len(envs[0])
    outs = call(
        functools.partial(right_kernel, groups, states, pieces),
        [half_out(channels // pieces, block, block)] * pieces + [float_out(ROWS, block)],
        [
            pltpu.VMEM((states * channels * block // PARTS, block), jnp.float32),
            pltpu.VMEM((states * channels * block, block), jnp.bfloat16),
        ],
        work(states, channels, block),
        (*(chunk for env in envs for chunk in env), own, tensors, weight),
    )
    return outs[:pieces], outs[pieces]


def front_scratch(states, channels, block):
    return [pltpu.VMEM((states * channels * block // PARTS, block), jnp.float32)]


def operator_front(env, weight, groups, classes):
    channels, block = count_channels(env), env[0].shape[1]
    states, pieces = classes[0].shape[0], len(env)
    return call(
        functools.partial(operator_front_kernel, groups, states, pieces),
        half_out(states * channels * block, block),
        front_scratch(states, channels, block),
        work(states, channels, block),
        (*env, weight, *classes),
    )


def operator_back(rights, squares, gathered, vector):
    channels, block = count_channels(rights[0]), rights[0][0].shape[1]
    states, pieces = len(rights), len(rights[0])
    return call(
        functools.partial(operator_back_kernel, states, pieces),
        (
            float_out(states, block, block),
            half_out(states * block + UNIT_ROWS, block),
            float_out(1, LANES),
        ),
        [],
        2 * states * channels * block**3,
        (*(chunk for right in rights for chunk in right), *squares, gathered, vector),
    )


def operator_whole(env, weight, groups, classes, rights):
    channels, block = count_channels(env), env[0].shape[1]
    states, pieces = len(rights), len(env)
    front = (*env, weight, *classes)
    return call(
        functools.partial(operator_whole_kernel, groups, states, pieces, len(front)),
        (float_out(states, block, block), float_out(1, LANES)),
        [
            pltpu.VMEM((states * channels * block, block), jnp.bfloat16),
            pltpu.VMEM((CLASSES, states, block, block), jnp.bfloat16),
            *front_scratch(states, channels, block),
        ],
        work(states, channels, block) + 2 * states * channels * block**3,
        (*front, *(chunk for right in rights for chunk in right)),
    )


def renewed(table, vector, image, second, unit, squares, entry_count):
    states, block, _ = vector.shape
    return call(
        functools.partial(renew_kernel, entry_count),
        (float_out(states, 2, block, block), float_out(1, LANES)),
        [],
        0,
        (table, vector, image, second, unit, *squares),
    )


def polar(both, table, centre, entry_count):
    states, _, block, _ = both.shape
    return call(
        functools.partial(polar_kernel, entry_count),
        half_out(states, block, block),
        [],
        600 * block**3,
        (both, table, centre),
    )


def energy_of(table, entry_count):
    return call(
        functools.partial(energy_kernel, entry_count), float_out(1, LANES), [], 0, (table,)
    )


def charge_mask(channels, states, sectors):
    charge = np.array([CHARGE_STEPS[channel % CLASSES] for channel in range(channels)])
    state = np.arange(states)
    balance = (
        charge[:, None, None, None]
        + state[None, None, None, :]
        - state[None, None, :, None]
        - charge[None, :, None, None]
    )
    return jnp.asarray((balance % sectors == 0).astype(np.float32)).astype(jnp.bfloat16)


def weight_matrices(mpo, pattern, sectors):
    channels, _, states, _ = mpo.shape
    allowed = charge_mask(channels, states, sectors)
    weights = mpo * pattern[:, :, None, None].astype(jnp.bfloat16) * allowed
    size = states * channels
    left = jnp.transpose(weights, (2, 1, 3, 0)).reshape(size, size)
    right = jnp.transpose(weights, (2, 0, 3, 1)).reshape(size, size)
    return jnp.stack([left, right])


def other_classes_of(places, x):
    one, minus = places.ahead(x, 1), places.ahead(x, -1)
    return one, minus, places.ahead(one, 1), places.ahead(minus, -1)


def classes_of(places, x):
    return jnp.stack([x, *other_classes_of(places, x)])


def other_classes_at_once(places, x):
    return tuple(places.ahead(x, charge) for charge in CHARGE_STEPS[1:])


def after(first, then):
    return lax.optimization_barrier((first, then))


def local(left_iso, right_iso, centre, left_env, right_env, mpo, pattern):
    sites, secs = lax.axis_size("site"), lax.axis_size("sec")
    places = Places(sites, secs)
    left_iso, right_iso, centre = left_iso[0, :, 0], right_iso[0, :, 0], centre[0, 0]
    states, block, _ = left_iso.shape
    channels = mpo.shape[1]
    entry_count = left_env.size * secs
    left_groups = label_groups(channels, states, secs, 1)
    right_groups = label_groups(channels, states, secs, -1)

    pieces = PIECES if channels % PIECES == 0 else 1

    def ahead(env, by, chain_by=0):
        return [places.ahead(chunk, by, chain_by) for chunk in env]

    first = places.fetch(jnp.concatenate([right_env[0, :, 0], left_iso, right_iso]))
    left_isos = [first[channels : channels + states]]
    right_isos = [first[channels + states :]]
    for step in range(1, ENV_STEPS):
        left_isos.append(places.fetch(left_iso, step))
        right_isos.append(places.fetch(right_iso, -step))
    own_tensors = places.fetch(jnp.concatenate([left_iso, centre[None]]), ENV_STEPS)
    right = jnp.split(first[:channels], pieces)
    right, left_env = after(right, left_env)
    left = jnp.split(places.fetch(left_env[0, :, 0]), pieces)
    rolled = [
        classes_of(places, jnp.concatenate([left_isos[step], right_isos[step]]))
        for step in range(ENV_STEPS)
    ]
    own_iso, own_centre = own_tensors[:states], own_tensors[states]
    centres = [own_centre] + [places.ahead(own_centre, s) for s in range(1, states)]

    gathered_weights = lax.all_gather(weight_matrices(mpo[0], pattern[0], secs), "site")
    chain = places.my_chain()

    def weight_of(site_by, kind):
        weight = lax.dynamic_index_in_dim(
            gathered_weights, (chain + site_by) % sites, 0, False
        )[kind]
        return expanded(weight, (left_groups, right_groups)[kind], channels, states)

    weights = (
        [weight_of(step, 0) for step in range(ENV_STEPS + 1)],
        [weight_of(-step, 1) for step in range(ENV_STEPS)],
    )
    vector = jnp.einsum(
        "sxy,syz->sxz", own_iso, jnp.stack(centres), preferred_element_type=jnp.float32
    )
    half_vector = vector.astype(jnp.bfloat16)
    rolled_vector = (half_vector, *other_classes_of(places, half_vector))
    right, (vector, weights) = after(right, (vector, weights))
    centre_float = own_centre.astype(jnp.float32)
    centre_square = jnp.sum((centre_float * centre_float).reshape(-1, ROWS, block), axis=0)

    left_squares, right_squares = [], []
    for step in range(ENV_STEPS):
        envs = [right]
        for t in range(1, states):
            if step == 0 and t == states - 1:
                left, envs[-1] = after(left, envs[-1])
            envs.append(ahead(envs[-1], 1))
        if step == 0:
            (rolled, rolled_vector), envs = after((rolled, rolled_vector), envs)
        right, square = right_whole(
            envs,
            right_isos[step],
            rolled[step][:, states:],
            weights[1][step],
            right_groups,
        )
        right_squares.append(square)

        gathered = left_front(left, rolled[step][:, :states], weights[0][step], left_groups)
        moved = [None] * pieces
        for s in reversed(range(1, states)):
            for piece in range(pieces):
                part = jnp.einsum(
                    "xy,vxz->vyz",
                    left_isos[step][s],
                    gathered[s][piece],
                    preferred_element_type=jnp.float32,
                )
                if moved[piece] is not None:
                    part = part + moved[piece].astype(jnp.float32)
                moved[piece] = places.ahead(part.astype(jnp.bfloat16), -1)
        closed = [
            left_close(left_isos[step][0], gathered[0][piece], moved[piece])
            for piece in range(pieces)
        ]
        left = [env for env, _ in closed]
        left_squares.append(sum(square for _, square in closed))

    if (2 * ENV_STEPS) % sites:
        right = ahead(right, 0, 2 * ENV_STEPS)
        right_squares = ahead(right_squares, 0, 2 * ENV_STEPS)
    squares = left_squares + right_squares + [centre_square]
    rights = [right]
    for s in range(1, states):
        rights.append(ahead(rights[-1], 1))
    weight = weights[0][ENV_STEPS]
    gathered = operator_front(left, weight, left_groups, rolled_vector)
    image, sent, own_sums = operator_back(rights, squares, gathered, vector)
    rolled_image = (sent, *other_classes_at_once(places, sent))
    second, unit = operator_whole(left, weight, left_groups, rolled_image, rights)
    table = places.collect(own_sums)
    both, own_sums = renewed(table, vector, image, second, unit, squares, entry_count)
    table = places.collect(own_sums)

    columns = jnp.stack([both[0]] + [places.ahead(both[s], -s) for s in range(1, states)])
    home_table = places.send_home(table, ENV_STEPS, 0)
    home_table, columns = after(home_table, columns)
    column_left = polar(columns, table, own_centre, entry_count)
    new_left = jnp.stack(
        [places.send_home(column_left[s], ENV_STEPS, -s) for s in range(states)]
    )
    energy = energy_of(home_table, entry_count)
    return new_left[None, :, None], energy[0, :1]


def solution(mesh):
    placed = (
        P("site", None, "sec", None, None),
        P("site", None, "sec", None, None),
        P("site", "sec", None, None),
        P("site", None, "sec", None, None),
        P("site", None, "sec", None, None),
        P("site", None, None, None, None),
        P("site", None, None),
    )
    return jax.shard_map(
        local,
        mesh=mesh,
        in_specs=placed,
        out_specs=(P("site", None, "sec", None, None), P("site")),
        check_vma=False,
    )
```

```python
import functools

import jax
import jax.numpy as jnp
import numpy as np
from jax import lax
from jax.experimental import pallas as pl
from jax.experimental.pallas import tpu as pltpu
from jax.sharding import PartitionSpec as P

ENV_STEPS = 2
POLAR = 6

TINY = 1e-06
HIGHEST = lax.Precision.HIGHEST
CHARGE_STEPS = (0, 1, -1, 2, -2)
CLASSES = len(CHARGE_STEPS)
BOTH = ("site", "sec")
VMEM_LIMIT = 20 * 1024 * 1024
PIECES = 2


class Places:
    def __init__(self, sites, secs):
        self.sites, self.secs = sites, secs
        self.half = secs // 2
        self.up = (self.half + 1) // 2

    def home(self, site, sector):
        return (site % self.sites) * self.secs + sector % self.secs

    def position(self, place):
        back = self.half - 1 + self.up - place
        if isinstance(place, int):
            return place if place < self.up else back
        return jnp.where(place < self.up, place, back)

    def slot(self, chain, sector):
        chain, sector = chain % self.sites, sector % self.secs
        place = chain % 2 * self.half + self.position(sector // 2)
        return (chain // 2 * 2 + sector % 2) * self.secs + place

    def pairs(self, source, target):
        return [
            (source(chain, sector), target(chain, sector))
            for chain in range(self.sites)
            for sector in range(self.secs)
        ]

    def fetch(self, x, site_by=0, sec_by=0):
        return lax.ppermute(
            x, BOTH, self.pairs(lambda g, k: self.home(g + site_by, k + sec_by), self.slot)
        )

    def send_home(self, x, site_by, sec_by):
        return lax.ppermute(
            x, BOTH, self.pairs(self.slot, lambda g, k: self.home(g + site_by, k + sec_by))
        )

    def ahead(self, x, by, chain_by=0):
        return lax.ppermute(
            x, BOTH, self.pairs(lambda g, k: self.slot(g + chain_by, k + by), self.slot)
        )

    def partner(self, x, bit):
        return lax.ppermute(x, BOTH, self.pairs(lambda g, k: self.slot(g, k ^ bit), self.slot))

    def my_chain(self):
        return lax.axis_index("site") // 2 * 2 + lax.axis_index("sec") // self.half

    def my_sector(self):
        position = self.position(lax.axis_index("sec") % self.half)
        return 2 * position + lax.axis_index("site") % 2

    def collect(self, values):
        sector = self.my_sector()
        table = values
        bit = 1
        while bit < self.secs:
            other = self.partner(table, bit)
            first = (sector & bit) == 0
            table = jnp.where(
                first, jnp.concatenate([table, other]), jnp.concatenate([other, table])
            )
            bit *= 2
        return table


ROWS = 8
PARTS = 2


def label_groups(channels, states, sectors, sign):
    groups = {}
    for state in range(states):
        for channel in range(channels):
            label = (state + sign * CHARGE_STEPS[channel % CLASSES]) % sectors
            groups.setdefault(label, []).append((state, channel))
    return [groups[label] for label in sorted(groups)]


def even(count):
    return count + count % 2


def spread_matrix(groups, channels, states):
    rows = []
    for group in groups:
        block = np.zeros((even(len(group)), ROWS, states * channels), np.float32)
        for index, (state, channel) in enumerate(group):
            block[index, :, state * channels + channel] = 1
        rows.append(block.reshape(-1, states * channels))
    return np.concatenate(rows)


def expand_kernel(sizes, weight_ref, spread_ref, out_ref):
    start = 0
    for size in sizes:
        spread = spread_ref[pl.ds(start, size), :]
        picked = jnp.dot(spread, weight_ref[...], preferred_element_type=jnp.float32)
        full = lax.dot_general(
            picked.astype(jnp.bfloat16),
            spread,
            (((1,), (1,)), ((), ())),
            preferred_element_type=jnp.float32,
        )
        row = lax.broadcasted_iota(jnp.int32, full.shape, 0)
        column = lax.broadcasted_iota(jnp.int32, full.shape, 1)
        same = lax.rem(row, ROWS) == lax.rem(column, ROWS)
        out_ref[pl.ds(start, size), pl.ds(0, size)] = jnp.where(same, full, 0.0).astype(
            jnp.bfloat16
        )
        start += size


def mix_channels(groups, channels, weight_ref, mixed_ref, write, offset, height):
    def step(index, carry):
        first = pl.multiple_of(index * 2 * ROWS, 2 * ROWS)
        start = 0
        for group in groups:
            size = even(len(group)) * ROWS
            parts = []
            for state, channel in group:
                rows = (state * channels + channel) * height + first
                halves = [
                    mixed_ref[pl.ds(pl.multiple_of(rows + half * ROWS, ROWS), ROWS), :]
                    for half in range(2)
                ]
                parts.append(jnp.concatenate(halves, axis=1))
            if len(group) % 2:
                parts.append(parts[0])
            operand = jnp.concatenate(parts, axis=0).astype(jnp.bfloat16)
            product = jnp.dot(
                weight_ref[pl.ds(start, size), pl.ds(0, size)],
                operand,
                preferred_element_type=jnp.float32,
            )
            block = product.shape[1] // 2
            for number, pair in enumerate(group):
                rows = product[number * ROWS : (number + 1) * ROWS]
                both = jnp.concatenate([rows[:, :block], rows[:, block:]], axis=0)
                write(*pair, pl.multiple_of(offset + first, 2 * ROWS), both.astype(jnp.bfloat16))
            start += size
        return carry

    lax.fori_loop(0, height // (2 * ROWS), step, 0)


def by_parts(block, body):
    height = block // PARTS

    def one(part, carry):
        body(pl.multiple_of(part * height, height), height)
        return carry

    lax.fori_loop(0, PARTS, one, 0)


def into(gathered_ref, channels, block):
    def write(state, channel, first, rows):
        start = (state * channels + channel) * block
        gathered_ref[pl.ds(pl.multiple_of(start + first, 2 * ROWS), 2 * ROWS), :] = rows

    return write


def batches(items, most):
    pieces = -(-len(items) // most)
    size = -(-len(items) // pieces)
    return [items[start : start + size] for start in range(0, len(items), size)]


def rows_of(chunks, channel, offset, height):
    size = chunks[0].shape[0]
    return chunks[channel // size][channel % size, pl.ds(offset, height), :]


def channel_of(chunks, channel):
    size = chunks[0].shape[0]
    return chunks[channel // size][channel % size]


def put_channel(chunks, channel, value):
    size = chunks[0].shape[0]
    chunks[channel // size][channel % size] = value


def count_channels(chunks):
    return sum(chunk.shape[0] for chunk in chunks)


def mix_left(env, tensors, mixed_ref, offset, height):
    channels, block = count_channels(env), env[0].shape[1]
    for cls in range(CLASSES):
        right = jnp.concatenate(tensors[cls], axis=1)
        for batch in batches(list(range(cls, channels, CLASSES)), 5):
            rows = jnp.concatenate(
                [rows_of(env, channel, offset, height) for channel in batch], axis=0
            )
            product = jnp.dot(rows, right, preferred_element_type=jnp.float32)
            for number, channel in enumerate(batch):
                for t in range(len(tensors[cls])):
                    mixed_ref[pl.ds((t * channels + channel) * height, height), :] = product[
                        number * height : (number + 1) * height, t * block : (t + 1) * block
                    ]


def left_kernel(groups, states, pieces, *refs):
    env, (tensor_ref, weight_ref) = refs[:pieces], refs[pieces : pieces + 2]
    outs, mixed_ref = refs[pieces + 2 : -1], refs[-1]
    channels, block = count_channels(env), env[0].shape[1]

    def write(state, channel, first, rows):
        size = channels // pieces
        out_ref = outs[state * pieces + channel // size]
        out_ref[channel % size, pl.ds(first, 2 * ROWS), :] = rows

    def body(offset, height):
        tensors = [[tensor_ref[cls, t] for t in range(states)] for cls in range(CLASSES)]
        mix_left(env, tensors, mixed_ref, offset, height)
        mix_channels(groups, channels, weight_ref, mixed_ref, write, offset, height)

    by_parts(block, body)


def left_close_kernel(iso_ref, gathered_ref, moved_ref, out_ref, square_ref):
    channels, block, _ = gathered_ref.shape
    square = jnp.zeros((ROWS, block), jnp.float32)
    for batch in batches(list(range(channels)), 2):
        right = jnp.concatenate([gathered_ref[channel] for channel in batch], axis=1)
        product = lax.dot_general(
            iso_ref[...], right, (((0,), (0,)), ((), ())), preferred_element_type=jnp.float32
        )
        for number, channel in enumerate(batch):
            part = product[:, number * block : (number + 1) * block]
            part = part + moved_ref[channel].astype(jnp.float32)
            out_ref[channel] = part.astype(jnp.bfloat16)
            square = square + jnp.sum((part * part).reshape(-1, ROWS, block), axis=0)
    square_ref[...] = square


def right_kernel(groups, states, pieces, *refs):
    envs = [refs[t * pieces : (t + 1) * pieces] for t in range(states)]
    refs = refs[states * pieces :]
    own_ref, tensor_ref, weight_ref = refs[:3]
    outs, (square_ref, mixed_ref, gathered_ref) = refs[3 : 3 + pieces], refs[3 + pieces :]
    channels, block = count_channels(envs[0]), envs[0][0].shape[1]
    zero = jnp.zeros((block, block), jnp.bfloat16)
    write = into(gathered_ref, channels, block)

    def body(offset, height):
        for pair in batches(list(range(states)), 2):
            own = jnp.concatenate(
                [
                    jnp.concatenate([own_ref[t] if t == other else zero for other in pair], axis=1)
                    for t in pair
                ],
                axis=0,
            )
            for batch in batches(list(range(channels)), 6):
                rows = jnp.concatenate(
                    [
                        jnp.concatenate(
                            [rows_of(envs[t], channel, offset, height) for channel in batch], axis=0
                        )
                        for t in pair
                    ],
                    axis=1,
                )
                product = lax.dot_general(
                    rows, own, (((1,), (1,)), ((), ())), preferred_element_type=jnp.float32
                )
                for number, t in enumerate(pair):
                    start = (t * channels + batch[0]) * height
                    mixed_ref[pl.ds(start, len(batch) * height), :] = product[
                        :, number * block : (number + 1) * block
                    ]
        mix_channels(groups, channels, weight_ref, mixed_ref, write, offset, height)

    by_parts(block, body)
    square = jnp.zeros((ROWS, block), jnp.float32)
    for cls in range(CLASSES):
        left = jnp.concatenate([tensor_ref[cls, s] for s in range(states)], axis=1)
        for batch in batches(list(range(cls, channels, CLASSES)), 2):
            right = jnp.concatenate(
                [
                    jnp.concatenate(
                        [
                            gathered_ref[pl.ds((s * channels + channel) * block, block), :]
                            for s in range(states)
                        ],
                        axis=0,
                    )
                    for channel in batch
                ],
                axis=1,
            )
            product = jnp.dot(left, right, preferred_element_type=jnp.float32)
            for number, channel in enumerate(batch):
                part = product[:, number * block : (number + 1) * block]
                put_channel(outs, channel, part.astype(jnp.bfloat16))
                square = square + jnp.sum((part * part).reshape(-1, ROWS, block), axis=0)
    square_ref[...] = square


ENV_LANE = 5
LANES = 128


def quotient(table, entry_count):
    def total(x):
        return jnp.sum(x, axis=0, keepdims=True)

    squares = [
        total(table[:, lane : lane + 1]) for lane in range(ENV_LANE, ENV_LANE + 2 * ENV_STEPS + 1)
    ]
    scale = jnp.ones((1, 1), jnp.float32)
    for side in range(2):
        side_scale = jnp.ones((1, 1), jnp.float32)
        for square in squares[side * ENV_STEPS : (side + 1) * ENV_STEPS]:
            side_scale = side_scale * lax.rsqrt(side_scale * side_scale * square / entry_count + TINY)
        scale = scale * side_scale
    a, b, e, c, unit = (table[:, lane : lane + 1] for lane in range(ENV_LANE))
    a, e, unit = scale * a, scale * e, scale * unit
    c = unit * unit * c
    whole_a, whole_b = total(a), total(b)
    energy = whole_a / (whole_b + TINY)
    off = e - energy
    residual_sq = total(c + 2.0 * off * (a - e * b) + off * off * b)
    factor = 0.5 * jnp.sqrt(whole_b / (residual_sq + TINY))
    square = whole_b - 2.0 * factor * (whole_a - energy * whole_b) + factor * factor * residual_sq
    return scale, energy, factor, square, squares[2 * ENV_STEPS]


def updated(vector, image, scale, energy, factor):
    return vector - factor * (scale * image - energy * vector)


def sum_all(x):
    return jnp.sum(jnp.sum(x, axis=0, keepdims=True), axis=1, keepdims=True)


def operator_front_kernel(groups, states, pieces, *refs):
    env, refs = refs[:pieces], refs[pieces:]
    weight_ref, classes, refs = refs[0], refs[1 : 1 + CLASSES], refs[1 + CLASSES :]
    gathered_ref, mixed_ref = refs
    channels, block = count_channels(env), env[0].shape[1]
    write = into(gathered_ref, channels, block)

    def body(offset, height):
        tensors = [[classes[cls][t] for t in range(states)] for cls in range(CLASSES)]
        mix_left(env, tensors, mixed_ref, offset, height)
        mix_channels(groups, channels, weight_ref, mixed_ref, write, offset, height)

    by_parts(block, body)


def products(rights, gathered_ref, s):
    channels, block = count_channels(rights[0]), rights[0][0].shape[1]
    total = jnp.zeros((block, block), jnp.float32)
    for batch in batches(list(range(channels)), 6):
        left = jnp.concatenate(
            [gathered_ref[pl.ds((s * channels + channel) * block, block), :] for channel in batch],
            axis=1,
        )
        right = jnp.concatenate([channel_of(rights[s], channel) for channel in batch], axis=0)
        total = total + jnp.dot(left, right, preferred_element_type=jnp.float32)
    return total


def write_sums(vector, image, squares, sums_ref):
    a, b = sum_all(vector * image), sum_all(vector * vector)
    e = jnp.where(b > 0, a / jnp.where(b > 0, b, 1.0), 0.0)
    residual = image - e * vector
    unit = jnp.max(jnp.max(jnp.abs(residual), axis=0, keepdims=True), axis=1, keepdims=True)
    unit = jnp.where(unit > 0, unit, 1.0)
    residual = residual / unit
    lane = lax.broadcasted_iota(jnp.int32, sums_ref.shape, 1)
    sums = jnp.zeros(sums_ref.shape, jnp.float32)
    values = (a, b, e, sum_all(residual * residual), unit, *(sum_all(x[...]) for x in squares))
    for place, value in enumerate(values):
        sums = jnp.where(lane == place, value, sums)
    sums_ref[...] = sums


def flat(ref):
    states, block, _ = ref.shape
    return ref[...].reshape(states * block, block)


UNIT_ROWS = 16


def power_above(x):
    top = jnp.max(jnp.max(jnp.abs(x), axis=0, keepdims=True), axis=1, keepdims=True)
    steps = jnp.ceil(jnp.log(jnp.where(top > 0, top, 1.0)) * (1 / np.log(2)))
    return jnp.exp(steps * np.log(2)).astype(jnp.bfloat16).astype(jnp.float32)


def operator_back_kernel(states, pieces, *refs):
    rights = [refs[t * pieces : (t + 1) * pieces] for t in range(states)]
    refs = refs[states * pieces :]
    squares, refs = refs[: 2 * ENV_STEPS + 1], refs[2 * ENV_STEPS + 1 :]
    gathered_ref, vector_ref, image_ref, half_ref, sums_ref = refs
    for s in range(states):
        image_ref[s] = products(rights, gathered_ref, s)
    image = flat(image_ref)
    unit = power_above(image)
    half_ref[: image.shape[0]] = (image / unit).astype(jnp.bfloat16)
    half_ref[image.shape[0] :] = jnp.broadcast_to(unit, (UNIT_ROWS, LANES)).astype(jnp.bfloat16)
    write_sums(flat(vector_ref), image, squares, sums_ref)


def operator_whole_kernel(groups, states, pieces, front_count, *refs):
    front, refs = refs[:front_count], refs[front_count:]
    env_and_weight, sent = front[:-CLASSES], front[-CLASSES:]
    rights = [refs[t * pieces : (t + 1) * pieces] for t in range(states)]
    image_ref, unit_ref, gathered_ref, tensor_ref, mixed_ref = refs[states * pieces :]
    block = image_ref.shape[1]
    units = [
        x[pl.ds(states * block, UNIT_ROWS), :].astype(jnp.float32)[:1, :1] for x in sent
    ]
    unit = functools.reduce(jnp.maximum, units)
    unit_ref[...] = jnp.broadcast_to(unit, unit_ref.shape)
    for cls in range(CLASSES):
        for t in range(states):
            tensor = sent[cls][pl.ds(t * block, block), :].astype(jnp.float32)
            tensor_ref[cls, t] = (tensor * (units[cls] / unit)).astype(jnp.bfloat16)
    classes = [tensor_ref.at[cls] for cls in range(CLASSES)]
    operator_front_kernel(groups, states, pieces, *env_and_weight, *classes, gathered_ref, mixed_ref)
    for s in range(states):
        image_ref[s] = products(rights, gathered_ref, s)


def renew_kernel(entry_count, *refs):
    table_ref, vector_ref, image_ref, second_ref, unit_ref = refs[:5]
    squares, (both_ref, sums_ref) = refs[5:-2], refs[-2:]
    states, block, _ = vector_ref.shape
    scale, energy, factor, _, _ = quotient(table_ref[...], entry_count)
    vector, image = flat(vector_ref), flat(image_ref)
    part = factor * (scale * unit_ref[:, :1])
    new_image = (1.0 + factor * energy) * image - part * flat(second_ref)
    new = updated(vector, image, scale, energy, factor)
    both_ref[:, 0] = new.reshape(states, block, block)
    both_ref[:, 1] = new_image.reshape(states, block, block)
    write_sums(new, new_image, squares, sums_ref)


def energy_kernel(entry_count, table_ref, out_ref):
    energy = quotient(table_ref[...], entry_count)[1]
    out_ref[...] = jnp.broadcast_to(energy, out_ref.shape)


def polar_kernel(entry_count, both_ref, table_ref, centre_ref, out_ref):
    states, _, block, _ = both_ref.shape
    rows = lax.broadcasted_iota(jnp.int32, (block, block), 0)
    columns = lax.broadcasted_iota(jnp.int32, (block, block), 1)
    unit = (rows == columns).astype(jnp.float32)

    def product(x, y, contract=((1,), (0,))):
        return lax.dot_general(
            x, y, (contract, ((), ())), precision=HIGHEST, preferred_element_type=jnp.float32
        )

    scale, energy, factor, square, centre_sq = quotient(table_ref[...], entry_count)
    vector = updated(
        both_ref[:, 0].reshape(states * block, block),
        both_ref[:, 1].reshape(states * block, block),
        scale,
        energy,
        factor,
    ) * lax.rsqrt(square + TINY)
    centre = centre_ref[...].astype(jnp.float32) * lax.rsqrt(centre_sq + TINY)
    grams = [product(x, x, ((0,), (0,))) for x in (vector, centre)]
    totals = [unit, unit]
    for step in range(POLAR):
        factors = [1.5 * unit - 0.5 * gram for gram in grams]
        totals = [
            factor if step == 0 else product(total, factor)
            for total, factor in zip(totals, factors)
        ]
        if step < POLAR - 1:
            grams = [
                product(product(factor, gram), factor) for gram, factor in zip(grams, factors)
            ]
    closing = product(totals[0], product(centre, totals[1]), ((1,), (1,)))
    out_ref[...] = product(vector, closing).reshape(states, block, block).astype(jnp.bfloat16)


def call(kernel, out_shape, scratch_shapes, flops, operands):
    return pl.pallas_call(
        kernel,
        out_shape=out_shape,
        scratch_shapes=scratch_shapes,
        compiler_params=pltpu.CompilerParams(vmem_limit_bytes=VMEM_LIMIT),
        cost_estimate=pl.CostEstimate(
            flops=flops,
            bytes_accessed=sum(int(np.prod(x.shape)) * x.dtype.itemsize for x in operands),
            transcendentals=0,
        ),
    )(*operands)


def float_out(*shape):
    return jax.ShapeDtypeStruct(shape, jnp.float32)


def half_out(*shape):
    return jax.ShapeDtypeStruct(shape, jnp.bfloat16)


def work(states, channels, block):
    return 4 * states * channels * block**3 + 2 * (states * channels * block) ** 2


def expanded(weight, groups, channels, states):
    spread = spread_matrix(groups, channels, states)
    sizes = tuple(even(len(group)) * ROWS for group in groups)
    return call(
        functools.partial(expand_kernel, sizes),
        half_out(spread.shape[0], -(-max(sizes) // 128) * 128),
        [],
        2 * spread.size * spread.shape[0],
        (weight, jnp.asarray(spread, jnp.bfloat16)),
    )


def left_front(env, tensors, weight, groups):
    channels, block = count_channels(env), env[0].shape[1]
    states, pieces = tensors.shape[1], len(env)
    outs = call(
        functools.partial(left_kernel, groups, states, pieces),
        [half_out(channels // pieces, block, block)] * (states * pieces),
        [pltpu.VMEM((states * channels * block // PARTS, block), jnp.float32)],
        work(states, channels, block),
        (*env, tensors, weight),
    )
    return [outs[s * pieces : (s + 1) * pieces] for s in range(states)]


def left_close(iso, gathered, moved):
    channels, block, _ = gathered.shape
    return call(
        left_close_kernel,
        (half_out(channels, block, block), float_out(ROWS, block)),
        [],
        2 * channels * block**3,
        (iso, gathered, moved),
    )


def right_whole(envs, own, tensors, weight, groups):
    channels, block = count_channels(envs[0]), envs[0][0].shape[1]
    states, pieces = len(envs), len(envs[0])
    outs = call(
        functools.partial(right_kernel, groups, states, pieces),
        [half_out(channels // pieces, block, block)] * pieces + [float_out(ROWS, block)],
        [
            pltpu.VMEM((states * channels * block // PARTS, block), jnp.float32),
            pltpu.VMEM((states * channels * block, block), jnp.bfloat16),
        ],
        work(states, channels, block),
        (*(chunk for env in envs for chunk in env), own, tensors, weight),
    )
    return outs[:pieces], outs[pieces]


def front_scratch(states, channels, block):
    return [pltpu.VMEM((states * channels * block // PARTS, block), jnp.float32)]


def operator_front(env, weight, groups, classes):
    channels, block = count_channels(env), env[0].shape[1]
    states, pieces = classes[0].shape[0], len(env)
    return call(
        functools.partial(operator_front_kernel, groups, states, pieces),
        half_out(states * channels * block, block),
        front_scratch(states, channels, block),
        work(states, channels, block),
        (*env, weight, *classes),
    )


def operator_back(rights, squares, gathered, vector):
    channels, block = count_channels(rights[0]), rights[0][0].shape[1]
    states, pieces = len(rights), len(rights[0])
    return call(
        functools.partial(operator_back_kernel, states, pieces),
        (
            float_out(states, block, block),
            half_out(states * block + UNIT_ROWS, block),
            float_out(1, LANES),
        ),
        [],
        2 * states * channels * block**3,
        (*(chunk for right in rights for chunk in right), *squares, gathered, vector),
    )


def operator_whole(env, weight, groups, classes, rights):
    channels, block = count_channels(env), env[0].shape[1]
    states, pieces = len(rights), len(env)
    front = (*env, weight, *classes)
    return call(
        functools.partial(operator_whole_kernel, groups, states, pieces, len(front)),
        (float_out(states, block, block), float_out(1, LANES)),
        [
            pltpu.VMEM((states * channels * block, block), jnp.bfloat16),
            pltpu.VMEM((CLASSES, states, block, block), jnp.bfloat16),
            *front_scratch(states, channels, block),
        ],
        work(states, channels, block) + 2 * states * channels * block**3,
        (*front, *(chunk for right in rights for chunk in right)),
    )


def renewed(table, vector, image, second, unit, squares, entry_count):
    states, block, _ = vector.shape
    return call(
        functools.partial(renew_kernel, entry_count),
        (float_out(states, 2, block, block), float_out(1, LANES)),
        [],
        0,
        (table, vector, image, second, unit, *squares),
    )


def polar(both, table, centre, entry_count):
    states, _, block, _ = both.shape
    return call(
        functools.partial(polar_kernel, entry_count),
        half_out(states, block, block),
        [],
        600 * block**3,
        (both, table, centre),
    )


def energy_of(table, entry_count):
    return call(
        functools.partial(energy_kernel, entry_count), float_out(1, LANES), [], 0, (table,)
    )


def charge_mask(channels, states, sectors):
    charge = np.array([CHARGE_STEPS[channel % CLASSES] for channel in range(channels)])
    state = np.arange(states)
    balance = (
        charge[:, None, None, None]
        + state[None, None, None, :]
        - state[None, None, :, None]
        - charge[None, :, None, None]
    )
    return jnp.asarray((balance % sectors == 0).astype(np.float32)).astype(jnp.bfloat16)


def weight_matrices(mpo, pattern, sectors):
    channels, _, states, _ = mpo.shape
    allowed = charge_mask(channels, states, sectors)
    weights = mpo * pattern[:, :, None, None].astype(jnp.bfloat16) * allowed
    size = states * channels
    left = jnp.transpose(weights, (2, 1, 3, 0)).reshape(size, size)
    right = jnp.transpose(weights, (2, 0, 3, 1)).reshape(size, size)
    return jnp.stack([left, right])


def other_classes_of(places, x):
    one, minus = places.ahead(x, 1), places.ahead(x, -1)
    return one, minus, places.ahead(one, 1), places.ahead(minus, -1)


def classes_of(places, x):
    return jnp.stack([x, *other_classes_of(places, x)])


def other_classes_at_once(places, x):
    return tuple(places.ahead(x, charge) for charge in CHARGE_STEPS[1:])


def after(first, then):
    return lax.optimization_barrier((first, then))


def local(left_iso, right_iso, centre, left_env, right_env, mpo, pattern):
    sites, secs = lax.axis_size("site"), lax.axis_size("sec")
    places = Places(sites, secs)
    left_iso, right_iso, centre = left_iso[0, :, 0], right_iso[0, :, 0], centre[0, 0]
    states, block, _ = left_iso.shape
    channels = mpo.shape[1]
    entry_count = left_env.size * secs
    left_groups = label_groups(channels, states, secs, 1)
    right_groups = label_groups(channels, states, secs, -1)

    pieces = PIECES if channels % PIECES == 0 else 1

    def ahead(env, by, chain_by=0):
        return [places.ahead(chunk, by, chain_by) for chunk in env]

    first = places.fetch(jnp.concatenate([right_env[0, :, 0], left_iso, right_iso]))
    left_isos = [first[channels : channels + states]]
    right_isos = [first[channels + states :]]
    for step in range(1, ENV_STEPS):
        left_isos.append(places.fetch(left_iso, step))
        right_isos.append(places.fetch(right_iso, -step))
    own_tensors = places.fetch(jnp.concatenate([left_iso, centre[None]]), ENV_STEPS)
    right = jnp.split(first[:channels], pieces)
    right, left_env = after(right, left_env)
    left = jnp.split(places.fetch(left_env[0, :, 0]), pieces)
    rolled = [
        classes_of(places, jnp.concatenate([left_isos[step], right_isos[step]]))
        for step in range(ENV_STEPS)
    ]
    own_iso, own_centre = own_tensors[:states], own_tensors[states]
    centres = [own_centre] + [places.ahead(own_centre, s) for s in range(1, states)]

    gathered_weights = lax.all_gather(weight_matrices(mpo[0], pattern[0], secs), "site")
    chain = places.my_chain()

    def weight_of(site_by, kind):
        weight = lax.dynamic_index_in_dim(
            gathered_weights, (chain + site_by) % sites, 0, False
        )[kind]
        return expanded(weight, (left_groups, right_groups)[kind], channels, states)

    weights = (
        [weight_of(step, 0) for step in range(ENV_STEPS + 1)],
        [weight_of(-step, 1) for step in range(ENV_STEPS)],
    )
    vector = jnp.einsum(
        "sxy,syz->sxz", own_iso, jnp.stack(centres), preferred_element_type=jnp.float32
    )
    half_vector = vector.astype(jnp.bfloat16)
    rolled_vector = (half_vector, *other_classes_of(places, half_vector))
    right, weights = after(right, weights)
    centre_float = own_centre.astype(jnp.float32)
    centre_square = jnp.sum((centre_float * centre_float).reshape(-1, ROWS, block), axis=0)

    left_squares, right_squares = [], []
    for step in range(ENV_STEPS):
        envs = [right]
        for t in range(1, states):
            if step == 0 and t == states - 1:
                left, envs[-1] = after(left, envs[-1])
            envs.append(ahead(envs[-1], 1))
        if step == 0:
            rolled, envs = after(rolled, envs)
        if step == 1:
            rolled_vector, envs = after(rolled_vector, envs)
        right, square = right_whole(
            envs,
            right_isos[step],
            rolled[step][:, states:],
            weights[1][step],
            right_groups,
        )
        right_squares.append(square)

        gathered = left_front(left, rolled[step][:, :states], weights[0][step], left_groups)
        moved = [None] * pieces
        for s in reversed(range(1, states)):
            for piece in range(pieces):
                part = jnp.einsum(
                    "xy,vxz->vyz",
                    left_isos[step][s],
                    gathered[s][piece],
                    preferred_element_type=jnp.float32,
                )
                if moved[piece] is not None:
                    part = part + moved[piece].astype(jnp.float32)
                moved[piece] = places.ahead(part.astype(jnp.bfloat16), -1)
        closed = [
            left_close(left_isos[step][0], gathered[0][piece], moved[piece])
            for piece in range(pieces)
        ]
        left = [env for env, _ in closed]
        left_squares.append(sum(square for _, square in closed))

    if (2 * ENV_STEPS) % sites:
        right = ahead(right, 0, 2 * ENV_STEPS)
        right_squares = ahead(right_squares, 0, 2 * ENV_STEPS)
    squares = left_squares + right_squares + [centre_square]
    rights = [right]
    for s in range(1, states):
        rights.append(ahead(rights[-1], 1))
    weight = weights[0][ENV_STEPS]
    gathered = operator_front(left, weight, left_groups, rolled_vector)
    image, sent, own_sums = operator_back(rights, squares, gathered, vector)
    rolled_image = (sent, *other_classes_at_once(places, sent))
    second, unit = operator_whole(left, weight, left_groups, rolled_image, rights)
    table = places.collect(own_sums)
    both, own_sums = renewed(table, vector, image, second, unit, squares, entry_count)
    table = places.collect(own_sums)

    columns = jnp.stack([both[0]] + [places.ahead(both[s], -s) for s in range(1, states)])
    home_table = places.send_home(table, ENV_STEPS, 0)
    home_table, columns = after(home_table, columns)
    column_left = polar(columns, table, own_centre, entry_count)
    new_left = jnp.stack(
        [places.send_home(column_left[s], ENV_STEPS, -s) for s in range(states)]
    )
    energy = energy_of(home_table, entry_count)
    return new_left[None, :, None], energy[0, :1]


def solution(mesh):
    placed = (
        P("site", None, "sec", None, None),
        P("site", None, "sec", None, None),
        P("site", "sec", None, None),
        P("site", None, "sec", None, None),
        P("site", None, "sec", None, None),
        P("site", None, None, None, None),
        P("site", None, None),
    )
    return jax.shard_map(
        local,
        mesh=mesh,
        in_specs=placed,
        out_specs=(P("site", None, "sec", None, None), P("site")),
        check_vma=False,
    )
```

```python
import functools

import jax
import jax.numpy as jnp
import numpy as np
from jax import lax
from jax.experimental import pallas as pl
from jax.experimental.pallas import tpu as pltpu
from jax.sharding import PartitionSpec as P

ENV_STEPS = 2
POLAR = 6

TINY = 1e-06
CHARGE_STEPS = (0, 1, -1, 2, -2)
CLASSES = len(CHARGE_STEPS)
BOTH = ("site", "sec")
VMEM_LIMIT = 20 * 1024 * 1024
PIECES = 2


class Places:
    def __init__(self, sites, secs):
        self.sites, self.secs = sites, secs
        self.half = secs // 2
        self.up = (self.half + 1) // 2

    def home(self, site, sector):
        return (site % self.sites) * self.secs + sector % self.secs

    def position(self, place):
        back = self.half - 1 + self.up - place
        if isinstance(place, int):
            return place if place < self.up else back
        return jnp.where(place < self.up, place, back)

    def slot(self, chain, sector):
        chain, sector = chain % self.sites, sector % self.secs
        place = chain % 2 * self.half + self.position(sector // 2)
        return (chain // 2 * 2 + sector % 2) * self.secs + place

    def pairs(self, source, target):
        return [
            (source(chain, sector), target(chain, sector))
            for chain in range(self.sites)
            for sector in range(self.secs)
        ]

    def fetch(self, x, site_by=0, sec_by=0):
        return lax.ppermute(
            x, BOTH, self.pairs(lambda g, k: self.home(g + site_by, k + sec_by), self.slot)
        )

    def send_home(self, x, site_by, sec_by):
        return lax.ppermute(
            x, BOTH, self.pairs(self.slot, lambda g, k: self.home(g + site_by, k + sec_by))
        )

    def ahead(self, x, by, chain_by=0):
        return lax.ppermute(
            x, BOTH, self.pairs(lambda g, k: self.slot(g + chain_by, k + by), self.slot)
        )

    def partner(self, x, bit):
        return lax.ppermute(x, BOTH, self.pairs(lambda g, k: self.slot(g, k ^ bit), self.slot))

    def my_chain(self):
        return lax.axis_index("site") // 2 * 2 + lax.axis_index("sec") // self.half

    def my_sector(self):
        position = self.position(lax.axis_index("sec") % self.half)
        return 2 * position + lax.axis_index("site") % 2

    def collect(self, values):
        sector = self.my_sector()
        table = values
        bit = 1
        while bit < self.secs:
            other = self.partner(table, bit)
            first = (sector & bit) == 0
            table = jnp.where(
                first, jnp.concatenate([table, other]), jnp.concatenate([other, table])
            )
            bit *= 2
        return table


ROWS = 8
PARTS = 2


def label_groups(channels, states, sectors, sign):
    groups = {}
    for state in range(states):
        for channel in range(channels):
            label = (state + sign * CHARGE_STEPS[channel % CLASSES]) % sectors
            groups.setdefault(label, []).append((state, channel))
    return [groups[label] for label in sorted(groups)]


def even(count):
    return count + count % 2


def spread_matrix(groups, channels, states):
    rows = []
    for group in groups:
        block = np.zeros((even(len(group)), ROWS, states * channels), np.float32)
        for index, (state, channel) in enumerate(group):
            block[index, :, state * channels + channel] = 1
        rows.append(block.reshape(-1, states * channels))
    return np.concatenate(rows)


def expand_kernel(sizes, weight_ref, spread_ref, out_ref):
    start = 0
    for size in sizes:
        spread = spread_ref[pl.ds(start, size), :]
        picked = jnp.dot(spread, weight_ref[...], preferred_element_type=jnp.float32)
        full = lax.dot_general(
            picked.astype(jnp.bfloat16),
            spread,
            (((1,), (1,)), ((), ())),
            preferred_element_type=jnp.float32,
        )
        row = lax.broadcasted_iota(jnp.int32, full.shape, 0)
        column = lax.broadcasted_iota(jnp.int32, full.shape, 1)
        same = lax.rem(row, ROWS) == lax.rem(column, ROWS)
        out_ref[pl.ds(start, size), pl.ds(0, size)] = jnp.where(same, full, 0.0).astype(
            jnp.bfloat16
        )
        start += size


def mix_channels(groups, channels, weight_ref, mixed_ref, write, offset, height):
    def step(index, carry):
        first = pl.multiple_of(index * 2 * ROWS, 2 * ROWS)
        start = 0
        for group in groups:
            size = even(len(group)) * ROWS
            parts = []
            for state, channel in group:
                rows = (state * channels + channel) * height + first
                halves = [
                    mixed_ref[pl.ds(pl.multiple_of(rows + half * ROWS, ROWS), ROWS), :]
                    for half in range(2)
                ]
                parts.append(jnp.concatenate(halves, axis=1))
            if len(group) % 2:
                parts.append(parts[0])
            operand = jnp.concatenate(parts, axis=0).astype(jnp.bfloat16)
            product = jnp.dot(
                weight_ref[pl.ds(start, size), pl.ds(0, size)],
                operand,
                preferred_element_type=jnp.float32,
            )
            block = product.shape[1] // 2
            for number, pair in enumerate(group):
                rows = product[number * ROWS : (number + 1) * ROWS]
                both = jnp.concatenate([rows[:, :block], rows[:, block:]], axis=0)
                write(*pair, pl.multiple_of(offset + first, 2 * ROWS), both.astype(jnp.bfloat16))
            start += size
        return carry

    lax.fori_loop(0, height // (2 * ROWS), step, 0)


def by_parts(block, body):
    height = block // PARTS

    def one(part, carry):
        body(pl.multiple_of(part * height, height), height)
        return carry

    lax.fori_loop(0, PARTS, one, 0)


def into(gathered_ref, channels, block):
    def write(state, channel, first, rows):
        start = (state * channels + channel) * block
        gathered_ref[pl.ds(pl.multiple_of(start + first, 2 * ROWS), 2 * ROWS), :] = rows

    return write


def batches(items, most):
    pieces = -(-len(items) // most)
    size = -(-len(items) // pieces)
    return [items[start : start + size] for start in range(0, len(items), size)]


def rows_of(chunks, channel, offset, height):
    size = chunks[0].shape[0]
    return chunks[channel // size][channel % size, pl.ds(offset, height), :]


def channel_of(chunks, channel):
    size = chunks[0].shape[0]
    return chunks[channel // size][channel % size]


def put_channel(chunks, channel, value):
    size = chunks[0].shape[0]
    chunks[channel // size][channel % size] = value


def count_channels(chunks):
    return sum(chunk.shape[0] for chunk in chunks)


def mix_left(env, tensors, mixed_ref, offset, height):
    channels, block = count_channels(env), env[0].shape[1]
    for cls in range(CLASSES):
        right = jnp.concatenate(tensors[cls], axis=1)
        for batch in batches(list(range(cls, channels, CLASSES)), 5):
            rows = jnp.concatenate(
                [rows_of(env, channel, offset, height) for channel in batch], axis=0
            )
            product = jnp.dot(rows, right, preferred_element_type=jnp.float32)
            for number, channel in enumerate(batch):
                for t in range(len(tensors[cls])):
                    mixed_ref[pl.ds((t * channels + channel) * height, height), :] = product[
                        number * height : (number + 1) * height, t * block : (t + 1) * block
                    ]


def left_kernel(groups, states, pieces, *refs):
    env, (tensor_ref, weight_ref) = refs[:pieces], refs[pieces : pieces + 2]
    outs, mixed_ref = refs[pieces + 2 : -1], refs[-1]
    channels, block = count_channels(env), env[0].shape[1]

    def write(state, channel, first, rows):
        size = channels // pieces
        out_ref = outs[state * pieces + channel // size]
        out_ref[channel % size, pl.ds(first, 2 * ROWS), :] = rows

    def body(offset, height):
        tensors = [[tensor_ref[cls, t] for t in range(states)] for cls in range(CLASSES)]
        mix_left(env, tensors, mixed_ref, offset, height)
        mix_channels(groups, channels, weight_ref, mixed_ref, write, offset, height)

    by_parts(block, body)


def left_close_kernel(iso_ref, gathered_ref, moved_ref, out_ref, square_ref):
    channels, block, _ = gathered_ref.shape
    square = jnp.zeros((ROWS, block), jnp.float32)
    for batch in batches(list(range(channels)), 2):
        right = jnp.concatenate([gathered_ref[channel] for channel in batch], axis=1)
        product = lax.dot_general(
            iso_ref[...], right, (((0,), (0,)), ((), ())), preferred_element_type=jnp.float32
        )
        for number, channel in enumerate(batch):
            part = product[:, number * block : (number + 1) * block]
            part = part + moved_ref[channel].astype(jnp.float32)
            out_ref[channel] = part.astype(jnp.bfloat16)
            square = square + jnp.sum((part * part).reshape(-1, ROWS, block), axis=0)
    square_ref[...] = square


def right_kernel(groups, states, pieces, *refs):
    envs = [refs[t * pieces : (t + 1) * pieces] for t in range(states)]
    refs = refs[states * pieces :]
    own_ref, tensor_ref, weight_ref = refs[:3]
    outs, (square_ref, mixed_ref, gathered_ref) = refs[3 : 3 + pieces], refs[3 + pieces :]
    channels, block = count_channels(envs[0]), envs[0][0].shape[1]
    zero = jnp.zeros((block, block), jnp.bfloat16)
    write = into(gathered_ref, channels, block)

    def body(offset, height):
        for pair in batches(list(range(states)), 2):
            own = jnp.concatenate(
                [
                    jnp.concatenate([own_ref[t] if t == other else zero for other in pair], axis=1)
                    for t in pair
                ],
                axis=0,
            )
            for batch in batches(list(range(channels)), 6):
                rows = jnp.concatenate(
                    [
                        jnp.concatenate(
                            [rows_of(envs[t], channel, offset, height) for channel in batch], axis=0
                        )
                        for t in pair
                    ],
                    axis=1,
                )
                product = lax.dot_general(
                    rows, own, (((1,), (1,)), ((), ())), preferred_element_type=jnp.float32
                )
                for number, t in enumerate(pair):
                    start = (t * channels + batch[0]) * height
                    mixed_ref[pl.ds(start, len(batch) * height), :] = product[
                        :, number * block : (number + 1) * block
                    ]
        mix_channels(groups, channels, weight_ref, mixed_ref, write, offset, height)

    by_parts(block, body)
    square = jnp.zeros((ROWS, block), jnp.float32)
    for cls in range(CLASSES):
        left = jnp.concatenate([tensor_ref[cls, s] for s in range(states)], axis=1)
        for batch in batches(list(range(cls, channels, CLASSES)), 2):
            right = jnp.concatenate(
                [
                    jnp.concatenate(
                        [
                            gathered_ref[pl.ds((s * channels + channel) * block, block), :]
                            for s in range(states)
                        ],
                        axis=0,
                    )
                    for channel in batch
                ],
                axis=1,
            )
            product = jnp.dot(left, right, preferred_element_type=jnp.float32)
            for number, channel in enumerate(batch):
                part = product[:, number * block : (number + 1) * block]
                put_channel(outs, channel, part.astype(jnp.bfloat16))
                square = square + jnp.sum((part * part).reshape(-1, ROWS, block), axis=0)
    square_ref[...] = square


ENV_LANE = 5
LANES = 128


def quotient(table, entry_count):
    def total(x):
        return jnp.sum(x, axis=0, keepdims=True)

    squares = [
        total(table[:, lane : lane + 1]) for lane in range(ENV_LANE, ENV_LANE + 2 * ENV_STEPS + 1)
    ]
    scale = jnp.ones((1, 1), jnp.float32)
    for side in range(2):
        side_scale = jnp.ones((1, 1), jnp.float32)
        for square in squares[side * ENV_STEPS : (side + 1) * ENV_STEPS]:
            side_scale = side_scale * lax.rsqrt(side_scale * side_scale * square / entry_count + TINY)
        scale = scale * side_scale
    a, b, e, c, unit = (table[:, lane : lane + 1] for lane in range(ENV_LANE))
    a, e, unit = scale * a, scale * e, scale * unit
    c = unit * unit * c
    whole_a, whole_b = total(a), total(b)
    energy = whole_a / (whole_b + TINY)
    off = e - energy
    residual_sq = total(c + 2.0 * off * (a - e * b) + off * off * b)
    factor = 0.5 * jnp.sqrt(whole_b / (residual_sq + TINY))
    square = whole_b - 2.0 * factor * (whole_a - energy * whole_b) + factor * factor * residual_sq
    return scale, energy, factor, square, squares[2 * ENV_STEPS]


def updated(vector, image, scale, energy, factor):
    return vector - factor * (scale * image - energy * vector)


def sum_all(x):
    return jnp.sum(jnp.sum(x, axis=0, keepdims=True), axis=1, keepdims=True)


def operator_front_kernel(groups, states, pieces, *refs):
    env, refs = refs[:pieces], refs[pieces:]
    weight_ref, classes, refs = refs[0], refs[1 : 1 + CLASSES], refs[1 + CLASSES :]
    gathered_ref, mixed_ref = refs
    channels, block = count_channels(env), env[0].shape[1]
    write = into(gathered_ref, channels, block)

    def body(offset, height):
        tensors = [[classes[cls][t] for t in range(states)] for cls in range(CLASSES)]
        mix_left(env, tensors, mixed_ref, offset, height)
        mix_channels(groups, channels, weight_ref, mixed_ref, write, offset, height)

    by_parts(block, body)


def products(rights, gathered_ref, s):
    channels, block = count_channels(rights[0]), rights[0][0].shape[1]
    total = jnp.zeros((block, block), jnp.float32)
    for batch in batches(list(range(channels)), 6):
        left = jnp.concatenate(
            [gathered_ref[pl.ds((s * channels + channel) * block, block), :] for channel in batch],
            axis=1,
        )
        right = jnp.concatenate([channel_of(rights[s], channel) for channel in batch], axis=0)
        total = total + jnp.dot(left, right, preferred_element_type=jnp.float32)
    return total


def write_sums(vector, image, squares, sums_ref):
    a, b = sum_all(vector * image), sum_all(vector * vector)
    e = jnp.where(b > 0, a / jnp.where(b > 0, b, 1.0), 0.0)
    residual = image - e * vector
    unit = jnp.max(jnp.max(jnp.abs(residual), axis=0, keepdims=True), axis=1, keepdims=True)
    unit = jnp.where(unit > 0, unit, 1.0)
    residual = residual / unit
    lane = lax.broadcasted_iota(jnp.int32, sums_ref.shape, 1)
    sums = jnp.zeros(sums_ref.shape, jnp.float32)
    values = (a, b, e, sum_all(residual * residual), unit, *(sum_all(x[...]) for x in squares))
    for place, value in enumerate(values):
        sums = jnp.where(lane == place, value, sums)
    sums_ref[...] = sums


def flat(ref):
    states, block, _ = ref.shape
    return ref[...].reshape(states * block, block)


UNIT_ROWS = 16


def power_above(x):
    top = jnp.max(jnp.max(jnp.abs(x), axis=0, keepdims=True), axis=1, keepdims=True)
    steps = jnp.ceil(jnp.log(jnp.where(top > 0, top, 1.0)) * (1 / np.log(2)))
    return jnp.exp(steps * np.log(2)).astype(jnp.bfloat16).astype(jnp.float32)


def operator_back_kernel(states, pieces, *refs):
    rights = [refs[t * pieces : (t + 1) * pieces] for t in range(states)]
    refs = refs[states * pieces :]
    squares, refs = refs[: 2 * ENV_STEPS + 1], refs[2 * ENV_STEPS + 1 :]
    gathered_ref, vector_ref, image_ref, half_ref, sums_ref = refs
    for s in range(states):
        image_ref[s] = products(rights, gathered_ref, s)
    image = flat(image_ref)
    unit = power_above(image)
    half_ref[: image.shape[0]] = (image / unit).astype(jnp.bfloat16)
    half_ref[image.shape[0] :] = jnp.broadcast_to(unit, (UNIT_ROWS, LANES)).astype(jnp.bfloat16)
    write_sums(flat(vector_ref), image, squares, sums_ref)


def operator_whole_kernel(groups, states, pieces, front_count, *refs):
    front, refs = refs[:front_count], refs[front_count:]
    env_and_weight, sent = front[:-CLASSES], front[-CLASSES:]
    rights = [refs[t * pieces : (t + 1) * pieces] for t in range(states)]
    image_ref, unit_ref, gathered_ref, tensor_ref, mixed_ref = refs[states * pieces :]
    block = image_ref.shape[1]
    units = [
        x[pl.ds(states * block, UNIT_ROWS), :].astype(jnp.float32)[:1, :1] for x in sent
    ]
    unit = functools.reduce(jnp.maximum, units)
    unit_ref[...] = jnp.broadcast_to(unit, unit_ref.shape)
    for cls in range(CLASSES):
        for t in range(states):
            tensor = sent[cls][pl.ds(t * block, block), :].astype(jnp.float32)
            tensor_ref[cls, t] = (tensor * (units[cls] / unit)).astype(jnp.bfloat16)
    classes = [tensor_ref.at[cls] for cls in range(CLASSES)]
    operator_front_kernel(groups, states, pieces, *env_and_weight, *classes, gathered_ref, mixed_ref)
    for s in range(states):
        image_ref[s] = products(rights, gathered_ref, s)


def renew_kernel(entry_count, *refs):
    table_ref, vector_ref, image_ref, second_ref, unit_ref = refs[:5]
    squares, (both_ref, sums_ref) = refs[5:-2], refs[-2:]
    states, block, _ = vector_ref.shape
    scale, energy, factor, _, _ = quotient(table_ref[...], entry_count)
    vector, image = flat(vector_ref), flat(image_ref)
    part = factor * (scale * unit_ref[:, :1])
    new_image = (1.0 + factor * energy) * image - part * flat(second_ref)
    new = updated(vector, image, scale, energy, factor)
    both_ref[:, 0] = new.reshape(states, block, block)
    both_ref[:, 1] = new_image.reshape(states, block, block)
    write_sums(new, new_image, squares, sums_ref)


def energy_kernel(entry_count, table_ref, out_ref):
    energy = quotient(table_ref[...], entry_count)[1]
    out_ref[...] = jnp.broadcast_to(energy, out_ref.shape)


def polar_kernel(entry_count, both_ref, table_ref, centre_ref, out_ref):
    states, _, block, _ = both_ref.shape
    rows = lax.broadcasted_iota(jnp.int32, (block, block), 0)
    columns = lax.broadcasted_iota(jnp.int32, (block, block), 1)
    unit = (rows == columns).astype(jnp.float32)

    def halves(x):
        high = x.astype(jnp.bfloat16)
        return high, (x - high.astype(jnp.float32)).astype(jnp.bfloat16)

    def product(x, y, contract=((1,), (0,))):
        (x_high, x_low), (y_high, y_low) = halves(x), halves(y)
        parts = [
            lax.dot_general(left, right, (contract, ((), ())), preferred_element_type=jnp.float32)
            for left, right in ((x_high, y_low), (x_low, y_high), (x_high, y_high))
        ]
        return parts[0] + parts[1] + parts[2]

    scale, energy, factor, square, centre_sq = quotient(table_ref[...], entry_count)
    vector = updated(
        both_ref[:, 0].reshape(states * block, block),
        both_ref[:, 1].reshape(states * block, block),
        scale,
        energy,
        factor,
    ) * lax.rsqrt(square + TINY)
    centre = centre_ref[...].astype(jnp.float32) * lax.rsqrt(centre_sq + TINY)
    grams = [product(x, x, ((0,), (0,))) for x in (vector, centre)]
    totals = [unit, unit]
    for step in range(POLAR):
        factors = [1.5 * unit - 0.5 * gram for gram in grams]
        totals = [
            factor if step == 0 else product(total, factor)
            for total, factor in zip(totals, factors)
        ]
        if step < POLAR - 1:
            grams = [
                product(product(factor, gram), factor) for gram, factor in zip(grams, factors)
            ]
    closing = product(totals[0], product(centre, totals[1]), ((1,), (1,)))
    out_ref[...] = product(vector, closing).reshape(states, block, block).astype(jnp.bfloat16)


def call(kernel, out_shape, scratch_shapes, flops, operands):
    return pl.pallas_call(
        kernel,
        out_shape=out_shape,
        scratch_shapes=scratch_shapes,
        compiler_params=pltpu.CompilerParams(vmem_limit_bytes=VMEM_LIMIT),
        cost_estimate=pl.CostEstimate(
            flops=flops,
            bytes_accessed=sum(int(np.prod(x.shape)) * x.dtype.itemsize for x in operands),
            transcendentals=0,
        ),
    )(*operands)


def float_out(*shape):
    return jax.ShapeDtypeStruct(shape, jnp.float32)


def half_out(*shape):
    return jax.ShapeDtypeStruct(shape, jnp.bfloat16)


def work(states, channels, block):
    return 4 * states * channels * block**3 + 2 * (states * channels * block) ** 2


def expanded(weight, groups, channels, states):
    spread = spread_matrix(groups, channels, states)
    sizes = tuple(even(len(group)) * ROWS for group in groups)
    return call(
        functools.partial(expand_kernel, sizes),
        half_out(spread.shape[0], -(-max(sizes) // 128) * 128),
        [],
        2 * spread.size * spread.shape[0],
        (weight, jnp.asarray(spread, jnp.bfloat16)),
    )


def left_front(env, tensors, weight, groups):
    channels, block = count_channels(env), env[0].shape[1]
    states, pieces = tensors.shape[1], len(env)
    outs = call(
        functools.partial(left_kernel, groups, states, pieces),
        [half_out(channels // pieces, block, block)] * (states * pieces),
        [pltpu.VMEM((states * channels * block // PARTS, block), jnp.float32)],
        work(states, channels, block),
        (*env, tensors, weight),
    )
    return [outs[s * pieces : (s + 1) * pieces] for s in range(states)]


def left_close(iso, gathered, moved):
    channels, block, _ = gathered.shape
    return call(
        left_close_kernel,
        (half_out(channels, block, block), float_out(ROWS, block)),
        [],
        2 * channels * block**3,
        (iso, gathered, moved),
    )


def right_whole(envs, own, tensors, weight, groups):
    channels, block = count_channels(envs[0]), envs[0][0].shape[1]
    states, pieces = len(envs), len(envs[0])
    outs = call(
        functools.partial(right_kernel, groups, states, pieces),
        [half_out(channels // pieces, block, block)] * pieces + [float_out(ROWS, block)],
        [
            pltpu.VMEM((states * channels * block // PARTS, block), jnp.float32),
            pltpu.VMEM((states * channels * block, block), jnp.bfloat16),
        ],
        work(states, channels, block),
        (*(chunk for env in envs for chunk in env), own, tensors, weight),
    )
    return outs[:pieces], outs[pieces]


def front_scratch(states, channels, block):
    return [pltpu.VMEM((states * channels * block // PARTS, block), jnp.float32)]


def operator_front(env, weight, groups, classes):
    channels, block = count_channels(env), env[0].shape[1]
    states, pieces = classes[0].shape[0], len(env)
    return call(
        functools.partial(operator_front_kernel, groups, states, pieces),
        half_out(states * channels * block, block),
        front_scratch(states, channels, block),
        work(states, channels, block),
        (*env, weight, *classes),
    )


def operator_back(rights, squares, gathered, vector):
    channels, block = count_channels(rights[0]), rights[0][0].shape[1]
    states, pieces = len(rights), len(rights[0])
    return call(
        functools.partial(operator_back_kernel, states, pieces),
        (
            float_out(states, block, block),
            half_out(states * block + UNIT_ROWS, block),
            float_out(1, LANES),
        ),
        [],
        2 * states * channels * block**3,
        (*(chunk for right in rights for chunk in right), *squares, gathered, vector),
    )


def operator_whole(env, weight, groups, classes, rights):
    channels, block = count_channels(env), env[0].shape[1]
    states, pieces = len(rights), len(env)
    front = (*env, weight, *classes)
    return call(
        functools.partial(operator_whole_kernel, groups, states, pieces, len(front)),
        (float_out(states, block, block), float_out(1, LANES)),
        [
            pltpu.VMEM((states * channels * block, block), jnp.bfloat16),
            pltpu.VMEM((CLASSES, states, block, block), jnp.bfloat16),
            *front_scratch(states, channels, block),
        ],
        work(states, channels, block) + 2 * states * channels * block**3,
        (*front, *(chunk for right in rights for chunk in right)),
    )


def renewed(table, vector, image, second, unit, squares, entry_count):
    states, block, _ = vector.shape
    return call(
        functools.partial(renew_kernel, entry_count),
        (float_out(states, 2, block, block), float_out(1, LANES)),
        [],
        0,
        (table, vector, image, second, unit, *squares),
    )


def polar(both, table, centre, entry_count):
    states, _, block, _ = both.shape
    return call(
        functools.partial(polar_kernel, entry_count),
        half_out(states, block, block),
        [],
        600 * block**3,
        (both, table, centre),
    )


def energy_of(table, entry_count):
    return call(
        functools.partial(energy_kernel, entry_count), float_out(1, LANES), [], 0, (table,)
    )


def charge_mask(channels, states, sectors):
    charge = np.array([CHARGE_STEPS[channel % CLASSES] for channel in range(channels)])
    state = np.arange(states)
    balance = (
        charge[:, None, None, None]
        + state[None, None, None, :]
        - state[None, None, :, None]
        - charge[None, :, None, None]
    )
    return jnp.asarray((balance % sectors == 0).astype(np.float32)).astype(jnp.bfloat16)


def weight_matrices(mpo, pattern, sectors):
    channels, _, states, _ = mpo.shape
    allowed = charge_mask(channels, states, sectors)
    weights = mpo * pattern[:, :, None, None].astype(jnp.bfloat16) * allowed
    size = states * channels
    left = jnp.transpose(weights, (2, 1, 3, 0)).reshape(size, size)
    right = jnp.transpose(weights, (2, 0, 3, 1)).reshape(size, size)
    return jnp.stack([left, right])


def other_classes_of(places, x):
    one, minus = places.ahead(x, 1), places.ahead(x, -1)
    return one, minus, places.ahead(one, 1), places.ahead(minus, -1)


def classes_of(places, x):
    return jnp.stack([x, *other_classes_of(places, x)])


def other_classes_at_once(places, x):
    return tuple(places.ahead(x, charge) for charge in CHARGE_STEPS[1:])


def after(first, then):
    return lax.optimization_barrier((first, then))


def local(left_iso, right_iso, centre, left_env, right_env, mpo, pattern):
    sites, secs = lax.axis_size("site"), lax.axis_size("sec")
    places = Places(sites, secs)
    left_iso, right_iso, centre = left_iso[0, :, 0], right_iso[0, :, 0], centre[0, 0]
    states, block, _ = left_iso.shape
    channels = mpo.shape[1]
    entry_count = left_env.size * secs
    left_groups = label_groups(channels, states, secs, 1)
    right_groups = label_groups(channels, states, secs, -1)

    pieces = PIECES if channels % PIECES == 0 else 1

    def ahead(env, by, chain_by=0):
        return [places.ahead(chunk, by, chain_by) for chunk in env]

    first = places.fetch(jnp.concatenate([right_env[0, :, 0], left_iso, right_iso]))
    left_isos = [first[channels : channels + states]]
    right_isos = [first[channels + states :]]
    for step in range(1, ENV_STEPS):
        left_isos.append(places.fetch(left_iso, step))
        right_isos.append(places.fetch(right_iso, -step))
    own_tensors = places.fetch(jnp.concatenate([left_iso, centre[None]]), ENV_STEPS)
    right = jnp.split(first[:channels], pieces)
    right, left_env = after(right, left_env)
    left = jnp.split(places.fetch(left_env[0, :, 0]), pieces)
    rolled = [
        classes_of(places, jnp.concatenate([left_isos[step], right_isos[step]]))
        for step in range(ENV_STEPS)
    ]
    own_iso, own_centre = own_tensors[:states], own_tensors[states]
    centres = [own_centre] + [places.ahead(own_centre, s) for s in range(1, states)]

    gathered_weights = lax.all_gather(weight_matrices(mpo[0], pattern[0], secs), "site")
    chain = places.my_chain()

    def weight_of(site_by, kind):
        weight = lax.dynamic_index_in_dim(
            gathered_weights, (chain + site_by) % sites, 0, False
        )[kind]
        return expanded(weight, (left_groups, right_groups)[kind], channels, states)

    weights = (
        [weight_of(step, 0) for step in range(ENV_STEPS + 1)],
        [weight_of(-step, 1) for step in range(ENV_STEPS)],
    )
    vector = jnp.einsum(
        "sxy,syz->sxz", own_iso, jnp.stack(centres), preferred_element_type=jnp.float32
    )
    half_vector = vector.astype(jnp.bfloat16)
    rolled_vector = (half_vector, *other_classes_of(places, half_vector))
    right, (vector, weights) = after(right, (vector, weights))
    centre_float = own_centre.astype(jnp.float32)
    centre_square = jnp.sum((centre_float * centre_float).reshape(-1, ROWS, block), axis=0)

    left_squares, right_squares = [], []
    for step in range(ENV_STEPS):
        envs = [right]
        for t in range(1, states):
            if step == 0 and t == states - 1:
                left, envs[-1] = after(left, envs[-1])
            if step == 1 and t == states - 1:
                rolled_vector, envs[-1] = after(rolled_vector, envs[-1])
            envs.append(ahead(envs[-1], 1))
        if step == 0:
            rolled, envs = after(rolled, envs)
        right, square = right_whole(
            envs,
            right_isos[step],
            rolled[step][:, states:],
            weights[1][step],
            right_groups,
        )
        right_squares.append(square)

        gathered = left_front(left, rolled[step][:, :states], weights[0][step], left_groups)
        moved = [None] * pieces
        for s in reversed(range(1, states)):
            for piece in range(pieces):
                part = jnp.einsum(
                    "xy,vxz->vyz",
                    left_isos[step][s],
                    gathered[s][piece],
                    preferred_element_type=jnp.float32,
                )
                if moved[piece] is not None:
                    part = part + moved[piece].astype(jnp.float32)
                moved[piece] = places.ahead(part.astype(jnp.bfloat16), -1)
        closed = [
            left_close(left_isos[step][0], gathered[0][piece], moved[piece])
            for piece in range(pieces)
        ]
        left = [env for env, _ in closed]
        left_squares.append(sum(square for _, square in closed))

    if (2 * ENV_STEPS) % sites:
        right = ahead(right, 0, 2 * ENV_STEPS)
        right_squares = ahead(right_squares, 0, 2 * ENV_STEPS)
    squares = left_squares + right_squares + [centre_square]
    rights = [right]
    for s in range(1, states):
        rights.append(ahead(rights[-1], 1))
    weight = weights[0][ENV_STEPS]
    gathered = operator_front(left, weight, left_groups, rolled_vector)
    image, sent, own_sums = operator_back(rights, squares, gathered, vector)
    rolled_image = (sent, *other_classes_at_once(places, sent))
    second, unit = operator_whole(left, weight, left_groups, rolled_image, rights)
    table = places.collect(own_sums)
    both, own_sums = renewed(table, vector, image, second, unit, squares, entry_count)
    table = places.collect(own_sums)

    columns = jnp.stack([both[0]] + [places.ahead(both[s], -s) for s in range(1, states)])
    home_table = places.send_home(table, ENV_STEPS, 0)
    home_table, columns = after(home_table, columns)
    column_left = polar(columns, table, own_centre, entry_count)
    new_left = jnp.stack(
        [places.send_home(column_left[s], ENV_STEPS, -s) for s in range(states)]
    )
    energy = energy_of(home_table, entry_count)
    return new_left[None, :, None], energy[0, :1]


def solution(mesh):
    placed = (
        P("site", None, "sec", None, None),
        P("site", None, "sec", None, None),
        P("site", "sec", None, None),
        P("site", None, "sec", None, None),
        P("site", None, "sec", None, None),
        P("site", None, None, None, None),
        P("site", None, None),
    )
    return jax.shard_map(
        local,
        mesh=mesh,
        in_specs=placed,
        out_specs=(P("site", None, "sec", None, None), P("site")),
        check_vma=False,
    )
```

```python
import functools

import jax
import jax.numpy as jnp
import numpy as np
from jax import lax
from jax.experimental import pallas as pl
from jax.experimental.pallas import tpu as pltpu
from jax.sharding import PartitionSpec as P

ENV_STEPS = 2
POLAR = 6

TINY = 1e-06
CHARGE_STEPS = (0, 1, -1, 2, -2)
CLASSES = len(CHARGE_STEPS)
BOTH = ("site", "sec")
VMEM_LIMIT = 20 * 1024 * 1024
PIECES = 2


class Places:
    def __init__(self, sites, secs):
        self.sites, self.secs = sites, secs
        self.half = secs // 2
        self.up = (self.half + 1) // 2

    def home(self, site, sector):
        return (site % self.sites) * self.secs + sector % self.secs

    def position(self, place):
        back = self.half - 1 + self.up - place
        if isinstance(place, int):
            return place if place < self.up else back
        return jnp.where(place < self.up, place, back)

    def slot(self, chain, sector):
        chain, sector = chain % self.sites, sector % self.secs
        place = chain % 2 * self.half + self.position(sector // 2)
        return (chain // 2 * 2 + sector % 2) * self.secs + place

    def pairs(self, source, target):
        return [
            (source(chain, sector), target(chain, sector))
            for chain in range(self.sites)
            for sector in range(self.secs)
        ]

    def fetch(self, x, site_by=0, sec_by=0):
        return lax.ppermute(
            x, BOTH, self.pairs(lambda g, k: self.home(g + site_by, k + sec_by), self.slot)
        )

    def send_home(self, x, site_by, sec_by):
        return lax.ppermute(
            x, BOTH, self.pairs(self.slot, lambda g, k: self.home(g + site_by, k + sec_by))
        )

    def ahead(self, x, by, chain_by=0):
        return lax.ppermute(
            x, BOTH, self.pairs(lambda g, k: self.slot(g + chain_by, k + by), self.slot)
        )

    def partner(self, x, bit):
        return lax.ppermute(x, BOTH, self.pairs(lambda g, k: self.slot(g, k ^ bit), self.slot))

    def my_chain(self):
        return lax.axis_index("site") // 2 * 2 + lax.axis_index("sec") // self.half

    def my_sector(self):
        position = self.position(lax.axis_index("sec") % self.half)
        return 2 * position + lax.axis_index("site") % 2

    def collect(self, values):
        sector = self.my_sector()
        table = values
        bit = 1
        while bit < self.secs:
            other = self.partner(table, bit)
            first = (sector & bit) == 0
            table = jnp.where(
                first, jnp.concatenate([table, other]), jnp.concatenate([other, table])
            )
            bit *= 2
        return table


ROWS = 8
PARTS = 2


def label_groups(channels, states, sectors, sign):
    groups = {}
    for state in range(states):
        for channel in range(channels):
            label = (state + sign * CHARGE_STEPS[channel % CLASSES]) % sectors
            groups.setdefault(label, []).append((state, channel))
    return [groups[label] for label in sorted(groups)]


def even(count):
    return count + count % 2


def spread_matrix(groups, channels, states):
    rows = []
    for group in groups:
        block = np.zeros((even(len(group)), ROWS, states * channels), np.float32)
        for index, (state, channel) in enumerate(group):
            block[index, :, state * channels + channel] = 1
        rows.append(block.reshape(-1, states * channels))
    return np.concatenate(rows)


def expand_kernel(sizes, weight_ref, spread_ref, out_ref):
    start = 0
    for size in sizes:
        spread = spread_ref[pl.ds(start, size), :]
        picked = jnp.dot(spread, weight_ref[...], preferred_element_type=jnp.float32)
        full = lax.dot_general(
            picked.astype(jnp.bfloat16),
            spread,
            (((1,), (1,)), ((), ())),
            preferred_element_type=jnp.float32,
        )
        row = lax.broadcasted_iota(jnp.int32, full.shape, 0)
        column = lax.broadcasted_iota(jnp.int32, full.shape, 1)
        same = lax.rem(row, ROWS) == lax.rem(column, ROWS)
        out_ref[pl.ds(start, size), pl.ds(0, size)] = jnp.where(same, full, 0.0).astype(
            jnp.bfloat16
        )
        start += size


def mix_channels(groups, channels, weight_ref, mixed_ref, write, offset, height):
    def step(index, carry):
        first = pl.multiple_of(index * 2 * ROWS, 2 * ROWS)
        start = 0
        for group in groups:
            size = even(len(group)) * ROWS
            parts = []
            for state, channel in group:
                rows = (state * channels + channel) * height + first
                halves = [
                    mixed_ref[pl.ds(pl.multiple_of(rows + half * ROWS, ROWS), ROWS), :]
                    for half in range(2)
                ]
                parts.append(jnp.concatenate(halves, axis=1))
            if len(group) % 2:
                parts.append(parts[0])
            operand = jnp.concatenate(parts, axis=0).astype(jnp.bfloat16)
            product = jnp.dot(
                weight_ref[pl.ds(start, size), pl.ds(0, size)],
                operand,
                preferred_element_type=jnp.float32,
            )
            block = product.shape[1] // 2
            for number, pair in enumerate(group):
                rows = product[number * ROWS : (number + 1) * ROWS]
                both = jnp.concatenate([rows[:, :block], rows[:, block:]], axis=0)
                write(*pair, pl.multiple_of(offset + first, 2 * ROWS), both.astype(jnp.bfloat16))
            start += size
        return carry

    lax.fori_loop(0, height // (2 * ROWS), step, 0)


def by_parts(block, body):
    height = block // PARTS

    def one(part, carry):
        body(pl.multiple_of(part * height, height), height)
        return carry

    lax.fori_loop(0, PARTS, one, 0)


def into(gathered_ref, channels, block):
    def write(state, channel, first, rows):
        start = (state * channels + channel) * block
        gathered_ref[pl.ds(pl.multiple_of(start + first, 2 * ROWS), 2 * ROWS), :] = rows

    return write


def batches(items, most):
    pieces = -(-len(items) // most)
    size = -(-len(items) // pieces)
    return [items[start : start + size] for start in range(0, len(items), size)]


def rows_of(chunks, channel, offset, height):
    size = chunks[0].shape[0]
    return chunks[channel // size][channel % size, pl.ds(offset, height), :]


def channel_of(chunks, channel):
    size = chunks[0].shape[0]
    return chunks[channel // size][channel % size]


def put_channel(chunks, channel, value):
    size = chunks[0].shape[0]
    chunks[channel // size][channel % size] = value


def count_channels(chunks):
    return sum(chunk.shape[0] for chunk in chunks)


def mix_left(env, tensors, mixed_ref, offset, height):
    channels, block = count_channels(env), env[0].shape[1]
    for cls in range(CLASSES):
        right = jnp.concatenate(tensors[cls], axis=1)
        for batch in batches(list(range(cls, channels, CLASSES)), 5):
            rows = jnp.concatenate(
                [rows_of(env, channel, offset, height) for channel in batch], axis=0
            )
            product = jnp.dot(rows, right, preferred_element_type=jnp.float32)
            for number, channel in enumerate(batch):
                for t in range(len(tensors[cls])):
                    mixed_ref[pl.ds((t * channels + channel) * height, height), :] = product[
                        number * height : (number + 1) * height, t * block : (t + 1) * block
                    ]


def left_kernel(groups, states, pieces, *refs):
    env, (tensor_ref, weight_ref) = refs[:pieces], refs[pieces : pieces + 2]
    outs, mixed_ref = refs[pieces + 2 : -1], refs[-1]
    channels, block = count_channels(env), env[0].shape[1]

    def write(state, channel, first, rows):
        size = channels // pieces
        out_ref = outs[state * pieces + channel // size]
        out_ref[channel % size, pl.ds(first, 2 * ROWS), :] = rows

    def body(offset, height):
        tensors = [[tensor_ref[cls, t] for t in range(states)] for cls in range(CLASSES)]
        mix_left(env, tensors, mixed_ref, offset, height)
        mix_channels(groups, channels, weight_ref, mixed_ref, write, offset, height)

    by_parts(block, body)


def left_close_kernel(iso_ref, gathered_ref, moved_ref, out_ref, square_ref):
    channels, block, _ = gathered_ref.shape
    square = jnp.zeros((ROWS, block), jnp.float32)
    for batch in batches(list(range(channels)), 2):
        right = jnp.concatenate([gathered_ref[channel] for channel in batch], axis=1)
        product = lax.dot_general(
            iso_ref[...], right, (((0,), (0,)), ((), ())), preferred_element_type=jnp.float32
        )
        for number, channel in enumerate(batch):
            part = product[:, number * block : (number + 1) * block]
            part = part + moved_ref[channel].astype(jnp.float32)
            out_ref[channel] = part.astype(jnp.bfloat16)
            square = square + jnp.sum((part * part).reshape(-1, ROWS, block), axis=0)
    square_ref[...] = square


def right_kernel(groups, states, pieces, *refs):
    envs = [refs[t * pieces : (t + 1) * pieces] for t in range(states)]
    refs = refs[states * pieces :]
    own_ref, tensor_ref, weight_ref = refs[:3]
    outs, (square_ref, mixed_ref, gathered_ref) = refs[3 : 3 + pieces], refs[3 + pieces :]
    channels, block = count_channels(envs[0]), envs[0][0].shape[1]
    zero = jnp.zeros((block, block), jnp.bfloat16)
    write = into(gathered_ref, channels, block)

    def body(offset, height):
        for pair in batches(list(range(states)), 2):
            own = jnp.concatenate(
                [
                    jnp.concatenate([own_ref[t] if t == other else zero for other in pair], axis=1)
                    for t in pair
                ],
                axis=0,
            )
            for batch in batches(list(range(channels)), 6):
                rows = jnp.concatenate(
                    [
                        jnp.concatenate(
                            [rows_of(envs[t], channel, offset, height) for channel in batch], axis=0
                        )
                        for t in pair
                    ],
                    axis=1,
                )
                product = lax.dot_general(
                    rows, own, (((1,), (1,)), ((), ())), preferred_element_type=jnp.float32
                )
                for number, t in enumerate(pair):
                    start = (t * channels + batch[0]) * height
                    mixed_ref[pl.ds(start, len(batch) * height), :] = product[
                        :, number * block : (number + 1) * block
                    ]
        mix_channels(groups, channels, weight_ref, mixed_ref, write, offset, height)

    by_parts(block, body)
    square = jnp.zeros((ROWS, block), jnp.float32)
    for cls in range(CLASSES):
        left = jnp.concatenate([tensor_ref[cls, s] for s in range(states)], axis=1)
        for batch in batches(list(range(cls, channels, CLASSES)), 2):
            right = jnp.concatenate(
                [
                    jnp.concatenate(
                        [
                            gathered_ref[pl.ds((s * channels + channel) * block, block), :]
                            for s in range(states)
                        ],
                        axis=0,
                    )
                    for channel in batch
                ],
                axis=1,
            )
            product = jnp.dot(left, right, preferred_element_type=jnp.float32)
            for number, channel in enumerate(batch):
                part = product[:, number * block : (number + 1) * block]
                put_channel(outs, channel, part.astype(jnp.bfloat16))
                square = square + jnp.sum((part * part).reshape(-1, ROWS, block), axis=0)
    square_ref[...] = square


ENV_LANE = 5
LANES = 128


def quotient(table, entry_count):
    def total(x):
        return jnp.sum(x, axis=0, keepdims=True)

    squares = [
        total(table[:, lane : lane + 1]) for lane in range(ENV_LANE, ENV_LANE + 2 * ENV_STEPS + 1)
    ]
    scale = jnp.ones((1, 1), jnp.float32)
    for side in range(2):
        side_scale = jnp.ones((1, 1), jnp.float32)
        for square in squares[side * ENV_STEPS : (side + 1) * ENV_STEPS]:
            side_scale = side_scale * lax.rsqrt(side_scale * side_scale * square / entry_count + TINY)
        scale = scale * side_scale
    a, b, e, c, unit = (table[:, lane : lane + 1] for lane in range(ENV_LANE))
    a, e, unit = scale * a, scale * e, scale * unit
    c = unit * unit * c
    whole_a, whole_b = total(a), total(b)
    energy = whole_a / (whole_b + TINY)
    off = e - energy
    residual_sq = total(c + 2.0 * off * (a - e * b) + off * off * b)
    factor = 0.5 * jnp.sqrt(whole_b / (residual_sq + TINY))
    square = whole_b - 2.0 * factor * (whole_a - energy * whole_b) + factor * factor * residual_sq
    return scale, energy, factor, square, squares[2 * ENV_STEPS]


def updated(vector, image, scale, energy, factor):
    return vector - factor * (scale * image - energy * vector)


def sum_all(x):
    return jnp.sum(jnp.sum(x, axis=0, keepdims=True), axis=1, keepdims=True)


def operator_front_kernel(groups, states, pieces, *refs):
    env, refs = refs[:pieces], refs[pieces:]
    weight_ref, classes, refs = refs[0], refs[1 : 1 + CLASSES], refs[1 + CLASSES :]
    gathered_ref, mixed_ref = refs
    channels, block = count_channels(env), env[0].shape[1]
    write = into(gathered_ref, channels, block)

    def body(offset, height):
        tensors = [[classes[cls][t] for t in range(states)] for cls in range(CLASSES)]
        mix_left(env, tensors, mixed_ref, offset, height)
        mix_channels(groups, channels, weight_ref, mixed_ref, write, offset, height)

    by_parts(block, body)


def products(rights, gathered_ref, s):
    channels, block = count_channels(rights[0]), rights[0][0].shape[1]
    total = jnp.zeros((block, block), jnp.float32)
    for batch in batches(list(range(channels)), 6):
        left = jnp.concatenate(
            [gathered_ref[pl.ds((s * channels + channel) * block, block), :] for channel in batch],
            axis=1,
        )
        right = jnp.concatenate([channel_of(rights[s], channel) for channel in batch], axis=0)
        total = total + jnp.dot(left, right, preferred_element_type=jnp.float32)
    return total


def write_sums(vector, image, squares, sums_ref):
    a, b = sum_all(vector * image), sum_all(vector * vector)
    e = jnp.where(b > 0, a / jnp.where(b > 0, b, 1.0), 0.0)
    residual = image - e * vector
    unit = jnp.max(jnp.max(jnp.abs(residual), axis=0, keepdims=True), axis=1, keepdims=True)
    unit = jnp.where(unit > 0, unit, 1.0)
    residual = residual / unit
    lane = lax.broadcasted_iota(jnp.int32, sums_ref.shape, 1)
    sums = jnp.zeros(sums_ref.shape, jnp.float32)
    values = (a, b, e, sum_all(residual * residual), unit, *(sum_all(x[...]) for x in squares))
    for place, value in enumerate(values):
        sums = jnp.where(lane == place, value, sums)
    sums_ref[...] = sums


def flat(ref):
    states, block, _ = ref.shape
    return ref[...].reshape(states * block, block)


UNIT_ROWS = 16


def power_above(x):
    top = jnp.max(jnp.max(jnp.abs(x), axis=0, keepdims=True), axis=1, keepdims=True)
    steps = jnp.ceil(jnp.log(jnp.where(top > 0, top, 1.0)) * (1 / np.log(2)))
    return jnp.exp(steps * np.log(2)).astype(jnp.bfloat16).astype(jnp.float32)


def operator_back_kernel(states, pieces, *refs):
    rights = [refs[t * pieces : (t + 1) * pieces] for t in range(states)]
    refs = refs[states * pieces :]
    squares, refs = refs[: 2 * ENV_STEPS + 1], refs[2 * ENV_STEPS + 1 :]
    gathered_ref, vector_ref, image_ref, half_ref, sums_ref = refs
    for s in range(states):
        image_ref[s] = products(rights, gathered_ref, s)
    image = flat(image_ref)
    unit = power_above(image)
    half_ref[: image.shape[0]] = (image / unit).astype(jnp.bfloat16)
    half_ref[image.shape[0] :] = jnp.broadcast_to(unit, (UNIT_ROWS, LANES)).astype(jnp.bfloat16)
    write_sums(flat(vector_ref), image, squares, sums_ref)


def operator_whole_kernel(groups, states, pieces, front_count, *refs):
    front, refs = refs[:front_count], refs[front_count:]
    env_and_weight, sent = front[:-CLASSES], front[-CLASSES:]
    rights = [refs[t * pieces : (t + 1) * pieces] for t in range(states)]
    image_ref, unit_ref, gathered_ref, tensor_ref, mixed_ref = refs[states * pieces :]
    block = image_ref.shape[1]
    units = [
        x[pl.ds(states * block, UNIT_ROWS), :].astype(jnp.float32)[:1, :1] for x in sent
    ]
    unit = functools.reduce(jnp.maximum, units)
    unit_ref[...] = jnp.broadcast_to(unit, unit_ref.shape)
    for cls in range(CLASSES):
        for t in range(states):
            tensor = sent[cls][pl.ds(t * block, block), :].astype(jnp.float32)
            tensor_ref[cls, t] = (tensor * (units[cls] / unit)).astype(jnp.bfloat16)
    classes = [tensor_ref.at[cls] for cls in range(CLASSES)]
    operator_front_kernel(groups, states, pieces, *env_and_weight, *classes, gathered_ref, mixed_ref)
    for s in range(states):
        image_ref[s] = products(rights, gathered_ref, s)


def renew_kernel(entry_count, *refs):
    table_ref, vector_ref, image_ref, second_ref, unit_ref = refs[:5]
    squares, (both_ref, sums_ref) = refs[5:-2], refs[-2:]
    states, block, _ = vector_ref.shape
    scale, energy, factor, _, _ = quotient(table_ref[...], entry_count)
    vector, image = flat(vector_ref), flat(image_ref)
    part = factor * (scale * unit_ref[:, :1])
    new_image = (1.0 + factor * energy) * image - part * flat(second_ref)
    new = updated(vector, image, scale, energy, factor)
    both_ref[:, 0] = new.reshape(states, block, block)
    both_ref[:, 1] = new_image.reshape(states, block, block)
    write_sums(new, new_image, squares, sums_ref)


def energy_kernel(entry_count, table_ref, out_ref):
    energy = quotient(table_ref[...], entry_count)[1]
    out_ref[...] = jnp.broadcast_to(energy, out_ref.shape)


def polar_kernel(entry_count, both_ref, table_ref, centre_ref, out_ref):
    states, _, block, _ = both_ref.shape
    rows = lax.broadcasted_iota(jnp.int32, (block, block), 0)
    columns = lax.broadcasted_iota(jnp.int32, (block, block), 1)
    unit = (rows == columns).astype(jnp.float32)

    def halves(x):
        high = x.astype(jnp.bfloat16)
        return high, (x - high.astype(jnp.float32)).astype(jnp.bfloat16)

    def product(x, y, contract=((1,), (0,))):
        (x_high, x_low), (y_high, y_low) = halves(x), halves(y)
        parts = [
            lax.dot_general(left, right, (contract, ((), ())), preferred_element_type=jnp.float32)
            for left, right in ((x_high, y_low), (x_low, y_high), (x_high, y_high))
        ]
        return parts[0] + parts[1] + parts[2]

    scale, energy, factor, square, centre_sq = quotient(table_ref[...], entry_count)
    vector = updated(
        both_ref[:, 0].reshape(states * block, block),
        both_ref[:, 1].reshape(states * block, block),
        scale,
        energy,
        factor,
    ) * lax.rsqrt(square + TINY)
    centre = centre_ref[...].astype(jnp.float32) * lax.rsqrt(centre_sq + TINY)
    grams = [product(x, x, ((0,), (0,))) for x in (vector, centre)]
    totals = [unit, unit]
    for step in range(POLAR):
        factors = [1.5 * unit - 0.5 * gram for gram in grams]
        totals = [
            factor if step == 0 else product(total, factor)
            for total, factor in zip(totals, factors)
        ]
        if step < POLAR - 1:
            grams = [
                product(product(factor, gram), factor) for gram, factor in zip(grams, factors)
            ]
    closing = product(totals[0], product(centre, totals[1]), ((1,), (1,)))
    out_ref[...] = product(vector, closing).reshape(states, block, block).astype(jnp.bfloat16)


def call(kernel, out_shape, scratch_shapes, flops, operands):
    return pl.pallas_call(
        kernel,
        out_shape=out_shape,
        scratch_shapes=scratch_shapes,
        compiler_params=pltpu.CompilerParams(vmem_limit_bytes=VMEM_LIMIT),
        cost_estimate=pl.CostEstimate(
            flops=flops,
            bytes_accessed=sum(int(np.prod(x.shape)) * x.dtype.itemsize for x in operands),
            transcendentals=0,
        ),
    )(*operands)


def float_out(*shape):
    return jax.ShapeDtypeStruct(shape, jnp.float32)


def half_out(*shape):
    return jax.ShapeDtypeStruct(shape, jnp.bfloat16)


def work(states, channels, block):
    return 4 * states * channels * block**3 + 2 * (states * channels * block) ** 2


def expanded(weight, groups, channels, states):
    spread = spread_matrix(groups, channels, states)
    sizes = tuple(even(len(group)) * ROWS for group in groups)
    return call(
        functools.partial(expand_kernel, sizes),
        half_out(spread.shape[0], -(-max(sizes) // 128) * 128),
        [],
        2 * spread.size * spread.shape[0],
        (weight, jnp.asarray(spread, jnp.bfloat16)),
    )


def left_front(env, tensors, weight, groups):
    channels, block = count_channels(env), env[0].shape[1]
    states, pieces = tensors.shape[1], len(env)
    outs = call(
        functools.partial(left_kernel, groups, states, pieces),
        [half_out(channels // pieces, block, block)] * (states * pieces),
        [pltpu.VMEM((states * channels * block // PARTS, block), jnp.float32)],
        work(states, channels, block),
        (*env, tensors, weight),
    )
    return [outs[s * pieces : (s + 1) * pieces] for s in range(states)]


def left_close(iso, gathered, moved):
    channels, block, _ = gathered.shape
    return call(
        left_close_kernel,
        (half_out(channels, block, block), float_out(ROWS, block)),
        [],
        2 * channels * block**3,
        (iso, gathered, moved),
    )


def right_whole(envs, own, tensors, weight, groups):
    channels, block = count_channels(envs[0]), envs[0][0].shape[1]
    states, pieces = len(envs), len(envs[0])
    outs = call(
        functools.partial(right_kernel, groups, states, pieces),
        [half_out(channels // pieces, block, block)] * pieces + [float_out(ROWS, block)],
        [
            pltpu.VMEM((states * channels * block // PARTS, block), jnp.float32),
            pltpu.VMEM((states * channels * block, block), jnp.bfloat16),
        ],
        work(states, channels, block),
        (*(chunk for env in envs for chunk in env), own, tensors, weight),
    )
    return outs[:pieces], outs[pieces]


def front_scratch(states, channels, block):
    return [pltpu.VMEM((states * channels * block // PARTS, block), jnp.float32)]


def operator_front(env, weight, groups, classes):
    channels, block = count_channels(env), env[0].shape[1]
    states, pieces = classes[0].shape[0], len(env)
    return call(
        functools.partial(operator_front_kernel, groups, states, pieces),
        half_out(states * channels * block, block),
        front_scratch(states, channels, block),
        work(states, channels, block),
        (*env, weight, *classes),
    )


def operator_back(rights, squares, gathered, vector):
    channels, block = count_channels(rights[0]), rights[0][0].shape[1]
    states, pieces = len(rights), len(rights[0])
    return call(
        functools.partial(operator_back_kernel, states, pieces),
        (
            float_out(states, block, block),
            half_out(states * block + UNIT_ROWS, block),
            float_out(1, LANES),
        ),
        [],
        2 * states * channels * block**3,
        (*(chunk for right in rights for chunk in right), *squares, gathered, vector),
    )


def operator_whole(env, weight, groups, classes, rights):
    channels, block = count_channels(env), env[0].shape[1]
    states, pieces = len(rights), len(env)
    front = (*env, weight, *classes)
    return call(
        functools.partial(operator_whole_kernel, groups, states, pieces, len(front)),
        (float_out(states, block, block), float_out(1, LANES)),
        [
            pltpu.VMEM((states * channels * block, block), jnp.bfloat16),
            pltpu.VMEM((CLASSES, states, block, block), jnp.bfloat16),
            *front_scratch(states, channels, block),
        ],
        work(states, channels, block) + 2 * states * channels * block**3,
        (*front, *(chunk for right in rights for chunk in right)),
    )


def renewed(table, vector, image, second, unit, squares, entry_count):
    states, block, _ = vector.shape
    return call(
        functools.partial(renew_kernel, entry_count),
        (float_out(states, 2, block, block), float_out(1, LANES)),
        [],
        0,
        (table, vector, image, second, unit, *squares),
    )


def polar(both, table, centre, entry_count):
    states, _, block, _ = both.shape
    return call(
        functools.partial(polar_kernel, entry_count),
        half_out(states, block, block),
        [],
        600 * block**3,
        (both, table, centre),
    )


def energy_of(table, entry_count):
    return call(
        functools.partial(energy_kernel, entry_count), float_out(1, LANES), [], 0, (table,)
    )


def charge_mask(channels, states, sectors):
    charge = np.array([CHARGE_STEPS[channel % CLASSES] for channel in range(channels)])
    state = np.arange(states)
    balance = (
        charge[:, None, None, None]
        + state[None, None, None, :]
        - state[None, None, :, None]
        - charge[None, :, None, None]
    )
    return jnp.asarray((balance % sectors == 0).astype(np.float32)).astype(jnp.bfloat16)


def weight_matrices(mpo, pattern, sectors):
    channels, _, states, _ = mpo.shape
    allowed = charge_mask(channels, states, sectors)
    weights = mpo * pattern[:, :, None, None].astype(jnp.bfloat16) * allowed
    size = states * channels
    left = jnp.transpose(weights, (2, 1, 3, 0)).reshape(size, size)
    right = jnp.transpose(weights, (2, 0, 3, 1)).reshape(size, size)
    return jnp.stack([left, right])


def other_classes_of(places, x):
    one, minus = places.ahead(x, 1), places.ahead(x, -1)
    return one, minus, places.ahead(one, 1), places.ahead(minus, -1)


def classes_of(places, x):
    return jnp.stack([x, *other_classes_of(places, x)])


def other_classes_at_once(places, x):
    return tuple(places.ahead(x, charge) for charge in CHARGE_STEPS[1:])


def after(first, then):
    return lax.optimization_barrier((first, then))


def local(left_iso, right_iso, centre, left_env, right_env, mpo, pattern):
    sites, secs = lax.axis_size("site"), lax.axis_size("sec")
    places = Places(sites, secs)
    left_iso, right_iso, centre = left_iso[0, :, 0], right_iso[0, :, 0], centre[0, 0]
    states, block, _ = left_iso.shape
    channels = mpo.shape[1]
    entry_count = left_env.size * secs
    left_groups = label_groups(channels, states, secs, 1)
    right_groups = label_groups(channels, states, secs, -1)

    pieces = PIECES if channels % PIECES == 0 else 1

    def ahead(env, by, chain_by=0):
        return [places.ahead(chunk, by, chain_by) for chunk in env]

    first = places.fetch(jnp.concatenate([right_env[0, :, 0], left_iso, right_iso]))
    left_isos = [first[channels : channels + states]]
    right_isos = [first[channels + states :]]
    for step in range(1, ENV_STEPS):
        left_isos.append(places.fetch(left_iso, step))
        right_isos.append(places.fetch(right_iso, -step))
    own_tensors = places.fetch(jnp.concatenate([left_iso, centre[None]]), ENV_STEPS)
    right = jnp.split(first[:channels], pieces)
    right, left_env = after(right, left_env)
    left = jnp.split(places.fetch(left_env[0, :, 0]), pieces)
    rolled = [
        classes_of(places, jnp.concatenate([left_isos[step], right_isos[step]]))
        for step in range(ENV_STEPS)
    ]
    own_iso, own_centre = own_tensors[:states], own_tensors[states]
    centres = [own_centre] + [places.ahead(own_centre, s) for s in range(1, states)]

    gathered_weights = lax.all_gather(weight_matrices(mpo[0], pattern[0], secs), "site")
    chain = places.my_chain()

    def weight_of(site_by, kind):
        weight = lax.dynamic_index_in_dim(
            gathered_weights, (chain + site_by) % sites, 0, False
        )[kind]
        return expanded(weight, (left_groups, right_groups)[kind], channels, states)

    weights = (
        [weight_of(step, 0) for step in range(ENV_STEPS + 1)],
        [weight_of(-step, 1) for step in range(ENV_STEPS)],
    )
    vector = jnp.einsum(
        "sxy,syz->sxz", own_iso, jnp.stack(centres), preferred_element_type=jnp.float32
    )
    half_vector = vector.astype(jnp.bfloat16)
    rolled_vector = (half_vector, *other_classes_of(places, half_vector))
    right, (vector, weights) = after(right, (vector, weights))
    centre_float = own_centre.astype(jnp.float32)
    centre_square = jnp.sum((centre_float * centre_float).reshape(-1, ROWS, block), axis=0)

    left_squares, right_squares = [], []
    for step in range(ENV_STEPS):
        envs = [right]
        for t in range(1, states):
            if step == 0 and t == states - 1:
                left, envs[-1] = after(left, envs[-1])
            envs.append(ahead(envs[-1], 1))
        gathered = left_front(left, rolled[step][:, :states], weights[0][step], left_groups)

        def left_part(s, piece):
            return jnp.einsum(
                "xy,vxz->vyz",
                left_isos[step][s],
                gathered[s][piece],
                preferred_element_type=jnp.float32,
            )

        sent = [left_part(states - 1, piece).astype(jnp.bfloat16) for piece in range(pieces)]
        if step == 0:
            (rolled, rolled_vector, sent), envs = after((rolled, rolled_vector, sent), envs)
        right, square = right_whole(
            envs,
            right_isos[step],
            rolled[step][:, states:],
            weights[1][step],
            right_groups,
        )
        right_squares.append(square)

        moved = [places.ahead(chunk, -1) for chunk in sent]
        for s in reversed(range(1, states - 1)):
            for piece in range(pieces):
                part = left_part(s, piece) + moved[piece].astype(jnp.float32)
                moved[piece] = places.ahead(part.astype(jnp.bfloat16), -1)
        closed = [
            left_close(left_isos[step][0], gathered[0][piece], moved[piece])
            for piece in range(pieces)
        ]
        left = [env for env, _ in closed]
        left_squares.append(sum(square for _, square in closed))

    if (2 * ENV_STEPS) % sites:
        right = ahead(right, 0, 2 * ENV_STEPS)
        right_squares = ahead(right_squares, 0, 2 * ENV_STEPS)
    squares = left_squares + right_squares + [centre_square]
    rights = [right]
    for s in range(1, states):
        rights.append(ahead(rights[-1], 1))
    weight = weights[0][ENV_STEPS]
    gathered = operator_front(left, weight, left_groups, rolled_vector)
    image, sent, own_sums = operator_back(rights, squares, gathered, vector)
    rolled_image = (sent, *other_classes_at_once(places, sent))
    second, unit = operator_whole(left, weight, left_groups, rolled_image, rights)
    table = places.collect(own_sums)
    both, own_sums = renewed(table, vector, image, second, unit, squares, entry_count)
    table = places.collect(own_sums)

    columns = jnp.stack([both[0]] + [places.ahead(both[s], -s) for s in range(1, states)])
    home_table = places.send_home(table, ENV_STEPS, 0)
    home_table, columns = after(home_table, columns)
    column_left = polar(columns, table, own_centre, entry_count)
    new_left = jnp.stack(
        [places.send_home(column_left[s], ENV_STEPS, -s) for s in range(states)]
    )
    energy = energy_of(home_table, entry_count)
    return new_left[None, :, None], energy[0, :1]


def solution(mesh):
    placed = (
        P("site", None, "sec", None, None),
        P("site", None, "sec", None, None),
        P("site", "sec", None, None),
        P("site", None, "sec", None, None),
        P("site", None, "sec", None, None),
        P("site", None, None, None, None),
        P("site", None, None),
    )
    return jax.shard_map(
        local,
        mesh=mesh,
        in_specs=placed,
        out_specs=(P("site", None, "sec", None, None), P("site")),
        check_vma=False,
    )
```

```python
import functools

import jax
import jax.numpy as jnp
import numpy as np
from jax import lax
from jax.experimental import pallas as pl
from jax.experimental.pallas import tpu as pltpu
from jax.sharding import PartitionSpec as P

ENV_STEPS = 2
POLAR = 6

TINY = 1e-06
CHARGE_STEPS = (0, 1, -1, 2, -2)
CLASSES = len(CHARGE_STEPS)
BOTH = ("site", "sec")
VMEM_LIMIT = 20 * 1024 * 1024
PIECES = 2


class Places:
    def __init__(self, sites, secs):
        self.sites, self.secs = sites, secs
        self.half = secs // 2
        self.up = (self.half + 1) // 2

    def home(self, site, sector):
        return (site % self.sites) * self.secs + sector % self.secs

    def position(self, place):
        back = self.half - 1 + self.up - place
        if isinstance(place, int):
            return place if place < self.up else back
        return jnp.where(place < self.up, place, back)

    def slot(self, chain, sector):
        chain, sector = chain % self.sites, sector % self.secs
        place = chain % 2 * self.half + self.position(sector // 2)
        return (chain // 2 * 2 + sector % 2) * self.secs + place

    def pairs(self, source, target):
        return [
            (source(chain, sector), target(chain, sector))
            for chain in range(self.sites)
            for sector in range(self.secs)
        ]

    def fetch(self, x, site_by=0, sec_by=0):
        return lax.ppermute(
            x, BOTH, self.pairs(lambda g, k: self.home(g + site_by, k + sec_by), self.slot)
        )

    def send_home(self, x, site_by, sec_by):
        return lax.ppermute(
            x, BOTH, self.pairs(self.slot, lambda g, k: self.home(g + site_by, k + sec_by))
        )

    def ahead(self, x, by, chain_by=0):
        return lax.ppermute(
            x, BOTH, self.pairs(lambda g, k: self.slot(g + chain_by, k + by), self.slot)
        )

    def partner(self, x, bit):
        return lax.ppermute(x, BOTH, self.pairs(lambda g, k: self.slot(g, k ^ bit), self.slot))

    def my_chain(self):
        return lax.axis_index("site") // 2 * 2 + lax.axis_index("sec") // self.half

    def my_sector(self):
        position = self.position(lax.axis_index("sec") % self.half)
        return 2 * position + lax.axis_index("site") % 2

    def collect(self, values):
        sector = self.my_sector()
        table = values
        bit = 1
        while bit < self.secs:
            other = self.partner(table, bit)
            first = (sector & bit) == 0
            table = jnp.where(
                first, jnp.concatenate([table, other]), jnp.concatenate([other, table])
            )
            bit *= 2
        return table


ROWS = 8
PARTS = 2


def label_groups(channels, states, sectors, sign):
    groups = {}
    for state in range(states):
        for channel in range(channels):
            label = (state + sign * CHARGE_STEPS[channel % CLASSES]) % sectors
            groups.setdefault(label, []).append((state, channel))
    return [groups[label] for label in sorted(groups)]


def even(count):
    return count + count % 2


def spread_matrix(groups, channels, states):
    rows = []
    for group in groups:
        block = np.zeros((even(len(group)), ROWS, states * channels), np.float32)
        for index, (state, channel) in enumerate(group):
            block[index, :, state * channels + channel] = 1
        rows.append(block.reshape(-1, states * channels))
    return np.concatenate(rows)


def expand_kernel(sizes, weight_ref, spread_ref, out_ref):
    start = 0
    for size in sizes:
        spread = spread_ref[pl.ds(start, size), :]
        picked = jnp.dot(spread, weight_ref[...], preferred_element_type=jnp.float32)
        full = lax.dot_general(
            picked.astype(jnp.bfloat16),
            spread,
            (((1,), (1,)), ((), ())),
            preferred_element_type=jnp.float32,
        )
        row = lax.broadcasted_iota(jnp.int32, full.shape, 0)
        column = lax.broadcasted_iota(jnp.int32, full.shape, 1)
        same = lax.rem(row, ROWS) == lax.rem(column, ROWS)
        out_ref[pl.ds(start, size), pl.ds(0, size)] = jnp.where(same, full, 0.0).astype(
            jnp.bfloat16
        )
        start += size


def mix_channels(groups, channels, weight_ref, mixed_ref, write, offset, height):
    def step(index, carry):
        first = pl.multiple_of(index * 2 * ROWS, 2 * ROWS)
        start = 0
        for group in groups:
            size = even(len(group)) * ROWS
            parts = []
            for state, channel in group:
                rows = (state * channels + channel) * height + first
                halves = [
                    mixed_ref[pl.ds(pl.multiple_of(rows + half * ROWS, ROWS), ROWS), :]
                    for half in range(2)
                ]
                parts.append(jnp.concatenate(halves, axis=1))
            if len(group) % 2:
                parts.append(parts[0])
            operand = jnp.concatenate(parts, axis=0).astype(jnp.bfloat16)
            product = jnp.dot(
                weight_ref[pl.ds(start, size), pl.ds(0, size)],
                operand,
                preferred_element_type=jnp.float32,
            )
            block = product.shape[1] // 2
            for number, pair in enumerate(group):
                rows = product[number * ROWS : (number + 1) * ROWS]
                both = jnp.concatenate([rows[:, :block], rows[:, block:]], axis=0)
                write(*pair, pl.multiple_of(offset + first, 2 * ROWS), both.astype(jnp.bfloat16))
            start += size
        return carry

    lax.fori_loop(0, height // (2 * ROWS), step, 0)


def by_parts(block, body):
    height = block // PARTS

    def one(part, carry):
        body(pl.multiple_of(part * height, height), height)
        return carry

    lax.fori_loop(0, PARTS, one, 0)


def into(gathered_ref, channels, block):
    def write(state, channel, first, rows):
        start = (state * channels + channel) * block
        gathered_ref[pl.ds(pl.multiple_of(start + first, 2 * ROWS), 2 * ROWS), :] = rows

    return write


def batches(items, most):
    pieces = -(-len(items) // most)
    size = -(-len(items) // pieces)
    return [items[start : start + size] for start in range(0, len(items), size)]


def rows_of(chunks, channel, offset, height):
    size = chunks[0].shape[0]
    return chunks[channel // size][channel % size, pl.ds(offset, height), :]


def channel_of(chunks, channel):
    size = chunks[0].shape[0]
    return chunks[channel // size][channel % size]


def put_channel(chunks, channel, value):
    size = chunks[0].shape[0]
    chunks[channel // size][channel % size] = value


def count_channels(chunks):
    return sum(chunk.shape[0] for chunk in chunks)


def mix_left(env, tensors, mixed_ref, offset, height):
    channels, block = count_channels(env), env[0].shape[1]
    for cls in range(CLASSES):
        right = jnp.concatenate(tensors[cls], axis=1)
        for batch in batches(list(range(cls, channels, CLASSES)), 5):
            rows = jnp.concatenate(
                [rows_of(env, channel, offset, height) for channel in batch], axis=0
            )
            product = jnp.dot(rows, right, preferred_element_type=jnp.float32)
            for number, channel in enumerate(batch):
                for t in range(len(tensors[cls])):
                    mixed_ref[pl.ds((t * channels + channel) * height, height), :] = product[
                        number * height : (number + 1) * height, t * block : (t + 1) * block
                    ]


def left_kernel(groups, states, pieces, *refs):
    env, (tensor_ref, weight_ref) = refs[:pieces], refs[pieces : pieces + 2]
    outs, mixed_ref = refs[pieces + 2 : -1], refs[-1]
    channels, block = count_channels(env), env[0].shape[1]

    def write(state, channel, first, rows):
        size = channels // pieces
        out_ref = outs[state * pieces + channel // size]
        out_ref[channel % size, pl.ds(first, 2 * ROWS), :] = rows

    def body(offset, height):
        tensors = [[tensor_ref[cls, t] for t in range(states)] for cls in range(CLASSES)]
        mix_left(env, tensors, mixed_ref, offset, height)
        mix_channels(groups, channels, weight_ref, mixed_ref, write, offset, height)

    by_parts(block, body)


def left_close_kernel(iso_ref, gathered_ref, moved_ref, out_ref, square_ref):
    channels, block, _ = gathered_ref.shape
    square = jnp.zeros((ROWS, block), jnp.float32)
    for batch in batches(list(range(channels)), 2):
        right = jnp.concatenate([gathered_ref[channel] for channel in batch], axis=1)
        product = lax.dot_general(
            iso_ref[...], right, (((0,), (0,)), ((), ())), preferred_element_type=jnp.float32
        )
        for number, channel in enumerate(batch):
            part = product[:, number * block : (number + 1) * block]
            part = part + moved_ref[channel].astype(jnp.float32)
            out_ref[channel] = part.astype(jnp.bfloat16)
            square = square + jnp.sum((part * part).reshape(-1, ROWS, block), axis=0)
    square_ref[...] = square


def right_kernel(groups, states, pieces, *refs):
    envs = [refs[t * pieces : (t + 1) * pieces] for t in range(states)]
    refs = refs[states * pieces :]
    own_ref, tensor_ref, weight_ref = refs[:3]
    outs, (square_ref, mixed_ref, gathered_ref) = refs[3 : 3 + pieces], refs[3 + pieces :]
    channels, block = count_channels(envs[0]), envs[0][0].shape[1]
    zero = jnp.zeros((block, block), jnp.bfloat16)
    write = into(gathered_ref, channels, block)

    def body(offset, height):
        for pair in batches(list(range(states)), 2):
            own = jnp.concatenate(
                [
                    jnp.concatenate([own_ref[t] if t == other else zero for other in pair], axis=1)
                    for t in pair
                ],
                axis=0,
            )
            for batch in batches(list(range(channels)), 6):
                rows = jnp.concatenate(
                    [
                        jnp.concatenate(
                            [rows_of(envs[t], channel, offset, height) for channel in batch], axis=0
                        )
                        for t in pair
                    ],
                    axis=1,
                )
                product = lax.dot_general(
                    rows, own, (((1,), (1,)), ((), ())), preferred_element_type=jnp.float32
                )
                for number, t in enumerate(pair):
                    start = (t * channels + batch[0]) * height
                    mixed_ref[pl.ds(start, len(batch) * height), :] = product[
                        :, number * block : (number + 1) * block
                    ]
        mix_channels(groups, channels, weight_ref, mixed_ref, write, offset, height)

    by_parts(block, body)
    square = jnp.zeros((ROWS, block), jnp.float32)
    for cls in range(CLASSES):
        left = jnp.concatenate([tensor_ref[cls, s] for s in range(states)], axis=1)
        for batch in batches(list(range(cls, channels, CLASSES)), 2):
            right = jnp.concatenate(
                [
                    jnp.concatenate(
                        [
                            gathered_ref[pl.ds((s * channels + channel) * block, block), :]
                            for s in range(states)
                        ],
                        axis=0,
                    )
                    for channel in batch
                ],
                axis=1,
            )
            product = jnp.dot(left, right, preferred_element_type=jnp.float32)
            for number, channel in enumerate(batch):
                part = product[:, number * block : (number + 1) * block]
                put_channel(outs, channel, part.astype(jnp.bfloat16))
                square = square + jnp.sum((part * part).reshape(-1, ROWS, block), axis=0)
    square_ref[...] = square


ENV_LANE = 5
LANES = 128


def quotient(table, entry_count):
    def total(x):
        return jnp.sum(x, axis=0, keepdims=True)

    squares = [
        total(table[:, lane : lane + 1]) for lane in range(ENV_LANE, ENV_LANE + 2 * ENV_STEPS + 1)
    ]
    scale = jnp.ones((1, 1), jnp.float32)
    for side in range(2):
        side_scale = jnp.ones((1, 1), jnp.float32)
        for square in squares[side * ENV_STEPS : (side + 1) * ENV_STEPS]:
            side_scale = side_scale * lax.rsqrt(side_scale * side_scale * square / entry_count + TINY)
        scale = scale * side_scale
    a, b, e, c, unit = (table[:, lane : lane + 1] for lane in range(ENV_LANE))
    a, e, unit = scale * a, scale * e, scale * unit
    c = unit * unit * c
    whole_a, whole_b = total(a), total(b)
    energy = whole_a / (whole_b + TINY)
    off = e - energy
    residual_sq = total(c + 2.0 * off * (a - e * b) + off * off * b)
    factor = 0.5 * jnp.sqrt(whole_b / (residual_sq + TINY))
    square = whole_b - 2.0 * factor * (whole_a - energy * whole_b) + factor * factor * residual_sq
    return scale, energy, factor, square, squares[2 * ENV_STEPS]


def updated(vector, image, scale, energy, factor):
    return vector - factor * (scale * image - energy * vector)


def sum_all(x):
    return jnp.sum(jnp.sum(x, axis=0, keepdims=True), axis=1, keepdims=True)


def operator_front_kernel(groups, states, pieces, *refs):
    env, refs = refs[:pieces], refs[pieces:]
    weight_ref, classes, refs = refs[0], refs[1 : 1 + CLASSES], refs[1 + CLASSES :]
    gathered_ref, mixed_ref = refs
    channels, block = count_channels(env), env[0].shape[1]
    write = into(gathered_ref, channels, block)

    def body(offset, height):
        tensors = [[classes[cls][t] for t in range(states)] for cls in range(CLASSES)]
        mix_left(env, tensors, mixed_ref, offset, height)
        mix_channels(groups, channels, weight_ref, mixed_ref, write, offset, height)

    by_parts(block, body)


def products(rights, gathered_ref, s):
    channels, block = count_channels(rights[0]), rights[0][0].shape[1]
    total = jnp.zeros((block, block), jnp.float32)
    for batch in batches(list(range(channels)), 6):
        left = jnp.concatenate(
            [gathered_ref[pl.ds((s * channels + channel) * block, block), :] for channel in batch],
            axis=1,
        )
        right = jnp.concatenate([channel_of(rights[s], channel) for channel in batch], axis=0)
        total = total + jnp.dot(left, right, preferred_element_type=jnp.float32)
    return total


def write_sums(vector, image, squares, sums_ref):
    a, b = sum_all(vector * image), sum_all(vector * vector)
    e = jnp.where(b > 0, a / jnp.where(b > 0, b, 1.0), 0.0)
    residual = image - e * vector
    unit = jnp.max(jnp.max(jnp.abs(residual), axis=0, keepdims=True), axis=1, keepdims=True)
    unit = jnp.where(unit > 0, unit, 1.0)
    residual = residual / unit
    lane = lax.broadcasted_iota(jnp.int32, sums_ref.shape, 1)
    sums = jnp.zeros(sums_ref.shape, jnp.float32)
    values = (a, b, e, sum_all(residual * residual), unit, *(sum_all(x[...]) for x in squares))
    for place, value in enumerate(values):
        sums = jnp.where(lane == place, value, sums)
    sums_ref[...] = sums


def flat(ref):
    states, block, _ = ref.shape
    return ref[...].reshape(states * block, block)


UNIT_ROWS = 16


def power_above(x):
    top = jnp.max(jnp.max(jnp.abs(x), axis=0, keepdims=True), axis=1, keepdims=True)
    steps = jnp.ceil(jnp.log(jnp.where(top > 0, top, 1.0)) * (1 / np.log(2)))
    return jnp.exp(steps * np.log(2)).astype(jnp.bfloat16).astype(jnp.float32)


def operator_back_kernel(states, pieces, *refs):
    rights = [refs[t * pieces : (t + 1) * pieces] for t in range(states)]
    refs = refs[states * pieces :]
    squares, refs = refs[: 2 * ENV_STEPS + 1], refs[2 * ENV_STEPS + 1 :]
    gathered_ref, vector_ref, image_ref, half_ref, sums_ref = refs
    for s in range(states):
        image_ref[s] = products(rights, gathered_ref, s)
    image = flat(image_ref)
    unit = power_above(image)
    half_ref[: image.shape[0]] = (image / unit).astype(jnp.bfloat16)
    half_ref[image.shape[0] :] = jnp.broadcast_to(unit, (UNIT_ROWS, LANES)).astype(jnp.bfloat16)
    write_sums(flat(vector_ref), image, squares, sums_ref)


def operator_whole_kernel(groups, states, pieces, front_count, *refs):
    front, refs = refs[:front_count], refs[front_count:]
    env_and_weight, sent = front[:-CLASSES], front[-CLASSES:]
    rights = [refs[t * pieces : (t + 1) * pieces] for t in range(states)]
    image_ref, unit_ref, gathered_ref, tensor_ref, mixed_ref = refs[states * pieces :]
    block = image_ref.shape[1]
    units = [
        x[pl.ds(states * block, UNIT_ROWS), :].astype(jnp.float32)[:1, :1] for x in sent
    ]
    unit = functools.reduce(jnp.maximum, units)
    unit_ref[...] = jnp.broadcast_to(unit, unit_ref.shape)
    for cls in range(CLASSES):
        for t in range(states):
            tensor = sent[cls][pl.ds(t * block, block), :].astype(jnp.float32)
            tensor_ref[cls, t] = (tensor * (units[cls] / unit)).astype(jnp.bfloat16)
    classes = [tensor_ref.at[cls] for cls in range(CLASSES)]
    operator_front_kernel(groups, states, pieces, *env_and_weight, *classes, gathered_ref, mixed_ref)
    for s in range(states):
        image_ref[s] = products(rights, gathered_ref, s)


def renew_kernel(entry_count, *refs):
    table_ref, vector_ref, image_ref, second_ref, unit_ref = refs[:5]
    squares, (both_ref, sums_ref) = refs[5:-2], refs[-2:]
    states, block, _ = vector_ref.shape
    scale, energy, factor, _, _ = quotient(table_ref[...], entry_count)
    vector, image = flat(vector_ref), flat(image_ref)
    part = factor * (scale * unit_ref[:, :1])
    new_image = (1.0 + factor * energy) * image - part * flat(second_ref)
    new = updated(vector, image, scale, energy, factor)
    both_ref[:, 0] = new.reshape(states, block, block)
    both_ref[:, 1] = new_image.reshape(states, block, block)
    write_sums(new, new_image, squares, sums_ref)


def energy_kernel(entry_count, table_ref, out_ref):
    energy = quotient(table_ref[...], entry_count)[1]
    out_ref[...] = jnp.broadcast_to(energy, out_ref.shape)


def polar_kernel(entry_count, both_ref, table_ref, centre_ref, out_ref):
    states, _, block, _ = both_ref.shape
    rows = lax.broadcasted_iota(jnp.int32, (block, block), 0)
    columns = lax.broadcasted_iota(jnp.int32, (block, block), 1)
    unit = (rows == columns).astype(jnp.float32)

    def halves(x):
        high = x.astype(jnp.bfloat16)
        return high, (x - high.astype(jnp.float32)).astype(jnp.bfloat16)

    def product(x, y, contract=((1,), (0,))):
        (x_high, x_low), (y_high, y_low) = halves(x), halves(y)
        parts = [
            lax.dot_general(left, right, (contract, ((), ())), preferred_element_type=jnp.float32)
            for left, right in ((x_high, y_low), (x_low, y_high), (x_high, y_high))
        ]
        return parts[0] + parts[1] + parts[2]

    scale, energy, factor, square, centre_sq = quotient(table_ref[...], entry_count)
    vector = updated(
        both_ref[:, 0].reshape(states * block, block),
        both_ref[:, 1].reshape(states * block, block),
        scale,
        energy,
        factor,
    ) * lax.rsqrt(square + TINY)
    centre = centre_ref[...].astype(jnp.float32) * lax.rsqrt(centre_sq + TINY)
    grams = [product(x, x, ((0,), (0,))) for x in (vector, centre)]
    totals = [unit, unit]
    for step in range(POLAR):
        factors = [1.5 * unit - 0.5 * gram for gram in grams]
        totals = [
            factor if step == 0 else product(total, factor)
            for total, factor in zip(totals, factors)
        ]
        if step < POLAR - 1:
            grams = [
                product(product(factor, gram), factor) for gram, factor in zip(grams, factors)
            ]
    closing = product(totals[0], product(centre, totals[1]), ((1,), (1,)))
    out_ref[...] = product(vector, closing).reshape(states, block, block).astype(jnp.bfloat16)


def call(kernel, out_shape, scratch_shapes, flops, operands):
    return pl.pallas_call(
        kernel,
        out_shape=out_shape,
        scratch_shapes=scratch_shapes,
        compiler_params=pltpu.CompilerParams(vmem_limit_bytes=VMEM_LIMIT),
        cost_estimate=pl.CostEstimate(
            flops=flops,
            bytes_accessed=sum(int(np.prod(x.shape)) * x.dtype.itemsize for x in operands),
            transcendentals=0,
        ),
    )(*operands)


def float_out(*shape):
    return jax.ShapeDtypeStruct(shape, jnp.float32)


def half_out(*shape):
    return jax.ShapeDtypeStruct(shape, jnp.bfloat16)


def work(states, channels, block):
    return 4 * states * channels * block**3 + 2 * (states * channels * block) ** 2


def expanded(weight, groups, channels, states):
    spread = spread_matrix(groups, channels, states)
    sizes = tuple(even(len(group)) * ROWS for group in groups)
    return call(
        functools.partial(expand_kernel, sizes),
        half_out(spread.shape[0], -(-max(sizes) // 128) * 128),
        [],
        2 * spread.size * spread.shape[0],
        (weight, jnp.asarray(spread, jnp.bfloat16)),
    )


def left_front(env, tensors, weight, groups):
    channels, block = count_channels(env), env[0].shape[1]
    states, pieces = tensors.shape[1], len(env)
    outs = call(
        functools.partial(left_kernel, groups, states, pieces),
        [half_out(channels // pieces, block, block)] * (states * pieces),
        [pltpu.VMEM((states * channels * block // PARTS, block), jnp.float32)],
        work(states, channels, block),
        (*env, tensors, weight),
    )
    return [outs[s * pieces : (s + 1) * pieces] for s in range(states)]


def left_close(iso, gathered, moved):
    channels, block, _ = gathered.shape
    return call(
        left_close_kernel,
        (half_out(channels, block, block), float_out(ROWS, block)),
        [],
        2 * channels * block**3,
        (iso, gathered, moved),
    )


def right_whole(envs, own, tensors, weight, groups):
    channels, block = count_channels(envs[0]), envs[0][0].shape[1]
    states, pieces = len(envs), len(envs[0])
    outs = call(
        functools.partial(right_kernel, groups, states, pieces),
        [half_out(channels // pieces, block, block)] * pieces + [float_out(ROWS, block)],
        [
            pltpu.VMEM((states * channels * block // PARTS, block), jnp.float32),
            pltpu.VMEM((states * channels * block, block), jnp.bfloat16),
        ],
        work(states, channels, block),
        (*(chunk for env in envs for chunk in env), own, tensors, weight),
    )
    return outs[:pieces], outs[pieces]


def front_scratch(states, channels, block):
    return [pltpu.VMEM((states * channels * block // PARTS, block), jnp.float32)]


def operator_front(env, weight, groups, classes):
    channels, block = count_channels(env), env[0].shape[1]
    states, pieces = classes[0].shape[0], len(env)
    return call(
        functools.partial(operator_front_kernel, groups, states, pieces),
        half_out(states * channels * block, block),
        front_scratch(states, channels, block),
        work(states, channels, block),
        (*env, weight, *classes),
    )


def operator_back(rights, squares, gathered, vector):
    channels, block = count_channels(rights[0]), rights[0][0].shape[1]
    states, pieces = len(rights), len(rights[0])
    return call(
        functools.partial(operator_back_kernel, states, pieces),
        (
            float_out(states, block, block),
            half_out(states * block + UNIT_ROWS, block),
            float_out(1, LANES),
        ),
        [],
        2 * states * channels * block**3,
        (*(chunk for right in rights for chunk in right), *squares, gathered, vector),
    )


def operator_whole(env, weight, groups, classes, rights):
    channels, block = count_channels(env), env[0].shape[1]
    states, pieces = len(rights), len(env)
    front = (*env, weight, *classes)
    return call(
        functools.partial(operator_whole_kernel, groups, states, pieces, len(front)),
        (float_out(states, block, block), float_out(1, LANES)),
        [
            pltpu.VMEM((states * channels * block, block), jnp.bfloat16),
            pltpu.VMEM((CLASSES, states, block, block), jnp.bfloat16),
            *front_scratch(states, channels, block),
        ],
        work(states, channels, block) + 2 * states * channels * block**3,
        (*front, *(chunk for right in rights for chunk in right)),
    )


def renewed(table, vector, image, second, unit, squares, entry_count):
    states, block, _ = vector.shape
    return call(
        functools.partial(renew_kernel, entry_count),
        (float_out(states, 2, block, block), float_out(1, LANES)),
        [],
        0,
        (table, vector, image, second, unit, *squares),
    )


def polar(both, table, centre, entry_count):
    states, _, block, _ = both.shape
    return call(
        functools.partial(polar_kernel, entry_count),
        half_out(states, block, block),
        [],
        600 * block**3,
        (both, table, centre),
    )


def energy_of(table, entry_count):
    return call(
        functools.partial(energy_kernel, entry_count), float_out(1, LANES), [], 0, (table,)
    )


def charge_mask(channels, states, sectors):
    charge = np.array([CHARGE_STEPS[channel % CLASSES] for channel in range(channels)])
    state = np.arange(states)
    balance = (
        charge[:, None, None, None]
        + state[None, None, None, :]
        - state[None, None, :, None]
        - charge[None, :, None, None]
    )
    return jnp.asarray((balance % sectors == 0).astype(np.float32)).astype(jnp.bfloat16)


def weight_matrices(mpo, pattern, sectors):
    channels, _, states, _ = mpo.shape
    allowed = charge_mask(channels, states, sectors)
    weights = mpo * pattern[:, :, None, None].astype(jnp.bfloat16) * allowed
    size = states * channels
    left = jnp.transpose(weights, (2, 1, 3, 0)).reshape(size, size)
    right = jnp.transpose(weights, (2, 0, 3, 1)).reshape(size, size)
    return jnp.stack([left, right])


def other_classes_of(places, x):
    one, minus = places.ahead(x, 1), places.ahead(x, -1)
    return one, minus, places.ahead(one, 1), places.ahead(minus, -1)


def other_classes_at_once(places, x):
    return tuple(places.ahead(x, charge) for charge in CHARGE_STEPS[1:])


def after(first, then):
    return lax.optimization_barrier((first, then))


def local(left_iso, right_iso, centre, left_env, right_env, mpo, pattern):
    sites, secs = lax.axis_size("site"), lax.axis_size("sec")
    places = Places(sites, secs)
    left_iso, right_iso, centre = left_iso[0, :, 0], right_iso[0, :, 0], centre[0, 0]
    states, block, _ = left_iso.shape
    channels = mpo.shape[1]
    entry_count = left_env.size * secs
    left_groups = label_groups(channels, states, secs, 1)
    right_groups = label_groups(channels, states, secs, -1)

    pieces = PIECES if channels % PIECES == 0 else 1

    def ahead(env, by, chain_by=0):
        return [places.ahead(chunk, by, chain_by) for chunk in env]

    first = places.fetch(jnp.concatenate([right_env[0, :, 0], left_iso, right_iso]))
    left_isos = [first[channels : channels + states]]
    right_isos = [first[channels + states :]]
    for step in range(1, ENV_STEPS):
        left_isos.append(places.fetch(left_iso, step))
        right_isos.append(places.fetch(right_iso, -step))
    own_tensors = places.fetch(jnp.concatenate([left_iso, centre[None]]), ENV_STEPS)
    right = jnp.split(first[:channels], pieces)
    right, left_env = after(right, left_env)
    left = jnp.split(places.fetch(left_env[0, :, 0]), pieces)
    rolled = []
    for step in range(ENV_STEPS):
        isos = jnp.concatenate([left_isos[step], right_isos[step]])
        others = other_classes_at_once if step == 0 else other_classes_of
        rolled.append(jnp.stack([isos, *others(places, isos)]))
    own_iso, own_centre = own_tensors[:states], own_tensors[states]
    centres = [own_centre] + [places.ahead(own_centre, s) for s in range(1, states)]

    gathered_weights = lax.all_gather(weight_matrices(mpo[0], pattern[0], secs), "site")
    chain = places.my_chain()

    def weight_of(site_by, kind):
        weight = lax.dynamic_index_in_dim(
            gathered_weights, (chain + site_by) % sites, 0, False
        )[kind]
        return expanded(weight, (left_groups, right_groups)[kind], channels, states)

    weights = (
        [weight_of(step, 0) for step in range(ENV_STEPS + 1)],
        [weight_of(-step, 1) for step in range(ENV_STEPS)],
    )
    vector = jnp.einsum(
        "sxy,syz->sxz", own_iso, jnp.stack(centres), preferred_element_type=jnp.float32
    )
    half_vector = vector.astype(jnp.bfloat16)
    rolled_vector = (half_vector, *other_classes_of(places, half_vector))
    right, (vector, weights) = after(right, (vector, weights))
    centre_float = own_centre.astype(jnp.float32)
    centre_square = jnp.sum((centre_float * centre_float).reshape(-1, ROWS, block), axis=0)

    left_squares, right_squares = [], []
    for step in range(ENV_STEPS):
        envs = [right]
        for t in range(1, states):
            if step == 0 and t == states - 1:
                left, envs[-1] = after(left, envs[-1])
            envs.append(ahead(envs[-1], 1))
        gathered = left_front(left, rolled[step][:, :states], weights[0][step], left_groups)

        def left_part(s, piece):
            return jnp.einsum(
                "xy,vxz->vyz",
                left_isos[step][s],
                gathered[s][piece],
                preferred_element_type=jnp.float32,
            )

        sent = [left_part(states - 1, piece).astype(jnp.bfloat16) for piece in range(pieces)]
        if step == 0:
            (rolled, rolled_vector, sent), envs = after((rolled, rolled_vector, sent), envs)
        right, square = right_whole(
            envs,
            right_isos[step],
            rolled[step][:, states:],
            weights[1][step],
            right_groups,
        )
        right_squares.append(square)

        moved = [places.ahead(chunk, -1) for chunk in sent]
        for s in reversed(range(1, states - 1)):
            for piece in range(pieces):
                part = left_part(s, piece) + moved[piece].astype(jnp.float32)
                moved[piece] = places.ahead(part.astype(jnp.bfloat16), -1)
        closed = [
            left_close(left_isos[step][0], gathered[0][piece], moved[piece])
            for piece in range(pieces)
        ]
        left = [env for env, _ in closed]
        left_squares.append(sum(square for _, square in closed))

    if (2 * ENV_STEPS) % sites:
        right = ahead(right, 0, 2 * ENV_STEPS)
        right_squares = ahead(right_squares, 0, 2 * ENV_STEPS)
    squares = left_squares + right_squares + [centre_square]
    rights = [right]
    for s in range(1, states):
        rights.append(ahead(rights[-1], 1))
    weight = weights[0][ENV_STEPS]
    gathered = operator_front(left, weight, left_groups, rolled_vector)
    image, sent, own_sums = operator_back(rights, squares, gathered, vector)
    rolled_image = (sent, *other_classes_at_once(places, sent))
    second, unit = operator_whole(left, weight, left_groups, rolled_image, rights)
    table = places.collect(own_sums)
    both, own_sums = renewed(table, vector, image, second, unit, squares, entry_count)
    table = places.collect(own_sums)

    columns = jnp.stack([both[0]] + [places.ahead(both[s], -s) for s in range(1, states)])
    home_table = places.send_home(table, ENV_STEPS, 0)
    home_table, columns = after(home_table, columns)
    column_left = polar(columns, table, own_centre, entry_count)
    new_left = jnp.stack(
        [places.send_home(column_left[s], ENV_STEPS, -s) for s in range(states)]
    )
    energy = energy_of(home_table, entry_count)
    return new_left[None, :, None], energy[0, :1]


def solution(mesh):
    placed = (
        P("site", None, "sec", None, None),
        P("site", None, "sec", None, None),
        P("site", "sec", None, None),
        P("site", None, "sec", None, None),
        P("site", None, "sec", None, None),
        P("site", None, None, None, None),
        P("site", None, None),
    )
    return jax.shard_map(
        local,
        mesh=mesh,
        in_specs=placed,
        out_specs=(P("site", None, "sec", None, None), P("site")),
        check_vma=False,
    )
```

```python
import functools

import jax
import jax.numpy as jnp
import numpy as np
from jax import lax
from jax.experimental import pallas as pl
from jax.experimental.pallas import tpu as pltpu
from jax.sharding import PartitionSpec as P

ENV_STEPS = 2
POLAR = 6

TINY = 1e-06
CHARGE_STEPS = (0, 1, -1, 2, -2)
CLASSES = len(CHARGE_STEPS)
BOTH = ("site", "sec")
VMEM_LIMIT = 20 * 1024 * 1024
PIECES = 2


class Places:
    def __init__(self, sites, secs):
        self.sites, self.secs = sites, secs
        self.half = secs // 2
        self.up = (self.half + 1) // 2

    def home(self, site, sector):
        return (site % self.sites) * self.secs + sector % self.secs

    def position(self, place):
        back = self.half - 1 + self.up - place
        if isinstance(place, int):
            return place if place < self.up else back
        return jnp.where(place < self.up, place, back)

    def slot(self, chain, sector):
        chain, sector = chain % self.sites, sector % self.secs
        place = chain % 2 * self.half + self.position(sector // 2)
        return (chain // 2 * 2 + sector % 2) * self.secs + place

    def pairs(self, source, target):
        return [
            (source(chain, sector), target(chain, sector))
            for chain in range(self.sites)
            for sector in range(self.secs)
        ]

    def fetch(self, x, site_by=0, sec_by=0):
        return lax.ppermute(
            x, BOTH, self.pairs(lambda g, k: self.home(g + site_by, k + sec_by), self.slot)
        )

    def send_home(self, x, site_by, sec_by):
        return lax.ppermute(
            x, BOTH, self.pairs(self.slot, lambda g, k: self.home(g + site_by, k + sec_by))
        )

    def ahead(self, x, by, chain_by=0):
        return lax.ppermute(
            x, BOTH, self.pairs(lambda g, k: self.slot(g + chain_by, k + by), self.slot)
        )

    def partner(self, x, bit):
        return lax.ppermute(x, BOTH, self.pairs(lambda g, k: self.slot(g, k ^ bit), self.slot))

    def my_chain(self):
        return lax.axis_index("site") // 2 * 2 + lax.axis_index("sec") // self.half

    def my_sector(self):
        position = self.position(lax.axis_index("sec") % self.half)
        return 2 * position + lax.axis_index("site") % 2

    def collect(self, values):
        sector = self.my_sector()
        table = values
        bit = 1
        while bit < self.secs:
            other = self.partner(table, bit)
            first = (sector & bit) == 0
            table = jnp.where(
                first, jnp.concatenate([table, other]), jnp.concatenate([other, table])
            )
            bit *= 2
        return table


ROWS = 8
PARTS = 2


def label_groups(channels, states, sectors, sign):
    groups = {}
    for state in range(states):
        for channel in range(channels):
            label = (state + sign * CHARGE_STEPS[channel % CLASSES]) % sectors
            groups.setdefault(label, []).append((state, channel))
    return [groups[label] for label in sorted(groups)]


def even(count):
    return count + count % 2


def spread_matrix(groups, channels, states):
    rows = []
    for group in groups:
        block = np.zeros((even(len(group)), ROWS, states * channels), np.float32)
        for index, (state, channel) in enumerate(group):
            block[index, :, state * channels + channel] = 1
        rows.append(block.reshape(-1, states * channels))
    return np.concatenate(rows)


def expand_kernel(sizes, weight_ref, spread_ref, out_ref):
    start = 0
    for size in sizes:
        spread = spread_ref[pl.ds(start, size), :]
        picked = jnp.dot(spread, weight_ref[...], preferred_element_type=jnp.float32)
        full = lax.dot_general(
            picked.astype(jnp.bfloat16),
            spread,
            (((1,), (1,)), ((), ())),
            preferred_element_type=jnp.float32,
        )
        row = lax.broadcasted_iota(jnp.int32, full.shape, 0)
        column = lax.broadcasted_iota(jnp.int32, full.shape, 1)
        same = lax.rem(row, ROWS) == lax.rem(column, ROWS)
        out_ref[pl.ds(start, size), pl.ds(0, size)] = jnp.where(same, full, 0.0).astype(
            jnp.bfloat16
        )
        start += size


def mix_channels(groups, channels, weight_ref, mixed_ref, write, offset, height):
    def step(index, carry):
        first = pl.multiple_of(index * 2 * ROWS, 2 * ROWS)
        start = 0
        for group in groups:
            size = even(len(group)) * ROWS
            parts = []
            for state, channel in group:
                rows = (state * channels + channel) * height + first
                halves = [
                    mixed_ref[pl.ds(pl.multiple_of(rows + half * ROWS, ROWS), ROWS), :]
                    for half in range(2)
                ]
                parts.append(jnp.concatenate(halves, axis=1))
            if len(group) % 2:
                parts.append(parts[0])
            operand = jnp.concatenate(parts, axis=0).astype(jnp.bfloat16)
            product = jnp.dot(
                weight_ref[pl.ds(start, size), pl.ds(0, size)],
                operand,
                preferred_element_type=jnp.float32,
            )
            block = product.shape[1] // 2
            for number, pair in enumerate(group):
                rows = product[number * ROWS : (number + 1) * ROWS]
                both = jnp.concatenate([rows[:, :block], rows[:, block:]], axis=0)
                write(*pair, pl.multiple_of(offset + first, 2 * ROWS), both.astype(jnp.bfloat16))
            start += size
        return carry

    lax.fori_loop(0, height // (2 * ROWS), step, 0)


def by_parts(block, body):
    height = block // PARTS

    def one(part, carry):
        body(pl.multiple_of(part * height, height), height)
        return carry

    lax.fori_loop(0, PARTS, one, 0)


def into(gathered_ref, channels, block):
    def write(state, channel, first, rows):
        start = (state * channels + channel) * block
        gathered_ref[pl.ds(pl.multiple_of(start + first, 2 * ROWS), 2 * ROWS), :] = rows

    return write


def batches(items, most):
    pieces = -(-len(items) // most)
    size = -(-len(items) // pieces)
    return [items[start : start + size] for start in range(0, len(items), size)]


def rows_of(chunks, channel, offset, height):
    size = chunks[0].shape[0]
    return chunks[channel // size][channel % size, pl.ds(offset, height), :]


def channel_of(chunks, channel):
    size = chunks[0].shape[0]
    return chunks[channel // size][channel % size]


def put_channel(chunks, channel, value):
    size = chunks[0].shape[0]
    chunks[channel // size][channel % size] = value


def count_channels(chunks):
    return sum(chunk.shape[0] for chunk in chunks)


def mix_left(env, tensors, mixed_ref, offset, height):
    channels, block = count_channels(env), env[0].shape[1]
    for cls in range(CLASSES):
        right = jnp.concatenate(tensors[cls], axis=1)
        for batch in batches(list(range(cls, channels, CLASSES)), 5):
            rows = jnp.concatenate(
                [rows_of(env, channel, offset, height) for channel in batch], axis=0
            )
            product = jnp.dot(rows, right, preferred_element_type=jnp.float32)
            for number, channel in enumerate(batch):
                for t in range(len(tensors[cls])):
                    mixed_ref[pl.ds((t * channels + channel) * height, height), :] = product[
                        number * height : (number + 1) * height, t * block : (t + 1) * block
                    ]


def left_kernel(groups, states, pieces, *refs):
    env, (tensor_ref, weight_ref) = refs[:pieces], refs[pieces : pieces + 2]
    outs, mixed_ref = refs[pieces + 2 : -1], refs[-1]
    channels, block = count_channels(env), env[0].shape[1]

    def write(state, channel, first, rows):
        size = channels // pieces
        out_ref = outs[state * pieces + channel // size]
        out_ref[channel % size, pl.ds(first, 2 * ROWS), :] = rows

    def body(offset, height):
        tensors = [[tensor_ref[cls, t] for t in range(states)] for cls in range(CLASSES)]
        mix_left(env, tensors, mixed_ref, offset, height)
        mix_channels(groups, channels, weight_ref, mixed_ref, write, offset, height)

    by_parts(block, body)


def left_close_kernel(iso_ref, gathered_ref, moved_ref, out_ref, square_ref):
    channels, block, _ = gathered_ref.shape
    square = jnp.zeros((ROWS, block), jnp.float32)
    for batch in batches(list(range(channels)), 2):
        right = jnp.concatenate([gathered_ref[channel] for channel in batch], axis=1)
        product = lax.dot_general(
            iso_ref[...], right, (((0,), (0,)), ((), ())), preferred_element_type=jnp.float32
        )
        for number, channel in enumerate(batch):
            part = product[:, number * block : (number + 1) * block]
            part = part + moved_ref[channel].astype(jnp.float32)
            out_ref[channel] = part.astype(jnp.bfloat16)
            square = square + jnp.sum((part * part).reshape(-1, ROWS, block), axis=0)
    square_ref[...] = square


def right_kernel(groups, states, pieces, *refs):
    envs = [refs[t * pieces : (t + 1) * pieces] for t in range(states)]
    refs = refs[states * pieces :]
    own_ref, tensor_ref, weight_ref = refs[:3]
    outs, (square_ref, mixed_ref, gathered_ref) = refs[3 : 3 + pieces], refs[3 + pieces :]
    channels, block = count_channels(envs[0]), envs[0][0].shape[1]
    zero = jnp.zeros((block, block), jnp.bfloat16)
    write = into(gathered_ref, channels, block)

    def body(offset, height):
        for pair in batches(list(range(states)), 2):
            own = jnp.concatenate(
                [
                    jnp.concatenate([own_ref[t] if t == other else zero for other in pair], axis=1)
                    for t in pair
                ],
                axis=0,
            )
            for batch in batches(list(range(channels)), 6):
                rows = jnp.concatenate(
                    [
                        jnp.concatenate(
                            [rows_of(envs[t], channel, offset, height) for channel in batch], axis=0
                        )
                        for t in pair
                    ],
                    axis=1,
                )
                product = lax.dot_general(
                    rows, own, (((1,), (1,)), ((), ())), preferred_element_type=jnp.float32
                )
                for number, t in enumerate(pair):
                    start = (t * channels + batch[0]) * height
                    mixed_ref[pl.ds(start, len(batch) * height), :] = product[
                        :, number * block : (number + 1) * block
                    ]
        mix_channels(groups, channels, weight_ref, mixed_ref, write, offset, height)

    by_parts(block, body)
    square = jnp.zeros((ROWS, block), jnp.float32)
    for cls in range(CLASSES):
        left = jnp.concatenate([tensor_ref[cls, s] for s in range(states)], axis=1)
        for batch in batches(list(range(cls, channels, CLASSES)), 2):
            right = jnp.concatenate(
                [
                    jnp.concatenate(
                        [
                            gathered_ref[pl.ds((s * channels + channel) * block, block), :]
                            for s in range(states)
                        ],
                        axis=0,
                    )
                    for channel in batch
                ],
                axis=1,
            )
            product = jnp.dot(left, right, preferred_element_type=jnp.float32)
            for number, channel in enumerate(batch):
                part = product[:, number * block : (number + 1) * block]
                put_channel(outs, channel, part.astype(jnp.bfloat16))
                square = square + jnp.sum((part * part).reshape(-1, ROWS, block), axis=0)
    square_ref[...] = square


ENV_LANE = 5
LANES = 128


def quotient(table, entry_count):
    def total(x):
        return jnp.sum(x, axis=0, keepdims=True)

    squares = [
        total(table[:, lane : lane + 1]) for lane in range(ENV_LANE, ENV_LANE + 2 * ENV_STEPS + 1)
    ]
    scale = jnp.ones((1, 1), jnp.float32)
    for side in range(2):
        side_scale = jnp.ones((1, 1), jnp.float32)
        for square in squares[side * ENV_STEPS : (side + 1) * ENV_STEPS]:
            side_scale = side_scale * lax.rsqrt(side_scale * side_scale * square / entry_count + TINY)
        scale = scale * side_scale
    a, b, e, c, unit = (table[:, lane : lane + 1] for lane in range(ENV_LANE))
    a, e, unit = scale * a, scale * e, scale * unit
    c = unit * unit * c
    whole_a, whole_b = total(a), total(b)
    energy = whole_a / (whole_b + TINY)
    off = e - energy
    residual_sq = total(c + 2.0 * off * (a - e * b) + off * off * b)
    factor = 0.5 * jnp.sqrt(whole_b / (residual_sq + TINY))
    square = whole_b - 2.0 * factor * (whole_a - energy * whole_b) + factor * factor * residual_sq
    return scale, energy, factor, square, squares[2 * ENV_STEPS]


def updated(vector, image, scale, energy, factor):
    return vector - factor * (scale * image - energy * vector)


def sum_all(x):
    return jnp.sum(jnp.sum(x, axis=0, keepdims=True), axis=1, keepdims=True)


def operator_front_kernel(groups, states, pieces, *refs):
    env, refs = refs[:pieces], refs[pieces:]
    weight_ref, classes, refs = refs[0], refs[1 : 1 + CLASSES], refs[1 + CLASSES :]
    gathered_ref, mixed_ref = refs
    channels, block = count_channels(env), env[0].shape[1]
    write = into(gathered_ref, channels, block)

    def body(offset, height):
        tensors = [[classes[cls][t] for t in range(states)] for cls in range(CLASSES)]
        mix_left(env, tensors, mixed_ref, offset, height)
        mix_channels(groups, channels, weight_ref, mixed_ref, write, offset, height)

    by_parts(block, body)


def products(rights, gathered_ref, s):
    channels, block = count_channels(rights[0]), rights[0][0].shape[1]
    total = jnp.zeros((block, block), jnp.float32)
    for batch in batches(list(range(channels)), 6):
        left = jnp.concatenate(
            [gathered_ref[pl.ds((s * channels + channel) * block, block), :] for channel in batch],
            axis=1,
        )
        right = jnp.concatenate([channel_of(rights[s], channel) for channel in batch], axis=0)
        total = total + jnp.dot(left, right, preferred_element_type=jnp.float32)
    return total


def write_sums(vector, image, squares, sums_ref):
    a, b = sum_all(vector * image), sum_all(vector * vector)
    e = jnp.where(b > 0, a / jnp.where(b > 0, b, 1.0), 0.0)
    residual = image - e * vector
    unit = jnp.max(jnp.max(jnp.abs(residual), axis=0, keepdims=True), axis=1, keepdims=True)
    unit = jnp.where(unit > 0, unit, 1.0)
    residual = residual / unit
    lane = lax.broadcasted_iota(jnp.int32, sums_ref.shape, 1)
    sums = jnp.zeros(sums_ref.shape, jnp.float32)
    values = (a, b, e, sum_all(residual * residual), unit, *(sum_all(x[...]) for x in squares))
    for place, value in enumerate(values):
        sums = jnp.where(lane == place, value, sums)
    sums_ref[...] = sums


def flat(ref):
    states, block, _ = ref.shape
    return ref[...].reshape(states * block, block)


UNIT_ROWS = 16


def power_above(x):
    top = jnp.max(jnp.max(jnp.abs(x), axis=0, keepdims=True), axis=1, keepdims=True)
    steps = jnp.ceil(jnp.log(jnp.where(top > 0, top, 1.0)) * (1 / np.log(2)))
    return jnp.exp(steps * np.log(2)).astype(jnp.bfloat16).astype(jnp.float32)


def operator_back_kernel(states, pieces, *refs):
    rights = [refs[t * pieces : (t + 1) * pieces] for t in range(states)]
    refs = refs[states * pieces :]
    squares, refs = refs[: 2 * ENV_STEPS + 1], refs[2 * ENV_STEPS + 1 :]
    gathered_ref, vector_ref, image_ref, half_ref, sums_ref = refs
    for s in range(states):
        image_ref[s] = products(rights, gathered_ref, s)
    image = flat(image_ref)
    unit = power_above(image)
    half_ref[: image.shape[0]] = (image / unit).astype(jnp.bfloat16)
    half_ref[image.shape[0] :] = jnp.broadcast_to(unit, (UNIT_ROWS, LANES)).astype(jnp.bfloat16)
    write_sums(flat(vector_ref), image, squares, sums_ref)


def operator_whole_kernel(groups, states, pieces, front_count, *refs):
    front, refs = refs[:front_count], refs[front_count:]
    env_and_weight, sent = front[:-CLASSES], front[-CLASSES:]
    rights = [refs[t * pieces : (t + 1) * pieces] for t in range(states)]
    image_ref, unit_ref, gathered_ref, tensor_ref, mixed_ref = refs[states * pieces :]
    block = image_ref.shape[1]
    units = [
        x[pl.ds(states * block, UNIT_ROWS), :].astype(jnp.float32)[:1, :1] for x in sent
    ]
    unit = functools.reduce(jnp.maximum, units)
    unit_ref[...] = jnp.broadcast_to(unit, unit_ref.shape)
    for cls in range(CLASSES):
        for t in range(states):
            tensor = sent[cls][pl.ds(t * block, block), :].astype(jnp.float32)
            tensor_ref[cls, t] = (tensor * (units[cls] / unit)).astype(jnp.bfloat16)
    classes = [tensor_ref.at[cls] for cls in range(CLASSES)]
    operator_front_kernel(groups, states, pieces, *env_and_weight, *classes, gathered_ref, mixed_ref)
    for s in range(states):
        image_ref[s] = products(rights, gathered_ref, s)


def renew_kernel(entry_count, *refs):
    table_ref, vector_ref, image_ref, second_ref, unit_ref = refs[:5]
    squares, (both_ref, sums_ref) = refs[5:-2], refs[-2:]
    states, block, _ = vector_ref.shape
    scale, energy, factor, _, _ = quotient(table_ref[...], entry_count)
    vector, image = flat(vector_ref), flat(image_ref)
    part = factor * (scale * unit_ref[:, :1])
    new_image = (1.0 + factor * energy) * image - part * flat(second_ref)
    new = updated(vector, image, scale, energy, factor)
    both_ref[:, 0] = new.reshape(states, block, block)
    both_ref[:, 1] = new_image.reshape(states, block, block)
    write_sums(new, new_image, squares, sums_ref)


def energy_kernel(entry_count, table_ref, out_ref):
    energy = quotient(table_ref[...], entry_count)[1]
    out_ref[...] = jnp.broadcast_to(energy, out_ref.shape)


def polar_kernel(entry_count, both_ref, table_ref, centre_ref, out_ref):
    states, _, block, _ = both_ref.shape
    rows = lax.broadcasted_iota(jnp.int32, (block, block), 0)
    columns = lax.broadcasted_iota(jnp.int32, (block, block), 1)
    unit = (rows == columns).astype(jnp.float32)

    def halves(x):
        high = x.astype(jnp.bfloat16)
        return high, (x - high.astype(jnp.float32)).astype(jnp.bfloat16)

    def product(x, y, contract=((1,), (0,))):
        (x_high, x_low), (y_high, y_low) = halves(x), halves(y)
        parts = [
            lax.dot_general(left, right, (contract, ((), ())), preferred_element_type=jnp.float32)
            for left, right in ((x_high, y_low), (x_low, y_high), (x_high, y_high))
        ]
        return parts[0] + parts[1] + parts[2]

    scale, energy, factor, square, centre_sq = quotient(table_ref[...], entry_count)
    vector = updated(
        both_ref[:, 0].reshape(states * block, block),
        both_ref[:, 1].reshape(states * block, block),
        scale,
        energy,
        factor,
    ) * lax.rsqrt(square + TINY)
    centre = centre_ref[...].astype(jnp.float32) * lax.rsqrt(centre_sq + TINY)
    grams = [product(x, x, ((0,), (0,))) for x in (vector, centre)]
    totals = [unit, unit]
    for step in range(POLAR):
        factors = [1.5 * unit - 0.5 * gram for gram in grams]
        totals = [
            factor if step == 0 else product(total, factor)
            for total, factor in zip(totals, factors)
        ]
        if step < POLAR - 1:
            grams = [
                product(product(factor, gram), factor) for gram, factor in zip(grams, factors)
            ]
    closing = product(totals[0], product(centre, totals[1]), ((1,), (1,)))
    out_ref[...] = product(vector, closing).reshape(states, block, block).astype(jnp.bfloat16)


def call(kernel, out_shape, scratch_shapes, flops, operands):
    return pl.pallas_call(
        kernel,
        out_shape=out_shape,
        scratch_shapes=scratch_shapes,
        compiler_params=pltpu.CompilerParams(vmem_limit_bytes=VMEM_LIMIT),
        cost_estimate=pl.CostEstimate(
            flops=flops,
            bytes_accessed=sum(int(np.prod(x.shape)) * x.dtype.itemsize for x in operands),
            transcendentals=0,
        ),
    )(*operands)


def float_out(*shape):
    return jax.ShapeDtypeStruct(shape, jnp.float32)


def half_out(*shape):
    return jax.ShapeDtypeStruct(shape, jnp.bfloat16)


def work(states, channels, block):
    return 4 * states * channels * block**3 + 2 * (states * channels * block) ** 2


def expanded(weight, groups, channels, states):
    spread = spread_matrix(groups, channels, states)
    sizes = tuple(even(len(group)) * ROWS for group in groups)
    return call(
        functools.partial(expand_kernel, sizes),
        half_out(spread.shape[0], -(-max(sizes) // 128) * 128),
        [],
        2 * spread.size * spread.shape[0],
        (weight, jnp.asarray(spread, jnp.bfloat16)),
    )


def left_front(env, tensors, weight, groups):
    channels, block = count_channels(env), env[0].shape[1]
    states, pieces = tensors.shape[1], len(env)
    outs = call(
        functools.partial(left_kernel, groups, states, pieces),
        [half_out(channels // pieces, block, block)] * (states * pieces),
        [pltpu.VMEM((states * channels * block // PARTS, block), jnp.float32)],
        work(states, channels, block),
        (*env, tensors, weight),
    )
    return [outs[s * pieces : (s + 1) * pieces] for s in range(states)]


def left_close(iso, gathered, moved):
    channels, block, _ = gathered.shape
    return call(
        left_close_kernel,
        (half_out(channels, block, block), float_out(ROWS, block)),
        [],
        2 * channels * block**3,
        (iso, gathered, moved),
    )


def right_whole(envs, own, tensors, weight, groups):
    channels, block = count_channels(envs[0]), envs[0][0].shape[1]
    states, pieces = len(envs), len(envs[0])
    outs = call(
        functools.partial(right_kernel, groups, states, pieces),
        [half_out(channels // pieces, block, block)] * pieces + [float_out(ROWS, block)],
        [
            pltpu.VMEM((states * channels * block // PARTS, block), jnp.float32),
            pltpu.VMEM((states * channels * block, block), jnp.bfloat16),
        ],
        work(states, channels, block),
        (*(chunk for env in envs for chunk in env), own, tensors, weight),
    )
    return outs[:pieces], outs[pieces]


def front_scratch(states, channels, block):
    return [pltpu.VMEM((states * channels * block // PARTS, block), jnp.float32)]


def operator_front(env, weight, groups, classes):
    channels, block = count_channels(env), env[0].shape[1]
    states, pieces = classes[0].shape[0], len(env)
    return call(
        functools.partial(operator_front_kernel, groups, states, pieces),
        half_out(states * channels * block, block),
        front_scratch(states, channels, block),
        work(states, channels, block),
        (*env, weight, *classes),
    )


def operator_back(rights, squares, gathered, vector):
    channels, block = count_channels(rights[0]), rights[0][0].shape[1]
    states, pieces = len(rights), len(rights[0])
    return call(
        functools.partial(operator_back_kernel, states, pieces),
        (
            float_out(states, block, block),
            half_out(states * block + UNIT_ROWS, block),
            float_out(1, LANES),
        ),
        [],
        2 * states * channels * block**3,
        (*(chunk for right in rights for chunk in right), *squares, gathered, vector),
    )


def operator_whole(env, weight, groups, classes, rights):
    channels, block = count_channels(env), env[0].shape[1]
    states, pieces = len(rights), len(env)
    front = (*env, weight, *classes)
    return call(
        functools.partial(operator_whole_kernel, groups, states, pieces, len(front)),
        (float_out(states, block, block), float_out(1, LANES)),
        [
            pltpu.VMEM((states * channels * block, block), jnp.bfloat16),
            pltpu.VMEM((CLASSES, states, block, block), jnp.bfloat16),
            *front_scratch(states, channels, block),
        ],
        work(states, channels, block) + 2 * states * channels * block**3,
        (*front, *(chunk for right in rights for chunk in right)),
    )


def renewed(table, vector, image, second, unit, squares, entry_count):
    states, block, _ = vector.shape
    return call(
        functools.partial(renew_kernel, entry_count),
        (float_out(states, 2, block, block), float_out(1, LANES)),
        [],
        0,
        (table, vector, image, second, unit, *squares),
    )


def polar(both, table, centre, entry_count):
    states, _, block, _ = both.shape
    return call(
        functools.partial(polar_kernel, entry_count),
        half_out(states, block, block),
        [],
        600 * block**3,
        (both, table, centre),
    )


def energy_of(table, entry_count):
    return call(
        functools.partial(energy_kernel, entry_count), float_out(1, LANES), [], 0, (table,)
    )


def charge_mask(channels, states, sectors):
    charge = np.array([CHARGE_STEPS[channel % CLASSES] for channel in range(channels)])
    state = np.arange(states)
    balance = (
        charge[:, None, None, None]
        + state[None, None, None, :]
        - state[None, None, :, None]
        - charge[None, :, None, None]
    )
    return jnp.asarray((balance % sectors == 0).astype(np.float32)).astype(jnp.bfloat16)


def weight_matrices(mpo, pattern, sectors):
    channels, _, states, _ = mpo.shape
    allowed = charge_mask(channels, states, sectors)
    weights = mpo * pattern[:, :, None, None].astype(jnp.bfloat16) * allowed
    size = states * channels
    left = jnp.transpose(weights, (2, 1, 3, 0)).reshape(size, size)
    right = jnp.transpose(weights, (2, 0, 3, 1)).reshape(size, size)
    return jnp.stack([left, right])


def other_classes_of(places, x):
    one, minus = places.ahead(x, 1), places.ahead(x, -1)
    return one, minus, places.ahead(one, 1), places.ahead(minus, -1)


def classes_of(places, x):
    return jnp.stack([x, *other_classes_of(places, x)])


def other_classes_at_once(places, x):
    return tuple(places.ahead(x, charge) for charge in CHARGE_STEPS[1:])


def after(first, then):
    return lax.optimization_barrier((first, then))


def local(left_iso, right_iso, centre, left_env, right_env, mpo, pattern):
    sites, secs = lax.axis_size("site"), lax.axis_size("sec")
    places = Places(sites, secs)
    left_iso, right_iso, centre = left_iso[0, :, 0], right_iso[0, :, 0], centre[0, 0]
    states, block, _ = left_iso.shape
    channels = mpo.shape[1]
    entry_count = left_env.size * secs
    left_groups = label_groups(channels, states, secs, 1)
    right_groups = label_groups(channels, states, secs, -1)

    pieces = PIECES if channels % PIECES == 0 else 1

    def ahead(env, by, chain_by=0):
        return [places.ahead(chunk, by, chain_by) for chunk in env]

    first = places.fetch(jnp.concatenate([right_env[0, :, 0], left_iso, right_iso]))
    left_isos = [first[channels : channels + states]]
    right_isos = [first[channels + states :]]
    for step in range(1, ENV_STEPS):
        left_isos.append(places.fetch(left_iso, step))
        right_isos.append(places.fetch(right_iso, -step))
    own_tensors = places.fetch(jnp.concatenate([left_iso, centre[None]]), ENV_STEPS)
    right = jnp.split(first[:channels], pieces)
    right, left_env = after(right, left_env)
    left = jnp.split(places.fetch(left_env[0, :, 0]), pieces)
    rolled = [
        classes_of(places, jnp.concatenate([left_isos[step], right_isos[step]]))
        for step in range(ENV_STEPS)
    ]
    own_iso, own_centre = own_tensors[:states], own_tensors[states]
    centres = [own_centre] + [places.ahead(own_centre, s) for s in range(1, states)]

    gathered_weights = lax.all_gather(weight_matrices(mpo[0], pattern[0], secs), "site")
    chain = places.my_chain()

    def weight_of(site_by, kind):
        weight = lax.dynamic_index_in_dim(
            gathered_weights, (chain + site_by) % sites, 0, False
        )[kind]
        return expanded(weight, (left_groups, right_groups)[kind], channels, states)

    weights = (
        [weight_of(step, 0) for step in range(ENV_STEPS + 1)],
        [weight_of(-step, 1) for step in range(ENV_STEPS)],
    )
    vector = jnp.einsum(
        "sxy,syz->sxz", own_iso, jnp.stack(centres), preferred_element_type=jnp.float32
    )
    half_vector = vector.astype(jnp.bfloat16)
    rolled_vector = (half_vector, *other_classes_of(places, half_vector))
    right, (vector, weights) = after(right, (vector, weights))
    centre_float = own_centre.astype(jnp.float32)
    centre_square = jnp.sum((centre_float * centre_float).reshape(-1, ROWS, block), axis=0)

    left_squares, right_squares = [], []
    for step in range(ENV_STEPS):
        envs = [right]
        for t in range(1, states):
            if step == 0 and t == states - 1:
                left, envs[-1] = after(left, envs[-1])
            envs.append(ahead(envs[-1], 1))
        if step == 0:
            (rolled, rolled_vector), envs = after((rolled, rolled_vector), envs)
        right, square = right_whole(
            envs,
            right_isos[step],
            rolled[step][:, states:],
            weights[1][step],
            right_groups,
        )
        right_squares.append(square)

        gathered = left_front(left, rolled[step][:, :states], weights[0][step], left_groups)
        moved = [None] * pieces
        for s in reversed(range(1, states)):
            for piece in range(pieces):
                part = jnp.einsum(
                    "xy,vxz->vyz",
                    left_isos[step][s],
                    gathered[s][piece],
                    preferred_element_type=jnp.float32,
                )
                if moved[piece] is not None:
                    part = part + moved[piece].astype(jnp.float32)
                moved[piece] = places.ahead(part.astype(jnp.bfloat16), -1)
        closed = [
            left_close(left_isos[step][0], gathered[0][piece], moved[piece])
            for piece in range(pieces)
        ]
        left = [env for env, _ in closed]
        left_squares.append(sum(square for _, square in closed))

    if (2 * ENV_STEPS) % sites:
        right = ahead(right, 0, 2 * ENV_STEPS)
        right_squares = ahead(right_squares, 0, 2 * ENV_STEPS)
    squares = left_squares + right_squares + [centre_square]
    rights = [right]
    for s in range(1, states):
        rights.append(ahead(rights[-1], 1))
    weight = weights[0][ENV_STEPS]
    gathered = operator_front(left, weight, left_groups, rolled_vector)
    image, sent, own_sums = operator_back(rights, squares, gathered, vector)
    rolled_image = (sent, *other_classes_at_once(places, sent))
    second, unit = operator_whole(left, weight, left_groups, rolled_image, rights)
    table = places.collect(own_sums)
    both, own_sums = renewed(table, vector, image, second, unit, squares, entry_count)
    table = places.collect(own_sums)

    columns = jnp.stack([both[0]] + [places.ahead(both[s], -s) for s in range(1, states)])
    home_table = places.send_home(table, ENV_STEPS, 0)
    home_table, columns = after(home_table, columns)
    column_left = polar(columns, table, own_centre, entry_count)
    new_left = jnp.stack(
        [places.send_home(column_left[s], ENV_STEPS, -s) for s in range(states)]
    )
    energy = energy_of(home_table, entry_count)
    return new_left[None, :, None], energy[0, :1]


def solution(mesh):
    placed = (
        P("site", None, "sec", None, None),
        P("site", None, "sec", None, None),
        P("site", "sec", None, None),
        P("site", None, "sec", None, None),
        P("site", None, "sec", None, None),
        P("site", None, None, None, None),
        P("site", None, None),
    )
    return jax.shard_map(
        local,
        mesh=mesh,
        in_specs=placed,
        out_specs=(P("site", None, "sec", None, None), P("site")),
        check_vma=False,
    )
```
